32 devices in a mesh: fsdp: 32 (over z, y, x, core).
Axes of the slice: x: 2, y: 2, z: 4, core: 2. Of those that a mesh axis runs over, the one named last changes fastest.
Arguments:
- tokens: bfloat16 [8192, 768], P('fsdp'), may hold values from -6 to 6
- row_kind: int32 [32], P('fsdp'), may hold values from 0 to 1, as said below
- w_qkv: bfloat16 [2, 768, 2304], P(None, 'fsdp'), may hold values from -0.21875 to 0.21875
- w_out: bfloat16 [2, 768, 768], P(None, 'fsdp'), may hold values from -0.875 to 0.875
- w_up: bfloat16 [2, 768, 3072], P(None, 'fsdp'), may hold values from -0.21875 to 0.21875
- w_down: bfloat16 [2, 3072, 768], P(None, 'fsdp'), may hold values from -0.109375 to 0.109375
- bias_vectors: bfloat16 [2, 6, 768], P(None, None, 'fsdp'), may hold values from -3 to 3
- gains: bfloat16 [2, 2, 768], P(None, None, 'fsdp'), may hold values from 0.25 to 1.75
- bias_up: bfloat16 [2, 3072], P(None, 'fsdp'), may hold values from -3 to 3
- cotangent: bfloat16 [8192, 768], P('fsdp'), may hold values from -6 to 6
Outputs:
- mixed: bfloat16 [8192, 768], P('fsdp')
- grad_tokens: float32 [8192, 768], P('fsdp')
- grad_w_qkv: float32 [2, 768, 2304], P(None, 'fsdp')
- grad_w_out: float32 [2, 768, 768], P(None, 'fsdp')
- grad_w_up: float32 [2, 768, 3072], P(None, 'fsdp')
- grad_w_down: float32 [2, 3072, 768], P(None, 'fsdp')
- grad_bias_vectors: float32 [2, 6, 768], P(None, None, 'fsdp')
- grad_gains: float32 [2, 2, 768], P(None, None, 'fsdp')
- grad_bias_up: float32 [2, 3072], P(None, 'fsdp')
The draws below stay inside these ranges and needn't reach their ends.
Inputs may be any that keep to these rules, and one draw needn't show every extreme that they name: row_kind[i] equals row_kind[i + 1] for every even i. Pair 0, pair 8192 // 1024 and the last pair hold long rows, pair 1 holds short rows.
All inputs are finite; a program needn't handle non-finite values.
Results may differ from the reference program's by a relative error of at most 0.018.
Values may be sent and summed in bfloat16 or wider, within the bound.
No kernel may reach another device: no remote copies, remote signals or barrier semaphores. Data moves between devices by JAX's collectives and lax.ppermute only.
A program may use at most 256 MiB of HBM per device.

```python
import jax
import jax.numpy as jnp
from jax import lax

D = 768
HEADS = 12
HEAD_DIM = 64
FF = 3072
LAYERS = 2
SHORT = 128
TOK_DEV = 256
TOKENS = 8192


def draw_row_kind(key, part):
    key = jax.random.fold_in(key, 7)
    pairs = TOKENS // (2 * TOK_DEV)
    kinds = jax.random.randint(key, (pairs,), 0, 2)
    kinds = kinds.at[0].set(1).at[1].set(0).at[pairs // 2].set(1).at[pairs - 1].set(1)
    return jnp.repeat(kinds, 2).astype(jnp.int32)


def levels(rng, extent, shards, low, high):
    def one(dim, shards_of):
        heights = jax.random.uniform(jax.random.fold_in(jax.random.fold_in(rng, 6), dim), (shards_of,), jnp.float32, low / len(shards), high / len(shards))
        return jnp.repeat(jnp.exp(heights), extent[dim] // shards_of).reshape((-1,) + (1,) * (len(extent) - dim - 1))

    gain = one(*shards[0])
    for cut in shards[1:]:
        gain = gain * one(*cut)
    return gain


def scatter_about(rng, dims, spread, reach, split=(), held_as=jnp.bfloat16):
    entries = jax.random.normal(rng, dims, jnp.float32) * spread
    if len(split) > 0:
        entries = levels(rng, dims, split, -0.22, 0.18) * entries
    return jnp.clip(entries, min=-reach, max=reach).astype(held_as)


def setup_inputs(seed: int = 0) -> dict:
    streams_of = jax.random.split(jax.random.key(seed), 11)
    return {
        "tokens": scatter_about(streams_of[0], (TOKENS, D), 1.0, 6.0, ((0, 32),)),
        "row_kind": draw_row_kind(jax.random.fold_in(streams_of[10], 71), 0),
        "w_qkv": scatter_about(streams_of[2], (LAYERS, D, 3 * D), D ** -0.5, 0.21875, ((1, 32),)),
        "w_out": scatter_about(streams_of[3], (LAYERS, D, D), (D // 16) ** -0.5, 0.875, ((1, 32),)),
        "w_up": scatter_about(streams_of[4], (LAYERS, D, FF), D ** -0.5, 0.21875, ((1, 32),)),
        "w_down": scatter_about(streams_of[5], (LAYERS, FF, D), FF ** -0.5, 0.109375, ((1, 32),)),
        "bias_vectors": scatter_about(streams_of[6], (LAYERS, 6, D), 0.5, 3.0, ((2, 32),)),
        "gains": jnp.clip(1.0 + 0.15 * jax.random.normal(streams_of[7], (LAYERS, 2, D), jnp.float32), 0.25, 1.75).astype(jnp.bfloat16),
        "bias_up": scatter_about(streams_of[8], (LAYERS, FF), 0.5, 3.0, ((1, 32),)),
        "cotangent": scatter_about(streams_of[9], (TOKENS, D), 1.0, 6.0, ((0, 32),)),
    }


EPSILON = 1e-05
MASKED_SCORE = -1e+30
HIGHEST = lax.Precision.HIGHEST

@jax.custom_vjp
def low(v):
    return lax.optimization_barrier(v.astype(jnp.bfloat16)).astype(jnp.float32)

@jax.custom_vjp
def low_back(v):
    return v

def low_keep(v):
    return (low(v), None)

def low_pass(kept, grad):
    return (grad,)

def back_keep(v):
    return (v, None)

def back_low(kept, grad):
    return (low(grad),)
low.defvjp(low_keep, low_pass)
low_back.defvjp(back_keep, back_low)

def layer_norm(values, gain_row, shift_row):
    centre = values - lax.optimization_barrier(jnp.mean(values, axis=-1, keepdims=True))
    variance = lax.optimization_barrier(jnp.mean(centre * centre, axis=-1, keepdims=True))
    return centre * lax.rsqrt(variance + EPSILON) * gain_row + shift_row

def attend_block(queries, keys_all, values_all, pair_types):
    span_len = queries.shape[1]
    position = jnp.arange(span_len)
    same_row = position[:, None] // SHORT == position[None, :] // SHORT
    allowed = same_row[None] | (pair_types[:, None, None] == 1)
    raw_scores = jnp.einsum('gqhd,gkhd->ghqk', queries, keys_all, precision=HIGHEST) * 0.125
    scores = low_back(jnp.where(allowed[:, None], raw_scores, MASKED_SCORE))
    probs = low(jax.nn.softmax(scores, axis=-1))
    return jnp.einsum('ghqk,gkhd->gqhd', probs, values_all, precision=HIGHEST)

def attention(queries, keys_all, values_all, pair_types):
    pairs = pair_types.shape[0]
    group_size = 8
    shape = (pairs // group_size, group_size, 2 * TOK_DEV, HEADS, HEAD_DIM)
    block_step = jax.checkpoint(attend_block)

    def scan_step(carried, pieces):
        return (carried, block_step(*pieces))
    packed = (queries.reshape(shape), keys_all.reshape(shape), values_all.reshape(shape), pair_types.reshape(pairs // group_size, group_size))
    _, result = lax.scan(scan_step, jnp.zeros((), jnp.float32), packed)
    return result.reshape(queries.shape[0], D)

def layer(inputs, w_qkv, w_out, w_up, w_down, vectors, gain_pair, bias_up, pair_types):
    zeros_vec = jnp.zeros_like(vectors[0])
    qkv = jnp.dot(low(inputs), w_qkv, precision=HIGHEST) + jnp.concatenate([vectors[0], zeros_vec, vectors[1]])
    qkv = low(low_back(qkv))
    context = attention(qkv[:, :D], qkv[:, D:2 * D], qkv[:, 2 * D:], pair_types)
    context = low(low_back(context))
    branch = low_back(jnp.dot(context, w_out, precision=HIGHEST) + vectors[2])
    normed = layer_norm(inputs + branch, gain_pair[0], vectors[4])
    pre_act = low_back(jnp.dot(low(normed), w_up, precision=HIGHEST) + bias_up)
    act = low(jax.nn.gelu(pre_act, approximate=False))
    ffn_out = low_back(jnp.dot(act, w_down, precision=HIGHEST) + vectors[3])
    return layer_norm(normed + ffn_out, gain_pair[1], vectors[5])

def reference(tokens, row_kind, w_qkv, w_out, w_up, w_down, bias_vectors, gains, bias_up, cotangent):
    pair_types = row_kind[::2]

    def forward(inputs, wq, wo, wu, wd, vecs, gain_all, bup):
        for layer_index in range(LAYERS):
            inputs = layer(inputs, wq[layer_index], wo[layer_index], wu[layer_index], wd[layer_index], vecs[layer_index], gain_all[layer_index], bup[layer_index], pair_types)
        return inputs
    floats = [a.astype(jnp.float32) for a in (tokens, w_qkv, w_out, w_up, w_down, bias_vectors, gains, bias_up)]
    result, pullback = jax.vjp(forward, *floats)
    grads = pullback(cotangent.astype(jnp.float32))
    return (result.astype(jnp.bfloat16), grads[0], grads[1], grads[2], grads[3], grads[4], grads[5], grads[6], grads[7])
```

```python
import jax
import jax.numpy as jnp
from jax import lax
from jax.sharding import PartitionSpec as P

HEADS = 12
LAYERS = 2
SHORT = 128


EPSILON = 1e-05
MASKED_SCORE = -1e30


def partner(value, axis, bit):
    mask = 2**bit
    pairs = [(source, source ^ mask) for source in range(lax.axis_size(axis))]
    return lax.ppermute(value, axis, pairs)


def layer_norm(values, gain_row, shift_row):
    centre = values - jnp.mean(values, axis=-1, keepdims=True)
    variance = jnp.mean(centre * centre, axis=-1, keepdims=True)
    return centre * lax.rsqrt(variance + EPSILON) * gain_row + shift_row


def gelu_exact(values):
    return jax.nn.gelu(values, approximate=False)


def attend(queries, keys_here, values_here, row_type):
    keys_far, values_far = partner((keys_here, values_here), "fsdp", 0)
    keys_all = jnp.concatenate([keys_here, keys_far], axis=0)
    values_all = jnp.concatenate([values_here, values_far], axis=0)
    count = queries.shape[0]
    query_pos = jnp.arange(count)
    key_pos = jnp.arange(2 * count)
    same_row = (key_pos[None, :] < count) & (
        query_pos[:, None] // SHORT == key_pos[None, :] // SHORT
    )
    allowed = same_row | (row_type == 1)
    raw_scores = (
        jnp.einsum("qhd,khd->hqk", queries, keys_all, preferred_element_type=jnp.float32) * 0.125
    )
    scores = jnp.where(allowed[None], raw_scores, MASKED_SCORE)
    probs = jax.nn.softmax(scores, axis=-1)
    probs_bf = probs.astype(jnp.bfloat16)
    context = jnp.einsum("hqk,khd->qhd", probs_bf, values_all, preferred_element_type=jnp.float32)
    return (context, (probs, probs_bf, keys_all, values_all))


def layer_forward(inputs, weights, row_type):
    w_qkv, w_out, w_up, w_down, vectors, gain_pair, bias_up = weights
    vectors = vectors.astype(jnp.float32)
    gain_pair = gain_pair.astype(jnp.float32)
    count = inputs.shape[0]
    inputs_bf = inputs.astype(jnp.bfloat16)
    zeros_vec = jnp.zeros_like(vectors[0])
    qkv = jnp.dot(inputs_bf, w_qkv, preferred_element_type=jnp.float32)
    qkv = qkv + jnp.concatenate([vectors[0], zeros_vec, vectors[1]])[None]
    qkv_bf = qkv.astype(jnp.bfloat16)
    width = qkv_bf.shape[1] // 3
    heads_shape = (count, HEADS, width // HEADS)
    queries = qkv_bf[:, :width].reshape(heads_shape)
    keys_here = qkv_bf[:, width : 2 * width].reshape(heads_shape)
    values_here = qkv_bf[:, 2 * width :].reshape(heads_shape)
    context, attended = attend(queries, keys_here, values_here, row_type)
    context_bf = context.reshape(count, width).astype(jnp.bfloat16)
    branch = jnp.dot(context_bf, w_out, preferred_element_type=jnp.float32) + vectors[2]
    first_sum = inputs + branch
    normed = layer_norm(first_sum, gain_pair[0], vectors[4])
    normed_bf = normed.astype(jnp.bfloat16)
    pre_act = jnp.dot(normed_bf, w_up, preferred_element_type=jnp.float32) + bias_up.astype(
        jnp.float32
    )
    act_bf = gelu_exact(pre_act).astype(jnp.bfloat16)
    ffn_out = jnp.dot(act_bf, w_down, preferred_element_type=jnp.float32) + vectors[3]
    second_sum = normed + ffn_out
    layer_out = layer_norm(second_sum, gain_pair[1], vectors[5])
    saved = (
        inputs_bf,
        queries,
        attended,
        context_bf,
        first_sum,
        normed_bf,
        pre_act,
        act_bf,
        second_sum,
    )
    return (layer_out, saved)


def layer_backward(upstream, saved, weights):
    w_qkv, w_out, w_up, w_down, vectors, gain_pair, bias_up = weights
    vectors = vectors.astype(jnp.float32)
    gain_pair = gain_pair.astype(jnp.float32)
    inputs_bf, queries, attended, context_bf, first_sum, normed_bf, pre_act, act_bf, second_sum = (
        saved
    )
    probs, probs_bf, keys_all, values_all = attended
    count = inputs_bf.shape[0]
    width = inputs_bf.shape[1]
    _, pull_second = jax.vjp(layer_norm, second_sum, gain_pair[1], vectors[5])
    grad_second, grad_gain2, grad_shift2 = pull_second(upstream)
    grad_ffn_bf = grad_second.astype(jnp.bfloat16)
    grad_down = jnp.einsum("tf,td->fd", act_bf, grad_ffn_bf, preferred_element_type=jnp.float32)
    grad_act = jnp.einsum("td,fd->tf", grad_ffn_bf, w_down, preferred_element_type=jnp.float32)
    _, pull_gelu = jax.vjp(gelu_exact, pre_act)
    grad_pre_bf = pull_gelu(grad_act)[0].astype(jnp.bfloat16)
    grad_up = jnp.einsum("td,tf->df", normed_bf, grad_pre_bf, preferred_element_type=jnp.float32)
    grad_normed = grad_second + jnp.einsum(
        "tf,df->td", grad_pre_bf, w_up, preferred_element_type=jnp.float32
    )
    _, pull_first = jax.vjp(layer_norm, first_sum, gain_pair[0], vectors[4])
    grad_first, grad_gain1, grad_shift1 = pull_first(grad_normed)
    grad_branch_bf = grad_first.astype(jnp.bfloat16)
    grad_out = jnp.einsum(
        "te,td->ed", context_bf, grad_branch_bf, preferred_element_type=jnp.float32
    )
    grad_context = jnp.einsum(
        "td,ed->te", grad_branch_bf, w_out, preferred_element_type=jnp.float32
    )
    grad_context_bf = grad_context.astype(jnp.bfloat16).reshape(queries.shape)
    grad_probs = jnp.einsum(
        "qhd,khd->hqk", grad_context_bf, values_all, preferred_element_type=jnp.float32
    )
    grad_values_all = jnp.einsum(
        "hqk,qhd->khd", probs_bf, grad_context_bf, preferred_element_type=jnp.float32
    )
    row_dot = jnp.sum(grad_probs * probs, axis=-1, keepdims=True)
    grad_scores_bf = (probs * (grad_probs - row_dot)).astype(jnp.bfloat16)
    grad_queries = (
        jnp.einsum("hqk,khd->qhd", grad_scores_bf, keys_all, preferred_element_type=jnp.float32)
        * 0.125
    )
    grad_keys_all = (
        jnp.einsum("hqk,qhd->khd", grad_scores_bf, queries, preferred_element_type=jnp.float32)
        * 0.125
    )
    back_keys, back_values = (
        partner(grad_keys_all[count:].astype(jnp.bfloat16), "fsdp", 0).astype(jnp.float32),
        partner(grad_values_all[count:].astype(jnp.bfloat16), "fsdp", 0).astype(jnp.float32),
    )
    grad_keys = grad_keys_all[:count] + back_keys
    grad_values = grad_values_all[:count] + back_values
    grad_qkv_bf = jnp.concatenate(
        [
            grad_queries.reshape(count, width),
            grad_keys.reshape(count, width),
            grad_values.reshape(count, width),
        ],
        axis=1,
    ).astype(jnp.bfloat16)
    grad_weight_qkv = jnp.einsum(
        "td,te->de", inputs_bf, grad_qkv_bf, preferred_element_type=jnp.float32
    )
    grad_inputs = grad_first + jnp.einsum(
        "te,de->td", grad_qkv_bf, w_qkv, preferred_element_type=jnp.float32
    )
    grad_qkv_sums = jnp.sum(grad_qkv_bf.astype(jnp.float32), axis=0)
    grad_vectors = jnp.stack(
        [
            grad_qkv_sums[:width],
            grad_qkv_sums[2 * width :],
            jnp.sum(grad_branch_bf.astype(jnp.float32), axis=0),
            jnp.sum(grad_ffn_bf.astype(jnp.float32), axis=0),
            grad_shift1,
            grad_shift2,
        ]
    )
    grad_gain_pair = jnp.stack([grad_gain1, grad_gain2])
    grad_bias_hidden = jnp.sum(grad_pre_bf.astype(jnp.float32), axis=0)
    terms = (
        grad_weight_qkv,
        grad_out,
        grad_up,
        grad_down,
        grad_vectors,
        grad_gain_pair,
        grad_bias_hidden,
    )
    return (grad_inputs, terms)


def pack_weights(w_qkv, w_out, w_up, w_down, vectors, gain_pair, bias_up):
    width = w_out.shape[1]
    panels = [w_qkv[:, i * width : (i + 1) * width] for i in range(w_qkv.shape[1] // width)]
    panels.append(w_out)
    panels += [w_up[:, i * width : (i + 1) * width] for i in range(w_up.shape[1] // width)]
    panels.append(w_down)
    small = jnp.concatenate([vectors.reshape(-1), gain_pair.reshape(-1), bias_up])
    panels.append(jnp.pad(small, (0, 8 * width - small.shape[0])).reshape(8, width))
    return jnp.concatenate(panels, axis=0)


def unpack_weights(packed, rows, width, hidden):
    count = packed.shape[0]
    full = rows * count
    place = 0

    def take(height):
        nonlocal place
        piece = packed[:, place : place + height].reshape(count * height, width)
        place += height
        return piece

    w_qkv = jnp.concatenate([take(rows) for _ in range(3)], axis=1)
    w_out = take(rows)
    w_up = jnp.concatenate([take(rows) for _ in range(hidden // width)], axis=1)
    w_down = take(hidden // count)
    small = packed[:, place:].reshape(count, -1)
    vectors = jnp.swapaxes(small[:, : 6 * rows].reshape(count, 6, rows), 0, 1).reshape(6, full)
    gain_pair = jnp.swapaxes(
        small[:, 6 * rows : 8 * rows].reshape(count, 2, rows), 0, 1
    ).reshape(2, full)
    bias_up = small[:, 8 * rows : 8 * rows + hidden // count].reshape(hidden)
    return (w_qkv, w_out, w_up, w_down, vectors, gain_pair, bias_up)


def pack_terms(terms, count):
    g_qkv, g_out, g_up, g_down, g_vectors, g_gains, g_bias = [
        term.astype(jnp.bfloat16) for term in terms
    ]
    width = g_out.shape[1]
    panels = [
        g_qkv[:, i * width : (i + 1) * width].reshape(count, -1, width)
        for i in range(g_qkv.shape[1] // width)
    ]
    panels.append(g_out.reshape(count, -1, width))
    panels += [
        g_up[:, i * width : (i + 1) * width].reshape(count, -1, width)
        for i in range(g_up.shape[1] // width)
    ]
    panels.append(g_down.reshape(count, -1, width))
    small = jnp.concatenate(
        [
            jnp.swapaxes(g_vectors.reshape(6, count, -1), 0, 1).reshape(count, -1),
            jnp.swapaxes(g_gains.reshape(2, count, -1), 0, 1).reshape(count, -1),
            g_bias.reshape(count, -1),
        ],
        axis=1,
    )
    small = jnp.pad(small, ((0, 0), (0, 8 * width - small.shape[1])))
    panels.append(small.reshape(count, 8, width))
    return jnp.concatenate(panels, axis=1)


def unpack_terms(share, rows, hidden_rows, hidden, width):
    share = share.astype(jnp.float32)
    place = 0

    def take(height):
        nonlocal place
        piece = share[place : place + height]
        place += height
        return piece

    g_qkv = jnp.concatenate([take(rows) for _ in range(3)], axis=1)
    g_out = take(rows)
    g_up = jnp.concatenate([take(rows) for _ in range(hidden // width)], axis=1)
    g_down = take(hidden_rows)
    small = share[place:].reshape(-1)
    return (
        g_qkv,
        g_out,
        g_up,
        g_down,
        small[: 6 * rows].reshape(6, rows),
        small[6 * rows : 8 * rows].reshape(2, rows),
        small[8 * rows : 8 * rows + hidden_rows],
    )


def shards(tokens, row_kind, w_qkv, w_out, w_up, w_down, bias_vectors, gains, bias_up, cotangent):
    row_type = row_kind[0]
    activations = tokens.astype(jnp.float32)
    count = lax.axis_size("fsdp")
    rows, width = w_out.shape[1:]
    hidden_rows = w_down.shape[1]
    hidden = w_up.shape[2]
    weights = []
    for layer_index in range(LAYERS):
        packed = pack_weights(
            w_qkv[layer_index],
            w_out[layer_index],
            w_up[layer_index],
            w_down[layer_index],
            bias_vectors[layer_index],
            gains[layer_index],
            bias_up[layer_index],
        )
        gathered = lax.all_gather(packed, "fsdp", axis=0, tiled=False)
        weights.append(unpack_weights(gathered, rows, width, hidden))
    kept = []
    for layer_index in range(LAYERS):
        activations, saved = layer_forward(activations, weights[layer_index], row_type)
        kept.append(saved)
    mixed = activations.astype(jnp.bfloat16)
    upstream = cotangent.astype(jnp.float32)
    shares_list = []
    for layer_index in reversed(range(LAYERS)):
        upstream, terms = layer_backward(upstream, kept[layer_index], weights[layer_index])
        share = lax.psum_scatter(pack_terms(terms, count), "fsdp", scatter_dimension=0)
        shares_list.append(unpack_terms(share, rows, hidden_rows, hidden, width))
    shares_list = shares_list[::-1]
    stacked = [jnp.stack([entry[member] for entry in shares_list]) for member in range(7)]
    return (
        mixed,
        upstream,
        stacked[0],
        stacked[1],
        stacked[2],
        stacked[3],
        stacked[4],
        stacked[5],
        stacked[6],
    )


def solution(mesh):
    placed = (
        P("fsdp", None),
        P("fsdp"),
        P(None, "fsdp", None),
        P(None, "fsdp", None),
        P(None, "fsdp", None),
        P(None, "fsdp", None),
        P(None, None, "fsdp"),
        P(None, None, "fsdp"),
        P(None, "fsdp"),
        P("fsdp", None),
    )
    return jax.shard_map(
        shards,
        mesh=mesh,
        in_specs=placed,
        out_specs=(
            P("fsdp", None),
            P("fsdp", None),
            P(None, "fsdp", None),
            P(None, "fsdp", None),
            P(None, "fsdp", None),
            P(None, "fsdp", None),
            P(None, None, "fsdp"),
            P(None, None, "fsdp"),
            P(None, "fsdp"),
        ),
        check_vma=False,
    )
```

```python
import jax
import jax.numpy as jnp
from jax import lax
from jax.sharding import PartitionSpec as P

HEADS = 12
LAYERS = 2
SHORT = 128
AXIS = "fsdp"

EPSILON = 1e-05
MASKED_SCORE = -1e30
BF = jnp.bfloat16
F32 = jnp.float32


def dot(left, right):
    return jnp.dot(left, right, preferred_element_type=F32)


def dot_tn(left, right):
    return lax.dot_general(left, right, (((0,), (0,)), ((), ())), preferred_element_type=F32)


def dot_nt(left, right):
    return lax.dot_general(left, right, (((1,), (1,)), ((), ())), preferred_element_type=F32)


def swap(value, mask):
    pairs = [(source, source ^ mask) for source in range(lax.axis_size(AXIS))]
    return lax.ppermute(value, AXIS, pairs)


def merge(mine, theirs, bit, axis):
    first = jnp.where(bit == 0, mine, theirs)
    second = jnp.where(bit == 0, theirs, mine)
    return jnp.stack([first, second], axis=axis)


class Chips:
    def __init__(self):
        device = lax.axis_index(AXIS)
        self.count = lax.axis_size(AXIS) // 2
        self.bits = self.count.bit_length() - 1
        self.core = device % 2
        self.chip = device // 2
        self.top = self.chip // (self.count // 4)
        self.low = list(range(self.bits - 2))

    def bit(self, place):
        return (self.chip // 2**place) % 2

    def order(self, kind):
        return self.low if kind == 0 else self.low[::-1]

    def gather(self, piece, kind):
        step = self.count // 4
        near, far, both = (swap(piece, 2 * step * k) for k in (1, 2, 3))
        low_bit, high_bit = self.top % 2, self.top // 2
        held = merge(merge(piece, near, low_bit, 0), merge(far, both, low_bit, 0), high_bit, 0)
        held = held.reshape((4,) + piece.shape)
        present = []
        for place in self.order(kind):
            axis = 1 + sum(other > place for other in present)
            held = merge(held, swap(held, 2 * 2**place), self.bit(place), axis)
            present.append(place)
        return held.reshape((self.count,) + piece.shape)

    def scatter(self, terms, kind):
        piece = terms.shape[1:]
        wire = terms.dtype
        held = terms.reshape((4,) + (2,) * (self.bits - 2) + piece)
        present = list(self.low)
        for place in self.order(kind)[::-1]:
            axis = 1 + sum(other > place for other in present)
            bit = self.bit(place)
            sent = lax.dynamic_index_in_dim(held, 1 - bit, axis, keepdims=False)
            kept = lax.dynamic_index_in_dim(held, bit, axis, keepdims=False)
            got = swap(sent, 2 * 2**place)
            held = (kept.astype(F32) + got.astype(F32)).astype(wire)
            present.remove(place)
        step = self.count // 4
        total = lax.dynamic_index_in_dim(held, self.top, 0, keepdims=False).astype(F32)
        for k in (1, 2, 3):
            sent = lax.dynamic_index_in_dim(held, self.top ^ k, 0, keepdims=False)
            total = total + swap(sent, 2 * step * k).astype(F32)
        return total


def layer_norm(values, gain_row, shift_row):
    centre = values - jnp.mean(values, axis=-1, keepdims=True)
    variance = jnp.mean(centre * centre, axis=-1, keepdims=True)
    return centre * lax.rsqrt(variance + EPSILON) * gain_row + shift_row


def gelu_exact(values):
    return jax.nn.gelu(values, approximate=False)


def pair_sum(partial):
    rounded = partial.astype(BF)
    return rounded.astype(F32) + swap(rounded, 1).astype(F32)


def attend(queries, keys, values, row_type):
    count = queries.shape[0]
    place = jnp.arange(count)
    allowed = (place[:, None] // SHORT == place[None, :] // SHORT) | (row_type == 1)
    raw = jnp.einsum("qhd,khd->hqk", queries, keys, preferred_element_type=F32) * 0.125
    probs = jax.nn.softmax(jnp.where(allowed[None], raw, MASKED_SCORE), axis=-1)
    probs_b = probs.astype(BF)
    context = jnp.einsum("hqk,khd->qhd", probs_b, values, preferred_element_type=F32)
    return context, (probs, probs_b)


def layer_forward(inputs, weights, row_type):
    w_qkv, w_out, w_up, w_down, qkv_bias, vectors, gain_pair, bias_up = weights
    count = inputs.shape[0]
    inputs_b = inputs.astype(BF)
    qkv = (dot(inputs_b, w_qkv) + qkv_bias[None]).astype(BF)
    half = qkv.shape[1] // 3
    heads_shape = (count, HEADS // 2, half // (HEADS // 2))
    queries, keys, values = (
        qkv[:, i * half : (i + 1) * half].reshape(heads_shape) for i in range(3)
    )
    context, attended = attend(queries, keys, values, row_type)
    context_b = context.reshape(count, half).astype(BF)
    first_sum = inputs + (pair_sum(dot(context_b, w_out)) + vectors[2])
    normed = layer_norm(first_sum, gain_pair[0], vectors[4])
    normed_b = normed.astype(BF)
    pre_act = dot(normed_b, w_up) + bias_up
    act = gelu_exact(pre_act).astype(BF)
    second_sum = normed + pair_sum(dot(act, w_down)) + vectors[3]
    output = layer_norm(second_sum, gain_pair[1], vectors[5])
    saved = (
        inputs_b, queries, keys, values, attended, context_b, first_sum, normed_b, pre_act, act,
        second_sum,
    )
    return output, saved


def layer_backward(upstream, saved, weights):
    w_qkv, w_out, w_up, w_down, qkv_bias, vectors, gain_pair, bias_up = weights
    (
        inputs_b, queries, keys, values, attended, context_b, first_sum, normed_b, pre_act, act,
        second_sum,
    ) = saved
    probs, probs_b = attended
    count = inputs_b.shape[0]
    _, pull_second = jax.vjp(layer_norm, second_sum, gain_pair[1], vectors[5])
    d_second, d_gain2, d_shift2 = pull_second(upstream)
    d_ffn = d_second.astype(BF)
    g_down = dot_tn(act, d_ffn).astype(BF)
    _, pull_gelu = jax.vjp(gelu_exact, pre_act)
    d_pre = pull_gelu(dot_nt(d_ffn, w_down))[0].astype(BF)
    g_up = dot_tn(normed_b, d_pre).astype(BF)
    d_normed = d_second + pair_sum(dot_nt(d_pre, w_up))
    _, pull_first = jax.vjp(layer_norm, first_sum, gain_pair[0], vectors[4])
    d_first, d_gain1, d_shift1 = pull_first(d_normed)
    d_branch = d_first.astype(BF)
    g_out = dot_tn(context_b, d_branch).astype(BF)
    d_context = dot_nt(d_branch, w_out).astype(BF).reshape(queries.shape)
    d_probs = jnp.einsum("qhd,khd->hqk", d_context, values, preferred_element_type=F32)
    d_values = jnp.einsum("hqk,qhd->khd", probs_b, d_context, preferred_element_type=F32)
    row_dot = jnp.sum(d_probs * probs, axis=-1, keepdims=True)
    d_scores = (probs * (d_probs - row_dot)).astype(BF)
    d_queries = jnp.einsum("hqk,khd->qhd", d_scores, keys, preferred_element_type=F32) * 0.125
    d_keys = jnp.einsum("hqk,qhd->khd", d_scores, queries, preferred_element_type=F32) * 0.125
    d_qkv = jnp.concatenate(
        [part.reshape(count, -1) for part in (d_queries, d_keys, d_values)], axis=1
    ).astype(BF)
    g_qkv = dot_tn(inputs_b, d_qkv).astype(BF)
    partial = dot_nt(d_qkv, w_qkv)
    qkv_sums = jnp.sum(d_qkv.astype(F32), axis=0)
    half = qkv_sums.shape[0] // 3
    sums = (
        jnp.stack([qkv_sums[:half], qkv_sums[2 * half :]]),
        jnp.stack(
            [
                jnp.sum(d_branch.astype(F32), axis=0),
                jnp.sum(d_ffn.astype(F32), axis=0),
                d_shift1,
                d_shift2,
                d_gain1,
                d_gain2,
            ]
        ),
        jnp.sum(d_pre.astype(F32), axis=0),
    )
    return d_first, partial, (g_qkv, g_out, g_up, g_down), sums


def hidden_order(width, hidden_rows):
    group = width // (2 * hidden_rows)
    target = jnp.arange(width)
    source = (
        (target % (width // 2)) // hidden_rows * (2 * hidden_rows)
        + target // (width // 2) * hidden_rows
        + target % hidden_rows
    )
    del group
    return jnp.arange(width)[:, None] == source[None, :]


def pick(pair, core, axis):
    return lax.dynamic_index_in_dim(pair, core, axis, keepdims=False)


def shards(tokens, row_kind, w_qkv, w_out, w_up, w_down, bias_vectors, gains, bias_up, cotangent):
    chips = Chips()
    core = chips.core
    count = chips.count
    row_type = row_kind[0]
    rows, width = w_out.shape[1:]
    hidden = w_up.shape[2]
    hidden_rows = w_down.shape[1]
    half = width // 2
    order = hidden_order(width, hidden_rows)

    small = jnp.concatenate(
        [
            jnp.concatenate([bias_vectors, gains], axis=1).reshape(LAYERS, 8 * rows),
            bias_up,
        ],
        axis=1,
    )
    small_size = small.shape[1]
    small_all = chips.gather(small, 0)
    small_pair = merge(small_all, swap(small_all, 1), core, 1)

    qkv_cols = w_qkv.reshape(LAYERS, rows, 3, 2, half)
    qkv_mine = pick(qkv_cols, core, 3)
    qkv_theirs = swap(pick(qkv_cols, 1 - core, 3), 1)
    qkv_rows = merge(qkv_mine, qkv_theirs, core, 1).reshape(LAYERS, 2, rows, 3 * half)
    up_cols = jnp.einsum(
        "lrgk,kp->lrgp", w_up.reshape(LAYERS, rows, hidden // width, width), order.astype(BF),
        preferred_element_type=F32,
    ).astype(BF).reshape(LAYERS, rows, hidden // width, 2, half)
    up_mine = pick(up_cols, core, 3)
    up_theirs = swap(pick(up_cols, 1 - core, 3), 1)
    up_rows = merge(up_mine, up_theirs, core, 1).reshape(LAYERS, 2, rows, hidden // 2)
    down_rows = w_down.reshape(LAYERS, 2, hidden_rows // 2, width)

    def gather_halves(halves):
        parts = [chips.gather(halves[kind], kind) for kind in range(2)]
        return jnp.stack(parts, axis=1)

    weights = []
    for layer in range(LAYERS):
        full_qkv = gather_halves(qkv_rows[layer]).reshape(width, 3 * half)
        out_all = chips.gather(w_out[layer], layer % 2).reshape(2, count // 2, rows, width)
        out_got = swap(pick(out_all, 1 - core, 0), 1)
        full_out = merge(pick(out_all, core, 0), out_got, core, 1).reshape(half, width)
        full_up = gather_halves(up_rows[layer]).reshape(width, hidden // 2)
        full_down = gather_halves(down_rows[layer]).reshape(hidden // 2, width)
        table = small_pair[:, :, layer, : 8 * rows].reshape(count, 2, 8, rows).astype(F32)
        table = jnp.transpose(table, (2, 0, 1, 3)).reshape(8, width)
        vectors, gain_pair = table[:6], table[6:]
        bias_hidden = small_all[:, layer, 8 * rows :].reshape(hidden // 2).astype(F32)
        bias_q, bias_v = (
            lax.dynamic_slice_in_dim(vectors[i], core * half, half) for i in range(2)
        )
        qkv_bias = jnp.concatenate([bias_q, jnp.zeros_like(bias_q), bias_v])
        weights.append(
            (full_qkv, full_out, full_up, full_down, qkv_bias, vectors, gain_pair, bias_hidden)
        )

    own = tokens.shape[0]

    def both(value):
        return merge(value, swap(value, 1), core, 0).reshape((2 * own,) + value.shape[1:])

    activations = both(tokens).astype(F32)
    upstream = both(cotangent).astype(F32)
    kept = []
    for layer in range(LAYERS):
        activations, saved = layer_forward(activations, weights[layer], row_type)
        kept.append(saved)
    mixed = lax.dynamic_slice_in_dim(activations, core * own, own).astype(BF)

    shares = [None] * LAYERS
    sums_list = [None] * LAYERS
    for layer in reversed(range(LAYERS)):
        d_first, partial, grads, sums = layer_backward(upstream, kept[layer], weights[layer])
        g_qkv, g_out, g_up, g_down = grads

        def scatter_halves(grad, height):
            terms = grad.reshape(count, 2, height, grad.shape[1])
            return [chips.scatter(terms[:, kind], kind) for kind in range(2)]

        down = jnp.concatenate(scatter_halves(g_down, hidden_rows // 2), axis=0)
        up = scatter_halves(g_up, rows)
        up_mine = jnp.where(core == 0, up[0], up[1])
        up_got = swap(jnp.where(core == 0, up[1], up[0]), 1)
        up_all = merge(
            up_mine.reshape(rows, hidden // width, half),
            up_got.reshape(rows, hidden // width, half), core, 2,
        ).reshape(rows, hidden // width, width)
        up_all = jnp.einsum(
            "rgp,kp->rgk", up_all, order.astype(F32), precision=lax.Precision.HIGHEST,
            preferred_element_type=F32,
        ).reshape(rows, hidden)
        out_pair = g_out.reshape(count // 2, 2, rows, width)
        out_got = swap(pick(out_pair, 1 - core, 1), 1)
        out_terms = merge(pick(out_pair, core, 1), out_got, core, 0)
        out = chips.scatter(out_terms.reshape(count, rows, width), layer % 2)
        qkv = scatter_halves(g_qkv, rows)
        qkv_mine = jnp.where(core == 0, qkv[0], qkv[1])
        qkv_got = swap(jnp.where(core == 0, qkv[1], qkv[0]), 1)
        qkv_all = merge(
            qkv_mine.reshape(rows, 3, half), qkv_got.reshape(rows, 3, half), core, 2
        ).reshape(rows, 6 * half)
        shares[layer] = (qkv_all, out, up_all, down)

        pair_sums, chip_sums, hidden_sums = sums
        pair_all = merge(pair_sums, swap(pair_sums, 1), core, 1).reshape(2, width)
        table = jnp.concatenate([pair_all, chip_sums], axis=0).reshape(8, count, 2, rows)
        table = jnp.transpose(pick(table, core, 2), (1, 0, 2)).reshape(count, 8 * rows)
        sums_list[layer] = jnp.concatenate([table, hidden_sums.reshape(count, -1)], axis=1)

        if layer > 0:
            upstream = d_first + pair_sum(partial)
        else:
            parts = partial.astype(BF).reshape(2, own, width)
            got = swap(pick(parts, 1 - core, 0), 1).astype(F32)
            mine = lax.dynamic_slice_in_dim(d_first, core * own, own)
            grad_tokens = mine + (pick(parts, core, 0).astype(F32) + got)

    small_sum = chips.scatter(jnp.stack(sums_list, axis=1), 0)
    small_sum = small_sum.reshape(LAYERS, small_size)
    table = small_sum[:, : 8 * rows].reshape(LAYERS, 8, rows)
    stacked = [jnp.stack([entry[member] for entry in shares]) for member in range(4)]
    return (
        mixed,
        grad_tokens,
        stacked[0],
        stacked[1],
        stacked[2],
        stacked[3],
        table[:, :6],
        table[:, 6:],
        small_sum[:, 8 * rows :],
    )


def solution(mesh):
    placed = (
        P("fsdp", None),
        P("fsdp"),
        P(None, "fsdp", None),
        P(None, "fsdp", None),
        P(None, "fsdp", None),
        P(None, "fsdp", None),
        P(None, None, "fsdp"),
        P(None, None, "fsdp"),
        P(None, "fsdp"),
        P("fsdp", None),
    )
    return jax.shard_map(
        shards,
        mesh=mesh,
        in_specs=placed,
        out_specs=(
            P("fsdp", None),
            P("fsdp", None),
            P(None, "fsdp", None),
            P(None, "fsdp", None),
            P(None, "fsdp", None),
            P(None, "fsdp", None),
            P(None, None, "fsdp"),
            P(None, None, "fsdp"),
            P(None, "fsdp"),
        ),
        check_vma=False,
    )
```

```python
import jax
import jax.numpy as jnp
from jax import lax
from jax.sharding import PartitionSpec as P

HEADS = 12
LAYERS = 2
SHORT = 128
AXIS = "fsdp"

EPSILON = 1e-05
MASKED_SCORE = -1e30
BF = jnp.bfloat16
F32 = jnp.float32


def dot(left, right):
    return jnp.dot(left, right, preferred_element_type=F32)


def dot_tn(left, right):
    return lax.dot_general(left, right, (((0,), (0,)), ((), ())), preferred_element_type=F32)


def dot_nt(left, right):
    return lax.dot_general(left, right, (((1,), (1,)), ((), ())), preferred_element_type=F32)


def swap(value, mask):
    pairs = [(source, source ^ mask) for source in range(lax.axis_size(AXIS))]
    return lax.ppermute(value, AXIS, pairs)


def merge(mine, theirs, bit, axis):
    first = jnp.where(bit == 0, mine, theirs)
    second = jnp.where(bit == 0, theirs, mine)
    return jnp.stack([first, second], axis=axis)


class Chips:
    def __init__(self):
        device = lax.axis_index(AXIS)
        self.count = lax.axis_size(AXIS) // 2
        self.core = device % 2

    def groups(self):
        return [list(range(core, 2 * self.count, 2)) for core in range(2)]

    def gather(self, piece):
        return lax.all_gather(piece, AXIS, axis=0, axis_index_groups=self.groups())

    def scatter(self, terms):
        return lax.psum_scatter(
            terms, AXIS, scatter_dimension=0, axis_index_groups=self.groups()
        )


def layer_norm(values, gain_row, shift_row):
    centre = values - jnp.mean(values, axis=-1, keepdims=True)
    variance = jnp.mean(centre * centre, axis=-1, keepdims=True)
    return centre * lax.rsqrt(variance + EPSILON) * gain_row + shift_row


def gelu_exact(values):
    return jax.nn.gelu(values, approximate=False)


def pair_sum(partial):
    rounded = partial.astype(BF)
    return rounded.astype(F32) + swap(rounded, 1).astype(F32)


def attend(queries, keys, values, row_type):
    count = queries.shape[0]
    place = jnp.arange(count)
    allowed = (place[:, None] // SHORT == place[None, :] // SHORT) | (row_type == 1)
    raw = jnp.einsum("qhd,khd->hqk", queries, keys, preferred_element_type=F32) * 0.125
    probs = jax.nn.softmax(jnp.where(allowed[None], raw, MASKED_SCORE), axis=-1)
    probs_b = probs.astype(BF)
    context = jnp.einsum("hqk,khd->qhd", probs_b, values, preferred_element_type=F32)
    return context, (probs, probs_b)


def layer_forward(inputs, weights, row_type):
    w_qkv, w_out, w_up, w_down, qkv_bias, vectors, gain_pair, bias_up = weights
    count = inputs.shape[0]
    inputs_b = inputs.astype(BF)
    qkv = (dot(inputs_b, w_qkv) + qkv_bias[None]).astype(BF)
    half = qkv.shape[1] // 3
    heads_shape = (count, HEADS // 2, half // (HEADS // 2))
    queries, keys, values = (
        qkv[:, i * half : (i + 1) * half].reshape(heads_shape) for i in range(3)
    )
    context, attended = attend(queries, keys, values, row_type)
    context_b = context.reshape(count, half).astype(BF)
    first_sum = inputs + (pair_sum(dot(context_b, w_out)) + vectors[2])
    normed = layer_norm(first_sum, gain_pair[0], vectors[4])
    normed_b = normed.astype(BF)
    pre_act = dot(normed_b, w_up) + bias_up
    act = gelu_exact(pre_act).astype(BF)
    second_sum = normed + pair_sum(dot(act, w_down)) + vectors[3]
    output = layer_norm(second_sum, gain_pair[1], vectors[5])
    saved = (
        inputs_b, queries, keys, values, attended, context_b, first_sum, normed_b, pre_act, act,
        second_sum,
    )
    return output, saved


def layer_backward(upstream, saved, weights):
    w_qkv, w_out, w_up, w_down, qkv_bias, vectors, gain_pair, bias_up = weights
    (
        inputs_b, queries, keys, values, attended, context_b, first_sum, normed_b, pre_act, act,
        second_sum,
    ) = saved
    probs, probs_b = attended
    count = inputs_b.shape[0]
    _, pull_second = jax.vjp(layer_norm, second_sum, gain_pair[1], vectors[5])
    d_second, d_gain2, d_shift2 = pull_second(upstream)
    d_ffn = d_second.astype(BF)
    g_down = dot_tn(act, d_ffn).astype(BF)
    _, pull_gelu = jax.vjp(gelu_exact, pre_act)
    d_pre = pull_gelu(dot_nt(d_ffn, w_down))[0].astype(BF)
    g_up = dot_tn(normed_b, d_pre).astype(BF)
    d_normed = d_second + pair_sum(dot_nt(d_pre, w_up))
    _, pull_first = jax.vjp(layer_norm, first_sum, gain_pair[0], vectors[4])
    d_first, d_gain1, d_shift1 = pull_first(d_normed)
    d_branch = d_first.astype(BF)
    g_out = dot_tn(context_b, d_branch).astype(BF)
    d_context = dot_nt(d_branch, w_out).astype(BF).reshape(queries.shape)
    d_probs = jnp.einsum("qhd,khd->hqk", d_context, values, preferred_element_type=F32)
    d_values = jnp.einsum("hqk,qhd->khd", probs_b, d_context, preferred_element_type=F32)
    row_dot = jnp.sum(d_probs * probs, axis=-1, keepdims=True)
    d_scores = (probs * (d_probs - row_dot)).astype(BF)
    d_queries = jnp.einsum("hqk,khd->qhd", d_scores, keys, preferred_element_type=F32) * 0.125
    d_keys = jnp.einsum("hqk,qhd->khd", d_scores, queries, preferred_element_type=F32) * 0.125
    d_qkv = jnp.concatenate(
        [part.reshape(count, -1) for part in (d_queries, d_keys, d_values)], axis=1
    ).astype(BF)
    g_qkv = dot_tn(inputs_b, d_qkv).astype(BF)
    partial = dot_nt(d_qkv, w_qkv)
    qkv_sums = jnp.sum(d_qkv.astype(F32), axis=0)
    half = qkv_sums.shape[0] // 3
    sums = (
        jnp.stack([qkv_sums[:half], qkv_sums[2 * half :]]),
        jnp.stack(
            [
                jnp.sum(d_branch.astype(F32), axis=0),
                jnp.sum(d_ffn.astype(F32), axis=0),
                d_shift1,
                d_shift2,
                d_gain1,
                d_gain2,
            ]
        ),
        jnp.sum(d_pre.astype(F32), axis=0),
    )
    return d_first, partial, (g_qkv, g_out, g_up, g_down), sums


def hidden_order(width, hidden_rows):
    group = width // (2 * hidden_rows)
    target = jnp.arange(width)
    source = (
        (target % (width // 2)) // hidden_rows * (2 * hidden_rows)
        + target // (width // 2) * hidden_rows
        + target % hidden_rows
    )
    del group
    return jnp.arange(width)[:, None] == source[None, :]


def pick(pair, core, axis):
    return lax.dynamic_index_in_dim(pair, core, axis, keepdims=False)


def shards(tokens, row_kind, w_qkv, w_out, w_up, w_down, bias_vectors, gains, bias_up, cotangent):
    chips = Chips()
    core = chips.core
    count = chips.count
    row_type = row_kind[0]
    rows, width = w_out.shape[1:]
    hidden = w_up.shape[2]
    hidden_rows = w_down.shape[1]
    half = width // 2
    order = hidden_order(width, hidden_rows)

    small = jnp.concatenate(
        [
            jnp.concatenate([bias_vectors, gains], axis=1).reshape(LAYERS, 8 * rows),
            bias_up,
        ],
        axis=1,
    )
    small_pair = merge(small, swap(small, 1), core, 1)
    qkv_cols = w_qkv.reshape(LAYERS, rows, 3, 2, half)
    qkv_mine = pick(qkv_cols, core, 3)
    qkv_theirs = swap(pick(qkv_cols, 1 - core, 3), 1)
    qkv_rows = merge(qkv_mine, qkv_theirs, core, 1)
    up_cols = jnp.einsum(
        "lrgk,kp->lrgp", w_up.reshape(LAYERS, rows, hidden // width, width), order.astype(BF),
        preferred_element_type=F32,
    ).astype(BF).reshape(LAYERS, rows, hidden // width, 2, half)
    up_mine = pick(up_cols, core, 3)
    up_theirs = swap(pick(up_cols, 1 - core, 3), 1)
    up_rows = merge(up_mine, up_theirs, core, 1).reshape(LAYERS, 2 * rows, hidden // 2)
    panels = hidden // 2 // width

    weights = []
    for layer in range(LAYERS):
        qkv = qkv_rows[layer]
        row = jnp.pad(small_pair[layer].reshape(-1), (0, 8 * width - 2 * small.shape[1]))
        packed = jnp.concatenate(
            [
                qkv[:, :, :2].reshape(2 * rows, width),
                jnp.concatenate([qkv[0, :, 2], qkv[1, :, 2]], axis=1),
                w_out[layer],
            ]
            + [up_rows[layer][:, i * width : (i + 1) * width] for i in range(panels)]
            + [w_down[layer], row.reshape(8, width)],
            axis=0,
        )
        got = chips.gather(packed)
        place = 0

        def take(height):
            nonlocal place
            place += height
            return got[:, place - height : place]

        full_qk = take(2 * rows).reshape(width, width)
        full_v = jnp.swapaxes(take(rows).reshape(count, rows, 2, half), 1, 2).reshape(width, half)
        full_qkv = jnp.concatenate([full_qk, full_v], axis=1)
        out_all = take(rows).reshape(2, count // 2, rows, width)
        out_got = swap(pick(out_all, 1 - core, 0), 1)
        full_out = merge(pick(out_all, core, 0), out_got, core, 1).reshape(half, width)
        full_up = jnp.concatenate(
            [take(2 * rows).reshape(width, width) for i in range(panels)], axis=1
        )
        full_down = take(hidden_rows).reshape(hidden // 2, width)
        table = take(8).reshape(count, -1)[:, : 2 * small.shape[1]].reshape(count, 2, -1)
        vector_table = table[:, :, : 8 * rows].reshape(count, 2, 8, rows).astype(F32)
        vector_table = jnp.transpose(vector_table, (2, 0, 1, 3)).reshape(8, width)
        vectors, gain_pair = vector_table[:6], vector_table[6:]
        bias_hidden = pick(table[:, :, 8 * rows :], core, 1).reshape(hidden // 2).astype(F32)
        bias_q, bias_v = (
            lax.dynamic_slice_in_dim(vectors[i], core * half, half) for i in range(2)
        )
        qkv_bias = jnp.concatenate([bias_q, jnp.zeros_like(bias_q), bias_v])
        weights.append(
            (full_qkv, full_out, full_up, full_down, qkv_bias, vectors, gain_pair, bias_hidden)
        )

    own = tokens.shape[0]

    def both(value):
        return merge(value, swap(value, 1), core, 0).reshape((2 * own,) + value.shape[1:])

    activations = both(tokens).astype(F32)
    upstream = both(cotangent).astype(F32)
    kept = []
    for layer in range(LAYERS):
        activations, saved = layer_forward(activations, weights[layer], row_type)
        kept.append(saved)
    mixed = lax.dynamic_slice_in_dim(activations, core * own, own).astype(BF)

    shares = [None] * LAYERS
    for layer in reversed(range(LAYERS)):
        d_first, partial, grads, sums = layer_backward(upstream, kept[layer], weights[layer])
        g_qkv, g_out, g_up, g_down = grads
        g_qkv = g_qkv.reshape(count, 2, rows, 3 * half)
        out_pair = g_out.reshape(count // 2, 2, rows, width)
        out_got = swap(pick(out_pair, 1 - core, 1), 1)
        out_terms = merge(pick(out_pair, core, 1), out_got, core, 0)
        pair_sums, chip_sums, hidden_sums = sums
        pair_sums = jnp.transpose(pair_sums.reshape(2, count // 2, 2, rows), (1, 2, 0, 3))
        pair_sums = pair_sums.reshape(count // 2, 4 * rows)
        pair_sums = merge(pair_sums, jnp.zeros_like(pair_sums), core, 0).reshape(count, -1)
        chip_sums = pick(chip_sums.reshape(6, count, 2, rows), core, 2)
        chip_sums = jnp.swapaxes(chip_sums, 0, 1).reshape(count, 6 * rows)
        row = jnp.concatenate([pair_sums, chip_sums, hidden_sums.reshape(count, -1)], axis=1)
        row_size = row.shape[1]
        row = jnp.pad(row.astype(BF), ((0, 0), (0, 8 * width - row_size)))
        terms = jnp.concatenate(
            [
                g_qkv[..., :width].reshape(count, 2 * rows, width),
                jnp.concatenate([g_qkv[:, 0, :, width:], g_qkv[:, 1, :, width:]], axis=2),
                out_terms.reshape(count, rows, width),
            ]
            + [
                g_up[:, i * width : (i + 1) * width].reshape(count, 2 * rows, width)
                for i in range(panels)
            ]
            + [g_down.reshape(count, hidden_rows, width), row.reshape(count, 8, width)],
            axis=1,
        )
        got = chips.scatter(terms).astype(F32)
        place = 0

        def take(height):
            nonlocal place
            place += height
            return got[place - height : place]

        qk = take(2 * rows).reshape(2, rows, width)
        v = take(rows).reshape(rows, 2, half)
        out = take(rows)
        up = [take(2 * rows).reshape(2, rows, width) for i in range(panels)]
        down = take(hidden_rows)
        row = take(8).reshape(-1)[:row_size]
        wide = jnp.concatenate([qk, jnp.swapaxes(v, 0, 1)] + up, axis=2)
        mine = pick(wide, core, 0)
        theirs = swap(pick(wide, 1 - core, 0), 1)
        both_cols = merge(
            mine.reshape(rows, -1, half), theirs.reshape(rows, -1, half), core, 2
        )
        qkv_all = both_cols[:, :3].reshape(rows, 3 * width)
        up_all = jnp.einsum(
            "rgp,kp->rgk", both_cols[:, 3:].reshape(rows, -1, width), order.astype(F32),
            precision=lax.Precision.HIGHEST, preferred_element_type=F32,
        ).reshape(rows, hidden)
        pair_row = row[: 4 * rows].reshape(2, 2, rows)
        pair_row = pick(pair_row, core, 0) + swap(pick(pair_row, 1 - core, 0), 1)
        chip_row = row[4 * rows : 10 * rows].reshape(6, rows)
        vector_row = jnp.concatenate([pair_row, chip_row[:4]], axis=0)
        shares[layer] = (qkv_all, out, up_all, down, vector_row, chip_row[4:], row[10 * rows :])

        if layer > 0:
            upstream = d_first + pair_sum(partial)
        else:
            parts = partial.astype(BF).reshape(2, own, width)
            got = swap(pick(parts, 1 - core, 0), 1).astype(F32)
            mine = lax.dynamic_slice_in_dim(d_first, core * own, own)
            grad_tokens = mine + (pick(parts, core, 0).astype(F32) + got)

    stacked = [jnp.stack([entry[member] for entry in shares]) for member in range(7)]
    return (mixed, grad_tokens, *stacked)


def solution(mesh):
    placed = (
        P("fsdp", None),
        P("fsdp"),
        P(None, "fsdp", None),
        P(None, "fsdp", None),
        P(None, "fsdp", None),
        P(None, "fsdp", None),
        P(None, None, "fsdp"),
        P(None, None, "fsdp"),
        P(None, "fsdp"),
        P("fsdp", None),
    )
    return jax.shard_map(
        shards,
        mesh=mesh,
        in_specs=placed,
        out_specs=(
            P("fsdp", None),
            P("fsdp", None),
            P(None, "fsdp", None),
            P(None, "fsdp", None),
            P(None, "fsdp", None),
            P(None, "fsdp", None),
            P(None, None, "fsdp"),
            P(None, None, "fsdp"),
            P(None, "fsdp"),
        ),
        check_vma=False,
    )
```

```python
import jax
import jax.numpy as jnp
from jax import lax
from jax.sharding import PartitionSpec as P

HEADS = 12
LAYERS = 2
SHORT = 128
AXIS = "fsdp"

EPSILON = 1e-05
MASKED_SCORE = -1e30
BF = jnp.bfloat16
F32 = jnp.float32


def dot(left, right):
    return jnp.dot(left, right, preferred_element_type=F32)


def dot_tn(left, right):
    return lax.dot_general(left, right, (((0,), (0,)), ((), ())), preferred_element_type=F32)


def dot_nt(left, right):
    return lax.dot_general(left, right, (((1,), (1,)), ((), ())), preferred_element_type=F32)


def swap(value, mask):
    pairs = [(source, source ^ mask) for source in range(lax.axis_size(AXIS))]
    return lax.ppermute(value, AXIS, pairs)


def merge(mine, theirs, bit, axis):
    first = jnp.where(bit == 0, mine, theirs)
    second = jnp.where(bit == 0, theirs, mine)
    return jnp.stack([first, second], axis=axis)


class Chips:
    def __init__(self):
        device = lax.axis_index(AXIS)
        self.count = lax.axis_size(AXIS) // 2
        self.core = device % 2
        self.top = device // 2 // (self.count // 4)

    def groups(self):
        plane = self.count // 4
        return [
            [2 * (top * plane + chip) + core for chip in range(plane)]
            for top in range(4)
            for core in range(2)
        ]

    def core_groups(self):
        return [list(range(core, 2 * self.count, 2)) for core in range(2)]

    def gather(self, piece):
        step = self.count // 4
        near, far, both = (swap(piece, 2 * step * k) for k in (1, 2, 3))
        low_bit, high_bit = self.top % 2, self.top // 2
        held = merge(merge(piece, near, low_bit, 0), merge(far, both, low_bit, 0), high_bit, 0)
        held = held.reshape((4,) + piece.shape)
        return lax.all_gather(held, AXIS, axis=0, axis_index_groups=self.groups())

    def scatter(self, terms):
        return lax.psum_scatter(
            terms, AXIS, scatter_dimension=0, axis_index_groups=self.core_groups()
        ).astype(F32)


def layer_norm(values, gain_row, shift_row):
    centre = values - jnp.mean(values, axis=-1, keepdims=True)
    variance = jnp.mean(centre * centre, axis=-1, keepdims=True)
    return centre * lax.rsqrt(variance + EPSILON) * gain_row + shift_row


def gelu_exact(values):
    return jax.nn.gelu(values, approximate=False)


def pair_sum(partial):
    rounded = partial.astype(BF)
    return rounded.astype(F32) + swap(rounded, 1).astype(F32)


def attend(queries, keys, values, row_type):
    count = queries.shape[0]
    place = jnp.arange(count)
    allowed = (place[:, None] // SHORT == place[None, :] // SHORT) | (row_type == 1)
    raw = jnp.einsum("qhd,khd->hqk", queries, keys, preferred_element_type=F32) * 0.125
    probs = jax.nn.softmax(jnp.where(allowed[None], raw, MASKED_SCORE), axis=-1)
    probs_b = probs.astype(BF)
    context = jnp.einsum("hqk,khd->qhd", probs_b, values, preferred_element_type=F32)
    return context, (probs, probs_b)


def layer_forward(inputs, weights, row_type):
    w_qkv, w_out, w_up, w_down, qkv_bias, vectors, gain_pair, bias_up = weights
    count = inputs.shape[0]
    inputs_b = inputs.astype(BF)
    qkv = (dot(inputs_b, w_qkv) + qkv_bias[None]).astype(BF)
    half = qkv.shape[1] // 3
    heads_shape = (count, HEADS // 2, half // (HEADS // 2))
    queries, keys, values = (
        qkv[:, i * half : (i + 1) * half].reshape(heads_shape) for i in range(3)
    )
    context, attended = attend(queries, keys, values, row_type)
    context_b = context.reshape(count, half).astype(BF)
    first_sum = inputs + (pair_sum(dot(context_b, w_out)) + vectors[2])
    normed = layer_norm(first_sum, gain_pair[0], vectors[4])
    normed_b = normed.astype(BF)
    pre_act = dot(normed_b, w_up) + bias_up
    act = gelu_exact(pre_act).astype(BF)
    second_sum = normed + pair_sum(dot(act, w_down)) + vectors[3]
    output = layer_norm(second_sum, gain_pair[1], vectors[5])
    saved = (
        inputs_b, queries, keys, values, attended, context_b, first_sum, normed_b, pre_act, act,
        second_sum,
    )
    return output, saved


def layer_backward(upstream, saved, weights):
    w_qkv, w_out, w_up, w_down, qkv_bias, vectors, gain_pair, bias_up = weights
    (
        inputs_b, queries, keys, values, attended, context_b, first_sum, normed_b, pre_act, act,
        second_sum,
    ) = saved
    probs, probs_b = attended
    count = inputs_b.shape[0]
    _, pull_second = jax.vjp(layer_norm, second_sum, gain_pair[1], vectors[5])
    d_second, d_gain2, d_shift2 = pull_second(upstream)
    d_ffn = d_second.astype(BF)
    g_down = dot_tn(act, d_ffn).astype(BF)
    _, pull_gelu = jax.vjp(gelu_exact, pre_act)
    d_pre = pull_gelu(dot_nt(d_ffn, w_down))[0].astype(BF)
    g_up = dot_tn(normed_b, d_pre).astype(BF)
    d_normed = d_second + pair_sum(dot_nt(d_pre, w_up))
    _, pull_first = jax.vjp(layer_norm, first_sum, gain_pair[0], vectors[4])
    d_first, d_gain1, d_shift1 = pull_first(d_normed)
    d_branch = d_first.astype(BF)
    g_out = dot_tn(context_b, d_branch).astype(BF)
    d_context = dot_nt(d_branch, w_out).astype(BF).reshape(queries.shape)
    d_probs = jnp.einsum("qhd,khd->hqk", d_context, values, preferred_element_type=F32)
    d_values = jnp.einsum("hqk,qhd->khd", probs_b, d_context, preferred_element_type=F32)
    row_dot = jnp.sum(d_probs * probs, axis=-1, keepdims=True)
    d_scores = (probs * (d_probs - row_dot)).astype(BF)
    d_queries = jnp.einsum("hqk,khd->qhd", d_scores, keys, preferred_element_type=F32) * 0.125
    d_keys = jnp.einsum("hqk,qhd->khd", d_scores, queries, preferred_element_type=F32) * 0.125
    d_qkv = jnp.concatenate(
        [part.reshape(count, -1) for part in (d_queries, d_keys, d_values)], axis=1
    ).astype(BF)
    g_qkv = dot_tn(inputs_b, d_qkv).astype(BF)
    partial = dot_nt(d_qkv, w_qkv)
    qkv_sums = jnp.sum(d_qkv.astype(F32), axis=0)
    half = qkv_sums.shape[0] // 3
    sums = (
        jnp.stack([qkv_sums[:half], qkv_sums[2 * half :]]),
        jnp.stack(
            [
                jnp.sum(d_branch.astype(F32), axis=0),
                jnp.sum(d_ffn.astype(F32), axis=0),
                d_shift1,
                d_shift2,
                d_gain1,
                d_gain2,
            ]
        ),
        jnp.sum(d_pre.astype(F32), axis=0),
    )
    return d_first, partial, (g_qkv, g_out, g_up, g_down), sums


def hidden_order(width, hidden_rows):
    group = width // (2 * hidden_rows)
    target = jnp.arange(width)
    source = (
        (target % (width // 2)) // hidden_rows * (2 * hidden_rows)
        + target // (width // 2) * hidden_rows
        + target % hidden_rows
    )
    del group
    return jnp.arange(width)[:, None] == source[None, :]


def pick(pair, core, axis):
    return lax.dynamic_index_in_dim(pair, core, axis, keepdims=False)


def shards(tokens, row_kind, w_qkv, w_out, w_up, w_down, bias_vectors, gains, bias_up, cotangent):
    chips = Chips()
    core = chips.core
    count = chips.count
    row_type = row_kind[0]
    rows, width = w_out.shape[1:]
    hidden = w_up.shape[2]
    hidden_rows = w_down.shape[1]
    half = width // 2
    order = hidden_order(width, hidden_rows)

    small = jnp.concatenate(
        [
            jnp.concatenate([bias_vectors, gains], axis=1).reshape(LAYERS, 8 * rows),
            bias_up,
        ],
        axis=1,
    )
    small_pair = merge(small, swap(small, 1), core, 1)
    qkv_cols = w_qkv.reshape(LAYERS, rows, 3, 2, half)
    qkv_mine = pick(qkv_cols, core, 3)
    qkv_theirs = swap(pick(qkv_cols, 1 - core, 3), 1)
    qkv_rows = merge(qkv_mine, qkv_theirs, core, 1)
    up_cols = jnp.einsum(
        "lrgk,kp->lrgp", w_up.reshape(LAYERS, rows, hidden // width, width), order.astype(BF),
        preferred_element_type=F32,
    ).astype(BF).reshape(LAYERS, rows, hidden // width, 2, half)
    up_mine = pick(up_cols, core, 3)
    up_theirs = swap(pick(up_cols, 1 - core, 3), 1)
    up_rows = merge(up_mine, up_theirs, core, 1).reshape(LAYERS, 2 * rows, hidden // 2)
    panels = hidden // 2 // width

    weights = []
    for layer in range(LAYERS):
        qkv = qkv_rows[layer]
        row = jnp.pad(small_pair[layer].reshape(-1), (0, 8 * width - 2 * small.shape[1]))
        packed = jnp.concatenate(
            [
                qkv[:, :, :2].reshape(2 * rows, width),
                jnp.concatenate([qkv[0, :, 2], qkv[1, :, 2]], axis=1),
                w_out[layer],
            ]
            + [up_rows[layer][:, i * width : (i + 1) * width] for i in range(panels)]
            + [w_down[layer], row.reshape(8, width)],
            axis=0,
        )
        got = chips.gather(packed)
        place = 0

        def take(height):
            nonlocal place
            place += height
            piece = jnp.swapaxes(got[:, :, place - height : place], 0, 1)
            return piece.reshape(count, height, width)

        full_qk = take(2 * rows).reshape(width, width)
        full_v = jnp.swapaxes(take(rows).reshape(count, rows, 2, half), 1, 2).reshape(width, half)
        full_qkv = jnp.concatenate([full_qk, full_v], axis=1)
        out_all = take(rows).reshape(2, count // 2, rows, width)
        out_got = swap(pick(out_all, 1 - core, 0), 1)
        full_out = merge(pick(out_all, core, 0), out_got, core, 1).reshape(half, width)
        full_up = jnp.concatenate(
            [take(2 * rows).reshape(width, width) for i in range(panels)], axis=1
        )
        full_down = take(hidden_rows).reshape(hidden // 2, width)
        table = take(8).reshape(count, -1)[:, : 2 * small.shape[1]].reshape(count, 2, -1)
        vector_table = table[:, :, : 8 * rows].reshape(count, 2, 8, rows).astype(F32)
        vector_table = jnp.transpose(vector_table, (2, 0, 1, 3)).reshape(8, width)
        vectors, gain_pair = vector_table[:6], vector_table[6:]
        bias_hidden = pick(table[:, :, 8 * rows :], core, 1).reshape(hidden // 2).astype(F32)
        bias_q, bias_v = (
            lax.dynamic_slice_in_dim(vectors[i], core * half, half) for i in range(2)
        )
        qkv_bias = jnp.concatenate([bias_q, jnp.zeros_like(bias_q), bias_v])
        weights.append(
            (full_qkv, full_out, full_up, full_down, qkv_bias, vectors, gain_pair, bias_hidden)
        )

    own = tokens.shape[0]

    def both(value):
        return merge(value, swap(value, 1), core, 0).reshape((2 * own,) + value.shape[1:])

    activations = both(tokens).astype(F32)
    upstream = both(cotangent).astype(F32)
    kept = []
    for layer in range(LAYERS):
        activations, saved = layer_forward(activations, weights[layer], row_type)
        kept.append(saved)
    mixed = lax.dynamic_slice_in_dim(activations, core * own, own).astype(BF)

    shares = [None] * LAYERS
    for layer in reversed(range(LAYERS)):
        d_first, partial, grads, sums = layer_backward(upstream, kept[layer], weights[layer])
        g_qkv, g_out, g_up, g_down = grads
        g_qkv = g_qkv.reshape(count, 2, rows, 3 * half)
        out_pair = g_out.reshape(count // 2, 2, rows, width)
        out_got = swap(pick(out_pair, 1 - core, 1), 1)
        out_terms = merge(pick(out_pair, core, 1), out_got, core, 0)
        pair_sums, chip_sums, hidden_sums = sums
        pair_sums = jnp.transpose(pair_sums.reshape(2, count // 2, 2, rows), (1, 2, 0, 3))
        pair_sums = pair_sums.reshape(count // 2, 4 * rows)
        pair_sums = merge(pair_sums, jnp.zeros_like(pair_sums), core, 0).reshape(count, -1)
        chip_sums = pick(chip_sums.reshape(6, count, 2, rows), core, 2)
        chip_sums = jnp.swapaxes(chip_sums, 0, 1).reshape(count, 6 * rows)
        row = jnp.concatenate([pair_sums, chip_sums, hidden_sums.reshape(count, -1)], axis=1)
        row_size = row.shape[1]
        row = jnp.pad(row.astype(BF), ((0, 0), (0, 8 * width - row_size)))
        terms = jnp.concatenate(
            [
                g_qkv[..., :width].reshape(count, 2 * rows, width),
                jnp.concatenate([g_qkv[:, 0, :, width:], g_qkv[:, 1, :, width:]], axis=2),
                out_terms.reshape(count, rows, width),
            ]
            + [
                g_up[:, i * width : (i + 1) * width].reshape(count, 2 * rows, width)
                for i in range(panels)
            ]
            + [g_down.reshape(count, hidden_rows, width), row.reshape(count, 8, width)],
            axis=1,
        )
        got = chips.scatter(terms)
        place = 0

        def take(height):
            nonlocal place
            place += height
            return got[place - height : place]

        qk = take(2 * rows).reshape(2, rows, width)
        v = take(rows).reshape(rows, 2, half)
        out = take(rows)
        up = [take(2 * rows).reshape(2, rows, width) for i in range(panels)]
        down = take(hidden_rows)
        row = take(8).reshape(-1)[:row_size]
        wide = jnp.concatenate([qk, jnp.swapaxes(v, 0, 1)] + up, axis=2)
        mine = pick(wide, core, 0)
        theirs = swap(pick(wide, 1 - core, 0), 1)
        both_cols = merge(
            mine.reshape(rows, -1, half), theirs.reshape(rows, -1, half), core, 2
        )
        qkv_all = both_cols[:, :3].reshape(rows, 3 * width)
        up_all = jnp.einsum(
            "rgp,kp->rgk", both_cols[:, 3:].reshape(rows, -1, width), order.astype(F32),
            precision=lax.Precision.HIGHEST, preferred_element_type=F32,
        ).reshape(rows, hidden)
        pair_row = row[: 4 * rows].reshape(2, 2, rows)
        pair_row = pick(pair_row, core, 0) + swap(pick(pair_row, 1 - core, 0), 1)
        chip_row = row[4 * rows : 10 * rows].reshape(6, rows)
        vector_row = jnp.concatenate([pair_row, chip_row[:4]], axis=0)
        shares[layer] = (qkv_all, out, up_all, down, vector_row, chip_row[4:], row[10 * rows :])

        if layer > 0:
            upstream = d_first + pair_sum(partial)
        else:
            parts = partial.astype(BF).reshape(2, own, width)
            got = swap(pick(parts, 1 - core, 0), 1).astype(F32)
            mine = lax.dynamic_slice_in_dim(d_first, core * own, own)
            grad_tokens = mine + (pick(parts, core, 0).astype(F32) + got)

    stacked = [jnp.stack([entry[member] for entry in shares]) for member in range(7)]
    return (mixed, grad_tokens, *stacked)


def solution(mesh):
    placed = (
        P("fsdp", None),
        P("fsdp"),
        P(None, "fsdp", None),
        P(None, "fsdp", None),
        P(None, "fsdp", None),
        P(None, "fsdp", None),
        P(None, None, "fsdp"),
        P(None, None, "fsdp"),
        P(None, "fsdp"),
        P("fsdp", None),
    )
    return jax.shard_map(
        shards,
        mesh=mesh,
        in_specs=placed,
        out_specs=(
            P("fsdp", None),
            P("fsdp", None),
            P(None, "fsdp", None),
            P(None, "fsdp", None),
            P(None, "fsdp", None),
            P(None, "fsdp", None),
            P(None, None, "fsdp"),
            P(None, None, "fsdp"),
            P(None, "fsdp"),
        ),
        check_vma=False,
    )
```

```python
import jax
import jax.numpy as jnp
from jax import lax
from jax.sharding import PartitionSpec as P

HEADS = 12
LAYERS = 2
SHORT = 128
AXIS = "fsdp"

EPSILON = 1e-05
MASKED_SCORE = -1e30
BF = jnp.bfloat16
F32 = jnp.float32


def dot(left, right):
    return jnp.dot(left, right, preferred_element_type=F32)


def dot_tn(left, right):
    return lax.dot_general(left, right, (((0,), (0,)), ((), ())), preferred_element_type=F32)


def dot_nt(left, right):
    return lax.dot_general(left, right, (((1,), (1,)), ((), ())), preferred_element_type=F32)


def swap(value, mask):
    pairs = [(source, source ^ mask) for source in range(lax.axis_size(AXIS))]
    return lax.ppermute(value, AXIS, pairs)


def merge(mine, theirs, bit, axis):
    first = jnp.where(bit == 0, mine, theirs)
    second = jnp.where(bit == 0, theirs, mine)
    return jnp.stack([first, second], axis=axis)


class Chips:
    def __init__(self):
        device = lax.axis_index(AXIS)
        self.count = lax.axis_size(AXIS) // 2
        self.core = device % 2
        self.chip = device // 2
        self.step = self.count // 4
        self.top = self.chip // self.step
        self.low = list(range(self.count.bit_length() - 3))

    def bit(self, place):
        return (self.chip // 2**place) % 2

    def order(self, kind):
        return self.low if kind == 0 else self.low[::-1]

    def gather(self, piece):
        groups = [list(range(core, 2 * self.count, 2)) for core in range(2)]
        return lax.all_gather(piece, AXIS, axis=0, axis_index_groups=groups)

    def gather_steps(self, piece, parts):
        near, far, both = (swap(piece, 2 * self.step * k) for k in (1, 2, 3))
        low_bit, high_bit = self.top % 2, self.top // 2
        helds = []
        for start, stop in parts:
            cut = [value[start:stop] for value in (piece, near, far, both)]
            pairs = [merge(cut[i], cut[i + 1], low_bit, 0) for i in (0, 2)]
            held = merge(pairs[0], pairs[1], high_bit, 0)
            helds.append(held.reshape((4,) + cut[0].shape))
        for step in range(len(self.low)):
            for kind in range(len(parts)):
                place = self.order(kind)[step]
                axis = 1 + sum(other > place for other in self.order(kind)[:step])
                held = helds[kind]
                helds[kind] = merge(held, swap(held, 2 * 2**place), self.bit(place), axis)
        return [
            held.reshape((self.count, stop - start) + piece.shape[1:])
            for held, (start, stop) in zip(helds, parts)
        ]

    def scatter(self, grads):
        addends = []
        left = []
        for grad in grads:
            addends.append([grad.reshape((4,) + (2,) * len(self.low) + grad.shape[1:])])
            left.append(list(self.low))
        for step in range(len(self.low)):
            for kind, held in enumerate(addends):
                place = self.order(kind)[::-1][step]
                axis = 1 + sum(other > place for other in left[kind])
                left[kind].remove(place)
                bit = self.bit(place)
                sent = [pick(value, 1 - bit, axis) for value in held]
                kept = [pick(value, bit, axis) for value in held]
                addends[kind] = kept + [swap(add_up(sent).astype(BF), 2 * 2**place)]
        totals = [add_up([pick(value, self.top, 0) for value in held]) for held in addends]
        width = grads[-1].shape[-1]
        totals = [stack_panels(total, width) for total in totals]
        total = jnp.concatenate(totals, axis=0)
        for k in (1, 2, 3):
            sent = [
                stack_panels(add_up([pick(value, self.top ^ k, 0) for value in held]), width)
                for held in addends
            ]
            sent = jnp.concatenate(sent, axis=0).astype(BF)
            total = total + swap(sent, 2 * self.step * k).astype(F32)
        height = totals[0].shape[0]
        return [total[:height], total[height:]]


def pick(pair, index, axis):
    return lax.dynamic_index_in_dim(pair, index, axis, keepdims=False)


def stack_panels(value, width):
    panels = [value[:, i : i + width] for i in range(0, value.shape[1], width)]
    return jnp.concatenate(panels, axis=0) if len(panels) > 1 else value


def add_up(values):
    total = values[0].astype(F32)
    for value in values[1:]:
        total = total + value.astype(F32)
    return total


def layer_norm(values, gain_row, shift_row):
    centre = values - jnp.mean(values, axis=-1, keepdims=True)
    variance = jnp.mean(centre * centre, axis=-1, keepdims=True)
    return centre * lax.rsqrt(variance + EPSILON) * gain_row + shift_row


def gelu_exact(values):
    return jax.nn.gelu(values, approximate=False)


def pair_sum(partial):
    rounded = partial.astype(BF)
    return rounded.astype(F32) + swap(rounded, 1).astype(F32)


def attend(queries, keys, values, row_type):
    count = queries.shape[0]
    place = jnp.arange(count)
    allowed = (place[:, None] // SHORT == place[None, :] // SHORT) | (row_type == 1)
    raw = jnp.einsum("qhd,khd->hqk", queries, keys, preferred_element_type=F32) * 0.125
    probs = jax.nn.softmax(jnp.where(allowed[None], raw, MASKED_SCORE), axis=-1)
    probs_b = probs.astype(BF)
    context = jnp.einsum("hqk,khd->qhd", probs_b, values, preferred_element_type=F32)
    return context, (probs, probs_b)


def layer_forward(inputs, weights, row_type):
    w_qkv, w_out, w_up, w_down, qkv_bias, vectors, gain_pair, bias_up = weights
    count = inputs.shape[0]
    inputs_b = inputs.astype(BF)
    qkv = (dot(inputs_b, w_qkv) + qkv_bias[None]).astype(BF)
    half = qkv.shape[1] // 3
    heads_shape = (count, HEADS // 2, half // (HEADS // 2))
    queries, keys, values = (
        qkv[:, i * half : (i + 1) * half].reshape(heads_shape) for i in range(3)
    )
    context, attended = attend(queries, keys, values, row_type)
    context_b = context.reshape(count, half).astype(BF)
    first_sum = inputs + (pair_sum(dot(context_b, w_out)) + vectors[2])
    normed = layer_norm(first_sum, gain_pair[0], vectors[4])
    normed_b = normed.astype(BF)
    pre_act = dot(normed_b, w_up) + bias_up
    act = gelu_exact(pre_act).astype(BF)
    second_sum = normed + pair_sum(dot(act, w_down)) + vectors[3]
    output = layer_norm(second_sum, gain_pair[1], vectors[5])
    saved = (
        inputs_b, queries, keys, values, attended, context_b, first_sum, normed_b, pre_act, act,
        second_sum,
    )
    return output, saved


def layer_backward(upstream, saved, weights):
    w_qkv, w_out, w_up, w_down, qkv_bias, vectors, gain_pair, bias_up = weights
    (
        inputs_b, queries, keys, values, attended, context_b, first_sum, normed_b, pre_act, act,
        second_sum,
    ) = saved
    probs, probs_b = attended
    count = inputs_b.shape[0]
    _, pull_second = jax.vjp(layer_norm, second_sum, gain_pair[1], vectors[5])
    d_second, d_gain2, d_shift2 = pull_second(upstream)
    d_ffn = d_second.astype(BF)
    g_down = dot_tn(act, d_ffn).astype(BF)
    _, pull_gelu = jax.vjp(gelu_exact, pre_act)
    d_pre = pull_gelu(dot_nt(d_ffn, w_down))[0].astype(BF)
    g_up = dot_tn(normed_b, d_pre).astype(BF)
    d_normed = d_second + pair_sum(dot_nt(d_pre, w_up))
    _, pull_first = jax.vjp(layer_norm, first_sum, gain_pair[0], vectors[4])
    d_first, d_gain1, d_shift1 = pull_first(d_normed)
    d_branch = d_first.astype(BF)
    g_out = dot_tn(context_b, d_branch).astype(BF)
    d_context = dot_nt(d_branch, w_out).astype(BF).reshape(queries.shape)
    d_probs = jnp.einsum("qhd,khd->hqk", d_context, values, preferred_element_type=F32)
    d_values = jnp.einsum("hqk,qhd->khd", probs_b, d_context, preferred_element_type=F32)
    row_dot = jnp.sum(d_probs * probs, axis=-1, keepdims=True)
    d_scores = (probs * (d_probs - row_dot)).astype(BF)
    d_queries = jnp.einsum("hqk,khd->qhd", d_scores, keys, preferred_element_type=F32) * 0.125
    d_keys = jnp.einsum("hqk,qhd->khd", d_scores, queries, preferred_element_type=F32) * 0.125
    d_qkv = jnp.concatenate(
        [part.reshape(count, -1) for part in (d_queries, d_keys, d_values)], axis=1
    ).astype(BF)
    g_qkv = dot_tn(inputs_b, d_qkv).astype(BF)
    partial = dot_nt(d_qkv, w_qkv)
    qkv_sums = jnp.sum(d_qkv.astype(F32), axis=0)
    half = qkv_sums.shape[0] // 3
    sums = (
        jnp.stack([qkv_sums[:half], qkv_sums[2 * half :]]),
        jnp.stack(
            [
                jnp.sum(d_branch.astype(F32), axis=0),
                jnp.sum(d_ffn.astype(F32), axis=0),
                d_shift1,
                d_shift2,
                d_gain1,
                d_gain2,
            ]
        ),
        jnp.sum(d_pre.astype(F32), axis=0),
    )
    return d_first, partial, (g_qkv, g_out, g_up, g_down), sums


def hidden_order(width, hidden_rows):
    group = width // (2 * hidden_rows)
    target = jnp.arange(width)
    source = (
        (target % (width // 2)) // hidden_rows * (2 * hidden_rows)
        + target // (width // 2) * hidden_rows
        + target % hidden_rows
    )
    del group
    return jnp.arange(width)[:, None] == source[None, :]


def shards(tokens, row_kind, w_qkv, w_out, w_up, w_down, bias_vectors, gains, bias_up, cotangent):
    chips = Chips()
    core = chips.core
    count = chips.count
    row_type = row_kind[0]
    rows, width = w_out.shape[1:]
    hidden = w_up.shape[2]
    hidden_rows = w_down.shape[1]
    half = width // 2
    order = hidden_order(width, hidden_rows)

    small = jnp.concatenate(
        [
            jnp.concatenate([bias_vectors, gains], axis=1).reshape(LAYERS, 8 * rows),
            bias_up,
        ],
        axis=1,
    )
    small_pair = merge(small, swap(small, 1), core, 1)
    panels = hidden // 2 // width
    weights = []
    for layer in range(LAYERS):
        up_cols = jnp.einsum(
            "rgk,kp->rgp", w_up[layer].reshape(rows, hidden // width, width), order.astype(BF),
            preferred_element_type=F32,
        ).astype(BF)
        cols = jnp.concatenate(
            [
                w_qkv[layer].reshape(rows, 3, 2, half),
                up_cols.reshape(rows, hidden // width, 2, half),
            ],
            axis=1,
        )
        cols_got = swap(pick(cols, 1 - core, 2), 1)
        cols = merge(pick(cols, core, 2), cols_got, core, 0)
        row = jnp.pad(small_pair[layer].reshape(-1), (0, 8 * width - 2 * small.shape[1]))
        packed = jnp.concatenate(
            [cols[:, :, :2].reshape(2 * rows, width)]
            + [
                cols[:, :, 3 + 2 * i : 5 + 2 * i].reshape(2 * rows, width)
                for i in range(panels)
            ]
            + [
                jnp.concatenate([cols[0, :, 2], cols[1, :, 2]], axis=1),
                w_out[layer],
                w_down[layer],
                row.reshape(8, width),
            ],
            axis=0,
        )
        first = 2 * rows * (1 + panels)
        if layer == 0:
            got = chips.gather(packed)
            got = [got[:, :first], got[:, first:]]
        else:
            got = chips.gather_steps(packed, [(0, first), (first, packed.shape[0])])
        place = 0

        def take(kind, height):
            nonlocal place
            place += height
            return got[kind][:, place - height : place]

        full_qk = take(0, 2 * rows).reshape(width, width)
        full_up = jnp.concatenate(
            [take(0, 2 * rows).reshape(width, width) for i in range(panels)], axis=1
        )
        place = 0
        full_v = jnp.swapaxes(take(1, rows).reshape(count, rows, 2, half), 1, 2)
        full_qkv = jnp.concatenate([full_qk, full_v.reshape(width, half)], axis=1)
        out_all = take(1, rows).reshape(2, count // 2, rows, width)
        out_got = swap(pick(out_all, 1 - core, 0), 1)
        full_out = merge(pick(out_all, core, 0), out_got, core, 1).reshape(half, width)
        full_down = take(1, hidden_rows).reshape(hidden // 2, width)
        table = take(1, 8).reshape(count, -1)[:, : 2 * small.shape[1]].reshape(count, 2, -1)
        vector_table = table[:, :, : 8 * rows].reshape(count, 2, 8, rows).astype(F32)
        vector_table = jnp.transpose(vector_table, (2, 0, 1, 3)).reshape(8, width)
        vectors, gain_pair = vector_table[:6], vector_table[6:]
        bias_hidden = pick(table[:, :, 8 * rows :], core, 1).reshape(hidden // 2).astype(F32)
        bias_q, bias_v = (
            lax.dynamic_slice_in_dim(vectors[i], core * half, half) for i in range(2)
        )
        qkv_bias = jnp.concatenate([bias_q, jnp.zeros_like(bias_q), bias_v])
        weights.append(
            (full_qkv, full_out, full_up, full_down, qkv_bias, vectors, gain_pair, bias_hidden)
        )

    own = tokens.shape[0]

    def both(value):
        return merge(value, swap(value, 1), core, 0).reshape((2 * own,) + value.shape[1:])

    activations = both(tokens).astype(F32)
    upstream = both(cotangent).astype(F32)
    kept = []
    for layer in range(LAYERS):
        activations, saved = layer_forward(activations, weights[layer], row_type)
        kept.append(saved)
    mixed = lax.dynamic_slice_in_dim(activations, core * own, own).astype(BF)

    shares = [None] * LAYERS
    for layer in reversed(range(LAYERS)):
        d_first, partial, grads, sums = layer_backward(upstream, kept[layer], weights[layer])
        g_qkv, g_out, g_up, g_down = grads
        up, down = chips.scatter(
            [
                g_up.reshape(count, 2 * rows, hidden // 2),
                g_down.reshape(count, hidden_rows, width),
            ]
        )
        g_qkv = g_qkv.reshape(count, 2, rows, 3 * half)
        out_pair = g_out.reshape(count // 2, 2, rows, width)
        out_got = swap(pick(out_pair, 1 - core, 1), 1)
        out_terms = merge(pick(out_pair, core, 1), out_got, core, 0)
        pair_sums, chip_sums, hidden_sums = sums
        pair_sums = jnp.transpose(pair_sums.reshape(2, count // 2, 2, rows), (1, 2, 0, 3))
        pair_sums = pair_sums.reshape(count // 2, 4 * rows)
        pair_sums = merge(pair_sums, jnp.zeros_like(pair_sums), core, 0).reshape(count, -1)
        chip_sums = pick(chip_sums.reshape(6, count, 2, rows), core, 2)
        chip_sums = jnp.swapaxes(chip_sums, 0, 1).reshape(count, 6 * rows)
        row = jnp.concatenate([pair_sums, chip_sums, hidden_sums.reshape(count, -1)], axis=1)
        row_size = row.shape[1]
        row = jnp.pad(row.astype(BF), ((0, 0), (0, 8 * width - row_size)))
        qk, rest = chips.scatter(
            [
                g_qkv[..., :width].reshape(count, 2 * rows, width),
                jnp.concatenate(
                    [
                        jnp.concatenate([g_qkv[:, 0, :, width:], g_qkv[:, 1, :, width:]], axis=2),
                        out_terms.reshape(count, rows, width),
                        row.reshape(count, 8, width),
                    ],
                    axis=1,
                ),
            ]
        )
        v = rest[:rows].reshape(rows, 2, half)
        out = rest[rows : 2 * rows]
        row = rest[2 * rows :].reshape(-1)[:row_size]

        def exchange(wide):
            theirs = swap(pick(wide, 1 - core, 0), 1).reshape(rows, -1, half)
            return merge(pick(wide, core, 0).reshape(rows, -1, half), theirs, core, 2)

        qkv_all = exchange(
            jnp.concatenate([qk.reshape(2, rows, width), jnp.swapaxes(v, 0, 1)], axis=2)
        ).reshape(rows, 3 * width)
        up = jnp.concatenate(
            [up[i * 2 * rows :][: 2 * rows].reshape(2, rows, width) for i in range(panels)], axis=2
        )
        up_all = jnp.einsum(
            "rgp,kp->rgk", exchange(up).reshape(rows, -1, width),
            order.astype(F32), precision=lax.Precision.HIGHEST, preferred_element_type=F32,
        ).reshape(rows, hidden)
        pair_row = row[: 4 * rows].reshape(2, 2, rows)
        pair_row = pick(pair_row, core, 0) + swap(pick(pair_row, 1 - core, 0), 1)
        chip_row = row[4 * rows : 10 * rows].reshape(6, rows)
        vector_row = jnp.concatenate([pair_row, chip_row[:4]], axis=0)
        shares[layer] = (qkv_all, out, up_all, down, vector_row, chip_row[4:], row[10 * rows :])

        if layer > 0:
            upstream = d_first + pair_sum(partial)
        else:
            parts = partial.astype(BF).reshape(2, own, width)
            got = swap(pick(parts, 1 - core, 0), 1).astype(F32)
            mine = lax.dynamic_slice_in_dim(d_first, core * own, own)
            grad_tokens = mine + (pick(parts, core, 0).astype(F32) + got)

    stacked = [jnp.stack([entry[member] for entry in shares]) for member in range(7)]
    return (mixed, grad_tokens, *stacked)


def solution(mesh):
    placed = (
        P("fsdp", None),
        P("fsdp"),
        P(None, "fsdp", None),
        P(None, "fsdp", None),
        P(None, "fsdp", None),
        P(None, "fsdp", None),
        P(None, None, "fsdp"),
        P(None, None, "fsdp"),
        P(None, "fsdp"),
        P("fsdp", None),
    )
    return jax.shard_map(
        shards,
        mesh=mesh,
        in_specs=placed,
        out_specs=(
            P("fsdp", None),
            P("fsdp", None),
            P(None, "fsdp", None),
            P(None, "fsdp", None),
            P(None, "fsdp", None),
            P(None, "fsdp", None),
            P(None, None, "fsdp"),
            P(None, None, "fsdp"),
            P(None, "fsdp"),
        ),
        check_vma=False,
    )
```

```python
import jax
import jax.numpy as jnp
from jax import lax
from jax.sharding import PartitionSpec as P

HEADS = 12
LAYERS = 2
SHORT = 128
AXIS = "fsdp"

EPSILON = 1e-05
MASKED_SCORE = -1e30
BF = jnp.bfloat16
F32 = jnp.float32


def dot(left, right):
    return jnp.dot(left, right, preferred_element_type=F32)


def dot_tn(left, right):
    return lax.dot_general(left, right, (((0,), (0,)), ((), ())), preferred_element_type=F32)


def dot_nt(left, right):
    return lax.dot_general(left, right, (((1,), (1,)), ((), ())), preferred_element_type=F32)


def swap(value, mask):
    pairs = [(source, source ^ mask) for source in range(lax.axis_size(AXIS))]
    return lax.ppermute(value, AXIS, pairs)


def merge(mine, theirs, bit, axis):
    first = jnp.where(bit == 0, mine, theirs)
    second = jnp.where(bit == 0, theirs, mine)
    return jnp.stack([first, second], axis=axis)


class Chips:
    def __init__(self):
        device = lax.axis_index(AXIS)
        self.count = lax.axis_size(AXIS) // 2
        self.core = device % 2
        self.chip = device // 2
        self.step = self.count // 4
        self.top = self.chip // self.step
        self.low = list(range(self.count.bit_length() - 3))

    def bit(self, place):
        return (self.chip // 2**place) % 2

    def order(self, kind):
        return self.low if kind == 0 else self.low[::-1]

def pick(pair, index, axis):
    return lax.dynamic_index_in_dim(pair, index, axis, keepdims=False)


def stack_panels(value, width):
    panels = [value[:, i : i + width] for i in range(0, value.shape[1], width)]
    return jnp.concatenate(panels, axis=0) if len(panels) > 1 else value


def add_up(values):
    total = values[0].astype(F32)
    for value in values[1:]:
        total = total + value.astype(F32)
    return total


class Sequence:
    def __init__(self):
        self.last = None

    def gate(self, values):
        if self.last is None:
            return values
        values, _ = lax.optimization_barrier((values, self.last))
        return values

    def mark(self, values):
        self.last = values


class Gather:
    def __init__(self, chips, sequence, first, second):
        self.chips, self.sequence = chips, sequence
        self.heights = (first.shape[0], second.shape[0])
        self.piece = jnp.concatenate([first, second], axis=0)
        self.steps_done = 0
        self.helds = None

    def start(self):
        self.piece = self.sequence.gate(self.piece)
        self.sequence.mark(self.piece)
        self.coming = [swap(self.piece, 2 * self.chips.step * k) for k in (1, 2, 3)]

    def advance(self):
        chips = self.chips
        coming = self.sequence.gate(self.coming)
        step = self.steps_done
        if step == 0:
            low_bit, high_bit = chips.top % 2, chips.top // 2
            helds = []
            place = 0
            for height in self.heights:
                cut = [value[place : place + height] for value in [self.piece] + coming]
                pairs = [merge(cut[i], cut[i + 1], low_bit, 0) for i in (0, 2)]
                held = merge(pairs[0], pairs[1], high_bit, 0)
                helds.append(held.reshape((4,) + cut[0].shape))
                place += height
        else:
            helds = []
            for kind in range(2):
                order = chips.order(kind)
                bit = order[step - 1]
                axis = 1 + sum(other > bit for other in order[: step - 1])
                helds.append(merge(self.helds[kind], coming[kind], chips.bit(bit), axis))
        self.helds = helds
        self.sequence.mark(helds)
        if step < len(chips.low):
            self.coming = [
                swap(held, 2 * 2 ** chips.order(kind)[step]) for kind, held in enumerate(helds)
            ]
        self.steps_done += 1

    def finish(self):
        while self.steps_done <= len(self.chips.low):
            self.advance()
        return [
            held.reshape((self.chips.count,) + held.shape[-2:]) for held in self.helds
        ]


class Scatter:
    def __init__(self, chips, sequence):
        self.chips, self.sequence = chips, sequence
        self.addends = [None, None]
        self.coming = [None, None]
        self.left = [list(chips.low), list(chips.low)]
        self.steps_done = 0

    def start(self, kind, terms):
        shape = (4,) + (2,) * len(self.chips.low) + terms.shape[1:]
        self.send(kind, [terms.reshape(shape)])

    def send(self, kind, held):
        chips = self.chips
        place = chips.order(kind)[::-1][self.steps_done]
        axis = 1 + sum(other > place for other in self.left[kind])
        self.left[kind].remove(place)
        bit = chips.bit(place)
        sent = add_up([pick(value, 1 - bit, axis) for value in held]).astype(BF)
        self.addends[kind] = [pick(value, bit, axis) for value in held]
        self.coming[kind] = swap(sent, 2 * 2**place)
        self.sent = sent

    def advance(self):
        chips = self.chips
        self.steps_done += 1
        coming = self.sequence.gate(self.coming)
        held = [addends + [got] for addends, got in zip(self.addends, coming)]
        if self.steps_done < len(chips.low):
            sents = []
            for kind in range(2):
                self.send(kind, held[kind])
                sents.append(self.sent)
            self.sequence.mark(sents)
            return
        width = coming[1].shape[-1]

        def total(place):
            sums = [add_up([pick(value, place, 0) for value in values]) for values in held]
            sums = [stack_panels(value, width) for value in sums]
            self.height = sums[0].shape[0]
            return jnp.concatenate(sums, axis=0)

        sents = [total(chips.top ^ k).astype(BF) for k in (1, 2, 3)]
        self.own = total(chips.top)
        self.sequence.mark(sents)
        self.coming = [swap(sent, 2 * chips.step * k) for sent, k in zip(sents, (1, 2, 3))]

    def finish(self):
        while self.steps_done < len(self.chips.low):
            self.advance()
        coming = self.sequence.gate(self.coming)
        total = add_up([self.own] + coming)
        self.sequence.mark(total)
        return total[: self.height], total[self.height :]


def layer_norm(values, gain_row, shift_row):
    centre = values - jnp.mean(values, axis=-1, keepdims=True)
    variance = jnp.mean(centre * centre, axis=-1, keepdims=True)
    return centre * lax.rsqrt(variance + EPSILON) * gain_row + shift_row


def gelu_exact(values):
    return jax.nn.gelu(values, approximate=False)


def pair_sum(partial):
    rounded = partial.astype(BF)
    return rounded.astype(F32) + swap(rounded, 1).astype(F32)


def attend(queries, keys, values, row_type):
    count = queries.shape[0]
    place = jnp.arange(count)
    allowed = (place[:, None] // SHORT == place[None, :] // SHORT) | (row_type == 1)
    raw = jnp.einsum("qhd,khd->hqk", queries, keys, preferred_element_type=F32) * 0.125
    probs = jax.nn.softmax(jnp.where(allowed[None], raw, MASKED_SCORE), axis=-1)
    probs_b = probs.astype(BF)
    context = jnp.einsum("hqk,khd->qhd", probs_b, values, preferred_element_type=F32)
    return context, (probs, probs_b)


def forward_attention(inputs, w_qk, w_v, w_out, qkv_bias, row_type):
    count = inputs.shape[0]
    inputs_b = inputs.astype(BF)
    half = w_v.shape[1]
    qk = (dot(inputs_b, w_qk) + qkv_bias[0]).astype(BF)
    v = (dot(inputs_b, w_v) + qkv_bias[1]).astype(BF)
    heads_shape = (count, HEADS // 2, half // (HEADS // 2))
    queries, keys, values = (
        part.reshape(heads_shape) for part in (qk[:, :half], qk[:, half:], v)
    )
    context, attended = attend(queries, keys, values, row_type)
    context_b = context.reshape(count, half).astype(BF)
    partial = dot(context_b, w_out).astype(BF)
    return partial, (inputs_b, queries, keys, values, attended, context_b)


def forward_hidden(inputs, branch, w_up, w_down, vectors, gain_pair, bias_up):
    first_sum = inputs + (branch + vectors[2])
    normed = layer_norm(first_sum, gain_pair[0], vectors[4])
    normed_b = normed.astype(BF)
    pre_act = jnp.concatenate([dot(normed_b, panel) for panel in w_up], axis=1) + bias_up
    act = gelu_exact(pre_act).astype(BF)
    partial = dot(act, w_down).astype(BF)
    return normed, partial, (first_sum, normed_b, pre_act, act)


def backward_attention(d_context, saved):
    inputs_b, queries, keys, values, (probs, probs_b), context_b = saved
    count = inputs_b.shape[0]
    d_context = d_context.astype(BF).reshape(queries.shape)
    d_probs = jnp.einsum("qhd,khd->hqk", d_context, values, preferred_element_type=F32)
    d_values = jnp.einsum("hqk,qhd->khd", probs_b, d_context, preferred_element_type=F32)
    row_dot = jnp.sum(d_probs * probs, axis=-1, keepdims=True)
    d_scores = (probs * (d_probs - row_dot)).astype(BF)
    d_queries = jnp.einsum("hqk,khd->qhd", d_scores, keys, preferred_element_type=F32) * 0.125
    d_keys = jnp.einsum("hqk,qhd->khd", d_scores, queries, preferred_element_type=F32) * 0.125
    d_qk = jnp.concatenate([d_queries.reshape(count, -1), d_keys.reshape(count, -1)], axis=1)
    return d_qk.astype(BF), d_values.reshape(count, -1).astype(BF)


def hidden_order(width, hidden_rows):
    group = width // (2 * hidden_rows)
    target = jnp.arange(width)
    source = (
        (target % (width // 2)) // hidden_rows * (2 * hidden_rows)
        + target // (width // 2) * hidden_rows
        + target % hidden_rows
    )
    del group
    return jnp.arange(width)[:, None] == source[None, :]


def shards(tokens, row_kind, w_qkv, w_out, w_up, w_down, bias_vectors, gains, bias_up, cotangent):
    chips = Chips()
    sequence = Sequence()
    core = chips.core
    count = chips.count
    device = 2 * chips.chip + core
    row_type = row_kind[0]
    rows, width = w_out.shape[1:]
    hidden = w_up.shape[2]
    hidden_rows = w_down.shape[1]
    half = width // 2
    panels = hidden // 2 // width
    own = tokens.shape[0]
    order = hidden_order(width, hidden_rows)

    qkv_cols = w_qkv.reshape(LAYERS, rows, 3, 2, half)
    qkv_got = swap(pick(qkv_cols, 1 - core, 3), 1)
    qkv_cols = merge(pick(qkv_cols, core, 3), qkv_got, core, 1)
    up_cols = jnp.einsum(
        "lrgk,kp->lrgp", w_up.reshape(LAYERS, rows, hidden // width, width), order.astype(BF),
        preferred_element_type=F32,
    ).astype(BF).reshape(LAYERS, rows, hidden // width, 2, half)
    up_got = swap(pick(up_cols, 1 - core, 3), 1)
    up_cols = merge(pick(up_cols, core, 3), up_got, core, 1)

    bundles = []
    for layer in range(LAYERS):
        cols = qkv_cols[layer]
        bundles.append(
            Gather(
                chips, sequence,
                cols[:, :, :2].reshape(2 * rows, width),
                jnp.concatenate(
                    [jnp.concatenate([cols[0, :, 2], cols[1, :, 2]], axis=1), w_out[layer]], axis=0
                ),
            )
        )
        cols = up_cols[layer]
        bundles.append(
            Gather(
                chips, sequence,
                jnp.concatenate(
                    [
                        cols[:, :, 2 * i : 2 * i + 2].reshape(2 * rows, width)
                        for i in range(panels)
                    ],
                    axis=0,
                ),
                w_down[layer],
            )
        )
    attn0, ffn0, attn1, ffn1 = bundles

    feature = jnp.arange(width)[None, :] - rows * device == jnp.arange(rows)[:, None]
    unit = jnp.arange(hidden // 2)[None, :] - hidden_rows * chips.chip
    unit = unit == jnp.arange(hidden_rows)[:, None]
    vector_rows = jnp.concatenate([bias_vectors, gains], axis=1).reshape(LAYERS * 8, rows)
    vector_rows = dot(vector_rows, feature.astype(BF)).astype(BF)
    unit_rows = [
        dot(bias_up, unit[:, i * width : (i + 1) * width].astype(BF)).astype(BF)
        for i in range(panels)
    ]
    attn0.start()
    vector_rows = vector_rows + swap(vector_rows, 1)
    table = jnp.concatenate([vector_rows] + unit_rows, axis=0)
    for place in range(count.bit_length() - 1):
        table = table + swap(table, 2 * 2**place)
    table = table.astype(F32)

    def both(value):
        return merge(value, swap(value, 1), core, 0).reshape((2 * own,) + value.shape[1:])

    def attention_weights(bundle, layer):
        first, second = bundle.finish()
        w_qk = first.reshape(width, width)
        w_v = jnp.swapaxes(second[:, :rows].reshape(count, rows, 2, half), 1, 2)
        w_v = w_v.reshape(width, half)
        out_all = second[:, rows:].reshape(2, count // 2, rows, width)
        out_got = swap(pick(out_all, 1 - core, 0), 1)
        full_out = merge(pick(out_all, core, 0), out_got, core, 1).reshape(half, width)
        vectors = table[8 * layer : 8 * layer + 8]
        halves = [pick(vectors[i].reshape(2, half), core, 0) for i in range(2)]
        qk_bias = jnp.concatenate([halves[0], jnp.zeros_like(halves[0])])
        return w_qk, w_v, full_out, (qk_bias, halves[1])

    def hidden_weights(bundle, layer):
        first, second = bundle.finish()
        up_panels = [
            first[:, 2 * rows * i : 2 * rows * (i + 1)].reshape(width, width)
            for i in range(panels)
        ]
        bias = jnp.concatenate(
            [table[8 * LAYERS + LAYERS * i + layer] for i in range(panels)]
        )
        return up_panels, second.reshape(hidden // 2, width), bias

    vectors = [table[8 * layer : 8 * layer + 6] for layer in range(LAYERS)]
    gain_pairs = [table[8 * layer + 6 : 8 * layer + 8] for layer in range(LAYERS)]
    x_0 = both(tokens).astype(F32)
    upstream = both(cotangent).astype(F32)

    ffn0.start()
    attn0.advance()
    attn0.advance()
    ffn0.advance()
    attn1.start()
    w_qk0, w_v0, w_out0, bias0 = attention_weights(attn0, 0)
    x_0, w_qk0 = sequence.gate((x_0, w_qk0))
    partial, saved0 = forward_attention(x_0, w_qk0, w_v0, w_out0, bias0, row_type)
    sequence.mark(partial)
    ffn0.advance()
    attn1.advance()
    ffn1.start()
    branch = partial.astype(F32) + swap(partial, 1).astype(F32)
    attn1.advance()
    w_up0, w_down0, bias_up0 = hidden_weights(ffn0, 0)
    branch = sequence.gate(branch)
    normed, partial, kept0 = forward_hidden(
        x_0, branch, w_up0, w_down0, vectors[0], gain_pairs[0], bias_up0
    )
    sequence.mark(partial)
    ffn1.advance()
    second0 = normed + (partial.astype(F32) + swap(partial, 1).astype(F32)) + vectors[0][3]
    x_1 = layer_norm(second0, gain_pairs[0][1], vectors[0][5])
    w_qk1, w_v1, w_out1, bias1 = attention_weights(attn1, 1)
    x_1 = sequence.gate(x_1)
    partial, saved1 = forward_attention(x_1, w_qk1, w_v1, w_out1, bias1, row_type)
    sequence.mark(partial)
    ffn1.advance()
    branch = partial.astype(F32) + swap(partial, 1).astype(F32)
    w_up1, w_down1, bias_up1 = hidden_weights(ffn1, 1)
    branch = sequence.gate(branch)
    normed, partial, kept1 = forward_hidden(
        x_1, branch, w_up1, w_down1, vectors[1], gain_pairs[1], bias_up1
    )
    second1 = normed + (partial.astype(F32) + swap(partial, 1).astype(F32)) + vectors[1][3]
    x_2 = layer_norm(second1, gain_pairs[1][1], vectors[1][5])
    mixed = lax.dynamic_slice_in_dim(x_2, core * own, own).astype(BF)

    sums = [None] * LAYERS
    shares = [None] * LAYERS

    def exchange(wide):
        theirs = swap(pick(wide, 1 - core, 0), 1).reshape(rows, -1, half)
        return merge(pick(wide, core, 0).reshape(rows, -1, half), theirs, core, 2)

    def finish_hidden(bundle):
        up, down = bundle.finish()
        up = jnp.concatenate(
            [up[i * 2 * rows :][: 2 * rows].reshape(2, rows, width) for i in range(panels)], axis=2
        )
        up = jnp.einsum(
            "rgp,kp->rgk", exchange(up).reshape(rows, -1, width),
            order.astype(F32), precision=lax.Precision.HIGHEST, preferred_element_type=F32,
        ).reshape(rows, hidden)
        return up, down

    def finish_attention(bundle):
        qk, rest = bundle.finish()
        v = rest[:rows].reshape(rows, 2, half)
        qkv = exchange(
            jnp.concatenate([qk.reshape(2, rows, width), jnp.swapaxes(v, 0, 1)], axis=2)
        ).reshape(rows, 3 * width)
        return qkv, rest[rows:]

    def column_sums(value):
        return jnp.sum(value.astype(F32), axis=0)

    def second_norm(upstream, second, layer):
        _, pull = jax.vjp(layer_norm, second, gain_pairs[layer][1], vectors[layer][5])
        d_second, d_gain2, d_shift2 = pull(upstream)
        return d_second, (d_gain2, d_shift2)

    def hidden_down(d_second, kept, w_down, bundle):
        d_ffn = d_second.astype(BF)
        act = kept[3]
        bundle.start(1, dot_tn(act, d_ffn).astype(BF).reshape(count, hidden_rows, width))
        _, pull_gelu = jax.vjp(gelu_exact, kept[2])
        return d_ffn, pull_gelu(dot_nt(d_ffn, w_down))[0].astype(BF)

    def hidden_up(d_pre, kept, w_up, bundle):
        bundle.start(0, dot_tn(kept[1], d_pre).astype(BF).reshape(count, 2 * rows, -1))
        sequence.mark(bundle.sent)
        return add_up(
            [dot_nt(d_pre[:, i * width : (i + 1) * width], w_up[i]) for i in range(panels)]
        ).astype(BF)

    def first_norm(d_normed, kept, layer):
        _, pull = jax.vjp(layer_norm, kept[0], gain_pairs[layer][0], vectors[layer][4])
        d_first, d_gain1, d_shift1 = pull(d_normed)
        return d_first, (d_gain1, d_shift1)

    def out_terms(context_b, d_branch):
        out_pair = dot_tn(context_b, d_branch).astype(BF).reshape(count // 2, 2, rows, width)
        out_got = swap(pick(out_pair, 1 - core, 1), 1)
        return merge(pick(out_pair, core, 1), out_got, core, 0).reshape(count, rows, width)

    def attention_terms(inputs_b, d_qk, d_v, out, bundle):
        g_qk = dot_tn(inputs_b, d_qk).astype(BF).reshape(count, 2 * rows, width)
        g_v = dot_tn(inputs_b, d_v).astype(BF).reshape(count, 2, rows, half)
        rest = jnp.concatenate(
            [jnp.concatenate([g_v[:, 0], g_v[:, 1]], axis=2), out], axis=1
        )
        bundle.start(0, g_qk)
        first = bundle.sent
        bundle.start(1, rest)
        sequence.mark((first, bundle.sent))

    def layer_sums(d_qk, d_v, d_branch, d_ffn, d_pre, norm1, norm2):
        pair = jnp.stack([column_sums(d_qk[:, :half]), column_sums(d_v)])
        pair = merge(pair, swap(pair, 1), core, 1).reshape(2, width)
        return jnp.concatenate(
            [
                pair,
                jnp.stack(
                    [
                        column_sums(d_branch),
                        column_sums(d_ffn),
                        norm1[1],
                        norm2[1],
                        norm1[0],
                        norm2[0],
                    ]
                ),
                column_sums(d_pre).reshape(panels, width),
            ],
            axis=0,
        )

    scatter_ffn1 = Scatter(chips, sequence)
    scatter_attn1 = Scatter(chips, sequence)
    scatter_ffn0 = Scatter(chips, sequence)
    scatter_attn0 = Scatter(chips, sequence)

    d_second, norm2 = second_norm(upstream, second1, 1)
    d_ffn, d_pre = hidden_down(d_second, kept1, w_down1, scatter_ffn1)
    partial = hidden_up(d_pre, kept1, w_up1, scatter_ffn1)
    partial = sequence.gate(partial)
    d_normed = d_second + (partial.astype(F32) + swap(partial, 1).astype(F32))
    d_first, norm1 = first_norm(d_normed, kept1, 1)
    d_branch = d_first.astype(BF)
    out = out_terms(saved1[5], d_branch)
    d_qk, d_v = backward_attention(dot_nt(d_branch, w_out1), saved1)
    sequence.mark(d_qk)
    scatter_ffn1.advance()
    d_qk, d_v = sequence.gate((d_qk, d_v))
    attention_terms(saved1[0], d_qk, d_v, out, scatter_attn1)
    sums[1] = layer_sums(d_qk, d_v, d_branch, d_ffn, d_pre, norm1, norm2)
    partial = (dot_nt(d_qk, w_qk1) + dot_nt(d_v, w_v1)).astype(BF)
    partial = sequence.gate(partial)
    upstream = d_first + (partial.astype(F32) + swap(partial, 1).astype(F32))

    d_second, norm2 = second_norm(upstream, second0, 0)
    sequence.mark(d_second)
    scatter_ffn1.advance()
    d_second = sequence.gate(d_second)
    d_ffn, d_pre = hidden_down(d_second, kept0, w_down0, scatter_ffn0)
    d_pre = sequence.gate(d_pre)
    sequence.mark(d_pre)
    scatter_attn1.advance()
    d_pre = sequence.gate(d_pre)
    partial = hidden_up(d_pre, kept0, w_up0, scatter_ffn0)
    partial = sequence.gate(partial)
    d_normed = d_second + (partial.astype(F32) + swap(partial, 1).astype(F32))
    d_first, norm1 = first_norm(d_normed, kept0, 0)
    sequence.mark(d_first)
    scatter_attn1.advance()
    up1, down1 = finish_hidden(scatter_ffn1)
    d_first = sequence.gate(d_first)
    d_branch = d_first.astype(BF)
    out = out_terms(saved0[5], d_branch)
    d_qk, d_v = backward_attention(dot_nt(d_branch, w_out0), saved0)
    sequence.mark(d_qk)
    scatter_ffn0.advance()
    d_qk, d_v = sequence.gate((d_qk, d_v))
    attention_terms(saved0[0], d_qk, d_v, out, scatter_attn0)
    sums[0] = layer_sums(d_qk, d_v, d_branch, d_ffn, d_pre, norm1, norm2)
    partial = (dot_nt(d_qk, w_qk0) + dot_nt(d_v, w_v0)).astype(BF).reshape(2, own, width)
    partial = sequence.gate(partial)
    got = swap(pick(partial, 1 - core, 0), 1).astype(F32)
    mine = lax.dynamic_slice_in_dim(d_first, core * own, own)
    grad_tokens = mine + (pick(partial, core, 0).astype(F32) + got)
    sequence.mark(grad_tokens)
    qkv1, out1 = finish_attention(scatter_attn1)
    scatter_ffn0.advance()
    scatter_attn0.advance()
    scatter_attn0.advance()
    up0, down0 = finish_hidden(scatter_ffn0)
    qkv0, out0 = finish_attention(scatter_attn0)

    total = jnp.stack(sums)
    for place in range(count.bit_length() - 1):
        total = total + swap(total, 2 * 2**place)
    features = lax.dynamic_slice_in_dim(total[:, :8], rows * device, rows, axis=2)
    units = total[:, 8:].reshape(LAYERS, hidden // 2)
    units = lax.dynamic_slice_in_dim(units, hidden_rows * chips.chip, hidden_rows, axis=1)
    return (
        mixed,
        grad_tokens,
        jnp.stack([qkv0, qkv1]),
        jnp.stack([out0, out1]),
        jnp.stack([up0, up1]),
        jnp.stack([down0, down1]),
        features[:, :6],
        features[:, 6:],
        units,
    )


def solution(mesh):
    placed = (
        P("fsdp", None),
        P("fsdp"),
        P(None, "fsdp", None),
        P(None, "fsdp", None),
        P(None, "fsdp", None),
        P(None, "fsdp", None),
        P(None, None, "fsdp"),
        P(None, None, "fsdp"),
        P(None, "fsdp"),
        P("fsdp", None),
    )
    return jax.shard_map(
        shards,
        mesh=mesh,
        in_specs=placed,
        out_specs=(
            P("fsdp", None),
            P("fsdp", None),
            P(None, "fsdp", None),
            P(None, "fsdp", None),
            P(None, "fsdp", None),
            P(None, "fsdp", None),
            P(None, None, "fsdp"),
            P(None, None, "fsdp"),
            P(None, "fsdp"),
        ),
        check_vma=False,
    )
```

```python
import jax
import jax.numpy as jnp
from jax import lax
from jax.experimental import pallas as pl
from jax.experimental.pallas import tpu as pltpu
from jax.sharding import PartitionSpec as P

HEADS = 12
HEAD_DIM = 64
LAYERS = 2
SHORT = 128
AXIS = "fsdp"

EPSILON = 1e-05
MASKED_SCORE = -1e30
BF = jnp.bfloat16
F32 = jnp.float32
LATENCY = 3.0


def dot(left, right):
    return jnp.dot(left, right, preferred_element_type=F32)


def dot_tn(left, right):
    return lax.dot_general(left, right, (((0,), (0,)), ((), ())), preferred_element_type=F32)


def dot_nt(left, right):
    return lax.dot_general(left, right, (((1,), (1,)), ((), ())), preferred_element_type=F32)


def swap(value, mask):
    pairs = [(source, source ^ mask) for source in range(lax.axis_size(AXIS))]
    return lax.ppermute(value, AXIS, pairs)


def merge(mine, theirs, bit, axis):
    first = jnp.where(bit == 0, mine, theirs)
    second = jnp.where(bit == 0, theirs, mine)
    return jnp.stack([first, second], axis=axis)


class Chips:
    def __init__(self):
        device = lax.axis_index(AXIS)
        self.count = lax.axis_size(AXIS) // 2
        self.core = device % 2
        self.chip = device // 2
        self.step = self.count // 4
        self.top = self.chip // self.step
        self.low = list(range(self.count.bit_length() - 3))

    def bit(self, place):
        return (self.chip // 2**place) % 2

    def order(self, kind):
        return self.low if kind == 0 else self.low[::-1]

def pick(pair, index, axis):
    return lax.dynamic_index_in_dim(pair, index, axis, keepdims=False)


def stack_panels(value, width):
    panels = [value[:, i : i + width] for i in range(0, value.shape[1], width)]
    return jnp.concatenate(panels, axis=0) if len(panels) > 1 else value


def add_up(values):
    total = values[0].astype(F32)
    for value in values[1:]:
        total = total + value.astype(F32)
    return total


class Sequence:
    def __init__(self):
        self.last = None

    def gate(self, values):
        if self.last is None:
            return values
        values, _ = lax.optimization_barrier((values, self.last))
        return values

    def mark(self, values):
        self.last = values


class Plan:
    def __init__(self):
        self.pieces = []

    def add(self, name, rank, cost, needs, run, sends=()):
        self.pieces.append((name, rank, cost, needs, run, sends))

    def run(self):
        now = 0.0
        ready = {}
        free = {}
        waiting = list(self.pieces)
        while waiting:
            known = [
                (max([ready[need] for need in piece[3]], default=0.0), piece)
                for piece in waiting
                if all(need in ready for need in piece[3])
            ]
            able = [(piece[1], place) for place, (time, piece) in enumerate(known) if time <= now]
            if able:
                _, place = min(able)
            else:
                _, place = min((time, place) for place, (time, _) in enumerate(known))
            time, piece = known[place]
            name, _, cost, _, run, sends = piece
            begin = max(now, time)
            now = begin + cost
            run()
            ready[name] = now
            for label, link, length in sends:
                end = max(now, free.get(link, 0.0)) + length
                free[link] = end
                ready[label] = end + LATENCY
            waiting.remove(piece)


class Gather:
    def __init__(self, chips, sequence, first, second):
        self.chips, self.sequence = chips, sequence
        self.heights = (first.shape[0], second.shape[0])
        self.piece = jnp.concatenate([first, second], axis=0)
        self.steps_done = 0
        self.helds = None

    def start(self):
        self.piece = self.sequence.gate(self.piece)
        self.sequence.mark(self.piece)
        self.coming = [swap(self.piece, 2 * self.chips.step * k) for k in (1, 2, 3)]

    def advance(self):
        chips = self.chips
        coming = self.sequence.gate(self.coming)
        step = self.steps_done
        if step == 0:
            low_bit, high_bit = chips.top % 2, chips.top // 2
            helds = []
            place = 0
            for height in self.heights:
                cut = [value[place : place + height] for value in [self.piece] + coming]
                pairs = [merge(cut[i], cut[i + 1], low_bit, 0) for i in (0, 2)]
                held = merge(pairs[0], pairs[1], high_bit, 0)
                helds.append(held.reshape((4,) + cut[0].shape))
                place += height
        else:
            helds = []
            for kind in range(2):
                order = chips.order(kind)
                bit = order[step - 1]
                axis = 1 + sum(other > bit for other in order[: step - 1])
                helds.append(merge(self.helds[kind], coming[kind], chips.bit(bit), axis))
        self.helds = helds
        self.sequence.mark(helds)
        if step < len(chips.low):
            self.coming = [
                swap(held, 2 * 2 ** chips.order(kind)[step]) for kind, held in enumerate(helds)
            ]
        self.steps_done += 1

    def finish(self):
        while self.steps_done <= len(self.chips.low):
            self.advance()
        return [
            held.reshape((self.chips.count,) + held.shape[-2:]) for held in self.helds
        ]


class Scatter:
    def __init__(self, chips, sequence):
        self.chips, self.sequence = chips, sequence
        self.addends = [None, None]
        self.coming = [None, None]
        self.left = [list(chips.low), list(chips.low)]
        self.steps_done = 0

    def start(self, kind, terms):
        shape = (4,) + (2,) * len(self.chips.low) + terms.shape[1:]
        self.send(kind, [terms.reshape(shape)])

    def send(self, kind, held):
        chips = self.chips
        place = chips.order(kind)[::-1][self.steps_done]
        axis = 1 + sum(other > place for other in self.left[kind])
        self.left[kind].remove(place)
        bit = chips.bit(place)
        sent = add_up([pick(value, 1 - bit, axis) for value in held]).astype(BF)
        self.addends[kind] = [pick(value, bit, axis) for value in held]
        self.coming[kind] = swap(sent, 2 * 2**place)
        self.sent = sent

    def advance(self):
        chips = self.chips
        self.steps_done += 1
        coming = self.sequence.gate(self.coming)
        held = [addends + [got] for addends, got in zip(self.addends, coming)]
        if self.steps_done < len(chips.low):
            sents = []
            for kind in range(2):
                self.send(kind, held[kind])
                sents.append(self.sent)
            self.sequence.mark(sents)
            return
        width = coming[1].shape[-1]

        def total(place):
            sums = [add_up([pick(value, place, 0) for value in values]) for values in held]
            sums = [stack_panels(value, width) for value in sums]
            self.height = sums[0].shape[0]
            return jnp.concatenate(sums, axis=0)

        sents = [total(chips.top ^ k).astype(BF) for k in (1, 2, 3)]
        self.own = total(chips.top)
        self.sequence.mark(sents)
        self.coming = [swap(sent, 2 * chips.step * k) for sent, k in zip(sents, (1, 2, 3))]

    def finish(self):
        while self.steps_done < len(self.chips.low):
            self.advance()
        coming = self.sequence.gate(self.coming)
        total = add_up([self.own] + coming)
        self.sequence.mark(total)
        return total[: self.height], total[self.height :]


def layer_norm(values, gain_row, shift_row):
    centre = values - jnp.mean(values, axis=-1, keepdims=True)
    variance = jnp.mean(centre * centre, axis=-1, keepdims=True)
    return centre * lax.rsqrt(variance + EPSILON) * gain_row + shift_row


def gelu_exact(values):
    return jax.nn.gelu(values, approximate=False)


def pair_sum(partial):
    rounded = partial.astype(BF)
    return rounded.astype(F32) + swap(rounded, 1).astype(F32)


def head_lanes(value, head):
    lane = lax.broadcasted_iota(jnp.int32, value.shape, 1)
    return (lane // (value.shape[1] // 2)) == head


def mask_row(kind, chunk, count):
    place = lax.broadcasted_iota(jnp.int32, (1, count), 1)
    allowed = (place // SHORT == chunk) | (kind == 1)
    return jnp.where(allowed, 0.0, MASKED_SCORE)


def attention_kernel(
    kind_ref, x_ref, wa_ref, wb_ref, bias_ref, wo_ref, partial_ref, qkv_ref, context_ref, lse_ref
):
    count = x_ref.shape[0]
    wide = wa_ref.shape[1]
    pair = 2 * HEAD_DIM
    kind = kind_ref[0]
    x = x_ref[...]
    bias = bias_ref[...]
    qkv_ref[:, :wide] = (dot(x, wa_ref[...]) + bias[:, :wide]).astype(BF)
    qkv_ref[:, wide:] = (dot(x, wb_ref[...]) + bias[:, wide:]).astype(BF)
    for p in range(HEADS // 4):
        keys = qkv_ref[:, (3 * p + 1) * pair : (3 * p + 2) * pair]
        values = qkv_ref[:, (3 * p + 2) * pair : (3 * p + 3) * pair]

        def chunk_step(chunk, carry):
            rows = pl.ds(pl.multiple_of(chunk * SHORT, SHORT), SHORT)
            queries = qkv_ref[rows, 3 * p * pair : (3 * p + 1) * pair] * jnp.asarray(0.125, BF)
            mask = mask_row(kind, chunk, count)
            found = []
            stats = lse_ref[rows, :] if p > 0 else jnp.zeros((SHORT, 128), F32)
            lane = lax.broadcasted_iota(jnp.int32, stats.shape, 1)
            for head in range(2):
                mine = jnp.where(head_lanes(queries, head), queries, jnp.zeros_like(queries))
                scores = dot_nt(mine, keys) + mask
                top = jnp.max(scores, axis=1, keepdims=True)
                powers = jnp.exp(scores - top)
                total = jnp.sum(powers, axis=1, keepdims=True)
                probs = powers * (1.0 / total)
                found.append(dot(probs.astype(BF), values))
                stats = jnp.where(lane == 2 * p + head, top + jnp.log(total), stats)
            lse_ref[rows, :] = stats
            both = jnp.where(head_lanes(found[0], 0), found[0], found[1])
            context_ref[rows, p * pair : (p + 1) * pair] = both.astype(BF)
            return carry

        lax.fori_loop(0, count // SHORT, chunk_step, 0)
    partial_ref[...] = dot(context_ref[...], wo_ref[...]).astype(BF)


def attention_backward_kernel(
    kind_ref, dbranch_ref, x_ref, qkv_ref, context_ref, lse_ref, wa_ref, wb_ref, wo_ref,
    ga_ref, gb_ref, gout_ref, partial_ref, sums_ref, dcontext_ref, dqkv_ref, dk_ref, dv_ref,
):
    count = x_ref.shape[0]
    wide = wa_ref.shape[1]
    pair = 2 * HEAD_DIM
    kind = kind_ref[0]
    d_branch = dbranch_ref[...]
    dcontext_ref[...] = dot_nt(d_branch, wo_ref[...]).astype(BF)
    gout_ref[...] = dot_tn(context_ref[...], d_branch).astype(BF)
    for p in range(HEADS // 4):
        keys = qkv_ref[:, (3 * p + 1) * pair : (3 * p + 2) * pair]
        values = qkv_ref[:, (3 * p + 2) * pair : (3 * p + 3) * pair]
        dk_ref[...] = jnp.zeros_like(dk_ref)
        dv_ref[...] = jnp.zeros_like(dv_ref)

        def chunk_step(chunk, carry):
            rows = pl.ds(pl.multiple_of(chunk * SHORT, SHORT), SHORT)
            queries = qkv_ref[rows, 3 * p * pair : (3 * p + 1) * pair] * jnp.asarray(0.125, BF)
            d_context = dcontext_ref[rows, p * pair : (p + 1) * pair]
            mask = mask_row(kind, chunk, count)
            stats = lse_ref[rows, :]
            found = []
            for head in range(2):
                mine = jnp.where(head_lanes(queries, head), queries, jnp.zeros_like(queries))
                theirs = jnp.where(
                    head_lanes(d_context, head), d_context, jnp.zeros_like(d_context)
                )
                lse = stats[:, 2 * p + head : 2 * p + head + 1]
                probs = jnp.exp(dot_nt(mine, keys) + mask - lse)
                d_probs = dot_nt(theirs, values)
                row_dot = jnp.sum(d_probs * probs, axis=1, keepdims=True)
                d_scores = (probs * (d_probs - row_dot)).astype(BF)
                found.append(
                    (
                        dot(d_scores, keys) * 0.125,
                        dot_tn(d_scores, queries),
                        dot_tn(probs.astype(BF), d_context),
                    )
                )
            merged = [
                jnp.where(head_lanes(one, 0), one, other) for one, other in zip(*found)
            ]
            dqkv_ref[rows, 3 * p * pair : (3 * p + 1) * pair] = merged[0].astype(BF)
            dk_ref[...] += merged[1]
            dv_ref[...] += merged[2]
            return carry

        lax.fori_loop(0, count // SHORT, chunk_step, 0)
        dqkv_ref[:, (3 * p + 1) * pair : (3 * p + 2) * pair] = dk_ref[...].astype(BF)
        dqkv_ref[:, (3 * p + 2) * pair : (3 * p + 3) * pair] = dv_ref[...].astype(BF)
    d_a = dqkv_ref[:, :wide]
    d_b = dqkv_ref[:, wide:]
    x = x_ref[...]
    ga_ref[...] = dot_tn(x, d_a).astype(BF)
    gb_ref[...] = dot_tn(x, d_b).astype(BF)
    partial_ref[...] = (dot_nt(d_a, wa_ref[...]) + dot_nt(d_b, wb_ref[...])).astype(BF)
    sums_ref[:, :wide] = jnp.sum(d_a.astype(F32), axis=0, keepdims=True)
    sums_ref[:, wide:] = jnp.sum(d_b.astype(F32), axis=0, keepdims=True)


def kernel_call(body, shapes, scratch, flops, *operands):
    in_vmem = pl.BlockSpec(memory_space=pltpu.VMEM)
    sizes = [value.size * value.dtype.itemsize for value in (*operands, *shapes)]
    return pl.pallas_call(
        body,
        out_shape=shapes,
        in_specs=[pl.BlockSpec(memory_space=pltpu.SMEM)] + [in_vmem] * (len(operands) - 1),
        out_specs=[in_vmem] * len(shapes),
        scratch_shapes=scratch,
        compiler_params=pltpu.CompilerParams(vmem_limit_bytes=40 * 2**20),
        cost_estimate=pl.CostEstimate(
            flops=flops, bytes_accessed=sum(sizes), transcendentals=0
        ),
    )(*operands)


def attention(row_kind, inputs_b, w_a, w_b, bias, w_out):
    count, width = inputs_b.shape
    half = w_out.shape[0]
    shapes = [
        jax.ShapeDtypeStruct((count, width), BF),
        jax.ShapeDtypeStruct((count, 3 * half), BF),
        jax.ShapeDtypeStruct((count, half), BF),
        jax.ShapeDtypeStruct((count, 128), F32),
    ]
    flops = 2 * count * half * (4 * width + 8 * count)
    return kernel_call(
        attention_kernel, shapes, [], flops, row_kind, inputs_b, w_a, w_b, bias, w_out
    )


def attention_backward(row_kind, d_branch, inputs_b, qkv, context, lse, w_a, w_b, w_out):
    count, width = inputs_b.shape
    half = w_out.shape[0]
    shapes = [
        jax.ShapeDtypeStruct(w_a.shape, BF),
        jax.ShapeDtypeStruct(w_b.shape, BF),
        jax.ShapeDtypeStruct(w_out.shape, BF),
        jax.ShapeDtypeStruct((count, width), BF),
        jax.ShapeDtypeStruct((1, 3 * half), F32),
    ]
    scratch = [
        pltpu.VMEM((count, half), BF),
        pltpu.VMEM((count, 3 * half), BF),
        pltpu.VMEM((count, 2 * HEAD_DIM), F32),
        pltpu.VMEM((count, 2 * HEAD_DIM), F32),
    ]
    flops = 2 * count * half * (8 * width + 20 * count)
    return kernel_call(
        attention_backward_kernel, shapes, scratch, flops,
        row_kind, d_branch, inputs_b, qkv, context, lse, w_a, w_b, w_out,
    )


def forward_hidden(inputs, branch, w_up, w_down, vectors, gain_pair, bias_up):
    first_sum = inputs + (branch + vectors[2])
    normed = layer_norm(first_sum, gain_pair[0], vectors[4])
    normed_b = normed.astype(BF)
    pre_act = jnp.concatenate([dot(normed_b, panel) for panel in w_up], axis=1) + bias_up
    act = gelu_exact(pre_act).astype(BF)
    partial = dot(act, w_down).astype(BF)
    return normed, partial, (first_sum, normed_b, pre_act, act)


def hidden_order(width, hidden_rows):
    group = width // (2 * hidden_rows)
    target = jnp.arange(width)
    source = (
        (target % (width // 2)) // hidden_rows * (2 * hidden_rows)
        + target // (width // 2) * hidden_rows
        + target % hidden_rows
    )
    del group
    return jnp.arange(width)[:, None] == source[None, :]


def shards(tokens, row_kind, w_qkv, w_out, w_up, w_down, bias_vectors, gains, bias_up, cotangent):
    chips = Chips()
    sequence = Sequence()
    core = chips.core
    count = chips.count
    device = 2 * chips.chip + core
    row_type = row_kind[0]
    rows, width = w_out.shape[1:]
    hidden = w_up.shape[2]
    hidden_rows = w_down.shape[1]
    half = width // 2
    panels = hidden // 2 // width
    own = tokens.shape[0]
    order = hidden_order(width, hidden_rows)

    pairs = HEADS // 4
    plan = Plan()
    state = {}

    def both(value):
        return merge(value, swap(value, 1), core, 0).reshape((2 * own,) + value.shape[1:])

    def pack_qkv():
        cols = w_qkv.reshape(LAYERS, rows, 3, 2, pairs, -1)

        def side(which):
            return jnp.swapaxes(pick(cols, which, 3), 2, 3).reshape(LAYERS, rows, 3 * half)

        got = swap(side(1 - core), 1)
        cols = merge(side(core), got, core, 1)
        for layer in range(LAYERS):
            last = cols[layer, :, :, width:]
            state["attn", layer] = Gather(
                chips, sequence,
                cols[layer, :, :, :width].reshape(2 * rows, width),
                jnp.concatenate(
                    [jnp.concatenate([last[0], last[1]], axis=1), w_out[layer]], axis=0
                ),
            )
        sequence.mark([state["attn", layer].piece for layer in range(LAYERS)])

    def pack_up():
        value = sequence.gate(w_up)
        cols = jnp.einsum(
            "lrgk,kp->lrgp", value.reshape(LAYERS, rows, hidden // width, width), order.astype(BF),
            preferred_element_type=F32,
        ).astype(BF).reshape(LAYERS, rows, hidden // width, 2, half)
        got = swap(pick(cols, 1 - core, 3), 1)
        cols = merge(pick(cols, core, 3), got, core, 1)
        for layer in range(LAYERS):
            state["ffn", layer] = Gather(
                chips, sequence,
                jnp.concatenate(
                    [
                        cols[layer, :, :, 2 * i : 2 * i + 2].reshape(2 * rows, width)
                        for i in range(panels)
                    ],
                    axis=0,
                ),
                w_down[layer],
            )
        sequence.mark([state["ffn", layer].piece for layer in range(LAYERS)])

    def vectors_start():
        values = sequence.gate((bias_vectors, gains, bias_up))
        feature = jnp.arange(width)[None, :] - rows * device == jnp.arange(rows)[:, None]
        unit = jnp.arange(hidden // 2)[None, :] - hidden_rows * chips.chip
        unit = unit == jnp.arange(hidden_rows)[:, None]
        table = jnp.concatenate(values[:2], axis=1).reshape(LAYERS * 8, rows)
        table = dot(table, feature.astype(BF)).astype(BF)
        units = [
            dot(values[2], unit[:, i * width : (i + 1) * width].astype(BF)).astype(BF)
            for i in range(panels)
        ]
        sequence.mark((table, units))
        state["table"] = jnp.concatenate([table + swap(table, 1)] + units, axis=0)

    def vectors_step(place):
        table = sequence.gate(state["table"])
        sequence.mark(table)
        state["table"] = table + swap(table, 2 * 2**place)

    def vectors_end():
        table = sequence.gate(state["table"]).astype(F32)
        sequence.mark(table)
        state["vectors"] = [table[8 * layer : 8 * layer + 6] for layer in range(LAYERS)]
        state["gains"] = [table[8 * layer + 6 : 8 * layer + 8] for layer in range(LAYERS)]
        state["bias_up"] = [
            jnp.concatenate([table[8 * LAYERS + LAYERS * i + layer] for i in range(panels)])
            for layer in range(LAYERS)
        ]

    def tokens_start():
        value = sequence.gate(tokens)
        state["x", 0] = both(value).astype(F32)

    def cotangent_start():
        value = sequence.gate(cotangent)
        state["upstream"] = both(value).astype(F32)

    def out_exchange(layer):
        first, second = state["attn", layer].finish()
        w_b = jnp.swapaxes(second[:, :rows].reshape(count, rows, 2, half), 1, 2)
        out_all = second[:, rows:].reshape(2, count // 2, rows, width)
        sent, w_b = pick(out_all, 1 - core, 0), w_b.reshape(width, half)
        sequence.mark((sent, w_b))
        full_out = merge(pick(out_all, core, 0), swap(sent, 1), core, 1).reshape(half, width)
        state["w_attn", layer] = (first.reshape(width, width), w_b, full_out)

    def hidden_weights(layer):
        first, second = state["ffn", layer].finish()
        state["w_up", layer] = [
            first[:, 2 * rows * i : 2 * rows * (i + 1)].reshape(width, width)
            for i in range(panels)
        ]
        state["w_down", layer] = second.reshape(hidden // 2, width)

    def run_attention(layer):
        x, weights = sequence.gate((state["x", layer], state["w_attn", layer]))
        vectors = state["vectors"][layer]
        bias_q, bias_v = (
            pick(vectors[i].reshape(2, half), core, 0).reshape(pairs, -1) for i in range(2)
        )
        bias = jnp.stack([bias_q, jnp.zeros_like(bias_q), bias_v], axis=1).reshape(1, 3 * half)
        inputs_b = x.astype(BF)
        partial, *saved = attention(row_kind, inputs_b, weights[0], weights[1], bias, weights[2])
        sequence.mark(partial)
        state["x", layer] = x
        state["w_attn", layer] = weights
        state["saved", layer] = (inputs_b, *saved)
        state["branch"] = (partial, swap(partial, 1))

    def run_up(layer):
        mine, theirs = sequence.gate(state["branch"])
        vectors, pair = state["vectors"][layer], state["gains"][layer]
        first_sum = state["x", layer] + (mine.astype(F32) + theirs.astype(F32) + vectors[2])
        normed = layer_norm(first_sum, pair[0], vectors[4])
        normed_b = normed.astype(BF)
        pre_act = jnp.concatenate(
            [dot(normed_b, panel) for panel in state["w_up", layer]], axis=1
        ) + state["bias_up"][layer]
        act = gelu_exact(pre_act).astype(BF)
        sequence.mark(act)
        state["normed"] = normed
        state["kept", layer] = (first_sum, normed_b, pre_act, act)

    def run_down(layer):
        act = sequence.gate(state["kept", layer][3])
        partial = dot(act, state["w_down", layer]).astype(BF)
        sequence.mark(partial)
        state["branch"] = (partial, swap(partial, 1))

    def run_norm(layer):
        mine, theirs = sequence.gate(state["branch"])
        vectors, pair = state["vectors"][layer], state["gains"][layer]
        second = state["normed"] + (mine.astype(F32) + theirs.astype(F32)) + vectors[3]
        output = layer_norm(second, pair[1], vectors[5])
        state["second", layer] = second
        state["x", layer + 1] = output
        sequence.mark(second)

    def column_sums(value):
        return jnp.sum(value.astype(F32), axis=0)

    def back_norm2(layer):
        upstream = sequence.gate(state["upstream"])
        if layer < LAYERS - 1:
            mine, theirs = upstream
            upstream = state["d_first"] + (mine.astype(F32) + theirs.astype(F32))
        vectors, pair = state["vectors"][layer], state["gains"][layer]
        _, pull = jax.vjp(layer_norm, state["second", layer], pair[1], vectors[5])
        d_second, d_gain2, d_shift2 = pull(upstream)
        d_ffn = d_second.astype(BF)
        state["d_second"], state["d_ffn"] = d_second, d_ffn
        state["sums2", layer] = (column_sums(d_ffn), d_gain2, d_shift2)
        sequence.mark(d_ffn)

    def back_down(layer):
        d_ffn, act = sequence.gate((state["d_ffn"], state["kept", layer][3]))
        bundle = state["s_ffn", layer]
        bundle.start(1, dot_tn(act, d_ffn).astype(BF).reshape(count, hidden_rows, width))
        sequence.mark(bundle.sent)

    def back_act(layer):
        d_ffn = sequence.gate(state["d_ffn"])
        _, pull_gelu = jax.vjp(gelu_exact, state["kept", layer][2])
        state["d_pre"] = pull_gelu(dot_nt(d_ffn, state["w_down", layer]))[0].astype(BF)
        sequence.mark(state["d_pre"])

    def back_up(layer):
        d_pre = sequence.gate(state["d_pre"])
        bundle = state["s_ffn", layer]
        normed_b = state["kept", layer][1]
        bundle.start(0, dot_tn(normed_b, d_pre).astype(BF).reshape(count, 2 * rows, -1))
        sequence.mark(bundle.sent)

    def back_partial(layer):
        d_pre = sequence.gate(state["d_pre"])
        partial = add_up(
            [
                dot_nt(d_pre[:, i * width : (i + 1) * width], state["w_up", layer][i])
                for i in range(panels)
            ]
        ).astype(BF)
        sequence.mark(partial)
        state["units", layer] = column_sums(d_pre)
        state["branch"] = (partial, swap(partial, 1))

    def back_norm1(layer):
        mine, theirs = sequence.gate(state["branch"])
        vectors, pair = state["vectors"][layer], state["gains"][layer]
        d_normed = state["d_second"] + (mine.astype(F32) + theirs.astype(F32))
        _, pull = jax.vjp(layer_norm, state["kept", layer][0], pair[0], vectors[4])
        d_first, d_gain1, d_shift1 = pull(d_normed)
        d_branch = d_first.astype(BF)
        state["d_first"], state["d_branch"] = d_first, d_branch
        state["sums1", layer] = (column_sums(d_branch), d_gain1, d_shift1)
        sequence.mark(d_branch)

    def back_attention(layer):
        d_branch = sequence.gate(state["d_branch"])
        inputs_b, qkv, context, lse = state["saved", layer]
        g_a, g_b, g_out, partial, sums = attention_backward(
            row_kind, d_branch, inputs_b, qkv, context, lse, *state["w_attn", layer]
        )
        sequence.mark(partial)
        sums = sums.reshape(pairs, 3, -1)
        state["pair", layer] = jnp.stack([sums[:, 0].reshape(half), sums[:, 2].reshape(half)])
        if layer > 0:
            state["upstream"] = (partial, swap(partial, 1))
        else:
            parts = partial.reshape(2, own, width)
            state["upstream"] = (pick(parts, core, 0), swap(pick(parts, 1 - core, 0), 1))
        state["g_attn", layer] = (g_a, g_b, g_out)

    def back_terms(layer):
        g_a, g_b, g_out = sequence.gate(state["g_attn", layer])
        bundle = state["s_attn", layer]
        bundle.start(0, g_a.reshape(count, 2 * rows, width))
        first = bundle.sent
        out_pair = g_out.reshape(count // 2, 2, rows, width)
        out_got = swap(pick(out_pair, 1 - core, 1), 1)
        out = merge(pick(out_pair, core, 1), out_got, core, 0).reshape(count, rows, width)
        g_b = g_b.reshape(count, 2, rows, half)
        last = jnp.concatenate([g_b[:, 0], g_b[:, 1]], axis=2)
        bundle.start(1, jnp.concatenate([last, out], axis=1))
        sequence.mark((first, bundle.sent))

    def grad_end():
        mine, theirs = sequence.gate(state["upstream"])
        d_first = lax.dynamic_slice_in_dim(state["d_first"], core * own, own)
        state["grad_tokens"] = d_first + (mine.astype(F32) + theirs.astype(F32))
        sequence.mark(state["grad_tokens"])

    def mixed_end():
        value = sequence.gate(state["x", LAYERS])
        state["mixed"] = lax.dynamic_slice_in_dim(value, core * own, own).astype(BF)
        sequence.mark(state["mixed"])

    def sums_start():
        pair = sequence.gate(jnp.stack([state["pair", layer] for layer in range(LAYERS)]))
        sequence.mark(pair)
        pair = merge(pair, swap(pair, 1), core, 2).reshape(LAYERS, 2, width)
        state["total"] = jnp.stack(
            [
                jnp.concatenate(
                    [
                        pair[layer],
                        jnp.stack(
                            [
                                state["sums1", layer][0],
                                state["sums2", layer][0],
                                state["sums1", layer][2],
                                state["sums2", layer][2],
                                state["sums1", layer][1],
                                state["sums2", layer][1],
                            ]
                        ),
                        state["units", layer].reshape(panels, width),
                    ],
                    axis=0,
                )
                for layer in range(LAYERS)
            ]
        )

    def sums_step(place):
        total = sequence.gate(state["total"])
        sequence.mark(total)
        state["total"] = total + swap(total, 2 * 2**place)

    def sums_end():
        total = sequence.gate(state["total"])
        features = lax.dynamic_slice_in_dim(total[:, :8], rows * device, rows, axis=2)
        units = total[:, 8:].reshape(LAYERS, hidden // 2)
        units = lax.dynamic_slice_in_dim(units, hidden_rows * chips.chip, hidden_rows, axis=1)
        state["small"] = (features[:, :6], features[:, 6:], units)
        sequence.mark(state["small"])

    def finish_hidden(layer):
        up, down = state["s_ffn", layer].finish()
        up = jnp.concatenate(
            [up[i * 2 * rows :][: 2 * rows].reshape(2, rows, width) for i in range(panels)], axis=2
        )
        state["up_pair", layer] = (pick(up, core, 0), swap(pick(up, 1 - core, 0), 1))
        state["down", layer] = down

    def end_hidden(layer):
        mine, theirs = sequence.gate(state["up_pair", layer])
        up = merge(mine.reshape(rows, -1, half), theirs.reshape(rows, -1, half), core, 2)
        state["up", layer] = jnp.einsum(
            "rgp,kp->rgk", up.reshape(rows, -1, width), order.astype(F32),
            precision=lax.Precision.HIGHEST, preferred_element_type=F32,
        ).reshape(rows, hidden)
        sequence.mark(state["up", layer])

    def finish_attention(layer):
        first, rest = state["s_attn", layer].finish()
        last = jnp.swapaxes(rest[:rows].reshape(rows, 2, half), 0, 1)
        cols = jnp.concatenate([first.reshape(2, rows, width), last], axis=2)
        state["qkv_pair", layer] = (pick(cols, core, 0), swap(pick(cols, 1 - core, 0), 1))
        state["out", layer] = rest[rows:]

    def end_attention(layer):
        values = [
            jnp.swapaxes(value.reshape(rows, pairs, 3, -1), 1, 2).reshape(rows, 3, half)
            for value in sequence.gate(state["qkv_pair", layer])
        ]
        state["qkv", layer] = merge(values[0], values[1], core, 2).reshape(rows, 6 * half)
        sequence.mark(state["qkv", layer])

    def call(function, *args):
        return lambda: function(*args)

    low = len(chips.low)
    size = {"attn": 1.0, "ffn": 2.0}
    plan.add("pack_qkv", 0, 3.0, [], pack_qkv)
    plan.add("pack_up", 2, 4.0, ["attn0"], pack_up)
    plan.add("vec", 1.5, 2.0, ["attn0"], vectors_start, [("vec-0", "v", 2.0)])
    for place in range(count.bit_length() - 1):
        plan.add(
            f"vec{place}", 1.5, 1.5, [f"vec-{place}"], call(vectors_step, place),
            [(f"vec-{place + 1}", "v", 3.0)],
        )
    plan.add("vec_end", 1.5, 0.5, [f"vec-{count.bit_length() - 1}"], vectors_end)
    plan.add("tokens", 3, 0.5, ["pack_up"], tokens_start, [("x0", "pair", 2.0)])
    plan.add("cotangent", 9, 0.5, ["main_up0"], cotangent_start)
    bundles = [("attn", 0), ("ffn", 0), ("attn", 1), ("ffn", 1)]
    before = "pack_qkv"
    for rank, (kind, layer) in enumerate(bundles):
        name = f"{kind}{layer}"
        z = 12.0 * size[kind]
        needs = ["pack_qkv" if kind == "attn" else "pack_up"]
        if rank > 0:
            needs.append(f"z-{bundles[rank - 1][0]}{bundles[rank - 1][1]}")

        def start(kind=kind, layer=layer):
            state[kind, layer].start()

        def advance(kind=kind, layer=layer):
            state[kind, layer].advance()

        plan.add(name, 1 + rank, 4.0, needs, start, [(f"z-{name}", "z", z)])
        length = 6.0 * size[kind]
        need = f"z-{name}"
        for step in range(low):
            plan.add(
                f"{name}.{step}", 1 + rank, 3.0 + size[kind], [need], advance,
                [(f"xy-{name}.{step}", "xy", length)],
            )
            need = f"xy-{name}.{step}"
            length *= 2
        if kind == "attn":
            plan.add(
                f"{name}.w", 1 + rank, 4.0, [need], call(out_exchange, layer),
                [(f"w-{name}", "pair", 1.0)],
            )
        else:
            plan.add(f"w-{name}", 1 + rank, 4.0, [need], call(hidden_weights, layer))
    need = "x0"
    for layer in range(LAYERS):
        plan.add(
            f"main_attn{layer}", 10, 9.0, [need, f"w-attn{layer}", "vec_end"],
            call(run_attention, layer), [(f"p-attn{layer}", "pair", 1.0)],
        )
        plan.add(
            f"main_up{layer}", 10, 13.0, [f"p-attn{layer}", f"w-ffn{layer}"], call(run_up, layer)
        )
        plan.add(
            f"main_down{layer}", 10, 2.0, [f"main_up{layer}"], call(run_down, layer),
            [(f"p-down{layer}", "pair", 1.0)],
        )
        need = f"main_norm{layer}"
        plan.add(need, 10, 4.0, [f"p-down{layer}"], call(run_norm, layer))
    plan.add("mixed", 20, 1.0, [need], mixed_end)

    needs = [need, "cotangent"]
    for layer in reversed(range(LAYERS)):
        state["s_ffn", layer] = Scatter(chips, sequence)
        state["s_attn", layer] = Scatter(chips, sequence)
        end = f"{layer}"
        plan.add("b_norm2" + end, 10, 5.0, needs, call(back_norm2, layer))
        plan.add(
            "b_down" + end, 10, 4.0, ["b_norm2" + end], call(back_down, layer),
            [("r-down" + end, "xy", 12.0)],
        )
        plan.add("b_act" + end, 10, 4.0, ["b_down" + end], call(back_act, layer))
        plan.add(
            "b_up" + end, 10, 4.0, ["b_act" + end], call(back_up, layer),
            [("r-up" + end, "xy", 12.0)],
        )
        plan.add(
            "b_partial" + end, 10, 3.0, ["b_up" + end], call(back_partial, layer),
            [("p-up" + end, "pair", 1.0)],
        )
        plan.add("b_norm1" + end, 10, 5.0, ["p-up" + end], call(back_norm1, layer))
        plan.add(
            "b_attn" + end, 10, 14.0, ["b_norm1" + end], call(back_attention, layer),
            [("p-dx" + end, "pair", 1.0)],
        )
        plan.add(
            "b_terms" + end, 9.5, 5.0, ["b_attn" + end], call(back_terms, layer),
            [("r-attn" + end, "xy", 12.0)],
        )
        needs = ["p-dx" + end]
        for kind in ("ffn", "attn"):
            name = f"{kind}{layer}"
            need = ["r-down" + end, "r-up" + end] if kind == "ffn" else ["r-attn" + end]
            rank = 1 + 2 * (LAYERS - 1 - layer) + (kind == "attn")

            def reduce(kind=kind, layer=layer):
                state["s_" + kind, layer].advance()

            length = 6.0 * size[kind]
            for step in range(low - 1):
                plan.add(
                    f"r.{name}.{step}", rank, 3.0 + size[kind], need, reduce,
                    [(f"r-{name}.{step}", "xy", length)],
                )
                need = [f"r-{name}.{step}"]
                length /= 2
            plan.add(
                f"r.{name}.z", rank, 5.0 + size[kind], need, reduce,
                [(f"rz-{name}", "z", 12.0 * size[kind])],
            )
            last = finish_hidden if kind == "ffn" else finish_attention
            plan.add(
                f"r.{name}.end", 19, 2.0, [f"rz-{name}"], call(last, layer),
                [(f"end-{name}", "pair", 2.0)],
            )
            last = end_hidden if kind == "ffn" else end_attention
            plan.add(f"r.{name}.out", 20, 3.0, [f"end-{name}"], call(last, layer))
    plan.add("grad", 18, 1.0, needs, grad_end)
    plan.add("sums", 17, 2.0, ["b_terms0"], sums_start, [("sums-0", "pair", 2.0)])
    for place in range(count.bit_length() - 1):
        plan.add(
            f"sums{place}", 17, 1.5, [f"sums-{place}"], call(sums_step, place),
            [(f"sums-{place + 1}", "v", 3.0)],
        )
    plan.add("sums_end", 20, 1.0, [f"sums-{count.bit_length() - 1}"], sums_end)
    plan.run()

    def stacked(name):
        return jnp.stack([state[name, layer] for layer in range(LAYERS)])

    return (
        state["mixed"],
        state["grad_tokens"],
        stacked("qkv"),
        stacked("out"),
        stacked("up"),
        stacked("down"),
        *state["small"],
    )


def solution(mesh):
    placed = (
        P("fsdp", None),
        P("fsdp"),
        P(None, "fsdp", None),
        P(None, "fsdp", None),
        P(None, "fsdp", None),
        P(None, "fsdp", None),
        P(None, None, "fsdp"),
        P(None, None, "fsdp"),
        P(None, "fsdp"),
        P("fsdp", None),
    )
    return jax.shard_map(
        shards,
        mesh=mesh,
        in_specs=placed,
        out_specs=(
            P("fsdp", None),
            P("fsdp", None),
            P(None, "fsdp", None),
            P(None, "fsdp", None),
            P(None, "fsdp", None),
            P(None, "fsdp", None),
            P(None, None, "fsdp"),
            P(None, None, "fsdp"),
            P(None, "fsdp"),
        ),
        check_vma=False,
    )
```

```python
import jax
import jax.numpy as jnp
from jax import lax
from jax.experimental import pallas as pl
from jax.experimental.pallas import tpu as pltpu
from jax.sharding import PartitionSpec as P

HEADS = 12
HEAD_DIM = 64
LAYERS = 2
SHORT = 128
AXIS = "fsdp"

EPSILON = 1e-05
MASKED_SCORE = -1e30
BF = jnp.bfloat16
F32 = jnp.float32
LATENCY = 3.0
ATTN, FFN = 0, 1
OPEN_SENDS = 4
TRACE = None


def dot(left, right):
    return jnp.dot(left, right, preferred_element_type=F32)


def dot_tn(left, right):
    return lax.dot_general(left, right, (((0,), (0,)), ((), ())), preferred_element_type=F32)


def dot_nt(left, right):
    return lax.dot_general(left, right, (((1,), (1,)), ((), ())), preferred_element_type=F32)


def swap(value, mask):
    pairs = [(source, source ^ mask) for source in range(lax.axis_size(AXIS))]
    return lax.ppermute(value, AXIS, pairs)


def merge(mine, theirs, bit, axis):
    first = jnp.where(bit == 0, mine, theirs)
    second = jnp.where(bit == 0, theirs, mine)
    return jnp.stack([first, second], axis=axis)


class Chips:
    def __init__(self):
        device = lax.axis_index(AXIS)
        self.count = lax.axis_size(AXIS) // 2
        self.core = device % 2
        self.chip = device // 2
        self.step = self.count // 4
        self.top = self.chip // self.step
        self.low = list(range(self.count.bit_length() - 3))

    def bit(self, place):
        return (self.chip // 2**place) % 2

    def order(self, kind):
        return self.low if kind == 0 else self.low[::-1]

def pick(pair, index, axis):
    return lax.dynamic_index_in_dim(pair, index, axis, keepdims=False)


def stack_panels(value, width):
    panels = [value[..., i : i + width] for i in range(0, value.shape[-1], width)]
    return jnp.concatenate(panels, axis=-2) if len(panels) > 1 else value


def add_up(values):
    total = values[0].astype(F32)
    for value in values[1:]:
        total = total + value.astype(F32)
    return total


class Sequence:
    def __init__(self):
        self.last = None

    def gate(self, values):
        if self.last is None:
            return values
        values, _ = lax.optimization_barrier((values, self.last))
        return values

    def mark(self, values):
        self.last = values


class State:
    def __getattr__(self, name):
        value = {}
        setattr(self, name, value)
        return value


class Plan:
    def __init__(self):
        self.pieces = []

    def add(self, name, rank, cost, needs, run, sends=()):
        self.pieces.append((name, rank, cost, needs, run, sends))

    def run(self):
        now = 0.0
        ready = {}
        free = {}
        open_sends = {}
        waiting = list(self.pieces)

        def fits(piece):
            count = sum(weight for label, weight in open_sends.items() if label not in piece[3])
            added = sum(weight for _, _, _, weight in piece[5])
            return added == 0 or count + added <= OPEN_SENDS

        while waiting:
            known = [
                (max([ready[need] for need in piece[3]], default=0.0), piece)
                for piece in waiting
                if all(need in ready for need in piece[3])
            ]
            known = [entry for entry in known if fits(entry[1])] or known
            able = [(piece[1], place) for place, (time, piece) in enumerate(known) if time <= now]
            if able:
                _, place = min(able)
            else:
                _, place = min((time, place) for place, (time, _) in enumerate(known))
            time, piece = known[place]
            name, _, cost, needs, run, sends = piece
            begin = max(now, time)
            now = begin + cost
            if TRACE is not None:
                TRACE.append((begin, now, name))
            run()
            ready[name] = now
            for need in needs:
                open_sends.pop(need, None)
            for label, link, length, weight in sends:
                end = max(now, free.get(link, 0.0)) + length
                free[link] = end
                ready[label] = end + LATENCY
                if weight > 0:
                    open_sends[label] = weight
            waiting.remove(piece)


class Gather:
    def __init__(self, chips, sequence, first, second):
        self.chips, self.sequence = chips, sequence
        self.heights = (first.shape[0], second.shape[0])
        self.piece = jnp.concatenate([first, second], axis=0)
        self.steps_done = 0
        self.helds = None

    def start(self):
        self.piece = self.sequence.gate(self.piece)
        self.sequence.mark(self.piece)
        self.coming = swap(self.piece, 2 * 2 * self.chips.step)

    def advance(self):
        chips = self.chips
        coming = self.sequence.gate(self.coming)
        step = self.steps_done
        self.steps_done += 1
        if step == 0:
            self.held = merge(self.piece, coming, chips.top // 2, 0)
            self.sequence.mark(self.held)
            self.coming = swap(self.held, 2 * chips.step)
            return
        helds = []
        if step == 1:
            place = 0
            for height in self.heights:
                cut = [value[:, place : place + height] for value in (self.held, coming)]
                held = merge(cut[0], cut[1], chips.top % 2, 1)
                helds.append(held.reshape((4,) + held.shape[2:]))
                place += height
        else:
            for kind in range(2):
                order = chips.order(kind)
                bit = order[step - 2]
                axis = 1 + sum(other > bit for other in order[: step - 2])
                helds.append(merge(self.helds[kind], coming[kind], chips.bit(bit), axis))
        self.helds = helds
        self.sequence.mark(helds)
        if step - 1 < len(chips.low):
            self.coming = [
                swap(held, 2 * 2 ** chips.order(kind)[step - 1])
                for kind, held in enumerate(helds)
            ]

    def finish(self):
        while self.steps_done <= len(self.chips.low) + 1:
            self.advance()
        return [
            held.reshape((self.chips.count,) + held.shape[-2:]) for held in self.helds
        ]


class Scatter:
    def __init__(self, chips, sequence):
        self.chips, self.sequence = chips, sequence
        self.addends = [None, None]
        self.coming = [None, None]
        self.left = [list(chips.low), list(chips.low)]
        self.steps_done = 0

    def start(self, kind, terms):
        shape = (4,) + (2,) * len(self.chips.low) + terms.shape[1:]
        self.send(kind, [terms.reshape(shape)])

    def send(self, kind, held):
        chips = self.chips
        place = chips.order(kind)[::-1][self.steps_done]
        axis = 1 + sum(other > place for other in self.left[kind])
        self.left[kind].remove(place)
        bit = chips.bit(place)
        sent = add_up([pick(value, 1 - bit, axis) for value in held]).astype(BF)
        self.addends[kind] = [pick(value, bit, axis) for value in held]
        self.coming[kind] = swap(sent, 2 * 2**place)
        self.sent = sent

    def advance(self):
        chips = self.chips
        self.steps_done += 1
        coming = self.sequence.gate(self.coming)
        if self.steps_done > len(chips.low):
            self.last_step(coming)
            return
        held = [addends + [got] for addends, got in zip(self.addends, coming)]
        if self.steps_done < len(chips.low):
            sents = []
            for kind in range(2):
                self.send(kind, held[kind])
                sents.append(self.sent)
            self.sequence.mark(sents)
            return
        low_bit = chips.top % 2
        width = coming[1].shape[-1]
        held = [[value.reshape((2, 2) + value.shape[1:]) for value in values] for values in held]

        def total(bit, high_bit=None):
            sums = []
            for values in held:
                values = [pick(value, bit, 1) for value in values]
                if high_bit is not None:
                    values = [pick(value, high_bit, 0) for value in values]
                sums.append(stack_panels(add_up(values), width))
            self.height = sums[0].shape[-2]
            return jnp.concatenate(sums, axis=-2)

        sent = total(1 - low_bit).astype(BF)
        self.sequence.mark(sent)
        self.total = lambda high_bit: total(low_bit, high_bit)
        self.coming = swap(sent, 2 * chips.step)

    def last_step(self, coming):
        high_bit = self.chips.top // 2
        sent = (self.total(1 - high_bit) + pick(coming, 1 - high_bit, 0).astype(F32)).astype(BF)
        self.sequence.mark(sent)
        self.own = self.total(high_bit) + pick(coming, high_bit, 0).astype(F32)
        self.coming = swap(sent, 4 * self.chips.step)

    def finish(self):
        while self.steps_done <= len(self.chips.low):
            self.advance()
        coming = self.sequence.gate(self.coming)
        total = self.own + coming.astype(F32)
        self.sequence.mark(total)
        return total[: self.height], total[self.height :]


def layer_norm(values, gain_row, shift_row):
    centre = values - jnp.mean(values, axis=-1, keepdims=True)
    variance = jnp.mean(centre * centre, axis=-1, keepdims=True)
    return centre * lax.rsqrt(variance + EPSILON) * gain_row + shift_row


def gelu_exact(values):
    return jax.nn.gelu(values, approximate=False)


def pair_sum(partial):
    rounded = partial.astype(BF)
    return rounded.astype(F32) + swap(rounded, 1).astype(F32)


def head_lanes(value, head):
    lane = lax.broadcasted_iota(jnp.int32, value.shape, 1)
    return (lane // (value.shape[1] // 2)) == head


def mask_row(kind, chunk, count):
    place = lax.broadcasted_iota(jnp.int32, (1, count), 1)
    allowed = (place // SHORT == chunk) | (kind == 1)
    return jnp.where(allowed, 0.0, MASKED_SCORE)


def attention_kernel(
    kind_ref, x_ref, wa_ref, wb_ref, bias_ref, wo_ref, partial_ref, qkv_ref, context_ref, lse_ref
):
    count = x_ref.shape[0]
    wide = wa_ref.shape[1]
    pair = 2 * HEAD_DIM
    kind = kind_ref[0]
    x = x_ref[...]
    bias = bias_ref[...]
    qkv_ref[:, :wide] = (dot(x, wa_ref[...]) + bias[:, :wide]).astype(BF)
    qkv_ref[:, wide:] = (dot(x, wb_ref[...]) + bias[:, wide:]).astype(BF)
    for p in range(HEADS // 4):
        keys = qkv_ref[:, (3 * p + 1) * pair : (3 * p + 2) * pair]
        values = qkv_ref[:, (3 * p + 2) * pair : (3 * p + 3) * pair]

        def chunk_step(chunk, carry):
            rows = pl.ds(pl.multiple_of(chunk * SHORT, SHORT), SHORT)
            queries = qkv_ref[rows, 3 * p * pair : (3 * p + 1) * pair] * jnp.asarray(0.125, BF)
            mask = mask_row(kind, chunk, count)
            found = []
            stats = lse_ref[rows, :] if p > 0 else jnp.zeros((SHORT, 128), F32)
            lane = lax.broadcasted_iota(jnp.int32, stats.shape, 1)
            for head in range(2):
                mine = jnp.where(head_lanes(queries, head), queries, jnp.zeros_like(queries))
                scores = dot_nt(mine, keys) + mask
                top = jnp.max(scores, axis=1, keepdims=True)
                powers = jnp.exp(scores - top)
                total = jnp.sum(powers, axis=1, keepdims=True)
                probs = powers * (1.0 / total)
                found.append(dot(probs.astype(BF), values))
                stats = jnp.where(lane == 2 * p + head, top + jnp.log(total), stats)
            lse_ref[rows, :] = stats
            both = jnp.where(head_lanes(found[0], 0), found[0], found[1])
            context_ref[rows, p * pair : (p + 1) * pair] = both.astype(BF)
            return carry

        lax.fori_loop(0, count // SHORT, chunk_step, 0)
    partial_ref[...] = dot(context_ref[...], wo_ref[...]).astype(BF)


def attention_backward_kernel(
    kind_ref, dbranch_ref, x_ref, qkv_ref, context_ref, lse_ref, wa_ref, wb_ref, wo_ref,
    ga_ref, gb_ref, gout_ref, partial_ref, sums_ref, dcontext_ref, dqkv_ref, dk_ref, dv_ref,
):
    count = x_ref.shape[0]
    wide = wa_ref.shape[1]
    pair = 2 * HEAD_DIM
    kind = kind_ref[0]
    d_branch = dbranch_ref[...]
    dcontext_ref[...] = dot_nt(d_branch, wo_ref[...]).astype(BF)
    gout_ref[...] = dot_tn(context_ref[...], d_branch).astype(BF)
    for p in range(HEADS // 4):
        keys = qkv_ref[:, (3 * p + 1) * pair : (3 * p + 2) * pair]
        values = qkv_ref[:, (3 * p + 2) * pair : (3 * p + 3) * pair]
        dk_ref[...] = jnp.zeros_like(dk_ref)
        dv_ref[...] = jnp.zeros_like(dv_ref)

        def chunk_step(chunk, carry):
            rows = pl.ds(pl.multiple_of(chunk * SHORT, SHORT), SHORT)
            queries = qkv_ref[rows, 3 * p * pair : (3 * p + 1) * pair] * jnp.asarray(0.125, BF)
            d_context = dcontext_ref[rows, p * pair : (p + 1) * pair]
            mask = mask_row(kind, chunk, count)
            stats = lse_ref[rows, :]
            found = []
            for head in range(2):
                mine = jnp.where(head_lanes(queries, head), queries, jnp.zeros_like(queries))
                theirs = jnp.where(
                    head_lanes(d_context, head), d_context, jnp.zeros_like(d_context)
                )
                lse = stats[:, 2 * p + head : 2 * p + head + 1]
                probs = jnp.exp(dot_nt(mine, keys) + mask - lse)
                d_probs = dot_nt(theirs, values)
                row_dot = jnp.sum(d_probs * probs, axis=1, keepdims=True)
                d_scores = (probs * (d_probs - row_dot)).astype(BF)
                found.append(
                    (
                        dot(d_scores, keys) * 0.125,
                        dot_tn(d_scores, queries),
                        dot_tn(probs.astype(BF), d_context),
                    )
                )
            merged = [
                jnp.where(head_lanes(one, 0), one, other) for one, other in zip(*found)
            ]
            dqkv_ref[rows, 3 * p * pair : (3 * p + 1) * pair] = merged[0].astype(BF)
            dk_ref[...] += merged[1]
            dv_ref[...] += merged[2]
            return carry

        lax.fori_loop(0, count // SHORT, chunk_step, 0)
        dqkv_ref[:, (3 * p + 1) * pair : (3 * p + 2) * pair] = dk_ref[...].astype(BF)
        dqkv_ref[:, (3 * p + 2) * pair : (3 * p + 3) * pair] = dv_ref[...].astype(BF)
    d_a = dqkv_ref[:, :wide]
    d_b = dqkv_ref[:, wide:]
    x = x_ref[...]
    ga_ref[...] = dot_tn(x, d_a).astype(BF)
    gb_ref[...] = dot_tn(x, d_b).astype(BF)
    partial_ref[...] = (dot_nt(d_a, wa_ref[...]) + dot_nt(d_b, wb_ref[...])).astype(BF)
    sums_ref[:, :wide] = jnp.sum(d_a.astype(F32), axis=0, keepdims=True)
    sums_ref[:, wide:] = jnp.sum(d_b.astype(F32), axis=0, keepdims=True)


def kernel_call(body, shapes, scratch, *operands):
    in_vmem = pl.BlockSpec(memory_space=pltpu.VMEM)
    return pl.pallas_call(
        body,
        out_shape=shapes,
        in_specs=[pl.BlockSpec(memory_space=pltpu.SMEM)] + [in_vmem] * (len(operands) - 1),
        out_specs=[in_vmem] * len(shapes),
        scratch_shapes=scratch,
        compiler_params=pltpu.CompilerParams(vmem_limit_bytes=40 * 2**20),
        cost_estimate=pl.CostEstimate(flops=0, bytes_accessed=0, transcendentals=0),
    )(*operands)


def attention(row_kind, inputs_b, w_a, w_b, bias, w_out):
    count, width = inputs_b.shape
    half = w_out.shape[0]
    shapes = [
        jax.ShapeDtypeStruct((count, width), BF),
        jax.ShapeDtypeStruct((count, 3 * half), BF),
        jax.ShapeDtypeStruct((count, half), BF),
        jax.ShapeDtypeStruct((count, 128), F32),
    ]
    return kernel_call(
        attention_kernel, shapes, [], row_kind, inputs_b, w_a, w_b, bias, w_out
    )


def attention_backward(row_kind, d_branch, inputs_b, qkv, context, lse, w_a, w_b, w_out):
    count, width = inputs_b.shape
    half = w_out.shape[0]
    shapes = [
        jax.ShapeDtypeStruct(w_a.shape, BF),
        jax.ShapeDtypeStruct(w_b.shape, BF),
        jax.ShapeDtypeStruct(w_out.shape, BF),
        jax.ShapeDtypeStruct((count, width), BF),
        jax.ShapeDtypeStruct((1, 3 * half), F32),
    ]
    scratch = [
        pltpu.VMEM((count, half), BF),
        pltpu.VMEM((count, 3 * half), BF),
        pltpu.VMEM((count, 2 * HEAD_DIM), F32),
        pltpu.VMEM((count, 2 * HEAD_DIM), F32),
    ]
    return kernel_call(
        attention_backward_kernel, shapes, scratch,
        row_kind, d_branch, inputs_b, qkv, context, lse, w_a, w_b, w_out,
    )


def forward_hidden(inputs, branch, w_up, w_down, vectors, gain_pair, bias_up):
    first_sum = inputs + (branch + vectors[2])
    normed = layer_norm(first_sum, gain_pair[0], vectors[4])
    normed_b = normed.astype(BF)
    pre_act = jnp.concatenate([dot(normed_b, panel) for panel in w_up], axis=1) + bias_up
    act = gelu_exact(pre_act).astype(BF)
    partial = dot(act, w_down).astype(BF)
    return normed, partial, (first_sum, normed_b, pre_act, act)


def hidden_order(width, hidden_rows):
    group = width // (2 * hidden_rows)
    target = jnp.arange(width)
    source = (
        (target % (width // 2)) // hidden_rows * (2 * hidden_rows)
        + target // (width // 2) * hidden_rows
        + target % hidden_rows
    )
    del group
    return jnp.arange(width)[:, None] == source[None, :]


def shards(tokens, row_kind, w_qkv, w_out, w_up, w_down, bias_vectors, gains, bias_up, cotangent):
    chips = Chips()
    sequence = Sequence()
    core = chips.core
    count = chips.count
    device = 2 * chips.chip + core
    row_type = row_kind[0]
    rows, width = w_out.shape[1:]
    hidden = w_up.shape[2]
    hidden_rows = w_down.shape[1]
    half = width // 2
    panels = hidden // 2 // width
    own = tokens.shape[0]
    order = hidden_order(width, hidden_rows)

    pairs = HEADS // 4
    plan = Plan()
    state = State()

    def both(value):
        return merge(value, swap(value, 1), core, 0).reshape((2 * own,) + value.shape[1:])

    def pack_qkv():
        cols = w_qkv.reshape(LAYERS, rows, 3, 2, pairs, -1)

        def side(which):
            return jnp.swapaxes(pick(cols, which, 3), 2, 3).reshape(LAYERS, rows, 3 * half)

        got = swap(side(1 - core), 1)
        cols = merge(side(core), got, core, 1)
        for layer in range(LAYERS):
            last = cols[layer, :, :, width:]
            state.gathers[ATTN, layer] = Gather(
                chips, sequence,
                cols[layer, :, :, :width].reshape(2 * rows, width),
                jnp.concatenate(
                    [jnp.concatenate([last[0], last[1]], axis=1), w_out[layer]], axis=0
                ),
            )
        sequence.mark([state.gathers[ATTN, layer].piece for layer in range(LAYERS)])

    def pack_up():
        value = sequence.gate(w_up)
        cols = jnp.einsum(
            "lrgk,kp->lrgp", value.reshape(LAYERS, rows, hidden // width, width), order.astype(BF),
            preferred_element_type=F32,
        ).astype(BF).reshape(LAYERS, rows, hidden // width, 2, half)
        got = swap(pick(cols, 1 - core, 3), 1)
        cols = merge(pick(cols, core, 3), got, core, 1)
        for layer in range(LAYERS):
            state.gathers[FFN, layer] = Gather(
                chips, sequence,
                jnp.concatenate(
                    [
                        cols[layer, :, :, 2 * i : 2 * i + 2].reshape(2 * rows, width)
                        for i in range(panels)
                    ],
                    axis=0,
                ),
                w_down[layer],
            )
        sequence.mark([state.gathers[FFN, layer].piece for layer in range(LAYERS)])

    def vectors_start():
        values = sequence.gate((bias_vectors, gains, bias_up))
        feature = jnp.arange(width)[None, :] - rows * device == jnp.arange(rows)[:, None]
        unit = jnp.arange(hidden // 2)[None, :] - hidden_rows * chips.chip
        unit = unit == jnp.arange(hidden_rows)[:, None]
        table = jnp.concatenate(values[:2], axis=1).reshape(LAYERS * 8, rows)
        table = dot(table, feature.astype(BF)).astype(BF)
        units = [
            dot(values[2], unit[:, i * width : (i + 1) * width].astype(BF)).astype(BF)
            for i in range(panels)
        ]
        sequence.mark((table, units))
        state.table = jnp.concatenate([table + swap(table, 1)] + units, axis=0)

    def vectors_step(place):
        table = sequence.gate(state.table)
        sequence.mark(table)
        state.table = table + swap(table, 2 * 2**place)

    def vectors_end():
        table = sequence.gate(state.table).astype(F32)
        sequence.mark(table)
        state.vectors = [table[8 * layer : 8 * layer + 6] for layer in range(LAYERS)]
        state.gains = [table[8 * layer + 6 : 8 * layer + 8] for layer in range(LAYERS)]
        state.bias_up = [
            jnp.concatenate([table[8 * LAYERS + LAYERS * i + layer] for i in range(panels)])
            for layer in range(LAYERS)
        ]

    def tokens_start():
        value = sequence.gate(tokens)
        state.x[0] = both(value).astype(F32)

    def cotangent_start():
        value = sequence.gate(cotangent)
        state.upstream = both(value).astype(F32)

    def out_exchange(layer):
        first, second = state.gathers[ATTN, layer].finish()
        w_b = jnp.swapaxes(second[:, :rows].reshape(count, rows, 2, half), 1, 2)
        out_all = second[:, rows:].reshape(2, count // 2, rows, width)
        sent, w_b = pick(out_all, 1 - core, 0), w_b.reshape(width, half)
        sequence.mark((sent, w_b))
        full_out = merge(pick(out_all, core, 0), swap(sent, 1), core, 1).reshape(half, width)
        state.w_attn[layer] = (first.reshape(width, width), w_b, full_out)

    def hidden_weights(layer):
        first, second = state.gathers[FFN, layer].finish()
        state.w_up[layer] = [
            first[:, 2 * rows * i : 2 * rows * (i + 1)].reshape(width, width)
            for i in range(panels)
        ]
        state.w_down[layer] = second.reshape(hidden // 2, width)

    def run_attention(layer):
        x, weights = sequence.gate((state.x[layer], state.w_attn[layer]))
        vectors = state.vectors[layer]
        bias_q, bias_v = (
            pick(vectors[i].reshape(2, half), core, 0).reshape(pairs, -1) for i in range(2)
        )
        bias = jnp.stack([bias_q, jnp.zeros_like(bias_q), bias_v], axis=1).reshape(1, 3 * half)
        inputs_b = x.astype(BF)
        partial, *saved = attention(row_kind, inputs_b, weights[0], weights[1], bias, weights[2])
        sequence.mark(partial)
        state.x[layer] = x
        state.w_attn[layer] = weights
        state.saved[layer] = (inputs_b, *saved)
        state.branch = (partial, swap(partial, 1))

    def run_up(layer):
        mine, theirs = sequence.gate(state.branch)
        vectors, pair = state.vectors[layer], state.gains[layer]
        first_sum = state.x[layer] + (mine.astype(F32) + theirs.astype(F32) + vectors[2])
        normed = layer_norm(first_sum, pair[0], vectors[4])
        normed_b = normed.astype(BF)
        pre_act = jnp.concatenate(
            [dot(normed_b, panel) for panel in state.w_up[layer]], axis=1
        ) + state.bias_up[layer]
        act = gelu_exact(pre_act).astype(BF)
        sequence.mark(act)
        state.normed = normed
        state.kept[layer] = (first_sum, normed_b, pre_act, act)

    def run_down(layer):
        act = sequence.gate(state.kept[layer][3])
        partial = dot(act, state.w_down[layer]).astype(BF)
        sequence.mark(partial)
        state.branch = (partial, swap(partial, 1))

    def run_norm(layer):
        mine, theirs = sequence.gate(state.branch)
        vectors, pair = state.vectors[layer], state.gains[layer]
        second = state.normed + (mine.astype(F32) + theirs.astype(F32)) + vectors[3]
        output = layer_norm(second, pair[1], vectors[5])
        state.second[layer] = second
        state.x[layer + 1] = output
        sequence.mark(second)

    def column_sums(value):
        return jnp.sum(value.astype(F32), axis=0)

    def back_norm2(layer):
        upstream = sequence.gate(state.upstream)
        if layer < LAYERS - 1:
            mine, theirs = upstream
            upstream = state.d_first + (mine.astype(F32) + theirs.astype(F32))
        vectors, pair = state.vectors[layer], state.gains[layer]
        _, pull = jax.vjp(layer_norm, state.second[layer], pair[1], vectors[5])
        d_second, d_gain2, d_shift2 = pull(upstream)
        d_ffn = d_second.astype(BF)
        state.d_second, state.d_ffn = d_second, d_ffn
        state.sums2[layer] = (column_sums(d_ffn), d_gain2, d_shift2)
        sequence.mark(d_ffn)

    def back_down(layer):
        d_ffn, act = sequence.gate((state.d_ffn, state.kept[layer][3]))
        bundle = state.scatters[FFN, layer]
        bundle.start(1, dot_tn(act, d_ffn).astype(BF).reshape(count, hidden_rows, width))
        sequence.mark(bundle.sent)

    def back_act(layer):
        d_ffn = sequence.gate(state.d_ffn)
        _, pull_gelu = jax.vjp(gelu_exact, state.kept[layer][2])
        state.d_pre = pull_gelu(dot_nt(d_ffn, state.w_down[layer]))[0].astype(BF)
        sequence.mark(state.d_pre)

    def back_up(layer):
        d_pre = sequence.gate(state.d_pre)
        bundle = state.scatters[FFN, layer]
        normed_b = state.kept[layer][1]
        bundle.start(0, dot_tn(normed_b, d_pre).astype(BF).reshape(count, 2 * rows, -1))
        sequence.mark(bundle.sent)

    def back_partial(layer):
        d_pre = sequence.gate(state.d_pre)
        partial = add_up(
            [
                dot_nt(d_pre[:, i * width : (i + 1) * width], state.w_up[layer][i])
                for i in range(panels)
            ]
        ).astype(BF)
        sequence.mark(partial)
        state.units[layer] = column_sums(d_pre)
        state.branch = (partial, swap(partial, 1))

    def back_norm1(layer):
        mine, theirs = sequence.gate(state.branch)
        vectors, pair = state.vectors[layer], state.gains[layer]
        d_normed = state.d_second + (mine.astype(F32) + theirs.astype(F32))
        _, pull = jax.vjp(layer_norm, state.kept[layer][0], pair[0], vectors[4])
        d_first, d_gain1, d_shift1 = pull(d_normed)
        d_branch = d_first.astype(BF)
        state.d_first, state.d_branch = d_first, d_branch
        state.sums1[layer] = (column_sums(d_branch), d_gain1, d_shift1)
        sequence.mark(d_branch)

    def back_attention(layer):
        d_branch = sequence.gate(state.d_branch)
        inputs_b, qkv, context, lse = state.saved[layer]
        g_a, g_b, g_out, partial, sums = attention_backward(
            row_kind, d_branch, inputs_b, qkv, context, lse, *state.w_attn[layer]
        )
        sequence.mark(partial)
        sums = sums.reshape(pairs, 3, -1)
        state.pair[layer] = jnp.stack([sums[:, 0].reshape(half), sums[:, 2].reshape(half)])
        if layer > 0:
            state.upstream = (partial, swap(partial, 1))
        else:
            parts = partial.reshape(2, own, width)
            state.upstream = (pick(parts, core, 0), swap(pick(parts, 1 - core, 0), 1))
        state.g_attn[layer] = (g_a, g_b, g_out)

    def back_terms(layer):
        g_a, g_b, g_out = sequence.gate(state.g_attn[layer])
        bundle = state.scatters[ATTN, layer]
        bundle.start(0, g_a.reshape(count, 2 * rows, width))
        first = bundle.sent
        out_pair = g_out.reshape(count // 2, 2, rows, width)
        out_got = swap(pick(out_pair, 1 - core, 1), 1)
        out = merge(pick(out_pair, core, 1), out_got, core, 0).reshape(count, rows, width)
        g_b = g_b.reshape(count, 2, rows, half)
        last = jnp.concatenate([g_b[:, 0], g_b[:, 1]], axis=2)
        bundle.start(1, jnp.concatenate([last, out], axis=1))
        sequence.mark((first, bundle.sent))

    def grad_end():
        mine, theirs = sequence.gate(state.upstream)
        d_first = lax.dynamic_slice_in_dim(state.d_first, core * own, own)
        state.grad_tokens = d_first + (mine.astype(F32) + theirs.astype(F32))
        sequence.mark(state.grad_tokens)

    def mixed_end():
        value = sequence.gate(state.x[LAYERS])
        state.mixed = lax.dynamic_slice_in_dim(value, core * own, own).astype(BF)
        sequence.mark(state.mixed)

    def sums_start():
        pair = sequence.gate(jnp.stack([state.pair[layer] for layer in range(LAYERS)]))
        sequence.mark(pair)
        pair = merge(pair, swap(pair, 1), core, 2).reshape(LAYERS, 2, width)
        state.total = jnp.stack(
            [
                jnp.concatenate(
                    [
                        pair[layer],
                        jnp.stack(
                            [
                                state.sums1[layer][0],
                                state.sums2[layer][0],
                                state.sums1[layer][2],
                                state.sums2[layer][2],
                                state.sums1[layer][1],
                                state.sums2[layer][1],
                            ]
                        ),
                        state.units[layer].reshape(panels, width),
                    ],
                    axis=0,
                )
                for layer in range(LAYERS)
            ]
        )

    def sums_step(place):
        total = sequence.gate(state.total)
        sequence.mark(total)
        state.total = total + swap(total, 2 * 2**place)

    def sums_end():
        total = sequence.gate(state.total)
        features = lax.dynamic_slice_in_dim(total[:, :8], rows * device, rows, axis=2)
        units = total[:, 8:].reshape(LAYERS, hidden // 2)
        units = lax.dynamic_slice_in_dim(units, hidden_rows * chips.chip, hidden_rows, axis=1)
        state.small = (features[:, :6], features[:, 6:], units)
        sequence.mark(state.small)

    def finish_hidden(layer):
        up, down = state.scatters[FFN, layer].finish()
        up = jnp.concatenate(
            [up[i * 2 * rows :][: 2 * rows].reshape(2, rows, width) for i in range(panels)], axis=2
        )
        state.up_pair[layer] = (pick(up, core, 0), swap(pick(up, 1 - core, 0), 1))
        state.down[layer] = down

    def end_hidden(layer):
        mine, theirs = sequence.gate(state.up_pair[layer])
        up = merge(mine.reshape(rows, -1, half), theirs.reshape(rows, -1, half), core, 2)
        state.up[layer] = jnp.einsum(
            "rgp,kp->rgk", up.reshape(rows, -1, width), order.astype(F32),
            precision=lax.Precision.HIGHEST, preferred_element_type=F32,
        ).reshape(rows, hidden)
        sequence.mark(state.up[layer])

    def finish_attention(layer):
        first, rest = state.scatters[ATTN, layer].finish()
        last = jnp.swapaxes(rest[:rows].reshape(rows, 2, half), 0, 1)
        cols = jnp.concatenate([first.reshape(2, rows, width), last], axis=2)
        state.qkv_pair[layer] = (pick(cols, core, 0), swap(pick(cols, 1 - core, 0), 1))
        state.out[layer] = rest[rows:]

    def end_attention(layer):
        values = [
            jnp.swapaxes(value.reshape(rows, pairs, 3, -1), 1, 2).reshape(rows, 3, half)
            for value in sequence.gate(state.qkv_pair[layer])
        ]
        state.qkv[layer] = merge(values[0], values[1], core, 2).reshape(rows, 6 * half)
        sequence.mark(state.qkv[layer])

    def call(function, *args):
        return lambda: function(*args)

    low = len(chips.low)
    places = count.bit_length() - 1
    size = (1.0, 2.0)
    add = plan.add
    add("pq", 0, 3.0, [], pack_qkv)
    add("pu", 2, 4.0, [("g", ATTN, 0)], pack_up)
    add("vec", 8, 2.5, [("g", FFN, 0)], vectors_start, [(("v", 0), "v", 1.0, 1)])
    for place in range(places):
        add(
            ("vs", place), 8, 1.5, [("v", place)], call(vectors_step, place),
            [(("v", place + 1), "v", 1.5, 1)],
        )
    add("ve", 8, 0.5, [("v", places)], vectors_end)
    add("tok", 8, 0.5, ["vec"], tokens_start, [("x0", "p", 2.0, 0)])
    add("cot", 9, 0.5, [("m", 1, 0)], cotangent_start)
    bundles = [(ATTN, 0), (FFN, 0), (ATTN, 1), (FFN, 1)]
    for rank, (kind, layer) in enumerate(bundles):
        needs = ["pq" if kind == ATTN else "pu"]
        if rank > 0:
            needs.append(("h", *bundles[rank - 1]))

        def start(kind=kind, layer=layer):
            state.gathers[kind, layer].start()

        def advance(kind=kind, layer=layer):
            state.gathers[kind, layer].advance()

        need = ("y", kind, layer)
        add(("g", kind, layer), 1 + rank, 2.5, needs, start, [(need, "y", 6.0 * size[kind], 1)])
        sent = ("z", kind, layer)
        add(("h", kind, layer), 1 + rank, 2.5, [need], advance, [(sent, "z", 6.0 * size[kind], 1)])
        need = sent
        length = 6.0 * size[kind]
        for step in range(low):
            sent = ("xy", kind, layer, step)
            add(("gs", kind, layer, step), 1 + rank, 4.5, [need], advance, [(sent, "xy", length, 2)])
            need = sent
            length *= 2
        if kind == ATTN:
            add(
                ("go", layer), 1 + rank, 4.0, [need], call(out_exchange, layer),
                [(("w", kind, layer), "p", 0.0, 0)],
            )
        else:
            add(("w", kind, layer), 1 + rank, 4.0, [need], call(hidden_weights, layer))
    need = "x0"
    for layer in range(LAYERS):
        add(
            ("m", 0, layer), 10, 12.0, [need, ("w", ATTN, layer), "ve"],
            call(run_attention, layer), [(("p", 0, layer), "p", 0.0, 0)],
        )
        add(("m", 1, layer), 10, 11.0, [("p", 0, layer), ("w", FFN, layer)], call(run_up, layer))
        add(
            ("m", 2, layer), 10, 2.5, [("m", 1, layer)], call(run_down, layer),
            [(("p", 1, layer), "p", 0.0, 0)],
        )
        need = ("m", 3, layer)
        add(need, 10, 4.0, [("p", 1, layer)], call(run_norm, layer))
    add("mix", 20, 1.0, [need], mixed_end)

    needs = [need, "cot"]
    for layer in reversed(range(LAYERS)):
        state.scatters[FFN, layer] = Scatter(chips, sequence)
        state.scatters[ATTN, layer] = Scatter(chips, sequence)
        add(("b", 0, layer), 10, 5.0, needs, call(back_norm2, layer))
        add(
            ("b", 1, layer), 10, 3.0, [("b", 0, layer)], call(back_down, layer),
            [(("r", FFN, layer, 0), "xy", 12.0, 1)],
        )
        add(("b", 2, layer), 10, 4.0, [("b", 1, layer)], call(back_act, layer))
        add(
            ("b", 3, layer), 10, 4.0, [("b", 2, layer)], call(back_up, layer),
            [(("r", FFN, layer, 1), "xy", 12.0, 1)],
        )
        add(
            ("b", 4, layer), 10, 3.0, [("b", 3, layer)], call(back_partial, layer),
            [(("p", 2, layer), "p", 0.0, 0)],
        )
        add(("b", 5, layer), 10, 6.0, [("p", 2, layer)], call(back_norm1, layer))
        add(
            ("b", 6, layer), 10, 15.0, [("b", 5, layer)], call(back_attention, layer),
            [(("p", 3, layer), "p", 0.0, 0)],
        )
        add(
            ("b", 7, layer), 9.5, 4.0, [("b", 6, layer)], call(back_terms, layer),
            [(("r", ATTN, layer, 0), "xy", 12.0, 2)],
        )
        needs = [("p", 3, layer)]
        for kind in (FFN, ATTN):
            need = [("r", kind, layer, part) for part in range(1 + kind)]
            rank = 1 + 2 * (LAYERS - 1 - layer) + (kind == ATTN)

            def reduce(kind=kind, layer=layer):
                state.scatters[kind, layer].advance()

            length = 6.0 * size[kind]
            for step in range(low - 1):
                sent = ("r", kind, layer, 2 + step)
                add(("rs", kind, layer, step), rank, 4.0, need, reduce, [(sent, "xy", length, 2)])
                need = [sent]
                length /= 2
            sent = ("rz", kind, layer)
            add(
                ("rs", kind, layer, low), rank, 3.5, need, reduce,
                [(sent, "z", 6.0 * size[kind], 1)],
            )
            need = sent
            sent = ("ry", kind, layer)
            add(
                ("rs", kind, layer, low + 1), rank, 4.0, [need], reduce,
                [(sent, "y", 6.0 * size[kind], 1)],
            )
            last = finish_hidden if kind == FFN else finish_attention
            add(
                ("rf", kind, layer), 19, 2.0, [sent], call(last, layer),
                [(("re", kind, layer), "p", 1.0, 0)],
            )
            last = end_hidden if kind == FFN else end_attention
            add(("ro", kind, layer), 20, 3.0, [("re", kind, layer)], call(last, layer))
    add("grad", 18, 1.0, needs, grad_end)
    add("sum", 17, 2.0, [("b", 7, 0)], sums_start, [(("s", 0), "p", 1.0, 0)])
    for place in range(places):
        add(
            ("ss", place), 17, 1.5, [("s", place)], call(sums_step, place),
            [(("s", place + 1), "v", 2.0, 1)],
        )
    add("se", 20, 1.0, [("s", places)], sums_end)
    plan.run()

    def stacked(values):
        return jnp.stack([values[layer] for layer in range(LAYERS)])

    return (
        state.mixed,
        state.grad_tokens,
        stacked(state.qkv),
        stacked(state.out),
        stacked(state.up),
        stacked(state.down),
        *state.small,
    )


def solution(mesh):
    placed = (
        P("fsdp", None),
        P("fsdp"),
        P(None, "fsdp", None),
        P(None, "fsdp", None),
        P(None, "fsdp", None),
        P(None, "fsdp", None),
        P(None, None, "fsdp"),
        P(None, None, "fsdp"),
        P(None, "fsdp"),
        P("fsdp", None),
    )
    return jax.shard_map(
        shards,
        mesh=mesh,
        in_specs=placed,
        out_specs=(
            P("fsdp", None),
            P("fsdp", None),
            P(None, "fsdp", None),
            P(None, "fsdp", None),
            P(None, "fsdp", None),
            P(None, "fsdp", None),
            P(None, None, "fsdp"),
            P(None, None, "fsdp"),
            P(None, "fsdp"),
        ),
        check_vma=False,
    )
```

```python
import functools

import jax
import jax.numpy as jnp
from jax import lax
from jax.experimental import pallas as pl
from jax.experimental.pallas import tpu as pltpu
from jax.sharding import PartitionSpec as P

HEADS = 12
HEAD_DIM = 64
LAYERS = 2
SHORT = 128
AXIS = "fsdp"

EPSILON = 1e-05
MASKED_SCORE = -1e30
BF = jnp.bfloat16
F32 = jnp.float32
LATENCY = 3.0
ATTN, FFN = 0, 1
OPEN_SENDS = 5
VMEM_LIMIT = 24 * 2**20
TRACE = None


def dot(left, right):
    return jnp.dot(left, right, preferred_element_type=F32)


def dot_tn(left, right):
    return lax.dot_general(left, right, (((0,), (0,)), ((), ())), preferred_element_type=F32)


def dot_nt(left, right):
    return lax.dot_general(left, right, (((1,), (1,)), ((), ())), preferred_element_type=F32)


def swap(value, mask):
    pairs = [(source, source ^ mask) for source in range(lax.axis_size(AXIS))]
    return lax.ppermute(value, AXIS, pairs)


def merge(mine, theirs, bit, axis):
    first = jnp.where(bit == 0, mine, theirs)
    second = jnp.where(bit == 0, theirs, mine)
    return jnp.stack([first, second], axis=axis)


class Chips:
    def __init__(self):
        device = lax.axis_index(AXIS)
        self.count = lax.axis_size(AXIS) // 2
        self.core = device % 2
        self.chip = device // 2
        self.step = self.count // 4
        self.top = self.chip // self.step
        self.low = list(range(self.count.bit_length() - 3))

    def bit(self, place):
        return (self.chip // 2**place) % 2

    def order(self, kind):
        return self.low if kind == 0 else self.low[::-1]

def pick(pair, index, axis):
    return lax.dynamic_index_in_dim(pair, index, axis, keepdims=False)


def stack_panels(value, width):
    panels = [value[..., i : i + width] for i in range(0, value.shape[-1], width)]
    return jnp.concatenate(panels, axis=-2) if len(panels) > 1 else value


def add_up(values):
    total = values[0].astype(F32)
    for value in values[1:]:
        total = total + value.astype(F32)
    return total


class Sequence:
    def __init__(self):
        self.last = None

    def gate(self, values):
        if self.last is None:
            return values
        values, _ = lax.optimization_barrier((values, self.last))
        return values

    def mark(self, values):
        self.last = values


class State:
    def __getattr__(self, name):
        value = {}
        setattr(self, name, value)
        return value


class Plan:
    def __init__(self):
        self.pieces = []

    def add(self, name, rank, cost, needs, run, sends=()):
        self.pieces.append((name, rank, cost, needs, run, sends))

    def run(self):
        now = 0.0
        ready = {}
        free = {}
        open_sends = {}
        waiting = list(self.pieces)

        def fits(piece):
            count = sum(weight for label, weight in open_sends.items() if label not in piece[3])
            added = sum(weight for _, _, weight in piece[5])
            return added == 0 or count + added <= OPEN_SENDS

        while waiting:
            known = [
                (max([ready[need] for need in piece[3]], default=0.0), piece)
                for piece in waiting
                if all(need in ready for need in piece[3])
            ]
            known = [entry for entry in known if fits(entry[1])] or known
            able = [(piece[1], place) for place, (time, piece) in enumerate(known) if time <= now]
            if able:
                _, place = min(able)
            else:
                _, place = min((time, place) for place, (time, _) in enumerate(known))
            time, piece = known[place]
            name, _, cost, needs, run, sends = piece
            begin = max(now, time)
            now = begin + cost
            if TRACE is not None:
                TRACE.append((begin, now, name))
            run()
            ready[name] = now
            for need in needs:
                open_sends.pop(need, None)
            for label, links, weight in sends:
                ready[label] = 0.0
                for link, length in links:
                    free[link] = max(now, free.get(link, 0.0)) + length
                    ready[label] = max(ready[label], free[link] + LATENCY)
                if weight > 0:
                    open_sends[label] = weight
            waiting.remove(piece)


class Gather:
    def __init__(self, chips, sequence, direct, first, second):
        self.chips, self.sequence = chips, sequence
        self.direct = direct
        self.heights = (first.shape[0], second.shape[0])
        self.piece = jnp.concatenate([first, second], axis=0)
        self.steps_done = 0
        self.helds = None

    def start(self):
        self.piece = self.sequence.gate(self.piece)
        self.sequence.mark(self.piece)
        if self.direct:
            self.coming = [swap(self.piece, 2 * self.chips.step * k) for k in (1, 2, 3)]
            self.steps_done = 1
        else:
            self.coming = swap(self.piece, 2 * 2 * self.chips.step)

    def advance(self):
        chips = self.chips
        coming = self.sequence.gate(self.coming)
        step = self.steps_done
        self.steps_done += 1
        if step == 0:
            self.held = merge(self.piece, coming, chips.top // 2, 0)
            self.sequence.mark(self.held)
            self.coming = swap(self.held, 2 * chips.step)
            return
        helds = []
        if step == 1:
            place = 0
            for height in self.heights:
                if self.direct:
                    cut = [value[place : place + height] for value in [self.piece] + coming]
                    cut = [merge(cut[i], cut[i + 1], chips.top % 2, 0) for i in (0, 2)]
                    held = merge(cut[0], cut[1], chips.top // 2, 0)
                else:
                    cut = [value[:, place : place + height] for value in (self.held, coming)]
                    held = merge(cut[0], cut[1], chips.top % 2, 1)
                helds.append(held.reshape((4,) + held.shape[2:]))
                place += height
        else:
            for kind in range(2):
                order = chips.order(kind)
                bit = order[step - 2]
                axis = 1 + sum(other > bit for other in order[: step - 2])
                helds.append(merge(self.helds[kind], coming[kind], chips.bit(bit), axis))
        self.helds = helds
        self.sequence.mark(helds)
        if step - 1 < len(chips.low):
            self.coming = [
                swap(held, 2 * 2 ** chips.order(kind)[step - 1])
                for kind, held in enumerate(helds)
            ]

    def finish(self):
        while self.steps_done <= len(self.chips.low) + 1:
            self.advance()
        return [
            held.reshape((self.chips.count,) + held.shape[-2:]) for held in self.helds
        ]


class Scatter:
    def __init__(self, chips, sequence):
        self.chips, self.sequence = chips, sequence
        self.addends = [None, None]
        self.coming = [None, None]
        self.left = [list(chips.low), list(chips.low)]
        self.steps_done = 0

    def start(self, kind, terms):
        shape = (4,) + (2,) * len(self.chips.low) + terms.shape[1:]
        self.send(kind, [terms.reshape(shape)])

    def send(self, kind, held):
        chips = self.chips
        place = chips.order(kind)[::-1][self.steps_done]
        axis = 1 + sum(other > place for other in self.left[kind])
        self.left[kind].remove(place)
        bit = chips.bit(place)
        sent = add_up([pick(value, 1 - bit, axis) for value in held]).astype(BF)
        self.addends[kind] = [pick(value, bit, axis) for value in held]
        self.coming[kind] = swap(sent, 2 * 2**place)
        self.sent = sent

    def advance(self):
        chips = self.chips
        self.steps_done += 1
        coming = self.sequence.gate(self.coming)
        if self.steps_done > len(chips.low):
            self.last_step(coming)
            return
        held = [addends + [got] for addends, got in zip(self.addends, coming)]
        if self.steps_done < len(chips.low):
            sents = []
            for kind in range(2):
                self.send(kind, held[kind])
                sents.append(self.sent)
            self.sequence.mark(sents)
            return
        low_bit = chips.top % 2
        width = coming[1].shape[-1]
        held = [[value.reshape((2, 2) + value.shape[1:]) for value in values] for values in held]

        def total(bit, high_bit=None):
            sums = []
            for values in held:
                values = [pick(value, bit, 1) for value in values]
                if high_bit is not None:
                    values = [pick(value, high_bit, 0) for value in values]
                sums.append(stack_panels(add_up(values), width))
            self.height = sums[0].shape[-2]
            return jnp.concatenate(sums, axis=-2)

        sent = total(1 - low_bit).astype(BF)
        self.sequence.mark(sent)
        self.total = lambda high_bit: total(low_bit, high_bit)
        self.coming = swap(sent, 2 * chips.step)

    def last_step(self, coming):
        high_bit = self.chips.top // 2
        sent = (self.total(1 - high_bit) + pick(coming, 1 - high_bit, 0).astype(F32)).astype(BF)
        self.sequence.mark(sent)
        self.own = self.total(high_bit) + pick(coming, high_bit, 0).astype(F32)
        self.coming = swap(sent, 4 * self.chips.step)

    def finish(self):
        while self.steps_done <= len(self.chips.low):
            self.advance()
        coming = self.sequence.gate(self.coming)
        total = self.own + coming.astype(F32)
        self.sequence.mark(total)
        return total[: self.height], total[self.height :]


ROOT_HALF = 0.7071067811865476
DENSITY = 0.3989422804014327


def unit_rows(values):
    centre = values - jnp.mean(values, axis=1, keepdims=True)
    scale = lax.rsqrt(jnp.mean(centre * centre, axis=1, keepdims=True) + EPSILON)
    return centre * scale, scale


def norm_kernel(base_ref, mine_ref, theirs_ref, vec_ref, sum_ref, out_ref, out_b_ref):
    def chunk_step(chunk, carry):
        rows = pl.ds(pl.multiple_of(chunk * SHORT, SHORT), SHORT)
        total = base_ref[rows, :] + (
            mine_ref[rows, :].astype(F32) + theirs_ref[rows, :].astype(F32)
        ) + vec_ref[3:4, :]
        sum_ref[rows, :] = total
        unit, _ = unit_rows(total)
        output = unit * vec_ref[7:8, :] + vec_ref[5:6, :]
        out_ref[rows, :] = output
        out_b_ref[rows, :] = output.astype(BF)
        return carry

    lax.fori_loop(0, base_ref.shape[0] // SHORT, chunk_step, 0)


def hidden_kernel(
    x_ref, mine_ref, theirs_ref, vec_ref, bias_ref, up0_ref, up1_ref, down_ref,
    sum_ref, normed_ref, normed_b_ref, act_ref, slope_ref, partial_ref,
):
    def chunk_step(chunk, carry):
        rows = pl.ds(pl.multiple_of(chunk * SHORT, SHORT), SHORT)
        total = x_ref[rows, :] + (
            mine_ref[rows, :].astype(F32) + theirs_ref[rows, :].astype(F32) + vec_ref[2:3, :]
        )
        sum_ref[rows, :] = total
        unit, _ = unit_rows(total)
        normed = unit * vec_ref[6:7, :] + vec_ref[4:5, :]
        normed_ref[rows, :] = normed
        normed_b_ref[rows, :] = normed.astype(BF)
        return carry

    lax.fori_loop(0, x_ref.shape[0] // SHORT, chunk_step, 0)
    width = up0_ref.shape[1]
    step = 256
    for panel, up_ref in enumerate((up0_ref, up1_ref)):
        for start in range(0, width, step):
            place = panel * width + start
            pre = dot(normed_b_ref[...], up_ref[:, start : start + step])
            pre = pre + bias_ref[:, place : place + step]
            share = 0.5 + 0.5 * lax.erf(pre * ROOT_HALF)
            slope = share + pre * (DENSITY * jnp.exp(pre * pre * -0.5))
            act_ref[:, place : place + step] = (pre * share).astype(BF)
            slope_ref[:, place : place + step] = slope.astype(BF)
    partial_ref[...] = dot(act_ref[...], down_ref[...]).astype(BF)


def norm_back(upstream, total, gain):
    unit, scale = unit_rows(total)
    scaled = upstream * gain
    first = jnp.mean(scaled, axis=1, keepdims=True)
    second = jnp.mean(scaled * unit, axis=1, keepdims=True)
    return (
        scale * (scaled - first - unit * second),
        jnp.sum(upstream * unit, axis=0, keepdims=True),
        jnp.sum(upstream, axis=0, keepdims=True),
    )


def back_second_kernel(has_base, *refs):
    base_refs, refs = refs[: 3 if has_base else 1], refs[3 if has_base else 1 :]
    sum_ref, vec_ref, act_ref, d_second_ref, d_ffn_ref, g_down_ref, sums_ref = refs
    sums_ref[...] = jnp.zeros_like(sums_ref)

    def chunk_step(chunk, carry):
        rows = pl.ds(pl.multiple_of(chunk * SHORT, SHORT), SHORT)
        upstream = base_refs[0][rows, :].astype(F32)
        if has_base:
            upstream = upstream + (
                base_refs[1][rows, :].astype(F32) + base_refs[2][rows, :].astype(F32)
            )
        d_second, d_gain, d_shift = norm_back(upstream, sum_ref[rows, :], vec_ref[7:8, :])
        d_second_ref[rows, :] = d_second
        d_ffn = d_second.astype(BF)
        d_ffn_ref[rows, :] = d_ffn
        sums_ref[1:2, :] += jnp.sum(d_ffn.astype(F32), axis=0, keepdims=True)
        sums_ref[3:4, :] += d_shift
        sums_ref[5:6, :] += d_gain
        return carry

    lax.fori_loop(0, sum_ref.shape[0] // SHORT, chunk_step, 0)
    g_down_ref[...] = dot_tn(act_ref[...], d_ffn_ref[...]).astype(BF)


def back_hidden_kernel(
    d_ffn_ref, slope_ref, normed_b_ref, down_ref, up0_ref, up1_ref,
    g_up_ref, partial_ref, sums_ref, d_pre_ref,
):
    hidden = slope_ref.shape[1]
    step = 256
    for place in range(0, hidden, step):
        d_act = dot_nt(d_ffn_ref[...], down_ref[place : place + step, :])
        d_pre = (d_act * slope_ref[:, place : place + step].astype(F32)).astype(BF)
        d_pre_ref[:, place : place + step] = d_pre
        sums_ref[:, place : place + step] = jnp.sum(d_pre.astype(F32), axis=0, keepdims=True)
    g_up_ref[...] = dot_tn(normed_b_ref[...], d_pre_ref[...]).astype(BF)
    width = up0_ref.shape[1]
    partial_ref[...] = (
        dot_nt(d_pre_ref[:, :width], up0_ref[...]) + dot_nt(d_pre_ref[:, width:], up1_ref[...])
    ).astype(BF)


def back_first(
    d_second_ref, mine_ref, theirs_ref, sum_ref, vec_ref, d_first_ref, dbranch_ref, sums_ref
):
    sums_ref[...] = jnp.zeros_like(sums_ref)

    def chunk_step(chunk, carry):
        rows = pl.ds(pl.multiple_of(chunk * SHORT, SHORT), SHORT)
        upstream = d_second_ref[rows, :] + (
            mine_ref[rows, :].astype(F32) + theirs_ref[rows, :].astype(F32)
        )
        d_first, d_gain, d_shift = norm_back(upstream, sum_ref[rows, :], vec_ref[6:7, :])
        d_first_ref[rows, :] = d_first
        d_branch = d_first.astype(BF)
        dbranch_ref[rows, :] = d_branch
        sums_ref[0:1, :] += jnp.sum(d_branch.astype(F32), axis=0, keepdims=True)
        sums_ref[2:3, :] += d_shift
        sums_ref[4:5, :] += d_gain
        return carry

    lax.fori_loop(0, sum_ref.shape[0] // SHORT, chunk_step, 0)


def head_lanes(value, head):
    lane = lax.broadcasted_iota(jnp.int32, value.shape, 1)
    return (lane // (value.shape[1] // 2)) == head


def mask_row(kind, chunk, count):
    place = lax.broadcasted_iota(jnp.int32, (1, count), 1)
    allowed = (place // SHORT == chunk) | (kind == 1)
    return jnp.where(allowed, 0.0, MASKED_SCORE)


def attention_kernel(
    kind_ref, x_ref, wa_ref, wb_ref, bias_ref, wo_ref, partial_ref, qkv_ref, context_ref, lse_ref
):
    count = x_ref.shape[0]
    wide = wa_ref.shape[1]
    pair = 2 * HEAD_DIM
    kind = kind_ref[0]
    x = x_ref[...]
    bias = bias_ref[...]
    qkv_ref[:, :wide] = (dot(x, wa_ref[...]) + bias[:, :wide]).astype(BF)
    qkv_ref[:, wide:] = (dot(x, wb_ref[...]) + bias[:, wide:]).astype(BF)
    for p in range(HEADS // 4):
        keys = qkv_ref[:, (3 * p + 1) * pair : (3 * p + 2) * pair]
        values = qkv_ref[:, (3 * p + 2) * pair : (3 * p + 3) * pair]

        def chunk_step(chunk, carry):
            rows = pl.ds(pl.multiple_of(chunk * SHORT, SHORT), SHORT)
            queries = qkv_ref[rows, 3 * p * pair : (3 * p + 1) * pair] * jnp.asarray(0.125, BF)
            mask = mask_row(kind, chunk, count)
            found = []
            stats = lse_ref[rows, :] if p > 0 else jnp.zeros((SHORT, 128), F32)
            lane = lax.broadcasted_iota(jnp.int32, stats.shape, 1)
            for head in range(2):
                mine = jnp.where(head_lanes(queries, head), queries, jnp.zeros_like(queries))
                scores = dot_nt(mine, keys) + mask
                top = jnp.max(scores, axis=1, keepdims=True)
                powers = jnp.exp(scores - top)
                total = jnp.sum(powers, axis=1, keepdims=True)
                probs = powers * (1.0 / total)
                found.append(dot(probs.astype(BF), values))
                stats = jnp.where(lane == 2 * p + head, top + jnp.log(total), stats)
            lse_ref[rows, :] = stats
            both = jnp.where(head_lanes(found[0], 0), found[0], found[1])
            context_ref[rows, p * pair : (p + 1) * pair] = both.astype(BF)
            return carry

        lax.fori_loop(0, count // SHORT, chunk_step, 0)
    partial_ref[...] = dot(context_ref[...], wo_ref[...]).astype(BF)


def attention_backward_kernel(
    kind_ref, d_second_ref, mine_ref, theirs_ref, sum_ref, vec_ref,
    x_ref, qkv_ref, context_ref, lse_ref, wa_ref, wb_ref, wo_ref,
    ga_ref, gb_ref, gout_ref, partial_ref, sums_ref, d_first_ref, norm_sums_ref,
    dbranch_ref, dcontext_ref, dqkv_ref, dk_ref, dv_ref,
):
    back_first(
        d_second_ref, mine_ref, theirs_ref, sum_ref, vec_ref,
        d_first_ref, dbranch_ref, norm_sums_ref,
    )
    count = x_ref.shape[0]
    wide = wa_ref.shape[1]
    pair = 2 * HEAD_DIM
    kind = kind_ref[0]
    d_branch = dbranch_ref[...]
    dcontext_ref[...] = dot_nt(d_branch, wo_ref[...]).astype(BF)
    gout_ref[...] = dot_tn(context_ref[...], d_branch).astype(BF)
    for p in range(HEADS // 4):
        keys = qkv_ref[:, (3 * p + 1) * pair : (3 * p + 2) * pair]
        values = qkv_ref[:, (3 * p + 2) * pair : (3 * p + 3) * pair]
        dk_ref[...] = jnp.zeros_like(dk_ref)
        dv_ref[...] = jnp.zeros_like(dv_ref)

        def chunk_step(chunk, carry):
            rows = pl.ds(pl.multiple_of(chunk * SHORT, SHORT), SHORT)
            queries = qkv_ref[rows, 3 * p * pair : (3 * p + 1) * pair] * jnp.asarray(0.125, BF)
            d_context = dcontext_ref[rows, p * pair : (p + 1) * pair]
            mask = mask_row(kind, chunk, count)
            stats = lse_ref[rows, :]
            found = []
            for head in range(2):
                mine = jnp.where(head_lanes(queries, head), queries, jnp.zeros_like(queries))
                theirs = jnp.where(
                    head_lanes(d_context, head), d_context, jnp.zeros_like(d_context)
                )
                lse = stats[:, 2 * p + head : 2 * p + head + 1]
                probs = jnp.exp(dot_nt(mine, keys) + mask - lse)
                d_probs = dot_nt(theirs, values)
                row_dot = jnp.sum(d_probs * probs, axis=1, keepdims=True)
                d_scores = (probs * (d_probs - row_dot)).astype(BF)
                found.append(
                    (
                        dot(d_scores, keys) * 0.125,
                        dot_tn(d_scores, queries),
                        dot_tn(probs.astype(BF), d_context),
                    )
                )
            merged = [
                jnp.where(head_lanes(one, 0), one, other) for one, other in zip(*found)
            ]
            dqkv_ref[rows, 3 * p * pair : (3 * p + 1) * pair] = merged[0].astype(BF)
            dk_ref[...] += merged[1]
            dv_ref[...] += merged[2]
            return carry

        lax.fori_loop(0, count // SHORT, chunk_step, 0)
        dqkv_ref[:, (3 * p + 1) * pair : (3 * p + 2) * pair] = dk_ref[...].astype(BF)
        dqkv_ref[:, (3 * p + 2) * pair : (3 * p + 3) * pair] = dv_ref[...].astype(BF)
    d_a = dqkv_ref[:, :wide]
    d_b = dqkv_ref[:, wide:]
    x = x_ref[...]
    ga_ref[...] = dot_tn(x, d_a).astype(BF)
    gb_ref[...] = dot_tn(x, d_b).astype(BF)
    partial_ref[...] = (dot_nt(d_a, wa_ref[...]) + dot_nt(d_b, wb_ref[...])).astype(BF)
    sums_ref[:, :wide] = jnp.sum(d_a.astype(F32), axis=0, keepdims=True)
    sums_ref[:, wide:] = jnp.sum(d_b.astype(F32), axis=0, keepdims=True)


def kernel_call(body, shapes, scratch, *operands):
    in_vmem = pl.BlockSpec(memory_space=pltpu.VMEM)
    in_smem = pl.BlockSpec(memory_space=pltpu.SMEM)
    return pl.pallas_call(
        body,
        out_shape=shapes,
        in_specs=[in_smem if value.dtype == jnp.int32 else in_vmem for value in operands],
        out_specs=[in_vmem] * len(shapes),
        scratch_shapes=scratch,
        compiler_params=pltpu.CompilerParams(vmem_limit_bytes=VMEM_LIMIT),
        cost_estimate=pl.CostEstimate(flops=0, bytes_accessed=0, transcendentals=0),
    )(*operands)


def attention(row_kind, inputs_b, w_a, w_b, bias, w_out):
    count, width = inputs_b.shape
    half = w_out.shape[0]
    shapes = [
        jax.ShapeDtypeStruct((count, width), BF),
        jax.ShapeDtypeStruct((count, 3 * half), BF),
        jax.ShapeDtypeStruct((count, half), BF),
        jax.ShapeDtypeStruct((count, 128), F32),
    ]
    return kernel_call(
        attention_kernel, shapes, [], row_kind, inputs_b, w_a, w_b, bias, w_out
    )


def attention_backward(
    row_kind, d_second, mine, theirs, first_sum, vec, inputs_b, qkv, context, lse, w_a, w_b, w_out
):
    count, width = inputs_b.shape
    half = w_out.shape[0]
    shapes = [
        jax.ShapeDtypeStruct(w_a.shape, BF),
        jax.ShapeDtypeStruct(w_b.shape, BF),
        jax.ShapeDtypeStruct(w_out.shape, BF),
        jax.ShapeDtypeStruct((count, width), BF),
        jax.ShapeDtypeStruct((1, 3 * half), F32),
        jax.ShapeDtypeStruct((count, width), F32),
        jax.ShapeDtypeStruct((8, width), F32),
    ]
    scratch = [
        pltpu.VMEM((count, width), BF),
        pltpu.VMEM((count, half), BF),
        pltpu.VMEM((count, 3 * half), BF),
        pltpu.VMEM((count, 2 * HEAD_DIM), F32),
        pltpu.VMEM((count, 2 * HEAD_DIM), F32),
    ]
    return kernel_call(
        attention_backward_kernel, shapes, scratch, row_kind, d_second, mine, theirs, first_sum,
        vec, inputs_b, qkv, context, lse, w_a, w_b, w_out,
    )


def norm_rows(base, mine, theirs, vec):
    shapes = [jax.ShapeDtypeStruct(base.shape, kind) for kind in (F32, F32, BF)]
    return kernel_call(norm_kernel, shapes, [], base, mine, theirs, vec)


def hidden_layer(x, mine, theirs, vec, bias, up0, up1, down):
    count, hidden = x.shape[0], down.shape[0]
    shapes = [jax.ShapeDtypeStruct(x.shape, kind) for kind in (F32, F32, BF)]
    shapes += [jax.ShapeDtypeStruct((count, hidden), BF)] * 2
    shapes.append(jax.ShapeDtypeStruct(x.shape, BF))
    return kernel_call(
        hidden_kernel, shapes, [], x, mine, theirs, vec, bias, up0, up1, down
    )


def back_second(upstream, total, vec, act):
    shapes = [
        jax.ShapeDtypeStruct(total.shape, F32),
        jax.ShapeDtypeStruct(total.shape, BF),
        jax.ShapeDtypeStruct((act.shape[1], total.shape[1]), BF),
        jax.ShapeDtypeStruct((8, total.shape[1]), F32),
    ]
    body = functools.partial(back_second_kernel, len(upstream) > 1)
    return kernel_call(body, shapes, [], *upstream, total, vec, act)


def back_hidden(d_ffn, slope, normed_b, down, up0, up1):
    count, hidden = slope.shape
    width = normed_b.shape[1]
    shapes = [
        jax.ShapeDtypeStruct((width, hidden), BF),
        jax.ShapeDtypeStruct((count, width), BF),
        jax.ShapeDtypeStruct((1, hidden), F32),
    ]
    scratch = [pltpu.VMEM((count, hidden), BF)]
    return kernel_call(
        back_hidden_kernel, shapes, scratch, d_ffn, slope, normed_b, down, up0, up1
    )


def hidden_order(width, hidden_rows):
    group = width // (2 * hidden_rows)
    target = jnp.arange(width)
    source = (
        (target % (width // 2)) // hidden_rows * (2 * hidden_rows)
        + target // (width // 2) * hidden_rows
        + target % hidden_rows
    )
    del group
    return jnp.arange(width)[:, None] == source[None, :]


def shards(tokens, row_kind, w_qkv, w_out, w_up, w_down, bias_vectors, gains, bias_up, cotangent):
    chips = Chips()
    sequence = Sequence()
    core = chips.core
    count = chips.count
    device = 2 * chips.chip + core
    row_type = row_kind[0]
    rows, width = w_out.shape[1:]
    hidden = w_up.shape[2]
    hidden_rows = w_down.shape[1]
    half = width // 2
    panels = hidden // 2 // width
    own = tokens.shape[0]
    order = hidden_order(width, hidden_rows)

    pairs = HEADS // 4
    lane = half // pairs
    plan = Plan()
    state = State()

    def ordered(mine, theirs):
        return jnp.where(core == 0, mine, theirs), jnp.where(core == 0, theirs, mine)

    def both(value):
        return jnp.concatenate(ordered(value, swap(value, 1)), axis=0)

    def pack_qkv():
        sides = [
            jnp.concatenate(
                [
                    w_qkv[..., t * width + side * half + p * lane :][..., :lane]
                    for p in range(pairs)
                    for t in range(3)
                ],
                axis=-1,
            )
            for side in range(2)
        ]
        mine, sent = ordered(*sides)
        first, second = ordered(mine, swap(sent, 1))
        for layer in range(LAYERS):
            state.gathers[ATTN, layer] = Gather(
                chips, sequence, layer == 0,
                jnp.concatenate([first[layer, :, :width], second[layer, :, :width]], axis=0),
                jnp.concatenate(
                    [
                        jnp.concatenate(
                            [first[layer, :, width:], second[layer, :, width:]], axis=1
                        ),
                        w_out[layer],
                    ],
                    axis=0,
                ),
            )
        sequence.mark([state.gathers[ATTN, layer].piece for layer in range(LAYERS)])

    groups = hidden // width

    def pack_up():
        value = sequence.gate(w_up).reshape(LAYERS * rows, hidden)
        stacked = jnp.concatenate(
            [value[:, i * width : (i + 1) * width] for i in range(groups)], axis=0
        )
        stacked = dot(stacked, order.astype(BF)).astype(BF)
        mine, sent = ordered(stacked[:, :half], stacked[:, half:])
        first, second = ordered(mine, swap(sent, 1))
        for layer in range(LAYERS):
            parts = []
            for i in range(panels):
                for value in (first, second):
                    cut = [
                        value[((2 * i + j) * LAYERS + layer) * rows :][:rows] for j in range(2)
                    ]
                    parts.append(jnp.concatenate(cut, axis=1))
            state.gathers[FFN, layer] = Gather(
                chips, sequence, layer == 0, jnp.concatenate(parts, axis=0), w_down[layer]
            )
        sequence.mark([state.gathers[FFN, layer].piece for layer in range(LAYERS)])

    def vectors_start():
        values = sequence.gate((bias_vectors, gains, bias_up))
        feature = jnp.arange(width)[None, :] - rows * device == jnp.arange(rows)[:, None]
        unit = jnp.arange(hidden // 2)[None, :] - hidden_rows * chips.chip
        unit = unit == jnp.arange(hidden_rows)[:, None]
        table = jnp.concatenate(values[:2], axis=1).reshape(LAYERS * 8, rows)
        table = dot(table, feature.astype(BF)).astype(BF)
        units = [
            dot(values[2], unit[:, i * width : (i + 1) * width].astype(BF)).astype(BF)
            for i in range(panels)
        ]
        sequence.mark((table, units))
        state.table = jnp.concatenate([table + swap(table, 1)] + units, axis=0)

    def vectors_step(place):
        table = sequence.gate(state.table)
        sequence.mark(table)
        state.table = table + swap(table, 2 * 2**place)

    def vectors_end():
        table = sequence.gate(state.table).astype(F32)
        sequence.mark(table)
        for layer in range(LAYERS):
            vec = table[8 * layer : 8 * layer + 8]
            bias_q, bias_v = (
                jnp.where(core == 0, vec[i : i + 1, :half], vec[i : i + 1, half:])
                for i in range(2)
            )
            bias = []
            for p in range(pairs):
                cut = slice(p * lane, (p + 1) * lane)
                bias += [bias_q[:, cut], jnp.zeros((1, lane), F32), bias_v[:, cut]]
            state.vec[layer] = vec
            state.bias_qkv[layer] = jnp.concatenate(bias, axis=1)
            places = [8 * LAYERS + LAYERS * i + layer for i in range(panels)]
            state.bias_up[layer] = jnp.concatenate([table[i : i + 1] for i in places], axis=1)

    def tokens_start():
        value = sequence.gate(tokens)
        state.x_b[0] = both(value)
        state.x[0] = state.x_b[0].astype(F32)

    def cotangent_start():
        value = sequence.gate(cotangent)
        state.upstream = (both(value),)

    def out_exchange(layer):
        first, second = state.gathers[ATTN, layer].finish()
        w_b = jnp.swapaxes(second[:, :rows].reshape(count, rows, 2, half), 1, 2)
        out_all = second[:, rows:].reshape(2, count // 2, rows, width)
        sent, w_b = pick(out_all, 1 - core, 0), w_b.reshape(width, half)
        sequence.mark((sent, w_b))
        full_out = merge(pick(out_all, core, 0), swap(sent, 1), core, 1).reshape(half, width)
        state.w_attn[layer] = (first.reshape(width, width), w_b, full_out)

    def hidden_weights(layer):
        first, second = state.gathers[FFN, layer].finish()
        state.w_hidden[layer] = (
            second.reshape(hidden // 2, width),
            *(
                first[:, 2 * rows * i : 2 * rows * (i + 1)].reshape(width, width)
                for i in range(panels)
            ),
        )

    def run_attention(layer):
        x_b, weights = sequence.gate((state.x_b[layer], state.w_attn[layer]))
        w_a, w_b, full_out = weights
        partial, *saved = attention(row_kind, x_b, w_a, w_b, state.bias_qkv[layer], full_out)
        sequence.mark(partial)
        state.w_attn[layer] = weights
        state.saved[layer] = (x_b, *saved)
        state.branch = (partial, swap(partial, 1))

    def run_hidden(layer):
        mine, theirs = sequence.gate(state.branch)
        down, up0, up1 = state.w_hidden[layer]
        first_sum, state.normed, *kept, partial = hidden_layer(
            state.x[layer], mine, theirs, state.vec[layer], state.bias_up[layer], up0, up1, down
        )
        sequence.mark(partial)
        state.first_sum[layer] = first_sum
        state.kept[layer] = kept
        state.branch = (partial, swap(partial, 1))

    def run_norm(layer):
        mine, theirs = sequence.gate(state.branch)
        second, x, x_b = norm_rows(state.normed, mine, theirs, state.vec[layer])
        state.second[layer], state.x[layer + 1], state.x_b[layer + 1] = second, x, x_b
        sequence.mark(second)

    def run_back_second(layer):
        upstream = sequence.gate(state.upstream)
        if layer < LAYERS - 1:
            upstream = (state.d_first, *upstream)
        act = state.kept[layer][1]
        d_second, d_ffn, g_down, sums = back_second(
            upstream, state.second[layer], state.vec[layer], act
        )
        state.d_second, state.d_ffn = d_second, d_ffn
        state.sums2[layer] = sums
        bundle = state.scatters[FFN, layer]
        bundle.start(1, g_down.reshape(count, hidden_rows, width))
        sequence.mark((d_ffn, bundle.sent))

    def run_back_hidden(layer):
        d_ffn = sequence.gate(state.d_ffn)
        normed_b, _, slope = state.kept[layer]
        g_up, partial, units = back_hidden(d_ffn, slope, normed_b, *state.w_hidden[layer])
        bundle = state.scatters[FFN, layer]
        bundle.start(0, g_up.reshape(count, 2 * rows, hidden // 2))
        sequence.mark((partial, bundle.sent))
        state.units[layer] = units
        state.branch = (partial, swap(partial, 1))

    def run_back_attention(layer):
        mine, theirs = sequence.gate(state.branch)
        x_b, qkv, context, lse = state.saved[layer]
        g_a, g_b, g_out, partial, sums, state.d_first, state.sums1[layer] = attention_backward(
            row_kind, state.d_second, mine, theirs, state.first_sum[layer], state.vec[layer],
            x_b, qkv, context, lse, *state.w_attn[layer],
        )
        sequence.mark(partial)
        state.pair[layer] = jnp.concatenate(
            [
                jnp.concatenate(
                    [sums[:, (3 * p + t) * lane :][:, :lane] for p in range(pairs)], axis=1
                )
                for t in (0, 2)
            ],
            axis=0,
        )
        if layer > 0:
            state.upstream = (partial, swap(partial, 1))
        else:
            mine, sent = ordered(partial[:own], partial[own:])
            state.upstream = (mine, swap(sent, 1))
        state.g_attn[layer] = (g_a, g_b, g_out)

    def back_terms(layer):
        g_a, g_b, g_out = sequence.gate(state.g_attn[layer])
        bundle = state.scatters[ATTN, layer]
        bundle.start(0, g_a.reshape(count, 2 * rows, width))
        first = bundle.sent
        out_pair = g_out.reshape(count // 2, 2, rows, width)
        out_got = swap(pick(out_pair, 1 - core, 1), 1)
        out = merge(pick(out_pair, core, 1), out_got, core, 0).reshape(count, rows, width)
        g_b = g_b.reshape(count, 2, rows, half)
        last = jnp.concatenate([g_b[:, 0], g_b[:, 1]], axis=2)
        bundle.start(1, jnp.concatenate([last, out], axis=1))
        sequence.mark((first, bundle.sent))

    def grad_end():
        mine, theirs = sequence.gate(state.upstream)
        d_first = lax.dynamic_slice_in_dim(state.d_first, core * own, own)
        state.grad_tokens = d_first + (mine.astype(F32) + theirs.astype(F32))
        sequence.mark(state.grad_tokens)

    def mixed_end():
        value = sequence.gate(state.x_b[LAYERS])
        state.mixed = lax.dynamic_slice_in_dim(value, core * own, own)
        sequence.mark(state.mixed)

    def sums_start():
        pair = jnp.concatenate([state.pair[layer] for layer in range(LAYERS)], axis=0)
        pair = sequence.gate(pair)
        sequence.mark(pair)
        pair = jnp.concatenate(ordered(pair, swap(pair, 1)), axis=1)
        table = []
        for layer in range(LAYERS):
            table += [state.sums1[layer] + state.sums2[layer], pair[2 * layer : 2 * layer + 2]]
            units = state.units[layer]
            table += [units[:, i * width : (i + 1) * width] for i in range(panels)]
        state.total = jnp.concatenate(table, axis=0)

    def sums_step(place):
        total = sequence.gate(state.total)
        sequence.mark(total)
        state.total = total + swap(total, 2 * 2**place)

    def sums_end():
        total = sequence.gate(state.total).reshape(LAYERS, 10 + panels, width)
        features = lax.dynamic_slice_in_dim(total, rows * device, rows, axis=2)
        per_row = width // hidden_rows
        units = lax.dynamic_slice(
            total,
            (0, 10 + chips.chip // per_row, hidden_rows * (chips.chip % per_row)),
            (LAYERS, 1, hidden_rows),
        )
        vectors = jnp.concatenate([features[:, 8:10], features[:, :4]], axis=1)
        state.small = (vectors, features[:, 4:6], units.reshape(LAYERS, hidden_rows))
        sequence.mark(state.small)

    def finish_hidden(layer):
        up, down = state.scatters[FFN, layer].finish()
        sides = [
            jnp.concatenate(
                [up[(2 * i + side) * rows :][:rows] for i in range(panels)], axis=1
            )
            for side in range(2)
        ]
        mine, sent = ordered(*sides)
        state.up_pair[layer] = (mine, swap(sent, 1))
        state.down[layer] = down

    def end_hidden(layer):
        first, second = ordered(*sequence.gate(state.up_pair[layer]))
        stacked = jnp.concatenate(
            [
                jnp.concatenate(
                    [value[:, i * half : (i + 1) * half] for value in (first, second)], axis=1
                )
                for i in range(groups)
            ],
            axis=0,
        )
        stacked = lax.dot_general(
            stacked, order.astype(F32), (((1,), (1,)), ((), ())),
            precision=lax.Precision.HIGHEST, preferred_element_type=F32,
        )
        state.up[layer] = jnp.concatenate(
            [stacked[i * rows : (i + 1) * rows] for i in range(groups)], axis=1
        )
        sequence.mark(state.up[layer])

    def finish_attention(layer):
        first, rest = state.scatters[ATTN, layer].finish()
        sides = [
            jnp.concatenate(
                [
                    first[side * rows : (side + 1) * rows],
                    rest[:rows, side * half : (side + 1) * half],
                ],
                axis=1,
            )
            for side in range(2)
        ]
        mine, sent = ordered(*sides)
        state.qkv_pair[layer] = (mine, swap(sent, 1))
        state.out[layer] = rest[rows:]

    def end_attention(layer):
        values = ordered(*sequence.gate(state.qkv_pair[layer]))
        state.qkv[layer] = jnp.concatenate(
            [
                value[:, (3 * p + t) * lane :][:, :lane]
                for t in range(3)
                for value in values
                for p in range(pairs)
            ],
            axis=1,
        )
        sequence.mark(state.qkv[layer])

    def call(function, *args):
        return lambda: function(*args)

    low = len(chips.low)
    places = count.bit_length() - 1
    size = (1.0, 2.0)
    add = plan.add

    def pair_send(label):
        return [(label, (("p", 0.0),), 1)]

    def plane(length):
        return (("x", length), ("y", length))

    add("pq", 0, 3.0, [], pack_qkv)
    add("pu", 2, 4.0, [("g", ATTN, 0)], pack_up)
    add("vec", 8, 2.5, [("g", FFN, 0)], vectors_start, [(("v", 0), (("v", 1.0),), 1)])
    for place in range(places):
        add(
            ("vs", place), 8, 1.5, [("v", place)], call(vectors_step, place),
            [(("v", place + 1), (("v", 1.5),), 1)],
        )
    add("ve", 8, 0.5, [("v", places)], vectors_end)
    add("tok", 8, 0.5, ["vec"], tokens_start, pair_send("x0"))
    add("cot", 9, 0.5, [("m", 1, 0)], cotangent_start, pair_send("ct"))
    bundles = [(ATTN, 0), (FFN, 0), (ATTN, 1), (FFN, 1)]
    for rank, (kind, layer) in enumerate(bundles):
        needs = ["pq" if kind == ATTN else "pu"]
        if rank > 0:
            needs.append(("h", *bundles[rank - 1]))

        def start(kind=kind, layer=layer):
            state.gathers[kind, layer].start()

        def advance(kind=kind, layer=layer):
            state.gathers[kind, layer].advance()

        z = 6.0 * size[kind]
        if layer == 0:
            need = ("z", kind, layer)
            add(("g", kind, layer), 1 + rank, 5.0, needs, start, [(need, (("z", 2 * z),), 3)])
            add(("h", kind, layer), 0, 0.0, [("g", kind, layer)], lambda: None)
        else:
            need = ("y", kind, layer)
            add(("g", kind, layer), 1 + rank, 2.5, needs, start, [(need, (("y", z),), 1)])
            sent = ("z", kind, layer)
            add(("h", kind, layer), 1 + rank, 2.5, [need], advance, [(sent, (("z", z),), 1)])
            need = sent
        length = 6.0 * size[kind]
        for step in range(low):
            sent = ("xy", kind, layer, step)
            add(
                ("gs", kind, layer, step), 1 + rank, 4.5, [need], advance,
                [(sent, plane(length), 2)],
            )
            need = sent
            length *= 2
        if kind == ATTN:
            add(
                ("go", layer), 1 + rank, 4.0, [need], call(out_exchange, layer),
                pair_send(("w", kind, layer)),
            )
        else:
            add(("w", kind, layer), 1 + rank, 4.0, [need], call(hidden_weights, layer))
    need = "x0"
    for layer in range(LAYERS):
        add(
            ("m", 0, layer), 10, 12.0, [need, ("w", ATTN, layer), "ve"],
            call(run_attention, layer), pair_send(("p", 0, layer)),
        )
        add(
            ("m", 1, layer), 10, 11.0, [("p", 0, layer), ("w", FFN, layer)],
            call(run_hidden, layer), pair_send(("p", 1, layer)),
        )
        need = ("m", 2, layer)
        add(need, 10, 3.0, [("p", 1, layer)], call(run_norm, layer))
    add("mix", 20, 1.0, [need], mixed_end)

    needs = [need, "ct"]
    for layer in reversed(range(LAYERS)):
        state.scatters[FFN, layer] = Scatter(chips, sequence)
        state.scatters[ATTN, layer] = Scatter(chips, sequence)
        add(
            ("b", 0, layer), 10, 7.0, needs, call(run_back_second, layer),
            [(("r", FFN, layer, 0), (("x", 24.0),), 1)],
        )
        add(
            ("b", 1, layer), 10, 9.0, [("b", 0, layer)], call(run_back_hidden, layer),
            [(("r", FFN, layer, 1), (("y", 24.0),), 1)] + pair_send(("p", 2, layer)),
        )
        add(
            ("b", 2, layer), 10, 17.0, [("p", 2, layer)], call(run_back_attention, layer),
            pair_send(("p", 3, layer)),
        )
        add(
            ("b", 3, layer), 9.5, 4.0, [("b", 2, layer)], call(back_terms, layer),
            [(("r", ATTN, layer, 0), plane(12.0), 2)],
        )
        needs = [("p", 3, layer)]
        for kind in (FFN, ATTN):
            need = [("r", kind, layer, part) for part in range(1 + kind)]
            rank = 1 + 2 * (LAYERS - 1 - layer) + (kind == ATTN)

            def reduce(kind=kind, layer=layer):
                state.scatters[kind, layer].advance()

            length = 6.0 * size[kind]
            for step in range(low - 1):
                sent = ("r", kind, layer, 2 + step)
                add(
                    ("rs", kind, layer, step), rank, 4.0, need, reduce,
                    [(sent, plane(length), 2)],
                )
                need = [sent]
                length /= 2
            z = 6.0 * size[kind]
            sent = ("rz", kind, layer)
            add(("rs", kind, layer, low), rank, 3.5, need, reduce, [(sent, (("z", z),), 1)])
            need = sent
            sent = ("ry", kind, layer)
            add(("rs", kind, layer, low + 1), rank, 4.0, [need], reduce, [(sent, (("y", z),), 1)])
            last = finish_hidden if kind == FFN else finish_attention
            add(
                ("rf", kind, layer), 19, 2.0, [sent], call(last, layer),
                pair_send(("re", kind, layer)),
            )
            last = end_hidden if kind == FFN else end_attention
            add(("ro", kind, layer), 20, 3.0, [("re", kind, layer)], call(last, layer))
    add("grad", 18, 1.0, needs, grad_end)
    add("sum", 17, 2.0, [("b", 3, 0)], sums_start, pair_send(("s", 0)))
    for place in range(places):
        add(
            ("ss", place), 17, 1.5, [("s", place)], call(sums_step, place),
            [(("s", place + 1), (("v", 2.0),), 1)],
        )
    add("se", 20, 1.0, [("s", places)], sums_end)
    plan.run()

    def stacked(values):
        return jnp.stack([values[layer] for layer in range(LAYERS)])

    return (
        state.mixed,
        state.grad_tokens,
        stacked(state.qkv),
        stacked(state.out),
        stacked(state.up),
        stacked(state.down),
        *state.small,
    )


def solution(mesh):
    placed = (
        P("fsdp", None),
        P("fsdp"),
        P(None, "fsdp", None),
        P(None, "fsdp", None),
        P(None, "fsdp", None),
        P(None, "fsdp", None),
        P(None, None, "fsdp"),
        P(None, None, "fsdp"),
        P(None, "fsdp"),
        P("fsdp", None),
    )
    return jax.shard_map(
        shards,
        mesh=mesh,
        in_specs=placed,
        out_specs=(
            P("fsdp", None),
            P("fsdp", None),
            P(None, "fsdp", None),
            P(None, "fsdp", None),
            P(None, "fsdp", None),
            P(None, "fsdp", None),
            P(None, None, "fsdp"),
            P(None, None, "fsdp"),
            P(None, "fsdp"),
        ),
        check_vma=False,
    )
```

```python
import functools

import jax
import jax.numpy as jnp
from jax import lax
from jax.experimental import pallas as pl
from jax.experimental.pallas import tpu as pltpu
from jax.sharding import PartitionSpec as P

HEADS = 12
HEAD_DIM = 64
LAYERS = 2
SHORT = 128
AXIS = "fsdp"

EPSILON = 1e-05
MASKED_SCORE = -1e30
BF = jnp.bfloat16
F32 = jnp.float32
LATENCY = 3.0
UNIT = 1.48
ATTN, FFN = 0, 1
OPEN_SENDS = 5
VMEM_LIMIT = 24 * 2**20
DIRECT = (True, False, False, False)
ORDER = (
    0, 4, 1, 5, 9, 6, 10, 7, 11, 14, 8, 2, 15, 24, 12, 19, 20, 13, 16, 21, 17, 25, 26, 22,
    3, 18, 27, 23, 28, 29, 31, 32, 33, 34, 35, 40, 45, 36, 41, 46, 37, 47, 38, 49, 39, 30,
    59, 48, 50, 54, 42, 51, 55, 43, 44, 56, 52, 57, 53, 58,
)


def dot(left, right):
    return jnp.dot(left, right, preferred_element_type=F32)


def dot_tn(left, right):
    return lax.dot_general(left, right, (((0,), (0,)), ((), ())), preferred_element_type=F32)


def dot_nt(left, right):
    return lax.dot_general(left, right, (((1,), (1,)), ((), ())), preferred_element_type=F32)


def swap(value, mask):
    pairs = [(source, source ^ mask) for source in range(lax.axis_size(AXIS))]
    return lax.ppermute(value, AXIS, pairs)


def merge(mine, theirs, bit, axis):
    first = jnp.where(bit == 0, mine, theirs)
    second = jnp.where(bit == 0, theirs, mine)
    return jnp.stack([first, second], axis=axis)


class Chips:
    def __init__(self):
        device = lax.axis_index(AXIS)
        self.count = lax.axis_size(AXIS) // 2
        self.core = device % 2
        self.chip = device // 2
        self.step = self.count // 4
        self.top = self.chip // self.step
        self.low = list(range(self.count.bit_length() - 3))

    def bit(self, place):
        return (self.chip // 2**place) % 2

    def order(self, kind):
        return self.low if kind == 0 else self.low[::-1]

def pick(pair, index, axis):
    return lax.dynamic_index_in_dim(pair, index, axis, keepdims=False)


def stack_panels(value, width):
    panels = [value[..., i : i + width] for i in range(0, value.shape[-1], width)]
    return jnp.concatenate(panels, axis=-2) if len(panels) > 1 else value


def add_up(values):
    total = values[0].astype(F32)
    for value in values[1:]:
        total = total + value.astype(F32)
    return total


class Sequence:
    def __init__(self):
        self.last = None

    def gate(self, values):
        if self.last is None:
            return values
        values, _ = lax.optimization_barrier((values, self.last))
        return values

    def mark(self, values):
        self.last = values


class State:
    def __getattr__(self, name):
        value = {}
        setattr(self, name, value)
        return value


class Plan:
    def __init__(self):
        self.pieces = []

    def add(self, name, rank, cost, needs, run, sends=()):
        self.pieces.append((name, rank, cost, needs, run, sends))

    def greedy(self):
        now = 0.0
        ready = {}
        free = {}
        open_sends = {}
        waiting = list(range(len(self.pieces)))
        order = []

        def fits(piece):
            held = sum(weight for label, weight in open_sends.items() if label not in piece[3])
            added = sum(weight for _, _, weight in piece[5])
            return added == 0 or held + added <= OPEN_SENDS

        while waiting:
            known = []
            for place in waiting:
                piece = self.pieces[place]
                if all(need in ready for need in piece[3]):
                    time = max([ready[need] for need in piece[3]], default=0.0)
                    known.append((time, piece[1], place))
            known = [entry for entry in known if fits(self.pieces[entry[2]])] or known
            able = [entry[1:] for entry in known if entry[0] <= now]
            place = min(able)[1] if able else min(known)[2]
            name, _, cost, needs, _, sends = self.pieces[place]
            now = max([now] + [ready[need] for need in needs]) + cost
            ready[name] = now
            for need in needs:
                open_sends.pop(need, None)
            for label, links, weight in sends:
                ready[label] = 0.0
                for link, length in links:
                    free[link] = max(now, free.get(link, 0.0)) + length
                    ready[label] = max(ready[label], free[link] + LATENCY)
                if weight > 0:
                    open_sends[label] = weight
            waiting.remove(place)
            order.append(place)
        return order

    def run(self):
        order = ORDER if len(ORDER) == len(self.pieces) else self.greedy()
        for place in order:
            self.pieces[place][4]()


class Gather:
    def __init__(self, chips, sequence, direct, first, second):
        self.chips, self.sequence = chips, sequence
        self.direct = direct
        self.heights = (first.shape[0], second.shape[0])
        self.piece = jnp.concatenate([first, second], axis=0)
        self.steps_done = 0
        self.helds = None

    def start(self):
        self.piece = self.sequence.gate(self.piece)
        self.sequence.mark(self.piece)
        if self.direct:
            self.coming = [swap(self.piece, 2 * self.chips.step * k) for k in (1, 2, 3)]
            self.steps_done = 1
        else:
            self.coming = swap(self.piece, 2 * 2 * self.chips.step)

    def advance(self):
        chips = self.chips
        coming = self.sequence.gate(self.coming)
        step = self.steps_done
        self.steps_done += 1
        if step == 0:
            self.held = merge(self.piece, coming, chips.top // 2, 0)
            self.sequence.mark(self.held)
            self.coming = swap(self.held, 2 * chips.step)
            return
        helds = []
        if step == 1:
            place = 0
            for height in self.heights:
                if self.direct:
                    cut = [value[place : place + height] for value in [self.piece] + coming]
                    cut = [merge(cut[i], cut[i + 1], chips.top % 2, 0) for i in (0, 2)]
                    held = merge(cut[0], cut[1], chips.top // 2, 0)
                else:
                    cut = [value[:, place : place + height] for value in (self.held, coming)]
                    held = merge(cut[0], cut[1], chips.top % 2, 1)
                helds.append(held.reshape((4,) + held.shape[2:]))
                place += height
        else:
            for kind in range(2):
                order = chips.order(kind)
                bit = order[step - 2]
                axis = 1 + sum(other > bit for other in order[: step - 2])
                helds.append(merge(self.helds[kind], coming[kind], chips.bit(bit), axis))
        self.helds = helds
        self.sequence.mark(helds)
        if step - 1 < len(chips.low):
            self.coming = [
                swap(held, 2 * 2 ** chips.order(kind)[step - 1])
                for kind, held in enumerate(helds)
            ]

    def finish(self):
        while self.steps_done <= len(self.chips.low) + 1:
            self.advance()
        return [
            held.reshape((self.chips.count,) + held.shape[-2:]) for held in self.helds
        ]


class Scatter:
    def __init__(self, chips, sequence):
        self.chips, self.sequence = chips, sequence
        self.addends = [None, None]
        self.coming = [None, None]
        self.left = [list(chips.low), list(chips.low)]
        self.steps_done = 0

    def start(self, kind, terms):
        shape = (4,) + (2,) * len(self.chips.low) + terms.shape[1:]
        self.send(kind, [terms.reshape(shape)])

    def send(self, kind, held):
        chips = self.chips
        place = chips.order(kind)[::-1][self.steps_done]
        axis = 1 + sum(other > place for other in self.left[kind])
        self.left[kind].remove(place)
        bit = chips.bit(place)
        sent = add_up([pick(value, 1 - bit, axis) for value in held]).astype(BF)
        self.addends[kind] = [pick(value, bit, axis) for value in held]
        self.coming[kind] = swap(sent, 2 * 2**place)
        self.sent = sent

    def advance(self):
        chips = self.chips
        self.steps_done += 1
        coming = self.sequence.gate(self.coming)
        if self.steps_done > len(chips.low):
            self.last_step(coming)
            return
        held = [addends + [got] for addends, got in zip(self.addends, coming)]
        if self.steps_done < len(chips.low):
            sents = []
            for kind in range(2):
                self.send(kind, held[kind])
                sents.append(self.sent)
            self.sequence.mark(sents)
            return
        low_bit = chips.top % 2
        width = coming[1].shape[-1]
        held = [[value.reshape((2, 2) + value.shape[1:]) for value in values] for values in held]

        def total(bit, high_bit=None):
            sums = []
            for values in held:
                values = [pick(value, bit, 1) for value in values]
                if high_bit is not None:
                    values = [pick(value, high_bit, 0) for value in values]
                sums.append(stack_panels(add_up(values), width))
            self.height = sums[0].shape[-2]
            return jnp.concatenate(sums, axis=-2)

        sent = total(1 - low_bit).astype(BF)
        self.sequence.mark(sent)
        self.total = lambda high_bit: total(low_bit, high_bit)
        self.coming = swap(sent, 2 * chips.step)

    def last_step(self, coming):
        high_bit = self.chips.top // 2
        sent = (self.total(1 - high_bit) + pick(coming, 1 - high_bit, 0).astype(F32)).astype(BF)
        self.sequence.mark(sent)
        self.own = self.total(high_bit) + pick(coming, high_bit, 0).astype(F32)
        self.coming = swap(sent, 4 * self.chips.step)

    def finish(self):
        while self.steps_done <= len(self.chips.low):
            self.advance()
        coming = self.sequence.gate(self.coming)
        total = self.own + coming.astype(F32)
        self.sequence.mark(total)
        return total[: self.height], total[self.height :]


ROOT_HALF = 0.7071067811865476
DENSITY = 0.3989422804014327


def unit_rows(values):
    centre = values - jnp.mean(values, axis=1, keepdims=True)
    scale = lax.rsqrt(jnp.mean(centre * centre, axis=1, keepdims=True) + EPSILON)
    return centre * scale, scale


def norm_kernel(base_ref, mine_ref, theirs_ref, vec_ref, sum_ref, out_ref, out_b_ref):
    def chunk_step(chunk, carry):
        rows = pl.ds(pl.multiple_of(chunk * SHORT, SHORT), SHORT)
        total = base_ref[rows, :] + (
            mine_ref[rows, :].astype(F32) + theirs_ref[rows, :].astype(F32)
        ) + vec_ref[3:4, :]
        sum_ref[rows, :] = total
        unit, _ = unit_rows(total)
        output = unit * vec_ref[7:8, :] + vec_ref[5:6, :]
        out_ref[rows, :] = output
        out_b_ref[rows, :] = output.astype(BF)
        return carry

    lax.fori_loop(0, base_ref.shape[0] // SHORT, chunk_step, 0)


def hidden_kernel(
    x_ref, mine_ref, theirs_ref, vec_ref, bias_ref, up0_ref, up1_ref, down_ref,
    sum_ref, normed_ref, normed_b_ref, act_ref, slope_ref, partial_ref,
):
    def chunk_step(chunk, carry):
        rows = pl.ds(pl.multiple_of(chunk * SHORT, SHORT), SHORT)
        total = x_ref[rows, :] + (
            mine_ref[rows, :].astype(F32) + theirs_ref[rows, :].astype(F32) + vec_ref[2:3, :]
        )
        sum_ref[rows, :] = total
        unit, _ = unit_rows(total)
        normed = unit * vec_ref[6:7, :] + vec_ref[4:5, :]
        normed_ref[rows, :] = normed
        normed_b_ref[rows, :] = normed.astype(BF)
        return carry

    lax.fori_loop(0, x_ref.shape[0] // SHORT, chunk_step, 0)
    width = up0_ref.shape[1]
    step = 256
    for panel, up_ref in enumerate((up0_ref, up1_ref)):
        for start in range(0, width, step):
            place = panel * width + start
            pre = dot(normed_b_ref[...], up_ref[:, start : start + step])
            pre = pre + bias_ref[:, place : place + step]
            share = 0.5 + 0.5 * lax.erf(pre * ROOT_HALF)
            slope = share + pre * (DENSITY * jnp.exp(pre * pre * -0.5))
            act_ref[:, place : place + step] = (pre * share).astype(BF)
            slope_ref[:, place : place + step] = slope.astype(BF)
    partial_ref[...] = dot(act_ref[...], down_ref[...]).astype(BF)


def norm_back(upstream, total, gain):
    unit, scale = unit_rows(total)
    scaled = upstream * gain
    first = jnp.mean(scaled, axis=1, keepdims=True)
    second = jnp.mean(scaled * unit, axis=1, keepdims=True)
    return (
        scale * (scaled - first - unit * second),
        jnp.sum(upstream * unit, axis=0, keepdims=True),
        jnp.sum(upstream, axis=0, keepdims=True),
    )


def back_second_kernel(has_base, *refs):
    base_refs, refs = refs[: 3 if has_base else 1], refs[3 if has_base else 1 :]
    sum_ref, vec_ref, act_ref, d_second_ref, d_ffn_ref, g_down_ref, sums_ref = refs
    sums_ref[...] = jnp.zeros_like(sums_ref)

    def chunk_step(chunk, carry):
        rows = pl.ds(pl.multiple_of(chunk * SHORT, SHORT), SHORT)
        upstream = base_refs[0][rows, :].astype(F32)
        if has_base:
            upstream = upstream + (
                base_refs[1][rows, :].astype(F32) + base_refs[2][rows, :].astype(F32)
            )
        d_second, d_gain, d_shift = norm_back(upstream, sum_ref[rows, :], vec_ref[7:8, :])
        d_second_ref[rows, :] = d_second
        d_ffn = d_second.astype(BF)
        d_ffn_ref[rows, :] = d_ffn
        sums_ref[1:2, :] += jnp.sum(d_ffn.astype(F32), axis=0, keepdims=True)
        sums_ref[3:4, :] += d_shift
        sums_ref[5:6, :] += d_gain
        return carry

    lax.fori_loop(0, sum_ref.shape[0] // SHORT, chunk_step, 0)
    g_down_ref[...] = dot_tn(act_ref[...], d_ffn_ref[...]).astype(BF)


def back_hidden_kernel(
    d_ffn_ref, slope_ref, normed_b_ref, down_ref, up0_ref, up1_ref,
    g_up_ref, partial_ref, sums_ref, d_pre_ref,
):
    hidden = slope_ref.shape[1]
    step = 256
    for place in range(0, hidden, step):
        d_act = dot_nt(d_ffn_ref[...], down_ref[place : place + step, :])
        d_pre = (d_act * slope_ref[:, place : place + step].astype(F32)).astype(BF)
        d_pre_ref[:, place : place + step] = d_pre
        sums_ref[:, place : place + step] = jnp.sum(d_pre.astype(F32), axis=0, keepdims=True)
    g_up_ref[...] = dot_tn(normed_b_ref[...], d_pre_ref[...]).astype(BF)
    width = up0_ref.shape[1]
    partial_ref[...] = (
        dot_nt(d_pre_ref[:, :width], up0_ref[...]) + dot_nt(d_pre_ref[:, width:], up1_ref[...])
    ).astype(BF)


def back_first(
    d_second_ref, mine_ref, theirs_ref, sum_ref, vec_ref, d_first_ref, dbranch_ref, sums_ref
):
    sums_ref[...] = jnp.zeros_like(sums_ref)

    def chunk_step(chunk, carry):
        rows = pl.ds(pl.multiple_of(chunk * SHORT, SHORT), SHORT)
        upstream = d_second_ref[rows, :] + (
            mine_ref[rows, :].astype(F32) + theirs_ref[rows, :].astype(F32)
        )
        d_first, d_gain, d_shift = norm_back(upstream, sum_ref[rows, :], vec_ref[6:7, :])
        d_first_ref[rows, :] = d_first
        d_branch = d_first.astype(BF)
        dbranch_ref[rows, :] = d_branch
        sums_ref[0:1, :] += jnp.sum(d_branch.astype(F32), axis=0, keepdims=True)
        sums_ref[2:3, :] += d_shift
        sums_ref[4:5, :] += d_gain
        return carry

    lax.fori_loop(0, sum_ref.shape[0] // SHORT, chunk_step, 0)


def head_lanes(value, head):
    lane = lax.broadcasted_iota(jnp.int32, value.shape, 1)
    return (lane // (value.shape[1] // 2)) == head


def mask_row(kind, chunk, count):
    place = lax.broadcasted_iota(jnp.int32, (1, count), 1)
    allowed = (place // SHORT == chunk) | (kind == 1)
    return jnp.where(allowed, 0.0, MASKED_SCORE)


def attention_kernel(
    kind_ref, x_ref, wa_ref, wb_ref, bias_ref, wo_ref, partial_ref, qkv_ref, context_ref, lse_ref
):
    count = x_ref.shape[0]
    wide = wa_ref.shape[1]
    pair = 2 * HEAD_DIM
    kind = kind_ref[0]
    x = x_ref[...]
    bias = bias_ref[...]
    qkv_ref[:, :wide] = (dot(x, wa_ref[...]) + bias[:, :wide]).astype(BF)
    qkv_ref[:, wide:] = (dot(x, wb_ref[...]) + bias[:, wide:]).astype(BF)
    for p in range(HEADS // 4):
        keys = qkv_ref[:, (3 * p + 1) * pair : (3 * p + 2) * pair]
        values = qkv_ref[:, (3 * p + 2) * pair : (3 * p + 3) * pair]

        def chunk_step(chunk, carry):
            rows = pl.ds(pl.multiple_of(chunk * SHORT, SHORT), SHORT)
            queries = qkv_ref[rows, 3 * p * pair : (3 * p + 1) * pair] * jnp.asarray(0.125, BF)
            mask = mask_row(kind, chunk, count)
            found = []
            stats = lse_ref[rows, :] if p > 0 else jnp.zeros((SHORT, 128), F32)
            lane = lax.broadcasted_iota(jnp.int32, stats.shape, 1)
            for head in range(2):
                mine = jnp.where(head_lanes(queries, head), queries, jnp.zeros_like(queries))
                scores = dot_nt(mine, keys) + mask
                top = jnp.max(scores, axis=1, keepdims=True)
                powers = jnp.exp(scores - top)
                total = jnp.sum(powers, axis=1, keepdims=True)
                probs = powers * (1.0 / total)
                found.append(dot(probs.astype(BF), values))
                stats = jnp.where(lane == 2 * p + head, top + jnp.log(total), stats)
            lse_ref[rows, :] = stats
            both = jnp.where(head_lanes(found[0], 0), found[0], found[1])
            context_ref[rows, p * pair : (p + 1) * pair] = both.astype(BF)
            return carry

        lax.fori_loop(0, count // SHORT, chunk_step, 0)
    partial_ref[...] = dot(context_ref[...], wo_ref[...]).astype(BF)


def attention_backward_kernel(
    kind_ref, d_second_ref, mine_ref, theirs_ref, sum_ref, vec_ref,
    x_ref, qkv_ref, context_ref, lse_ref, wa_ref, wb_ref, wo_ref,
    ga_ref, gb_ref, gout_ref, partial_ref, sums_ref, d_first_ref, norm_sums_ref,
    dbranch_ref, dcontext_ref, dqkv_ref, dk_ref, dv_ref,
):
    back_first(
        d_second_ref, mine_ref, theirs_ref, sum_ref, vec_ref,
        d_first_ref, dbranch_ref, norm_sums_ref,
    )
    count = x_ref.shape[0]
    wide = wa_ref.shape[1]
    pair = 2 * HEAD_DIM
    kind = kind_ref[0]
    d_branch = dbranch_ref[...]
    dcontext_ref[...] = dot_nt(d_branch, wo_ref[...]).astype(BF)
    gout_ref[...] = dot_tn(context_ref[...], d_branch).astype(BF)
    for p in range(HEADS // 4):
        keys = qkv_ref[:, (3 * p + 1) * pair : (3 * p + 2) * pair]
        values = qkv_ref[:, (3 * p + 2) * pair : (3 * p + 3) * pair]
        dk_ref[...] = jnp.zeros_like(dk_ref)
        dv_ref[...] = jnp.zeros_like(dv_ref)

        def chunk_step(chunk, carry):
            rows = pl.ds(pl.multiple_of(chunk * SHORT, SHORT), SHORT)
            queries = qkv_ref[rows, 3 * p * pair : (3 * p + 1) * pair] * jnp.asarray(0.125, BF)
            d_context = dcontext_ref[rows, p * pair : (p + 1) * pair]
            mask = mask_row(kind, chunk, count)
            stats = lse_ref[rows, :]
            found = []
            for head in range(2):
                mine = jnp.where(head_lanes(queries, head), queries, jnp.zeros_like(queries))
                theirs = jnp.where(
                    head_lanes(d_context, head), d_context, jnp.zeros_like(d_context)
                )
                lse = stats[:, 2 * p + head : 2 * p + head + 1]
                probs = jnp.exp(dot_nt(mine, keys) + mask - lse)
                d_probs = dot_nt(theirs, values)
                row_dot = jnp.sum(d_probs * probs, axis=1, keepdims=True)
                d_scores = (probs * (d_probs - row_dot)).astype(BF)
                found.append(
                    (
                        dot(d_scores, keys) * 0.125,
                        dot_tn(d_scores, queries),
                        dot_tn(probs.astype(BF), d_context),
                    )
                )
            merged = [
                jnp.where(head_lanes(one, 0), one, other) for one, other in zip(*found)
            ]
            dqkv_ref[rows, 3 * p * pair : (3 * p + 1) * pair] = merged[0].astype(BF)
            dk_ref[...] += merged[1]
            dv_ref[...] += merged[2]
            return carry

        lax.fori_loop(0, count // SHORT, chunk_step, 0)
        dqkv_ref[:, (3 * p + 1) * pair : (3 * p + 2) * pair] = dk_ref[...].astype(BF)
        dqkv_ref[:, (3 * p + 2) * pair : (3 * p + 3) * pair] = dv_ref[...].astype(BF)
    d_a = dqkv_ref[:, :wide]
    d_b = dqkv_ref[:, wide:]
    x = x_ref[...]
    ga_ref[...] = dot_tn(x, d_a).astype(BF)
    gb_ref[...] = dot_tn(x, d_b).astype(BF)
    partial_ref[...] = (dot_nt(d_a, wa_ref[...]) + dot_nt(d_b, wb_ref[...])).astype(BF)
    sums_ref[:, :wide] = jnp.sum(d_a.astype(F32), axis=0, keepdims=True)
    sums_ref[:, wide:] = jnp.sum(d_b.astype(F32), axis=0, keepdims=True)


def kernel_call(body, shapes, scratch, *operands):
    in_vmem = pl.BlockSpec(memory_space=pltpu.VMEM)
    in_smem = pl.BlockSpec(memory_space=pltpu.SMEM)
    return pl.pallas_call(
        body,
        out_shape=shapes,
        in_specs=[in_smem if value.dtype == jnp.int32 else in_vmem for value in operands],
        out_specs=[in_vmem] * len(shapes),
        scratch_shapes=scratch,
        compiler_params=pltpu.CompilerParams(vmem_limit_bytes=VMEM_LIMIT),
        cost_estimate=pl.CostEstimate(flops=0, bytes_accessed=0, transcendentals=0),
    )(*operands)


def attention(row_kind, inputs_b, w_a, w_b, bias, w_out):
    count, width = inputs_b.shape
    half = w_out.shape[0]
    shapes = [
        jax.ShapeDtypeStruct((count, width), BF),
        jax.ShapeDtypeStruct((count, 3 * half), BF),
        jax.ShapeDtypeStruct((count, half), BF),
        jax.ShapeDtypeStruct((count, 128), F32),
    ]
    return kernel_call(
        attention_kernel, shapes, [], row_kind, inputs_b, w_a, w_b, bias, w_out
    )


def attention_backward(
    row_kind, d_second, mine, theirs, first_sum, vec, inputs_b, qkv, context, lse, w_a, w_b, w_out
):
    count, width = inputs_b.shape
    half = w_out.shape[0]
    shapes = [
        jax.ShapeDtypeStruct(w_a.shape, BF),
        jax.ShapeDtypeStruct(w_b.shape, BF),
        jax.ShapeDtypeStruct(w_out.shape, BF),
        jax.ShapeDtypeStruct((count, width), BF),
        jax.ShapeDtypeStruct((1, 3 * half), F32),
        jax.ShapeDtypeStruct((count, width), F32),
        jax.ShapeDtypeStruct((8, width), F32),
    ]
    scratch = [
        pltpu.VMEM((count, width), BF),
        pltpu.VMEM((count, half), BF),
        pltpu.VMEM((count, 3 * half), BF),
        pltpu.VMEM((count, 2 * HEAD_DIM), F32),
        pltpu.VMEM((count, 2 * HEAD_DIM), F32),
    ]
    return kernel_call(
        attention_backward_kernel, shapes, scratch, row_kind, d_second, mine, theirs, first_sum,
        vec, inputs_b, qkv, context, lse, w_a, w_b, w_out,
    )


def norm_rows(base, mine, theirs, vec):
    shapes = [jax.ShapeDtypeStruct(base.shape, kind) for kind in (F32, F32, BF)]
    return kernel_call(norm_kernel, shapes, [], base, mine, theirs, vec)


def hidden_layer(x, mine, theirs, vec, bias, up0, up1, down):
    count, hidden = x.shape[0], down.shape[0]
    shapes = [jax.ShapeDtypeStruct(x.shape, kind) for kind in (F32, F32, BF)]
    shapes += [jax.ShapeDtypeStruct((count, hidden), BF)] * 2
    shapes.append(jax.ShapeDtypeStruct(x.shape, BF))
    return kernel_call(
        hidden_kernel, shapes, [], x, mine, theirs, vec, bias, up0, up1, down
    )


def back_second(upstream, total, vec, act):
    shapes = [
        jax.ShapeDtypeStruct(total.shape, F32),
        jax.ShapeDtypeStruct(total.shape, BF),
        jax.ShapeDtypeStruct((act.shape[1], total.shape[1]), BF),
        jax.ShapeDtypeStruct((8, total.shape[1]), F32),
    ]
    body = functools.partial(back_second_kernel, len(upstream) > 1)
    return kernel_call(body, shapes, [], *upstream, total, vec, act)


def back_hidden(d_ffn, slope, normed_b, down, up0, up1):
    count, hidden = slope.shape
    width = normed_b.shape[1]
    shapes = [
        jax.ShapeDtypeStruct((width, hidden), BF),
        jax.ShapeDtypeStruct((count, width), BF),
        jax.ShapeDtypeStruct((1, hidden), F32),
    ]
    scratch = [pltpu.VMEM((count, hidden), BF)]
    return kernel_call(
        back_hidden_kernel, shapes, scratch, d_ffn, slope, normed_b, down, up0, up1
    )


def hidden_order(width, hidden_rows):
    group = width // (2 * hidden_rows)
    target = jnp.arange(width)
    source = (
        (target % (width // 2)) // hidden_rows * (2 * hidden_rows)
        + target // (width // 2) * hidden_rows
        + target % hidden_rows
    )
    del group
    return jnp.arange(width)[:, None] == source[None, :]


def shards(tokens, row_kind, w_qkv, w_out, w_up, w_down, bias_vectors, gains, bias_up, cotangent):
    chips = Chips()
    sequence = Sequence()
    core = chips.core
    count = chips.count
    device = 2 * chips.chip + core
    row_type = row_kind[0]
    rows, width = w_out.shape[1:]
    hidden = w_up.shape[2]
    hidden_rows = w_down.shape[1]
    half = width // 2
    panels = hidden // 2 // width
    own = tokens.shape[0]
    order = hidden_order(width, hidden_rows)

    pairs = HEADS // 4
    lane = half // pairs
    plan = Plan()
    state = State()

    def ordered(mine, theirs):
        return jnp.where(core == 0, mine, theirs), jnp.where(core == 0, theirs, mine)

    def both(value):
        return jnp.concatenate(ordered(value, swap(value, 1)), axis=0)

    def pack_qkv():
        cols = w_qkv.reshape(LAYERS, rows, 3, 2, pairs, lane)

        def side(which):
            return jnp.swapaxes(pick(cols, which, 3), 2, 3).reshape(LAYERS, rows, 3 * half)

        feature = jnp.arange(width)[None, :] - rows * device == jnp.arange(rows)[:, None]
        unit = jnp.arange(hidden // 2)[None, :] - hidden_rows * chips.chip
        unit = unit == jnp.arange(hidden_rows)[:, None]
        table = jnp.concatenate([bias_vectors, gains], axis=1).reshape(LAYERS * 8, rows)
        table = dot(table, feature.astype(BF)).astype(BF)
        units = dot(bias_up, unit.astype(BF)).astype(BF)
        got = swap(side(1 - core), 1)
        table = table + swap(table, 1)
        cols = merge(side(core), got, core, 1)
        for layer in range(LAYERS):
            last = cols[layer, :, :, width:]
            vectors = [table[8 * layer : 8 * layer + 8]]
            vectors += [units[layer : layer + 1, i * width :][:, :width] for i in range(panels)]
            vectors.append(jnp.zeros((8 - panels, width), BF))
            state.gathers[ATTN, layer] = Gather(
                chips, sequence, DIRECT[layer],
                cols[layer, :, :, :width].reshape(2 * rows, width),
                jnp.concatenate(
                    [jnp.concatenate([last[0], last[1]], axis=1), w_out[layer], *vectors], axis=0
                ),
            )
        sequence.mark([state.gathers[ATTN, layer].piece for layer in range(LAYERS)])

    groups = hidden // width

    def pack_up():
        value = sequence.gate(w_up).reshape(LAYERS * rows, hidden)
        stacked = jnp.concatenate(
            [value[:, i * width : (i + 1) * width] for i in range(groups)], axis=0
        )
        stacked = dot(stacked, order.astype(BF)).astype(BF)
        mine, sent = ordered(stacked[:, :half], stacked[:, half:])
        first, second = ordered(mine, swap(sent, 1))
        for layer in range(LAYERS):
            parts = []
            for i in range(panels):
                for value in (first, second):
                    cut = [
                        value[((2 * i + j) * LAYERS + layer) * rows :][:rows] for j in range(2)
                    ]
                    parts.append(jnp.concatenate(cut, axis=1))
            state.gathers[FFN, layer] = Gather(
                chips, sequence, DIRECT[LAYERS + layer], jnp.concatenate(parts, axis=0),
                w_down[layer],
            )
        sequence.mark([state.gathers[FFN, layer].piece for layer in range(LAYERS)])

    def read_vectors(layer, table):
        table = jnp.sum(table.astype(F32), axis=0)
        vec = table[:8]
        bias_q, bias_v = (
            jnp.where(core == 0, vec[i : i + 1, :half], vec[i : i + 1, half:]) for i in range(2)
        )
        bias = []
        for p in range(pairs):
            cut = slice(p * lane, (p + 1) * lane)
            bias += [bias_q[:, cut], jnp.zeros((1, lane), F32), bias_v[:, cut]]
        state.vec[layer] = vec
        state.bias_qkv[layer] = jnp.concatenate(bias, axis=1)
        state.bias_up[layer] = jnp.concatenate(
            [table[8 + i : 9 + i] for i in range(panels)], axis=1
        )

    def tokens_start():
        value = sequence.gate(tokens)
        state.x_b[0] = both(value)
        state.x[0] = state.x_b[0].astype(F32)

    def cotangent_start():
        value = sequence.gate(cotangent)
        state.upstream = (both(value),)

    def out_exchange(layer):
        first, second = state.gathers[ATTN, layer].finish()
        w_b = jnp.swapaxes(second[:, :rows].reshape(count, rows, 2, half), 1, 2)
        out_all = second[:, rows : 2 * rows].reshape(2, count // 2, rows, width)
        sent, w_b = pick(out_all, 1 - core, 0), w_b.reshape(width, half)
        read_vectors(layer, second[:, 2 * rows :])
        sequence.mark((sent, w_b, state.vec[layer]))
        full_out = merge(pick(out_all, core, 0), swap(sent, 1), core, 1).reshape(half, width)
        state.w_attn[layer] = (first.reshape(width, width), w_b, full_out)

    def hidden_weights(layer):
        first, second = state.gathers[FFN, layer].finish()
        state.w_hidden[layer] = (
            second.reshape(hidden // 2, width),
            *(
                first[:, 2 * rows * i : 2 * rows * (i + 1)].reshape(width, width)
                for i in range(panels)
            ),
        )

    def run_attention(layer):
        x_b, weights = sequence.gate((state.x_b[layer], state.w_attn[layer]))
        w_a, w_b, full_out = weights
        partial, *saved = attention(row_kind, x_b, w_a, w_b, state.bias_qkv[layer], full_out)
        sequence.mark(partial)
        state.w_attn[layer] = weights
        state.saved[layer] = (x_b, *saved)
        state.branch = (partial, swap(partial, 1))

    def run_hidden(layer):
        mine, theirs = sequence.gate(state.branch)
        down, up0, up1 = state.w_hidden[layer]
        first_sum, state.normed, *kept, partial = hidden_layer(
            state.x[layer], mine, theirs, state.vec[layer], state.bias_up[layer], up0, up1, down
        )
        sequence.mark(partial)
        state.first_sum[layer] = first_sum
        state.kept[layer] = kept
        state.branch = (partial, swap(partial, 1))

    def run_norm(layer):
        mine, theirs = sequence.gate(state.branch)
        second, x, x_b = norm_rows(state.normed, mine, theirs, state.vec[layer])
        state.second[layer], state.x[layer + 1], state.x_b[layer + 1] = second, x, x_b
        sequence.mark(second)

    def run_back_second(layer):
        upstream = sequence.gate(state.upstream)
        if layer < LAYERS - 1:
            upstream = (state.d_first, *upstream)
        act = state.kept[layer][1]
        d_second, d_ffn, g_down, sums = back_second(
            upstream, state.second[layer], state.vec[layer], act
        )
        state.d_second, state.d_ffn = d_second, d_ffn
        state.sums2[layer] = sums
        bundle = state.scatters[FFN, layer]
        bundle.start(1, g_down.reshape(count, hidden_rows, width))
        sequence.mark((d_ffn, bundle.sent))

    def run_back_hidden(layer):
        d_ffn = sequence.gate(state.d_ffn)
        normed_b, _, slope = state.kept[layer]
        g_up, partial, units = back_hidden(d_ffn, slope, normed_b, *state.w_hidden[layer])
        bundle = state.scatters[FFN, layer]
        bundle.start(0, g_up.reshape(count, 2 * rows, hidden // 2))
        sequence.mark((partial, bundle.sent))
        state.units[layer] = units
        state.branch = (partial, swap(partial, 1))

    def run_back_attention(layer):
        mine, theirs = sequence.gate(state.branch)
        x_b, qkv, context, lse = state.saved[layer]
        g_a, g_b, g_out, partial, sums, state.d_first, state.sums1[layer] = attention_backward(
            row_kind, state.d_second, mine, theirs, state.first_sum[layer], state.vec[layer],
            x_b, qkv, context, lse, *state.w_attn[layer],
        )
        sequence.mark(partial)
        state.pair[layer] = jnp.concatenate(
            [
                jnp.concatenate(
                    [sums[:, (3 * p + t) * lane :][:, :lane] for p in range(pairs)], axis=1
                )
                for t in (0, 2)
            ],
            axis=0,
        )
        if layer > 0:
            state.upstream = (partial, swap(partial, 1))
        else:
            mine, sent = ordered(partial[:own], partial[own:])
            state.upstream = (mine, swap(sent, 1))
        state.g_attn[layer] = (g_a, g_b, g_out)

    def sum_rows(layer):
        pair = state.pair[layer]
        nothing = jnp.zeros_like(pair)
        pair = jnp.concatenate(ordered(pair, nothing), axis=1)
        units = [state.units[layer][:, i * width :][:, :width] for i in range(panels)]
        small = jnp.concatenate([state.sums1[layer] + state.sums2[layer], pair, *units], axis=0)
        small = jnp.pad(small.astype(BF), ((0, 16 - small.shape[0]), (0, 0)))
        line = jnp.arange(16)[:, None]
        place = jnp.arange(width)[None, :]
        owner = jnp.where(
            line < 10, place // (2 * rows), ((line - 10) * width + place) // hidden_rows
        )
        mine = owner[None] == jnp.arange(count)[:, None, None]
        return jnp.where(mine, small[None], jnp.zeros((), BF))

    def back_terms(layer):
        g_a, g_b, g_out = sequence.gate(state.g_attn[layer])
        bundle = state.scatters[ATTN, layer]
        bundle.start(0, g_a.reshape(count, 2 * rows, width))
        first = bundle.sent
        out_pair = g_out.reshape(count // 2, 2, rows, width)
        out_got = swap(pick(out_pair, 1 - core, 1), 1)
        out = merge(pick(out_pair, core, 1), out_got, core, 0).reshape(count, rows, width)
        g_b = g_b.reshape(count, 2, rows, half)
        last = jnp.concatenate([g_b[:, 0], g_b[:, 1]], axis=2)
        bundle.start(1, jnp.concatenate([last, out, sum_rows(layer)], axis=1))
        sequence.mark((first, bundle.sent))

    def grad_end():
        mine, theirs = sequence.gate(state.upstream)
        d_first = lax.dynamic_slice_in_dim(state.d_first, core * own, own)
        state.grad_tokens = d_first + (mine.astype(F32) + theirs.astype(F32))
        sequence.mark(state.grad_tokens)

    def mixed_end():
        value = sequence.gate(state.x_b[LAYERS])
        state.mixed = lax.dynamic_slice_in_dim(value, core * own, own)
        sequence.mark(state.mixed)

    def finish_hidden(layer):
        up, down = state.scatters[FFN, layer].finish()
        sides = [
            jnp.concatenate(
                [up[(2 * i + side) * rows :][:rows] for i in range(panels)], axis=1
            )
            for side in range(2)
        ]
        mine, sent = ordered(*sides)
        state.up_pair[layer] = (mine, swap(sent, 1))
        state.down[layer] = down

    def end_hidden(layer):
        first, second = ordered(*sequence.gate(state.up_pair[layer]))
        stacked = jnp.concatenate(
            [
                jnp.concatenate(
                    [value[:, i * half : (i + 1) * half] for value in (first, second)], axis=1
                )
                for i in range(groups)
            ],
            axis=0,
        )
        stacked = lax.dot_general(
            stacked, order.astype(F32), (((1,), (1,)), ((), ())),
            precision=lax.Precision.HIGHEST, preferred_element_type=F32,
        )
        state.up[layer] = jnp.concatenate(
            [stacked[i * rows : (i + 1) * rows] for i in range(groups)], axis=1
        )
        sequence.mark(state.up[layer])

    def finish_attention(layer):
        first, rest = state.scatters[ATTN, layer].finish()
        sides = [
            jnp.concatenate(
                [
                    first[side * rows : (side + 1) * rows],
                    rest[:rows, side * half : (side + 1) * half],
                ],
                axis=1,
            )
            for side in range(2)
        ]
        mine, sent = ordered(*sides)
        small = rest[2 * rows :]
        pair = jnp.pad(small[8:], ((0, 0), (0, mine.shape[1] - width)))
        sent = jnp.concatenate([sent, pair], axis=0)
        state.qkv_pair[layer] = (mine, swap(sent, 1))
        state.out[layer] = rest[rows : 2 * rows]
        state.small_rows[layer] = small

    def end_attention(layer):
        mine, theirs = sequence.gate(state.qkv_pair[layer])
        small = state.small_rows[layer]
        small = jnp.concatenate([theirs[rows : rows + 2, :width] + small[8:10], small], axis=0)
        features = lax.dynamic_slice_in_dim(small, rows * device, rows, axis=1)
        per_row = width // hidden_rows
        units = lax.dynamic_slice(
            small,
            (12 + chips.chip // per_row, hidden_rows * (chips.chip % per_row)),
            (1, hidden_rows),
        )
        state.vectors[layer] = features[:6]
        state.gains[layer] = features[6:8]
        state.unit_sums[layer] = units[0]
        values = ordered(mine, theirs[:rows])
        state.qkv[layer] = jnp.concatenate(
            [
                value[:, (3 * p + t) * lane :][:, :lane]
                for t in range(3)
                for value in values
                for p in range(pairs)
            ],
            axis=1,
        )
        sequence.mark(state.qkv[layer])

    def call(function, *args):
        return lambda: function(*args)

    low = len(chips.low)
    size = (1.0, 2.0)
    add = plan.add

    def pair_send(label):
        return [(label, (("p", 0.0),), 1)]

    def plane(length):
        return (("x", length), ("y", length))

    add("pq", 0, 6.0, [], pack_qkv)
    add("pu", 2, 3.0, [("g", ATTN, 0)], pack_up)
    add("tok", 8, 0.5, ["pu"], tokens_start, pair_send("x0"))
    add("cot", 9, 0.5, [("m", 1, 0)], cotangent_start, pair_send("ct"))
    bundles = [(ATTN, 0), (FFN, 0), (ATTN, 1), (FFN, 1)]
    for rank, (kind, layer) in enumerate(bundles):
        needs = ["pq" if kind == ATTN else "pu"]
        if rank > 0:
            needs.append(("h", *bundles[rank - 1]))

        def start(kind=kind, layer=layer):
            state.gathers[kind, layer].start()

        def advance(kind=kind, layer=layer):
            state.gathers[kind, layer].advance()

        parts = (1.0, 4.0 / 3) if kind == ATTN else (2.0, 2.0)
        z = UNIT * 2 * sum(parts)
        if DIRECT[LAYERS * kind + layer]:
            need = ("z", kind, layer)
            add(("g", kind, layer), 1 + rank, 5.0, needs, start, [(need, (("z", 2 * z),), 3)])
            add(("h", kind, layer), 0, 0.0, [("g", kind, layer)], lambda: None)
        else:
            need = ("y", kind, layer)
            add(("g", kind, layer), 1 + rank, 3.0, needs, start, [(need, (("w", z),), 1)])
            sent = ("z", kind, layer)
            add(("h", kind, layer), 1 + rank, 2.2, [need], advance, [(sent, (("z", z),), 1)])
            need = sent
        length = UNIT * 4
        for step in range(low):
            sent = ("xy", kind, layer, step)
            links = (("x", length * parts[step % 2]), ("y", length * parts[1 - step % 2]))
            add(
                ("gs", kind, layer, step), 1 + rank, 5.0 + 0.5 * kind, [need], advance,
                [(sent, links, 2)],
            )
            need = sent
            length *= 2
        if kind == ATTN:
            add(
                ("go", layer), 1 + rank, 5.0, [need], call(out_exchange, layer),
                pair_send(("w", kind, layer)),
            )
        else:
            add(("w", kind, layer), 1 + rank, 3.5, [need], call(hidden_weights, layer))
    need = "x0"
    for layer in range(LAYERS):
        add(
            ("m", 0, layer), 10, 12.7, [need, ("w", ATTN, layer)],
            call(run_attention, layer), pair_send(("p", 0, layer)),
        )
        add(
            ("m", 1, layer), 10, 6.0, [("p", 0, layer), ("w", FFN, layer)],
            call(run_hidden, layer), pair_send(("p", 1, layer)),
        )
        need = ("m", 2, layer)
        add(need, 10, 3.0, [("p", 1, layer)], call(run_norm, layer))
    add("mix", 20, 1.0, [need], mixed_end)

    needs = [need, "ct"]
    for layer in reversed(range(LAYERS)):
        state.scatters[FFN, layer] = Scatter(chips, sequence)
        state.scatters[ATTN, layer] = Scatter(chips, sequence)
        add(
            ("b", 0, layer), 10, 5.0, needs, call(run_back_second, layer),
            [(("r", FFN, layer, 0), (("x", UNIT * 16),), 1)],
        )
        add(
            ("b", 1, layer), 10, 6.5, [("b", 0, layer)], call(run_back_hidden, layer),
            [(("r", FFN, layer, 1), (("y", UNIT * 16),), 1)] + pair_send(("p", 2, layer)),
        )
        add(
            ("b", 2, layer), 10, 17.2, [("p", 2, layer)], call(run_back_attention, layer),
            pair_send(("p", 3, layer)),
        )
        add(
            ("b", 3, layer), 9.5, 6.0, [("b", 2, layer)], call(back_terms, layer),
            [(("r", ATTN, layer, 0), (("x", UNIT * 8 * 4 / 3), ("y", UNIT * 8)), 2)],
        )
        needs = [("p", 3, layer)]
        for kind in (FFN, ATTN):
            need = [("r", kind, layer, part) for part in range(1 + kind)]
            rank = 1 + 2 * (LAYERS - 1 - layer) + (kind == ATTN)

            def reduce(kind=kind, layer=layer):
                state.scatters[kind, layer].advance()

            parts = (1.0, 4.0 / 3) if kind == ATTN else (2.0, 2.0)
            length = UNIT * 4
            for step in range(low - 1):
                sent = ("r", kind, layer, 2 + step)
                links = (("x", length * parts[step % 2]), ("y", length * parts[1 - step % 2]))
                add(
                    ("rs", kind, layer, step), rank, 5.5 + kind, need, reduce, [(sent, links, 2)]
                )
                need = [sent]
                length /= 2
            z = UNIT * 2 * sum(parts)
            sent = ("rz", kind, layer)
            add(("rs", kind, layer, low), rank, 4.0, need, reduce, [(sent, (("z", z),), 1)])
            need = sent
            sent = ("ry", kind, layer)
            add(("rs", kind, layer, low + 1), rank, 3.8, [need], reduce, [(sent, (("w", z),), 1)])
            last = finish_hidden if kind == FFN else finish_attention
            add(
                ("rf", kind, layer), 19, 2.0, [sent], call(last, layer),
                pair_send(("re", kind, layer)),
            )
            last = end_hidden if kind == FFN else end_attention
            add(("ro", kind, layer), 20, 2.5, [("re", kind, layer)], call(last, layer))
    add("grad", 18, 1.2, needs, grad_end)
    plan.run()

    def stacked(values):
        return jnp.stack([values[layer] for layer in range(LAYERS)])

    return (
        state.mixed,
        state.grad_tokens,
        stacked(state.qkv),
        stacked(state.out),
        stacked(state.up),
        stacked(state.down),
        stacked(state.vectors),
        stacked(state.gains),
        stacked(state.unit_sums),
    )


def solution(mesh):
    placed = (
        P("fsdp", None),
        P("fsdp"),
        P(None, "fsdp", None),
        P(None, "fsdp", None),
        P(None, "fsdp", None),
        P(None, "fsdp", None),
        P(None, None, "fsdp"),
        P(None, None, "fsdp"),
        P(None, "fsdp"),
        P("fsdp", None),
    )
    return jax.shard_map(
        shards,
        mesh=mesh,
        in_specs=placed,
        out_specs=(
            P("fsdp", None),
            P("fsdp", None),
            P(None, "fsdp", None),
            P(None, "fsdp", None),
            P(None, "fsdp", None),
            P(None, "fsdp", None),
            P(None, None, "fsdp"),
            P(None, None, "fsdp"),
            P(None, "fsdp"),
        ),
        check_vma=False,
    )
```

```python
import functools

import jax
import jax.numpy as jnp
from jax import lax
from jax.experimental import pallas as pl
from jax.experimental.pallas import tpu as pltpu
from jax.sharding import PartitionSpec as P

HEADS = 12
HEAD_DIM = 64
LAYERS = 2
SHORT = 128
AXIS = "fsdp"

EPSILON = 1e-05
MASKED_SCORE = -1e30
BF = jnp.bfloat16
F32 = jnp.float32
LATENCY = 2.5
UNIT = 1.48
ATTN, FFN = 0, 1
OPEN_SENDS = 5
VMEM_LIMIT = 24 * 2**20
DIRECT = (False, False, False, False)
ORDER = (
    0, 5, 1, 10, 6, 2, 11, 3, 7, 12, 8, 13, 9, 21, 15, 14, 18, 16, 22, 4, 23, 19, 17, 24,
    20, 25, 26, 28, 29, 30, 32, 31, 42, 33, 43, 44, 34, 37, 46, 56, 35, 38, 36, 45, 39,
    47, 27, 51, 48, 52, 53, 49, 40, 50, 54, 41, 55,
)


def dot(left, right):
    return jnp.dot(left, right, preferred_element_type=F32)


def dot_tn(left, right):
    return lax.dot_general(left, right, (((0,), (0,)), ((), ())), preferred_element_type=F32)


def dot_nt(left, right):
    return lax.dot_general(left, right, (((1,), (1,)), ((), ())), preferred_element_type=F32)


def swap(value, mask):
    pairs = [(source, source ^ mask) for source in range(lax.axis_size(AXIS))]
    return lax.ppermute(value, AXIS, pairs)


def pair_trade(slots):
    pairs = [[first, first + 1] for first in range(0, lax.axis_size(AXIS), 2)]
    return lax.all_to_all(slots, AXIS, 0, 0, axis_index_groups=pairs)


def merge(mine, theirs, bit, axis):
    first = jnp.where(bit == 0, mine, theirs)
    second = jnp.where(bit == 0, theirs, mine)
    return jnp.stack([first, second], axis=axis)


class Chips:
    def __init__(self):
        device = lax.axis_index(AXIS)
        self.count = lax.axis_size(AXIS) // 2
        self.core = device % 2
        self.chip = device // 2
        self.step = self.count // 4
        self.top = self.chip // self.step
        self.low = list(range(self.count.bit_length() - 3))

    def bit(self, place):
        return (self.chip // 2**place) % 2

    def order(self, kind):
        return self.low if kind == 0 else self.low[::-1]

def pick(pair, index, axis):
    return lax.dynamic_index_in_dim(pair, index, axis, keepdims=False)


def stack_panels(value, width):
    panels = [value[..., i : i + width] for i in range(0, value.shape[-1], width)]
    return jnp.concatenate(panels, axis=-2) if len(panels) > 1 else value


def add_up(values):
    total = values[0].astype(F32)
    for value in values[1:]:
        total = total + value.astype(F32)
    return total


class Sequence:
    def __init__(self):
        self.last = None

    def gate(self, values):
        if self.last is None:
            return values
        values, _ = lax.optimization_barrier((values, self.last))
        return values

    def mark(self, values):
        self.last = values


class State:
    def __getattr__(self, name):
        value = {}
        setattr(self, name, value)
        return value


class Plan:
    def __init__(self):
        self.pieces = []

    def add(self, name, rank, cost, needs, run, sends=()):
        self.pieces.append((name, rank, cost, needs, run, sends))

    def greedy(self):
        now = 0.0
        ready = {}
        free = {}
        open_sends = {}
        waiting = list(range(len(self.pieces)))
        order = []

        def fits(piece):
            held = sum(weight for label, weight in open_sends.items() if label not in piece[3])
            added = sum(weight for _, _, weight in piece[5])
            return added == 0 or held + added <= OPEN_SENDS

        while waiting:
            known = []
            for place in waiting:
                piece = self.pieces[place]
                if all(need in ready for need in piece[3]):
                    time = max([ready[need] for need in piece[3]], default=0.0)
                    known.append((time, piece[1], place))
            known = [entry for entry in known if fits(self.pieces[entry[2]])] or known
            able = [entry[1:] for entry in known if entry[0] <= now]
            place = min(able)[1] if able else min(known)[2]
            name, _, cost, needs, _, sends = self.pieces[place]
            now = max([now] + [ready[need] for need in needs]) + cost
            ready[name] = now
            for need in needs:
                open_sends.pop(need, None)
            for label, links, weight in sends:
                ready[label] = 0.0
                for link, length in links:
                    free[link] = max(now, free.get(link, 0.0)) + length
                    ready[label] = max(ready[label], free[link] + LATENCY)
                if weight > 0:
                    open_sends[label] = weight
            waiting.remove(place)
            order.append(place)
        return order

    def run(self):
        order = ORDER if len(ORDER) == len(self.pieces) else self.greedy()
        for place in order:
            self.pieces[place][4]()


class Gather:
    def __init__(self, chips, sequence, direct, first, second):
        self.chips, self.sequence = chips, sequence
        self.direct = direct
        self.heights = (first.shape[0], second.shape[0])
        self.piece = jnp.concatenate([first, second], axis=0)
        self.steps_done = 0
        self.helds = None

    def begin(self, held):
        held = self.sequence.gate(held)
        first = self.heights[0]
        self.helds = [held[:, :first], held[:, first:]]
        self.sequence.mark(self.helds)
        self.steps_done = 2
        self.coming = [
            swap(held, 2 * 2 ** self.chips.order(kind)[0]) for kind, held in enumerate(self.helds)
        ]

    def start(self):
        self.piece = self.sequence.gate(self.piece)
        self.sequence.mark(self.piece)
        if self.direct:
            self.coming = [swap(self.piece, 2 * self.chips.step * k) for k in (1, 2, 3)]
            self.steps_done = 1
        else:
            self.coming = swap(self.piece, 2 * 2 * self.chips.step)

    def advance(self):
        chips = self.chips
        coming = self.sequence.gate(self.coming)
        step = self.steps_done
        self.steps_done += 1
        if step == 0:
            self.held = merge(self.piece, coming, chips.top // 2, 0)
            self.sequence.mark(self.held)
            self.coming = swap(self.held, 2 * chips.step)
            return
        helds = []
        if step == 1:
            place = 0
            for height in self.heights:
                if self.direct:
                    cut = [value[place : place + height] for value in [self.piece] + coming]
                    cut = [merge(cut[i], cut[i + 1], chips.top % 2, 0) for i in (0, 2)]
                    held = merge(cut[0], cut[1], chips.top // 2, 0)
                else:
                    cut = [value[:, place : place + height] for value in (self.held, coming)]
                    held = merge(cut[0], cut[1], chips.top % 2, 1)
                helds.append(held.reshape((4,) + held.shape[2:]))
                place += height
        else:
            for kind in range(2):
                order = chips.order(kind)
                bit = order[step - 2]
                axis = 1 + sum(other > bit for other in order[: step - 2])
                helds.append(merge(self.helds[kind], coming[kind], chips.bit(bit), axis))
        self.helds = helds
        self.sequence.mark(helds)
        if step - 1 < len(chips.low):
            self.coming = [
                swap(held, 2 * 2 ** chips.order(kind)[step - 1])
                for kind, held in enumerate(helds)
            ]

    def finish(self):
        while self.steps_done <= len(self.chips.low) + 1:
            self.advance()
        return [
            held.reshape((self.chips.count,) + held.shape[-2:]) for held in self.helds
        ]


class Scatter:
    def __init__(self, chips, sequence):
        self.chips, self.sequence = chips, sequence
        self.addends = [None, None]
        self.coming = [None, None]
        self.left = [list(chips.low), list(chips.low)]
        self.steps_done = 0

    def start(self, kind, terms):
        shape = (4,) + (2,) * len(self.chips.low) + terms.shape[1:]
        self.send(kind, [terms.reshape(shape)])

    def send(self, kind, held):
        chips = self.chips
        place = chips.order(kind)[::-1][self.steps_done]
        axis = 1 + sum(other > place for other in self.left[kind])
        self.left[kind].remove(place)
        bit = chips.bit(place)
        sent = add_up([pick(value, 1 - bit, axis) for value in held]).astype(BF)
        self.addends[kind] = [pick(value, bit, axis) for value in held]
        self.coming[kind] = swap(sent, 2 * 2**place)
        self.sent = sent

    def advance(self):
        chips = self.chips
        self.steps_done += 1
        coming = self.sequence.gate(self.coming)
        if self.steps_done > len(chips.low):
            self.last_step(coming)
            return
        held = [addends + [got] for addends, got in zip(self.addends, coming)]
        if self.steps_done < len(chips.low):
            sents = []
            for kind in range(2):
                self.send(kind, held[kind])
                sents.append(self.sent)
            self.sequence.mark(sents)
            return
        low_bit = chips.top % 2
        width = coming[1].shape[-1]
        held = [[value.reshape((2, 2) + value.shape[1:]) for value in values] for values in held]

        def total(bit, high_bit=None):
            sums = []
            for values in held:
                values = [pick(value, bit, 1) for value in values]
                if high_bit is not None:
                    values = [pick(value, high_bit, 0) for value in values]
                sums.append(stack_panels(add_up(values), width))
            self.height = sums[0].shape[-2]
            return jnp.concatenate(sums, axis=-2)

        sent = total(1 - low_bit).astype(BF)
        self.sequence.mark(sent)
        self.total = lambda high_bit: total(low_bit, high_bit)
        self.coming = swap(sent, 2 * chips.step)

    def last_step(self, coming):
        high_bit = self.chips.top // 2
        sent = (self.total(1 - high_bit) + pick(coming, 1 - high_bit, 0).astype(F32)).astype(BF)
        self.sequence.mark(sent)
        self.own = self.total(high_bit) + pick(coming, high_bit, 0).astype(F32)
        self.coming = swap(sent, 4 * self.chips.step)

    def finish(self):
        while self.steps_done <= len(self.chips.low):
            self.advance()
        coming = self.sequence.gate(self.coming)
        total = self.own + coming.astype(F32)
        self.sequence.mark(total)
        return total[: self.height], total[self.height :]


ROOT_HALF = 0.7071067811865476
DENSITY = 0.3989422804014327


def unit_rows(values):
    centre = values - jnp.mean(values, axis=1, keepdims=True)
    scale = lax.rsqrt(jnp.mean(centre * centre, axis=1, keepdims=True) + EPSILON)
    return centre * scale, scale


def pair_rows(both_ref, rows):
    return both_ref[0, rows, :].astype(F32) + both_ref[1, rows, :].astype(F32)


def set_both(partial_ref, value):
    value = value.astype(BF)
    partial_ref[0] = value
    partial_ref[1] = value


def norm_kernel(base_ref, both_ref, vec_ref, sum_ref, out_ref, out_b_ref):
    def chunk_step(chunk, carry):
        rows = pl.ds(pl.multiple_of(chunk * SHORT, SHORT), SHORT)
        total = base_ref[rows, :] + pair_rows(both_ref, rows) + vec_ref[3:4, :]
        sum_ref[rows, :] = total
        unit, _ = unit_rows(total)
        output = unit * vec_ref[7:8, :] + vec_ref[5:6, :]
        out_ref[rows, :] = output
        out_b_ref[rows, :] = output.astype(BF)
        return carry

    lax.fori_loop(0, base_ref.shape[0] // SHORT, chunk_step, 0)


def hidden_kernel(
    x_ref, both_ref, vec_ref, bias_ref, up0_ref, up1_ref, down_ref,
    sum_ref, normed_ref, normed_b_ref, act_ref, slope_ref, partial_ref,
):
    def chunk_step(chunk, carry):
        rows = pl.ds(pl.multiple_of(chunk * SHORT, SHORT), SHORT)
        total = x_ref[rows, :] + (pair_rows(both_ref, rows) + vec_ref[2:3, :])
        sum_ref[rows, :] = total
        unit, _ = unit_rows(total)
        normed = unit * vec_ref[6:7, :] + vec_ref[4:5, :]
        normed_ref[rows, :] = normed
        normed_b_ref[rows, :] = normed.astype(BF)
        return carry

    lax.fori_loop(0, x_ref.shape[0] // SHORT, chunk_step, 0)
    width = up0_ref.shape[1]
    step = 256
    for panel, up_ref in enumerate((up0_ref, up1_ref)):
        for start in range(0, width, step):
            place = panel * width + start
            pre = dot(normed_b_ref[...], up_ref[:, start : start + step])
            pre = pre + bias_ref[:, place : place + step]
            share = 0.5 + 0.5 * lax.erf(pre * ROOT_HALF)
            slope = share + pre * (DENSITY * jnp.exp(pre * pre * -0.5))
            act_ref[:, place : place + step] = (pre * share).astype(BF)
            slope_ref[:, place : place + step] = slope.astype(BF)
    set_both(partial_ref, dot(act_ref[...], down_ref[...]))


def norm_back(upstream, total, gain):
    unit, scale = unit_rows(total)
    scaled = upstream * gain
    first = jnp.mean(scaled, axis=1, keepdims=True)
    second = jnp.mean(scaled * unit, axis=1, keepdims=True)
    return (
        scale * (scaled - first - unit * second),
        jnp.sum(upstream * unit, axis=0, keepdims=True),
        jnp.sum(upstream, axis=0, keepdims=True),
    )


def back_second_kernel(has_base, *refs):
    base_refs, refs = refs[: 1 + has_base], refs[1 + has_base :]
    sum_ref, vec_ref, act_ref, d_second_ref, d_ffn_ref, g_down_ref, sums_ref = refs
    sums_ref[...] = jnp.zeros_like(sums_ref)

    def chunk_step(chunk, carry):
        rows = pl.ds(pl.multiple_of(chunk * SHORT, SHORT), SHORT)
        upstream = base_refs[0][rows, :].astype(F32)
        if has_base:
            upstream = upstream + pair_rows(base_refs[1], rows)
        d_second, d_gain, d_shift = norm_back(upstream, sum_ref[rows, :], vec_ref[7:8, :])
        d_second_ref[rows, :] = d_second
        d_ffn = d_second.astype(BF)
        d_ffn_ref[rows, :] = d_ffn
        sums_ref[1:2, :] += jnp.sum(d_ffn.astype(F32), axis=0, keepdims=True)
        sums_ref[3:4, :] += d_shift
        sums_ref[5:6, :] += d_gain
        return carry

    lax.fori_loop(0, sum_ref.shape[0] // SHORT, chunk_step, 0)
    g_down_ref[...] = dot_tn(act_ref[...], d_ffn_ref[...]).astype(BF)


def back_hidden_kernel(
    d_ffn_ref, slope_ref, normed_b_ref, down_ref, up0_ref, up1_ref,
    g_up_ref, partial_ref, sums_ref, d_pre_ref,
):
    hidden = slope_ref.shape[1]
    step = 256
    for place in range(0, hidden, step):
        d_act = dot_nt(d_ffn_ref[...], down_ref[place : place + step, :])
        d_pre = (d_act * slope_ref[:, place : place + step].astype(F32)).astype(BF)
        d_pre_ref[:, place : place + step] = d_pre
        sums_ref[:, place : place + step] = jnp.sum(d_pre.astype(F32), axis=0, keepdims=True)
    g_up_ref[...] = dot_tn(normed_b_ref[...], d_pre_ref[...]).astype(BF)
    width = up0_ref.shape[1]
    set_both(
        partial_ref,
        dot_nt(d_pre_ref[:, :width], up0_ref[...]) + dot_nt(d_pre_ref[:, width:], up1_ref[...]),
    )


def back_first(
    d_second_ref, both_ref, sum_ref, vec_ref, d_first_ref, dbranch_ref, sums_ref
):
    sums_ref[...] = jnp.zeros_like(sums_ref)

    def chunk_step(chunk, carry):
        rows = pl.ds(pl.multiple_of(chunk * SHORT, SHORT), SHORT)
        upstream = d_second_ref[rows, :] + pair_rows(both_ref, rows)
        d_first, d_gain, d_shift = norm_back(upstream, sum_ref[rows, :], vec_ref[6:7, :])
        d_first_ref[rows, :] = d_first
        d_branch = d_first.astype(BF)
        dbranch_ref[rows, :] = d_branch
        sums_ref[0:1, :] += jnp.sum(d_branch.astype(F32), axis=0, keepdims=True)
        sums_ref[2:3, :] += d_shift
        sums_ref[4:5, :] += d_gain
        return carry

    lax.fori_loop(0, sum_ref.shape[0] // SHORT, chunk_step, 0)


def head_lanes(value, head):
    lane = lax.broadcasted_iota(jnp.int32, value.shape, 1)
    return (lane // (value.shape[1] // 2)) == head


def mask_row(kind, chunk, count):
    place = lax.broadcasted_iota(jnp.int32, (1, count), 1)
    allowed = (place // SHORT == chunk) | (kind == 1)
    return jnp.where(allowed, 0.0, MASKED_SCORE)


def attention_kernel(
    kind_ref, x_ref, wa_ref, wb_ref, bias_ref, wo_ref, partial_ref, qkv_ref, context_ref, lse_ref
):
    count = x_ref.shape[0]
    wide = wa_ref.shape[1]
    pair = 2 * HEAD_DIM
    kind = kind_ref[0]
    x = x_ref[...]
    bias = bias_ref[...]
    qkv_ref[:, :wide] = (dot(x, wa_ref[...]) + bias[:, :wide]).astype(BF)
    qkv_ref[:, wide:] = (dot(x, wb_ref[...]) + bias[:, wide:]).astype(BF)
    for p in range(HEADS // 4):
        keys = qkv_ref[:, (3 * p + 1) * pair : (3 * p + 2) * pair]
        values = qkv_ref[:, (3 * p + 2) * pair : (3 * p + 3) * pair]

        def chunk_step(chunk, carry):
            rows = pl.ds(pl.multiple_of(chunk * SHORT, SHORT), SHORT)
            queries = qkv_ref[rows, 3 * p * pair : (3 * p + 1) * pair] * jnp.asarray(0.125, BF)
            mask = mask_row(kind, chunk, count)
            found = []
            stats = lse_ref[rows, :] if p > 0 else jnp.zeros((SHORT, 128), F32)
            lane = lax.broadcasted_iota(jnp.int32, stats.shape, 1)
            for head in range(2):
                mine = jnp.where(head_lanes(queries, head), queries, jnp.zeros_like(queries))
                scores = dot_nt(mine, keys) + mask
                top = jnp.max(scores, axis=1, keepdims=True)
                powers = jnp.exp(scores - top)
                total = jnp.sum(powers, axis=1, keepdims=True)
                probs = powers * (1.0 / total)
                found.append(dot(probs.astype(BF), values))
                stats = jnp.where(lane == 2 * p + head, top + jnp.log(total), stats)
            lse_ref[rows, :] = stats
            both = jnp.where(head_lanes(found[0], 0), found[0], found[1])
            context_ref[rows, p * pair : (p + 1) * pair] = both.astype(BF)
            return carry

        lax.fori_loop(0, count // SHORT, chunk_step, 0)
    set_both(partial_ref, dot(context_ref[...], wo_ref[...]))


def attention_backward_kernel(
    kind_ref, d_second_ref, both_ref, sum_ref, vec_ref,
    x_ref, qkv_ref, context_ref, lse_ref, wa_ref, wb_ref, wo_ref,
    ga_ref, gb_ref, gout_ref, partial_ref, sums_ref, d_first_ref, norm_sums_ref,
    dbranch_ref, dcontext_ref, dqkv_ref, dk_ref, dv_ref,
):
    back_first(
        d_second_ref, both_ref, sum_ref, vec_ref, d_first_ref, dbranch_ref, norm_sums_ref
    )
    count = x_ref.shape[0]
    wide = wa_ref.shape[1]
    pair = 2 * HEAD_DIM
    kind = kind_ref[0]
    d_branch = dbranch_ref[...]
    dcontext_ref[...] = dot_nt(d_branch, wo_ref[...]).astype(BF)
    gout_ref[...] = dot_tn(context_ref[...], d_branch).astype(BF)
    for p in range(HEADS // 4):
        keys = qkv_ref[:, (3 * p + 1) * pair : (3 * p + 2) * pair]
        values = qkv_ref[:, (3 * p + 2) * pair : (3 * p + 3) * pair]
        dk_ref[...] = jnp.zeros_like(dk_ref)
        dv_ref[...] = jnp.zeros_like(dv_ref)

        def chunk_step(chunk, carry):
            rows = pl.ds(pl.multiple_of(chunk * SHORT, SHORT), SHORT)
            queries = qkv_ref[rows, 3 * p * pair : (3 * p + 1) * pair] * jnp.asarray(0.125, BF)
            d_context = dcontext_ref[rows, p * pair : (p + 1) * pair]
            mask = mask_row(kind, chunk, count)
            stats = lse_ref[rows, :]
            found = []
            for head in range(2):
                mine = jnp.where(head_lanes(queries, head), queries, jnp.zeros_like(queries))
                theirs = jnp.where(
                    head_lanes(d_context, head), d_context, jnp.zeros_like(d_context)
                )
                lse = stats[:, 2 * p + head : 2 * p + head + 1]
                probs = jnp.exp(dot_nt(mine, keys) + mask - lse)
                d_probs = dot_nt(theirs, values)
                row_dot = jnp.sum(d_probs * probs, axis=1, keepdims=True)
                d_scores = (probs * (d_probs - row_dot)).astype(BF)
                found.append(
                    (
                        dot(d_scores, keys) * 0.125,
                        dot_tn(d_scores, queries),
                        dot_tn(probs.astype(BF), d_context),
                    )
                )
            merged = [
                jnp.where(head_lanes(one, 0), one, other) for one, other in zip(*found)
            ]
            dqkv_ref[rows, 3 * p * pair : (3 * p + 1) * pair] = merged[0].astype(BF)
            dk_ref[...] += merged[1]
            dv_ref[...] += merged[2]
            return carry

        lax.fori_loop(0, count // SHORT, chunk_step, 0)
        dqkv_ref[:, (3 * p + 1) * pair : (3 * p + 2) * pair] = dk_ref[...].astype(BF)
        dqkv_ref[:, (3 * p + 2) * pair : (3 * p + 3) * pair] = dv_ref[...].astype(BF)
    d_a = dqkv_ref[:, :wide]
    d_b = dqkv_ref[:, wide:]
    x = x_ref[...]
    ga_ref[...] = dot_tn(x, d_a).astype(BF)
    gb_ref[...] = dot_tn(x, d_b).astype(BF)
    partial = dot_nt(d_a, wa_ref[...]) + dot_nt(d_b, wb_ref[...])
    if len(partial_ref.shape) == 3:
        set_both(partial_ref, partial)
    else:
        partial_ref[...] = partial.astype(BF)
    sums_ref[:, :wide] = jnp.sum(d_a.astype(F32), axis=0, keepdims=True)
    sums_ref[:, wide:] = jnp.sum(d_b.astype(F32), axis=0, keepdims=True)


def kernel_call(body, shapes, scratch, *operands):
    in_vmem = pl.BlockSpec(memory_space=pltpu.VMEM)
    in_smem = pl.BlockSpec(memory_space=pltpu.SMEM)
    return pl.pallas_call(
        body,
        out_shape=shapes,
        in_specs=[in_smem if value.dtype == jnp.int32 else in_vmem for value in operands],
        out_specs=[in_vmem] * len(shapes),
        scratch_shapes=scratch,
        compiler_params=pltpu.CompilerParams(vmem_limit_bytes=VMEM_LIMIT),
        cost_estimate=pl.CostEstimate(flops=0, bytes_accessed=0, transcendentals=0),
    )(*operands)


def attention(row_kind, inputs_b, w_a, w_b, bias, w_out):
    count, width = inputs_b.shape
    half = w_out.shape[0]
    shapes = [
        jax.ShapeDtypeStruct((2, count, width), BF),
        jax.ShapeDtypeStruct((count, 3 * half), BF),
        jax.ShapeDtypeStruct((count, half), BF),
        jax.ShapeDtypeStruct((count, 128), F32),
    ]
    return kernel_call(
        attention_kernel, shapes, [], row_kind, inputs_b, w_a, w_b, bias, w_out
    )


def attention_backward(
    slots, row_kind, d_second, both, first_sum, vec, inputs_b, qkv, context, lse, w_a, w_b, w_out
):
    count, width = inputs_b.shape
    half = w_out.shape[0]
    shapes = [
        jax.ShapeDtypeStruct(w_a.shape, BF),
        jax.ShapeDtypeStruct(w_b.shape, BF),
        jax.ShapeDtypeStruct(w_out.shape, BF),
        jax.ShapeDtypeStruct((2, count, width) if slots else (count, width), BF),
        jax.ShapeDtypeStruct((1, 3 * half), F32),
        jax.ShapeDtypeStruct((count, width), F32),
        jax.ShapeDtypeStruct((8, width), F32),
    ]
    scratch = [
        pltpu.VMEM((count, width), BF),
        pltpu.VMEM((count, half), BF),
        pltpu.VMEM((count, 3 * half), BF),
        pltpu.VMEM((count, 2 * HEAD_DIM), F32),
        pltpu.VMEM((count, 2 * HEAD_DIM), F32),
    ]
    return kernel_call(
        attention_backward_kernel, shapes, scratch, row_kind, d_second, both, first_sum,
        vec, inputs_b, qkv, context, lse, w_a, w_b, w_out,
    )


def norm_rows(base, both, vec):
    shapes = [jax.ShapeDtypeStruct(base.shape, kind) for kind in (F32, F32, BF)]
    return kernel_call(norm_kernel, shapes, [], base, both, vec)


def hidden_layer(x, both, vec, bias, up0, up1, down):
    count, hidden = x.shape[0], down.shape[0]
    shapes = [jax.ShapeDtypeStruct(x.shape, kind) for kind in (F32, F32, BF)]
    shapes += [jax.ShapeDtypeStruct((count, hidden), BF)] * 2
    shapes.append(jax.ShapeDtypeStruct((2, *x.shape), BF))
    return kernel_call(
        hidden_kernel, shapes, [], x, both, vec, bias, up0, up1, down
    )


def back_second(upstream, total, vec, act):
    shapes = [
        jax.ShapeDtypeStruct(total.shape, F32),
        jax.ShapeDtypeStruct(total.shape, BF),
        jax.ShapeDtypeStruct((act.shape[1], total.shape[1]), BF),
        jax.ShapeDtypeStruct((8, total.shape[1]), F32),
    ]
    body = functools.partial(back_second_kernel, len(upstream) > 1)
    return kernel_call(body, shapes, [], *upstream, total, vec, act)


def back_hidden(d_ffn, slope, normed_b, down, up0, up1):
    count, hidden = slope.shape
    width = normed_b.shape[1]
    shapes = [
        jax.ShapeDtypeStruct((width, hidden), BF),
        jax.ShapeDtypeStruct((2, count, width), BF),
        jax.ShapeDtypeStruct((1, hidden), F32),
    ]
    scratch = [pltpu.VMEM((count, hidden), BF)]
    return kernel_call(
        back_hidden_kernel, shapes, scratch, d_ffn, slope, normed_b, down, up0, up1
    )


def hidden_order(width, hidden_rows):
    group = width // (2 * hidden_rows)
    target = jnp.arange(width)
    source = (
        (target % (width // 2)) // hidden_rows * (2 * hidden_rows)
        + target // (width // 2) * hidden_rows
        + target % hidden_rows
    )
    del group
    return jnp.arange(width)[:, None] == source[None, :]


def shards(tokens, row_kind, w_qkv, w_out, w_up, w_down, bias_vectors, gains, bias_up, cotangent):
    chips = Chips()
    sequence = Sequence()
    core = chips.core
    count = chips.count
    device = 2 * chips.chip + core
    row_type = row_kind[0]
    rows, width = w_out.shape[1:]
    hidden = w_up.shape[2]
    hidden_rows = w_down.shape[1]
    half = width // 2
    panels = hidden // 2 // width
    own = tokens.shape[0]
    order = hidden_order(width, hidden_rows)

    pairs = HEADS // 4
    lane = half // pairs
    plan = Plan()
    state = State()

    def ordered(mine, theirs):
        return jnp.where(core == 0, mine, theirs), jnp.where(core == 0, theirs, mine)

    def both(value):
        return jnp.concatenate(ordered(value, swap(value, 1)), axis=0)

    def pack_qkv():
        cols = w_qkv.reshape(LAYERS, rows, 3, 2, pairs, lane)

        def side(which):
            return jnp.swapaxes(pick(cols, which, 3), 2, 3).reshape(LAYERS, rows, 3 * half)

        feature = jnp.arange(width)[None, :] - rows * device == jnp.arange(rows)[:, None]
        unit = jnp.arange(hidden // 2)[None, :] - hidden_rows * chips.chip
        unit = unit == jnp.arange(hidden_rows)[:, None]
        table = jnp.concatenate([bias_vectors, gains], axis=1).reshape(LAYERS * 8, rows)
        table = dot(table, feature.astype(BF)).astype(BF)
        units = dot(bias_up, unit.astype(BF)).astype(BF)
        got = swap(side(1 - core), 1)
        table = table + swap(table, 1)
        cols = merge(side(core), got, core, 1)
        for layer in range(LAYERS):
            last = cols[layer, :, :, width:]
            vectors = [table[8 * layer : 8 * layer + 8]]
            vectors += [units[layer : layer + 1, i * width :][:, :width] for i in range(panels)]
            vectors.append(jnp.zeros((8 - panels, width), BF))
            state.gathers[ATTN, layer] = Gather(
                chips, sequence, DIRECT[layer],
                cols[layer, :, :, :width].reshape(2 * rows, width),
                jnp.concatenate(
                    [jnp.concatenate([last[0], last[1]], axis=1), w_out[layer], *vectors], axis=0
                ),
            )
        sequence.mark([state.gathers[ATTN, layer].piece for layer in range(LAYERS)])

    groups = hidden // width

    def pack_up():
        value = sequence.gate(w_up).reshape(LAYERS * rows, hidden)
        stacked = jnp.concatenate(
            [value[:, i * width : (i + 1) * width] for i in range(groups)], axis=0
        )
        stacked = dot(stacked, order.astype(BF)).astype(BF)
        mine, sent = ordered(stacked[:, :half], stacked[:, half:])
        first, second = ordered(mine, swap(sent, 1))
        for layer in range(LAYERS):
            parts = []
            for i in range(panels):
                for value in (first, second):
                    cut = [
                        value[((2 * i + j) * LAYERS + layer) * rows :][:rows] for j in range(2)
                    ]
                    parts.append(jnp.concatenate(cut, axis=1))
            state.gathers[FFN, layer] = Gather(
                chips, sequence, DIRECT[LAYERS + layer], jnp.concatenate(parts, axis=0),
                w_down[layer],
            )
        sequence.mark([state.gathers[FFN, layer].piece for layer in range(LAYERS)])

    def read_vectors(layer, table):
        table = jnp.sum(table.astype(F32), axis=0)
        vec = table[:8]
        bias_q, bias_v = (
            jnp.where(core == 0, vec[i : i + 1, :half], vec[i : i + 1, half:]) for i in range(2)
        )
        bias = []
        for p in range(pairs):
            cut = slice(p * lane, (p + 1) * lane)
            bias += [bias_q[:, cut], jnp.zeros((1, lane), F32), bias_v[:, cut]]
        state.vec[layer] = vec
        state.bias_qkv[layer] = jnp.concatenate(bias, axis=1)
        state.bias_up[layer] = jnp.concatenate(
            [table[8 + i : 9 + i] for i in range(panels)], axis=1
        )

    def gather_top():
        groups = [
            [2 * (top * chips.step + chip) + side for top in range(4)]
            for chip in range(chips.step)
            for side in range(2)
        ]
        bundles = [
            state.gathers[kind, layer] for layer in range(1, LAYERS) for kind in (ATTN, FFN)
        ]
        piece = jnp.concatenate([bundle.piece for bundle in bundles], axis=0)
        piece = sequence.gate(piece)
        sequence.mark(piece)
        held = lax.all_gather(piece, AXIS, axis=0, axis_index_groups=groups)
        place = 0
        for bundle in bundles:
            height = bundle.piece.shape[0]
            bundle.top_held = held[:, place : place + height]
            place += height

    def tokens_start():
        value = sequence.gate(tokens)
        state.x_b[0] = both(value)
        state.x[0] = state.x_b[0].astype(F32)

    def cotangent_start():
        value = sequence.gate(cotangent)
        state.upstream = (both(value),)

    def out_exchange(layer):
        first, second = state.gathers[ATTN, layer].finish()
        w_b = jnp.swapaxes(second[:, :rows].reshape(count, rows, 2, half), 1, 2)
        out_all = second[:, rows : 2 * rows].reshape(2, count // 2, rows, width)
        sent, w_b = pick(out_all, 1 - core, 0), w_b.reshape(width, half)
        read_vectors(layer, second[:, 2 * rows :])
        sequence.mark((sent, w_b, state.vec[layer]))
        full_out = merge(pick(out_all, core, 0), swap(sent, 1), core, 1).reshape(half, width)
        state.w_attn[layer] = (first.reshape(width, width), w_b, full_out)

    def hidden_weights(layer):
        first, second = state.gathers[FFN, layer].finish()
        state.w_hidden[layer] = (
            second.reshape(hidden // 2, width),
            *(
                first[:, 2 * rows * i : 2 * rows * (i + 1)].reshape(width, width)
                for i in range(panels)
            ),
        )

    def run_attention(layer):
        x_b, weights = sequence.gate((state.x_b[layer], state.w_attn[layer]))
        w_a, w_b, full_out = weights
        partial, *saved = attention(row_kind, x_b, w_a, w_b, state.bias_qkv[layer], full_out)
        sequence.mark(partial)
        state.w_attn[layer] = weights
        state.saved[layer] = (x_b, *saved)
        state.branch = pair_trade(partial)

    def run_hidden(layer):
        both_parts = sequence.gate(state.branch)
        down, up0, up1 = state.w_hidden[layer]
        first_sum, state.normed, *kept, partial = hidden_layer(
            state.x[layer], both_parts, state.vec[layer], state.bias_up[layer], up0, up1, down
        )
        sequence.mark(partial)
        state.first_sum[layer] = first_sum
        state.kept[layer] = kept
        state.branch = pair_trade(partial)

    def run_norm(layer):
        both_parts = sequence.gate(state.branch)
        second, x, x_b = norm_rows(state.normed, both_parts, state.vec[layer])
        state.second[layer], state.x[layer + 1], state.x_b[layer + 1] = second, x, x_b
        sequence.mark(second)

    def run_back_second(layer):
        upstream = sequence.gate(state.upstream)
        if layer < LAYERS - 1:
            upstream = (state.d_first, upstream)
        act = state.kept[layer][1]
        d_second, d_ffn, g_down, sums = back_second(
            upstream, state.second[layer], state.vec[layer], act
        )
        state.d_second, state.d_ffn = d_second, d_ffn
        state.sums2[layer] = sums
        bundle = state.scatters[FFN, layer]
        bundle.start(1, g_down.reshape(count, hidden_rows, width))
        sequence.mark((d_ffn, bundle.sent))

    def run_back_hidden(layer):
        d_ffn = sequence.gate(state.d_ffn)
        normed_b, _, slope = state.kept[layer]
        g_up, partial, units = back_hidden(d_ffn, slope, normed_b, *state.w_hidden[layer])
        bundle = state.scatters[FFN, layer]
        bundle.start(0, g_up.reshape(count, 2 * rows, hidden // 2))
        sequence.mark((partial, bundle.sent))
        state.units[layer] = units
        state.branch = pair_trade(partial)

    def run_back_attention(layer):
        both_parts = sequence.gate(state.branch)
        x_b, qkv, context, lse = state.saved[layer]
        g_a, g_b, g_out, partial, sums, state.d_first, state.sums1[layer] = attention_backward(
            layer > 0, row_kind, state.d_second, both_parts, state.first_sum[layer],
            state.vec[layer], x_b, qkv, context, lse, *state.w_attn[layer],
        )
        sequence.mark(partial)
        state.pair[layer] = jnp.concatenate(
            [
                jnp.concatenate(
                    [sums[:, (3 * p + t) * lane :][:, :lane] for p in range(pairs)], axis=1
                )
                for t in (0, 2)
            ],
            axis=0,
        )
        if layer == 0:
            partial = partial.reshape(2, own, width)
        state.upstream = pair_trade(partial)
        state.g_attn[layer] = (g_a, g_b, g_out)

    def sum_rows(layer):
        pair = state.pair[layer]
        nothing = jnp.zeros_like(pair)
        pair = jnp.concatenate(ordered(pair, nothing), axis=1)
        units = [state.units[layer][:, i * width :][:, :width] for i in range(panels)]
        small = jnp.concatenate([state.sums1[layer] + state.sums2[layer], pair, *units], axis=0)
        small = jnp.pad(small.astype(BF), ((0, 16 - small.shape[0]), (0, 0)))
        line = jnp.arange(16)[:, None]
        place = jnp.arange(width)[None, :]
        owner = jnp.where(
            line < 10, place // (2 * rows), ((line - 10) * width + place) // hidden_rows
        )
        mine = owner[None] == jnp.arange(count)[:, None, None]
        return jnp.where(mine, small[None], jnp.zeros((), BF))

    def back_terms(layer):
        g_a, g_b, g_out = sequence.gate(state.g_attn[layer])
        bundle = state.scatters[ATTN, layer]
        bundle.start(0, g_a.reshape(count, 2 * rows, width))
        first = bundle.sent
        out_pair = g_out.reshape(count // 2, 2, rows, width)
        out_got = swap(pick(out_pair, 1 - core, 1), 1)
        out = merge(pick(out_pair, core, 1), out_got, core, 0).reshape(count, rows, width)
        g_b = g_b.reshape(count, 2, rows, half)
        last = jnp.concatenate([g_b[:, 0], g_b[:, 1]], axis=2)
        bundle.start(1, jnp.concatenate([last, out, sum_rows(layer)], axis=1))
        sequence.mark((first, bundle.sent))

    def grad_end():
        parts = sequence.gate(state.upstream)
        d_first = lax.dynamic_slice_in_dim(state.d_first, core * own, own)
        state.grad_tokens = d_first + (parts[0].astype(F32) + parts[1].astype(F32))
        sequence.mark(state.grad_tokens)

    def mixed_end():
        value = sequence.gate(state.x_b[LAYERS])
        state.mixed = lax.dynamic_slice_in_dim(value, core * own, own)
        sequence.mark(state.mixed)

    def finish_hidden(layer):
        up, down = state.scatters[FFN, layer].finish()
        sides = [
            jnp.concatenate(
                [up[(2 * i + side) * rows :][:rows] for i in range(panels)], axis=1
            )
            for side in range(2)
        ]
        mine, sent = ordered(*sides)
        state.up_pair[layer] = (mine, swap(sent, 1))
        state.down[layer] = down

    def end_hidden(layer):
        first, second = ordered(*sequence.gate(state.up_pair[layer]))
        stacked = jnp.concatenate(
            [
                jnp.concatenate(
                    [value[:, i * half : (i + 1) * half] for value in (first, second)], axis=1
                )
                for i in range(groups)
            ],
            axis=0,
        )
        stacked = lax.dot_general(
            stacked, order.astype(F32), (((1,), (1,)), ((), ())),
            precision=lax.Precision.HIGHEST, preferred_element_type=F32,
        )
        state.up[layer] = jnp.concatenate(
            [stacked[i * rows : (i + 1) * rows] for i in range(groups)], axis=1
        )
        sequence.mark(state.up[layer])

    def finish_attention(layer):
        first, rest = state.scatters[ATTN, layer].finish()
        sides = [
            jnp.concatenate(
                [
                    first[side * rows : (side + 1) * rows],
                    rest[:rows, side * half : (side + 1) * half],
                ],
                axis=1,
            )
            for side in range(2)
        ]
        mine, sent = ordered(*sides)
        small = rest[2 * rows :]
        pair = jnp.pad(small[8:], ((0, 0), (0, mine.shape[1] - width)))
        sent = jnp.concatenate([sent, pair], axis=0)
        state.qkv_pair[layer] = (mine, swap(sent, 1))
        state.out[layer] = rest[rows : 2 * rows]
        state.small_rows[layer] = small

    def end_attention(layer):
        mine, theirs = sequence.gate(state.qkv_pair[layer])
        small = state.small_rows[layer]
        small = jnp.concatenate([theirs[rows : rows + 2, :width] + small[8:10], small], axis=0)
        features = lax.dynamic_slice_in_dim(small, rows * device, rows, axis=1)
        per_row = width // hidden_rows
        units = lax.dynamic_slice(
            small,
            (12 + chips.chip // per_row, hidden_rows * (chips.chip % per_row)),
            (1, hidden_rows),
        )
        state.vectors[layer] = features[:6]
        state.gains[layer] = features[6:8]
        state.unit_sums[layer] = units[0]
        values = ordered(mine, theirs[:rows])
        state.qkv[layer] = jnp.concatenate(
            [
                value[:, (3 * p + t) * lane :][:, :lane]
                for t in range(3)
                for value in values
                for p in range(pairs)
            ],
            axis=1,
        )
        sequence.mark(state.qkv[layer])

    def call(function, *args):
        return lambda: function(*args)

    low = len(chips.low)
    size = (1.0, 2.0)
    add = plan.add

    def pair_send(label):
        return [(label, (("p", 0.0),), 1)]

    def trade_send(label):
        return [(label, (("p", 0.0),), 0)]

    def plane(length):
        return (("x", length), ("y", length))

    add("pq", 0, 6.0, [], pack_qkv)
    add("pu", 2, 3.0, [("g", ATTN, 0)], pack_up)
    add("gt", 3, 1.5, ["pu"], gather_top, [("top", (("sc", 65.0),), 0)])
    add("tok", 8, 0.5, ["pu"], tokens_start, pair_send("x0"))
    add("cot", 9, 0.5, [("m", 1, 0)], cotangent_start, pair_send("ct"))
    bundles = [(ATTN, 0), (FFN, 0), (ATTN, 1), (FFN, 1)]
    for rank, (kind, layer) in enumerate(bundles):
        needs = ["pq" if kind == ATTN else "pu"]

        def start(kind=kind, layer=layer):
            state.gathers[kind, layer].start()

        def advance(kind=kind, layer=layer):
            state.gathers[kind, layer].advance()

        def begin(kind=kind, layer=layer):
            state.gathers[kind, layer].begin(state.gathers[kind, layer].top_held)

        parts = (1.0, 4.0 / 3) if kind == ATTN else (2.0, 2.0)
        z = UNIT * 2 * sum(parts)
        if layer > 0:
            need = "top"
            first_step = call(begin, kind, layer)
        elif DIRECT[LAYERS * kind + layer]:
            need = ("z", kind, layer)
            links = (("z", 1.5 * z), ("w", 2 * z))
            add(("g", kind, layer), 1 + rank, 5.0, needs, start, [(need, links, 3)])
            first_step = advance
        else:
            need = ("y", kind, layer)
            links = (("z", 0.5 * z), ("w", z))
            add(("g", kind, layer), 1 + rank, 3.0, needs, start, [(need, links, 1)])
            sent = ("z", kind, layer)
            add(("h", kind, layer), 1 + rank, 2.2, [need], advance, [(sent, (("z", z),), 1)])
            need = sent
            first_step = advance
        length = UNIT * 4
        for step in range(low):
            sent = ("xy", kind, layer, step)
            links = (("x", length * parts[step % 2]), ("y", length * parts[1 - step % 2]))
            add(
                ("gs", kind, layer, step), 1 + rank, 5.0 + 0.5 * kind, [need],
                first_step if step == 0 else advance, [(sent, links, 2)],
            )
            need = sent
            length *= 2
        if kind == ATTN:
            add(
                ("go", layer), 1 + rank, 5.0, [need], call(out_exchange, layer),
                pair_send(("w", kind, layer)),
            )
        else:
            add(("w", kind, layer), 1 + rank, 3.5, [need], call(hidden_weights, layer))
    need = "x0"
    for layer in range(LAYERS):
        add(
            ("m", 0, layer), 10, 12.7, [need, ("w", ATTN, layer)],
            call(run_attention, layer), trade_send(("p", 0, layer)),
        )
        add(
            ("m", 1, layer), 10, 6.0, [("p", 0, layer), ("w", FFN, layer)],
            call(run_hidden, layer), trade_send(("p", 1, layer)),
        )
        need = ("m", 2, layer)
        add(need, 10, 3.0, [("p", 1, layer)], call(run_norm, layer))
    add("mix", 20, 1.0, [need], mixed_end)

    needs = [need, "ct"]
    for layer in reversed(range(LAYERS)):
        state.scatters[FFN, layer] = Scatter(chips, sequence)
        state.scatters[ATTN, layer] = Scatter(chips, sequence)
        add(
            ("b", 0, layer), 10, 5.0, needs, call(run_back_second, layer),
            [(("r", FFN, layer, 0), (("x", UNIT * 16),), 1)],
        )
        add(
            ("b", 1, layer), 10, 6.5, [("b", 0, layer)], call(run_back_hidden, layer),
            [(("r", FFN, layer, 1), (("y", UNIT * 16),), 1)] + trade_send(("p", 2, layer)),
        )
        add(
            ("b", 2, layer), 10, 17.2, [("p", 2, layer)], call(run_back_attention, layer),
            trade_send(("p", 3, layer)),
        )
        add(
            ("b", 3, layer), 9.5, 6.0, [("b", 2, layer)], call(back_terms, layer),
            [(("r", ATTN, layer, 0), (("x", UNIT * 8 * 4 / 3), ("y", UNIT * 8)), 2)],
        )
        needs = [("p", 3, layer)]
        for kind in (FFN, ATTN):
            need = [("r", kind, layer, part) for part in range(1 + kind)]
            rank = 1 + 2 * (LAYERS - 1 - layer) + (kind == ATTN)

            def reduce(kind=kind, layer=layer):
                state.scatters[kind, layer].advance()

            parts = (1.0, 4.0 / 3) if kind == ATTN else (2.0, 2.0)
            length = UNIT * 4
            for step in range(low - 1):
                sent = ("r", kind, layer, 2 + step)
                links = (("x", length * parts[step % 2]), ("y", length * parts[1 - step % 2]))
                add(
                    ("rs", kind, layer, step), rank, 5.5 + kind, need, reduce, [(sent, links, 2)]
                )
                need = [sent]
                length /= 2
            z = UNIT * 2 * sum(parts)
            sent = ("rz", kind, layer)
            add(("rs", kind, layer, low), rank, 4.0, need, reduce, [(sent, (("z", z),), 1)])
            need = sent
            links = (("z", 0.5 * z), ("w", z))
            sent = ("ry", kind, layer)
            add(("rs", kind, layer, low + 1), rank, 3.8, [need], reduce, [(sent, links, 1)])
            last = finish_hidden if kind == FFN else finish_attention
            add(
                ("rf", kind, layer), 19, 2.0, [sent], call(last, layer),
                pair_send(("re", kind, layer)),
            )
            last = end_hidden if kind == FFN else end_attention
            add(("ro", kind, layer), 20, 2.5, [("re", kind, layer)], call(last, layer))
    add("grad", 18, 1.2, needs, grad_end)
    plan.run()

    def stacked(values):
        return jnp.stack([values[layer] for layer in range(LAYERS)])

    return (
        state.mixed,
        state.grad_tokens,
        stacked(state.qkv),
        stacked(state.out),
        stacked(state.up),
        stacked(state.down),
        stacked(state.vectors),
        stacked(state.gains),
        stacked(state.unit_sums),
    )


def solution(mesh):
    placed = (
        P("fsdp", None),
        P("fsdp"),
        P(None, "fsdp", None),
        P(None, "fsdp", None),
        P(None, "fsdp", None),
        P(None, "fsdp", None),
        P(None, None, "fsdp"),
        P(None, None, "fsdp"),
        P(None, "fsdp"),
        P("fsdp", None),
    )
    return jax.shard_map(
        shards,
        mesh=mesh,
        in_specs=placed,
        out_specs=(
            P("fsdp", None),
            P("fsdp", None),
            P(None, "fsdp", None),
            P(None, "fsdp", None),
            P(None, "fsdp", None),
            P(None, "fsdp", None),
            P(None, None, "fsdp"),
            P(None, None, "fsdp"),
            P(None, "fsdp"),
        ),
        check_vma=False,
    )
```

```python
import functools

import jax
import jax.numpy as jnp
from jax import lax
from jax.experimental import pallas as pl
from jax.experimental.pallas import tpu as pltpu
from jax.sharding import PartitionSpec as P

HEADS = 12
HEAD_DIM = 64
LAYERS = 2
SHORT = 128
AXIS = "fsdp"

EPSILON = 1e-05
MASKED_SCORE = -1e30
BF = jnp.bfloat16
F32 = jnp.float32
LATENCY = 2.5
UNIT = 1.48
ATTN, FFN = 0, 1
OPEN_SENDS = 5
VMEM_LIMIT = 24 * 2**20
DIRECT = (False, False, False, False)
ORDER = (
    0, 4, 14, 5, 1, 2, 15, 6, 9, 16, 7, 19, 10, 17, 20, 11, 21, 12, 8, 18, 22, 24, 13, 25,
    26, 27, 23, 28, 3, 29, 31, 32, 33, 35, 45, 46, 34, 47, 49, 48, 36, 40, 50, 37, 54, 51,
    41, 30, 38, 55, 42, 52, 56, 39, 43, 53, 59, 57, 44, 58,
)


def dot(left, right):
    return jnp.dot(left, right, preferred_element_type=F32)


def dot_tn(left, right):
    return lax.dot_general(left, right, (((0,), (0,)), ((), ())), preferred_element_type=F32)


def dot_nt(left, right):
    return lax.dot_general(left, right, (((1,), (1,)), ((), ())), preferred_element_type=F32)


def swap(value, mask):
    pairs = [(source, source ^ mask) for source in range(lax.axis_size(AXIS))]
    return lax.ppermute(value, AXIS, pairs)


def merge(mine, theirs, bit, axis):
    first = jnp.where(bit == 0, mine, theirs)
    second = jnp.where(bit == 0, theirs, mine)
    return jnp.stack([first, second], axis=axis)


class Chips:
    def __init__(self):
        device = lax.axis_index(AXIS)
        self.count = lax.axis_size(AXIS) // 2
        self.core = device % 2
        self.chip = device // 2
        self.step = self.count // 4
        self.top = self.chip // self.step
        self.low = list(range(self.count.bit_length() - 3))

    def bit(self, place):
        return (self.chip // 2**place) % 2

    def plane_bit(self, step):
        return jnp.where(self.core == 0, self.bit(step), self.bit(len(self.low) - 1 - step))

    def plane_swap(self, value, step):
        masks = (2 * 2**step, 2 * 2 ** (len(self.low) - 1 - step))
        pairs = [(source, source ^ masks[source % 2]) for source in range(2 * self.count)]
        return lax.ppermute(value, AXIS, pairs)

    def plane_merge(self, mine, theirs, step):
        bit = self.plane_bit(step)
        outer = merge(mine, theirs, bit, 1).reshape((4, 2 ** (step + 1)) + mine.shape[2:])
        inner = merge(mine, theirs, bit, 2).reshape(outer.shape)
        return jnp.where(self.core == 0, outer, inner)

    def plane_half(self, value, step, own):
        bit = self.plane_bit(step)
        bit = bit if own else 1 - bit
        half = 2**step
        outer = pick(value.reshape((4, 2, half) + value.shape[2:]), bit, 1)
        inner = pick(value.reshape((4, half, 2) + value.shape[2:]), bit, 2)
        return jnp.where(self.core == 0, outer, inner)

def pick(pair, index, axis):
    return lax.dynamic_index_in_dim(pair, index, axis, keepdims=False)


def add_up(values):
    total = values[0].astype(F32)
    for value in values[1:]:
        total = total + value.astype(F32)
    return total


class Sequence:
    def __init__(self):
        self.last = None

    def gate(self, values):
        if self.last is None:
            return values
        values, _ = lax.optimization_barrier((values, self.last))
        return values

    def mark(self, values):
        self.last = values


class State:
    def __getattr__(self, name):
        value = {}
        setattr(self, name, value)
        return value


class Plan:
    def __init__(self):
        self.pieces = []

    def add(self, name, rank, cost, needs, run, sends=()):
        self.pieces.append((name, rank, cost, needs, run, sends))

    def greedy(self):
        now = 0.0
        ready = {}
        free = {}
        open_sends = {}
        waiting = list(range(len(self.pieces)))
        order = []

        def fits(piece):
            held = sum(weight for label, weight in open_sends.items() if label not in piece[3])
            added = sum(weight for _, _, weight in piece[5])
            return added == 0 or held + added <= OPEN_SENDS

        while waiting:
            known = []
            for place in waiting:
                piece = self.pieces[place]
                if all(need in ready for need in piece[3]):
                    time = max([ready[need] for need in piece[3]], default=0.0)
                    known.append((time, piece[1], place))
            known = [entry for entry in known if fits(self.pieces[entry[2]])] or known
            able = [entry[1:] for entry in known if entry[0] <= now]
            place = min(able)[1] if able else min(known)[2]
            name, _, cost, needs, _, sends = self.pieces[place]
            now = max([now] + [ready[need] for need in needs]) + cost
            ready[name] = now
            for need in needs:
                open_sends.pop(need, None)
            for label, links, weight in sends:
                ready[label] = 0.0
                for link, length in links:
                    free[link] = max(now, free.get(link, 0.0)) + length
                    ready[label] = max(ready[label], free[link] + LATENCY)
                if weight > 0:
                    open_sends[label] = weight
            waiting.remove(place)
            order.append(place)
        return order

    def run(self):
        order = ORDER if len(ORDER) == len(self.pieces) else self.greedy()
        for place in order:
            self.pieces[place][4]()


class Gather:
    def __init__(self, chips, sequence, direct, piece):
        self.chips, self.sequence = chips, sequence
        self.direct = direct
        self.piece = piece
        self.steps_done = 0
        self.held = None

    def start(self):
        self.piece = self.sequence.gate(self.piece)
        self.sequence.mark(self.piece)
        if self.direct:
            self.coming = [swap(self.piece, 2 * self.chips.step * k) for k in (1, 2, 3)]
            self.steps_done = 1
        else:
            self.coming = swap(self.piece, 2 * 2 * self.chips.step)

    def advance(self):
        chips = self.chips
        coming = self.sequence.gate(self.coming)
        step = self.steps_done
        self.steps_done += 1
        if step == 0:
            self.held = merge(self.piece, coming, chips.top // 2, 0)
            self.sequence.mark(self.held)
            self.coming = swap(self.held, 2 * chips.step)
            return
        if step == 1:
            if self.direct:
                parts = [self.piece] + coming
                parts = [merge(parts[i], parts[i + 1], chips.top % 2, 0) for i in (0, 2)]
                held = merge(parts[0], parts[1], chips.top // 2, 0)
            else:
                held = merge(self.held, coming, chips.top % 2, 1)
            self.held = held.reshape((4, 1) + self.piece.shape)
        else:
            self.held = chips.plane_merge(self.held, coming, step - 2)
        self.sequence.mark(self.held)
        self.coming = chips.plane_swap(self.held, step - 1)

    def finish(self, ranges):
        chips = self.chips
        while self.steps_done <= len(chips.low):
            self.advance()
        coming = self.sequence.gate(self.coming)
        results = []
        for start, stop in ranges:
            cut = [value[:, :, start:stop] for value in (self.held, coming)]
            whole = chips.plane_merge(*cut, self.steps_done - 2)
            results.append(whole.reshape((chips.count,) + whole.shape[2:]))
        self.sequence.mark(results)
        return results


class Scatter:
    def __init__(self, chips, sequence, count):
        self.chips, self.sequence = chips, sequence
        self.steps_done = 0
        self.addends = [None] * count
        self.coming = [None] * count

    def start(self, part, arrays):
        chips = self.chips
        step = len(chips.low) - 1
        shape = (4, 2 ** len(chips.low))
        arrays = [value.reshape(shape + value.shape[1:]) for value in arrays]
        sent = jnp.concatenate([chips.plane_half(value, step, False) for value in arrays], axis=2)
        self.addends[part] = [[chips.plane_half(value, step, True)] for value in arrays]
        self.coming[part] = chips.plane_swap(sent, step)
        self.sent = sent

    def total(self, cut):
        return jnp.concatenate(
            [add_up([cut(value) for value in values]) for values in self.arrays], axis=-2
        )

    def keep(self, cut, got):
        place = 0
        arrays = []
        for values in self.arrays:
            height = values[0].shape[-2]
            kept = [cut(value) for value in values]
            arrays.append(kept + [got[..., place : place + height, :]])
            place += height
        self.arrays = arrays

    def advance(self):
        chips = self.chips
        coming = self.sequence.gate(self.coming)
        if self.steps_done == 0:
            self.arrays = []
            for addends, got in zip(self.addends, coming):
                place = 0
                for values in addends:
                    height = values[0].shape[2]
                    self.arrays.append(values + [got[:, :, place : place + height]])
                    place += height
        else:
            self.keep(self.kept, coming)
        self.steps_done += 1
        step = len(chips.low) - 1 - self.steps_done
        if step >= 0:
            sent = self.total(lambda value: chips.plane_half(value, step, False)).astype(BF)
            self.kept = lambda value: chips.plane_half(value, step, True)
            self.coming = chips.plane_swap(sent, step)
        elif step == -1:
            bit = chips.top % 2

            def half(value, which):
                return pick(value.reshape((2, 2) + value.shape[2:]), which, 1)

            sent = self.total(lambda value: half(value, 1 - bit)).astype(BF)
            self.kept = lambda value: half(value, bit)
            self.coming = swap(sent, 2 * chips.step)
        else:
            bit = chips.top // 2
            sent = self.total(lambda value: pick(value, 1 - bit, 0)).astype(BF)
            self.kept = lambda value: pick(value, bit, 0)
            self.coming = swap(sent, 4 * chips.step)
        self.sequence.mark(sent)

    def finish(self):
        coming = self.sequence.gate(self.coming)
        self.keep(self.kept, coming)
        totals = [add_up(values) for values in self.arrays]
        self.sequence.mark(totals)
        return totals


ROOT_HALF = 0.7071067811865476
DENSITY = 0.3989422804014327


def unit_rows(values):
    centre = values - jnp.mean(values, axis=1, keepdims=True)
    scale = lax.rsqrt(jnp.mean(centre * centre, axis=1, keepdims=True) + EPSILON)
    return centre * scale, scale


def norm_kernel(base_ref, mine_ref, theirs_ref, vec_ref, sum_ref, out_ref, out_b_ref):
    def chunk_step(chunk, carry):
        rows = pl.ds(pl.multiple_of(chunk * SHORT, SHORT), SHORT)
        total = base_ref[rows, :] + (
            mine_ref[rows, :].astype(F32) + theirs_ref[rows, :].astype(F32)
        ) + vec_ref[3:4, :]
        sum_ref[rows, :] = total
        unit, _ = unit_rows(total)
        output = unit * vec_ref[7:8, :] + vec_ref[5:6, :]
        out_ref[rows, :] = output
        out_b_ref[rows, :] = output.astype(BF)
        return carry

    lax.fori_loop(0, base_ref.shape[0] // SHORT, chunk_step, 0)


def hidden_kernel(
    x_ref, mine_ref, theirs_ref, vec_ref, bias_ref, up0_ref, up1_ref, down_ref,
    sum_ref, normed_ref, normed_b_ref, act_ref, slope_ref, partial_ref,
):
    def chunk_step(chunk, carry):
        rows = pl.ds(pl.multiple_of(chunk * SHORT, SHORT), SHORT)
        total = x_ref[rows, :] + (
            mine_ref[rows, :].astype(F32) + theirs_ref[rows, :].astype(F32) + vec_ref[2:3, :]
        )
        sum_ref[rows, :] = total
        unit, _ = unit_rows(total)
        normed = unit * vec_ref[6:7, :] + vec_ref[4:5, :]
        normed_ref[rows, :] = normed
        normed_b_ref[rows, :] = normed.astype(BF)
        return carry

    lax.fori_loop(0, x_ref.shape[0] // SHORT, chunk_step, 0)
    width = up0_ref.shape[1]
    step = 256
    for panel, up_ref in enumerate((up0_ref, up1_ref)):
        for start in range(0, width, step):
            place = panel * width + start
            pre = dot(normed_b_ref[...], up_ref[:, start : start + step])
            pre = pre + bias_ref[:, place : place + step]
            share = 0.5 + 0.5 * lax.erf(pre * ROOT_HALF)
            slope = share + pre * (DENSITY * jnp.exp(pre * pre * -0.5))
            act_ref[:, place : place + step] = (pre * share).astype(BF)
            slope_ref[:, place : place + step] = slope.astype(BF)
    partial_ref[...] = dot(act_ref[...], down_ref[...]).astype(BF)


def norm_back(upstream, total, gain):
    unit, scale = unit_rows(total)
    scaled = upstream * gain
    first = jnp.mean(scaled, axis=1, keepdims=True)
    second = jnp.mean(scaled * unit, axis=1, keepdims=True)
    return (
        scale * (scaled - first - unit * second),
        jnp.sum(upstream * unit, axis=0, keepdims=True),
        jnp.sum(upstream, axis=0, keepdims=True),
    )


def back_second_kernel(has_base, *refs):
    base_refs, refs = refs[: 3 if has_base else 1], refs[3 if has_base else 1 :]
    sum_ref, vec_ref, act_ref, d_second_ref, d_ffn_ref, g_down_ref, sums_ref = refs
    sums_ref[...] = jnp.zeros_like(sums_ref)

    def chunk_step(chunk, carry):
        rows = pl.ds(pl.multiple_of(chunk * SHORT, SHORT), SHORT)
        upstream = base_refs[0][rows, :].astype(F32)
        if has_base:
            upstream = upstream + (
                base_refs[1][rows, :].astype(F32) + base_refs[2][rows, :].astype(F32)
            )
        d_second, d_gain, d_shift = norm_back(upstream, sum_ref[rows, :], vec_ref[7:8, :])
        d_second_ref[rows, :] = d_second
        d_ffn = d_second.astype(BF)
        d_ffn_ref[rows, :] = d_ffn
        sums_ref[1:2, :] += jnp.sum(d_ffn.astype(F32), axis=0, keepdims=True)
        sums_ref[3:4, :] += d_shift
        sums_ref[5:6, :] += d_gain
        return carry

    lax.fori_loop(0, sum_ref.shape[0] // SHORT, chunk_step, 0)
    g_down_ref[...] = dot_tn(act_ref[...], d_ffn_ref[...]).astype(BF)


def back_hidden_kernel(
    d_ffn_ref, slope_ref, normed_b_ref, down_ref, up0_ref, up1_ref,
    g_up0_ref, g_up1_ref, partial_ref, sums_ref, d_pre_ref,
):
    hidden = slope_ref.shape[1]
    step = 256
    for place in range(0, hidden, step):
        d_act = dot_nt(d_ffn_ref[...], down_ref[place : place + step, :])
        d_pre = (d_act * slope_ref[:, place : place + step].astype(F32)).astype(BF)
        d_pre_ref[:, place : place + step] = d_pre
        sums_ref[:, place : place + step] = jnp.sum(d_pre.astype(F32), axis=0, keepdims=True)
    width = up0_ref.shape[1]
    g_up0_ref[...] = dot_tn(normed_b_ref[...], d_pre_ref[:, :width]).astype(BF)
    g_up1_ref[...] = dot_tn(normed_b_ref[...], d_pre_ref[:, width:]).astype(BF)
    partial_ref[...] = (
        dot_nt(d_pre_ref[:, :width], up0_ref[...]) + dot_nt(d_pre_ref[:, width:], up1_ref[...])
    ).astype(BF)


def back_first(
    d_second_ref, mine_ref, theirs_ref, sum_ref, vec_ref, d_first_ref, dbranch_ref, sums_ref
):
    sums_ref[...] = jnp.zeros_like(sums_ref)

    def chunk_step(chunk, carry):
        rows = pl.ds(pl.multiple_of(chunk * SHORT, SHORT), SHORT)
        upstream = d_second_ref[rows, :] + (
            mine_ref[rows, :].astype(F32) + theirs_ref[rows, :].astype(F32)
        )
        d_first, d_gain, d_shift = norm_back(upstream, sum_ref[rows, :], vec_ref[6:7, :])
        d_first_ref[rows, :] = d_first
        d_branch = d_first.astype(BF)
        dbranch_ref[rows, :] = d_branch
        sums_ref[0:1, :] += jnp.sum(d_branch.astype(F32), axis=0, keepdims=True)
        sums_ref[2:3, :] += d_shift
        sums_ref[4:5, :] += d_gain
        return carry

    lax.fori_loop(0, sum_ref.shape[0] // SHORT, chunk_step, 0)


def head_lanes(value, head):
    lane = lax.broadcasted_iota(jnp.int32, value.shape, 1)
    return (lane // (value.shape[1] // 2)) == head


def mask_row(kind, chunk, count):
    place = lax.broadcasted_iota(jnp.int32, (1, count), 1)
    allowed = (place // SHORT == chunk) | (kind == 1)
    return jnp.where(allowed, 0.0, MASKED_SCORE)


def attention_kernel(
    kind_ref, x_ref, wa_ref, wb_ref, bias_ref, wo_ref, partial_ref, qkv_ref, context_ref, lse_ref
):
    count = x_ref.shape[0]
    wide = wa_ref.shape[1]
    pair = 2 * HEAD_DIM
    kind = kind_ref[0]
    x = x_ref[...]
    bias = bias_ref[...]
    qkv_ref[:, :wide] = (dot(x, wa_ref[...]) + bias[:, :wide]).astype(BF)
    qkv_ref[:, wide:] = (dot(x, wb_ref[...]) + bias[:, wide:]).astype(BF)
    for p in range(HEADS // 4):
        keys = qkv_ref[:, (3 * p + 1) * pair : (3 * p + 2) * pair]
        values = qkv_ref[:, (3 * p + 2) * pair : (3 * p + 3) * pair]

        def chunk_step(chunk, carry):
            rows = pl.ds(pl.multiple_of(chunk * SHORT, SHORT), SHORT)
            queries = qkv_ref[rows, 3 * p * pair : (3 * p + 1) * pair] * jnp.asarray(0.125, BF)
            mask = mask_row(kind, chunk, count)
            found = []
            stats = lse_ref[rows, :] if p > 0 else jnp.zeros((SHORT, 128), F32)
            lane = lax.broadcasted_iota(jnp.int32, stats.shape, 1)
            for head in range(2):
                mine = jnp.where(head_lanes(queries, head), queries, jnp.zeros_like(queries))
                scores = dot_nt(mine, keys) + mask
                top = jnp.max(scores, axis=1, keepdims=True)
                powers = jnp.exp(scores - top)
                total = jnp.sum(powers, axis=1, keepdims=True)
                probs = powers * (1.0 / total)
                found.append(dot(probs.astype(BF), values))
                stats = jnp.where(lane == 2 * p + head, top + jnp.log(total), stats)
            lse_ref[rows, :] = stats
            both = jnp.where(head_lanes(found[0], 0), found[0], found[1])
            context_ref[rows, p * pair : (p + 1) * pair] = both.astype(BF)
            return carry

        lax.fori_loop(0, count // SHORT, chunk_step, 0)
    partial_ref[...] = dot(context_ref[...], wo_ref[...]).astype(BF)


def attention_backward_kernel(
    kind_ref, d_second_ref, mine_ref, theirs_ref, sum_ref, vec_ref,
    x_ref, qkv_ref, context_ref, lse_ref, wa_ref, wb_ref, wo_ref,
    ga_ref, gb_ref, gout_ref, partial_ref, sums_ref, d_first_ref, norm_sums_ref,
    dbranch_ref, dcontext_ref, dqkv_ref, dk_ref, dv_ref,
):
    back_first(
        d_second_ref, mine_ref, theirs_ref, sum_ref, vec_ref,
        d_first_ref, dbranch_ref, norm_sums_ref,
    )
    count = x_ref.shape[0]
    wide = wa_ref.shape[1]
    pair = 2 * HEAD_DIM
    kind = kind_ref[0]
    d_branch = dbranch_ref[...]
    dcontext_ref[...] = dot_nt(d_branch, wo_ref[...]).astype(BF)
    gout_ref[...] = dot_tn(context_ref[...], d_branch).astype(BF)
    for p in range(HEADS // 4):
        keys = qkv_ref[:, (3 * p + 1) * pair : (3 * p + 2) * pair]
        values = qkv_ref[:, (3 * p + 2) * pair : (3 * p + 3) * pair]
        dk_ref[...] = jnp.zeros_like(dk_ref)
        dv_ref[...] = jnp.zeros_like(dv_ref)

        def chunk_step(chunk, carry):
            rows = pl.ds(pl.multiple_of(chunk * SHORT, SHORT), SHORT)
            queries = qkv_ref[rows, 3 * p * pair : (3 * p + 1) * pair] * jnp.asarray(0.125, BF)
            d_context = dcontext_ref[rows, p * pair : (p + 1) * pair]
            mask = mask_row(kind, chunk, count)
            stats = lse_ref[rows, :]
            found = []
            for head in range(2):
                mine = jnp.where(head_lanes(queries, head), queries, jnp.zeros_like(queries))
                theirs = jnp.where(
                    head_lanes(d_context, head), d_context, jnp.zeros_like(d_context)
                )
                lse = stats[:, 2 * p + head : 2 * p + head + 1]
                probs = jnp.exp(dot_nt(mine, keys) + mask - lse)
                d_probs = dot_nt(theirs, values)
                row_dot = jnp.sum(d_probs * probs, axis=1, keepdims=True)
                d_scores = (probs * (d_probs - row_dot)).astype(BF)
                found.append(
                    (
                        dot(d_scores, keys) * 0.125,
                        dot_tn(d_scores, queries),
                        dot_tn(probs.astype(BF), d_context),
                    )
                )
            merged = [
                jnp.where(head_lanes(one, 0), one, other) for one, other in zip(*found)
            ]
            dqkv_ref[rows, 3 * p * pair : (3 * p + 1) * pair] = merged[0].astype(BF)
            dk_ref[...] += merged[1]
            dv_ref[...] += merged[2]
            return carry

        lax.fori_loop(0, count // SHORT, chunk_step, 0)
        dqkv_ref[:, (3 * p + 1) * pair : (3 * p + 2) * pair] = dk_ref[...].astype(BF)
        dqkv_ref[:, (3 * p + 2) * pair : (3 * p + 3) * pair] = dv_ref[...].astype(BF)
    d_a = dqkv_ref[:, :wide]
    d_b = dqkv_ref[:, wide:]
    x = x_ref[...]
    ga_ref[...] = dot_tn(x, d_a).astype(BF)
    gb_ref[...] = dot_tn(x, d_b).astype(BF)
    partial_ref[...] = (dot_nt(d_a, wa_ref[...]) + dot_nt(d_b, wb_ref[...])).astype(BF)
    sums_ref[:, :wide] = jnp.sum(d_a.astype(F32), axis=0, keepdims=True)
    sums_ref[:, wide:] = jnp.sum(d_b.astype(F32), axis=0, keepdims=True)


def kernel_call(body, shapes, scratch, *operands):
    in_vmem = pl.BlockSpec(memory_space=pltpu.VMEM)
    in_smem = pl.BlockSpec(memory_space=pltpu.SMEM)
    return pl.pallas_call(
        body,
        out_shape=shapes,
        in_specs=[in_smem if value.dtype == jnp.int32 else in_vmem for value in operands],
        out_specs=[in_vmem] * len(shapes),
        scratch_shapes=scratch,
        compiler_params=pltpu.CompilerParams(vmem_limit_bytes=VMEM_LIMIT),
        cost_estimate=pl.CostEstimate(flops=0, bytes_accessed=0, transcendentals=0),
    )(*operands)


def attention(row_kind, inputs_b, w_a, w_b, bias, w_out):
    count, width = inputs_b.shape
    half = w_out.shape[0]
    shapes = [
        jax.ShapeDtypeStruct((count, width), BF),
        jax.ShapeDtypeStruct((count, 3 * half), BF),
        jax.ShapeDtypeStruct((count, half), BF),
        jax.ShapeDtypeStruct((count, 128), F32),
    ]
    return kernel_call(
        attention_kernel, shapes, [], row_kind, inputs_b, w_a, w_b, bias, w_out
    )


def attention_backward(
    row_kind, d_second, mine, theirs, first_sum, vec, inputs_b, qkv, context, lse, w_a, w_b, w_out
):
    count, width = inputs_b.shape
    half = w_out.shape[0]
    shapes = [
        jax.ShapeDtypeStruct(w_a.shape, BF),
        jax.ShapeDtypeStruct(w_b.shape, BF),
        jax.ShapeDtypeStruct(w_out.shape, BF),
        jax.ShapeDtypeStruct((count, width), BF),
        jax.ShapeDtypeStruct((1, 3 * half), F32),
        jax.ShapeDtypeStruct((count, width), F32),
        jax.ShapeDtypeStruct((8, width), F32),
    ]
    scratch = [
        pltpu.VMEM((count, width), BF),
        pltpu.VMEM((count, half), BF),
        pltpu.VMEM((count, 3 * half), BF),
        pltpu.VMEM((count, 2 * HEAD_DIM), F32),
        pltpu.VMEM((count, 2 * HEAD_DIM), F32),
    ]
    return kernel_call(
        attention_backward_kernel, shapes, scratch, row_kind, d_second, mine, theirs, first_sum,
        vec, inputs_b, qkv, context, lse, w_a, w_b, w_out,
    )


def norm_rows(base, mine, theirs, vec):
    shapes = [jax.ShapeDtypeStruct(base.shape, kind) for kind in (F32, F32, BF)]
    return kernel_call(norm_kernel, shapes, [], base, mine, theirs, vec)


def hidden_layer(x, mine, theirs, vec, bias, up0, up1, down):
    count, hidden = x.shape[0], down.shape[0]
    shapes = [jax.ShapeDtypeStruct(x.shape, kind) for kind in (F32, F32, BF)]
    shapes += [jax.ShapeDtypeStruct((count, hidden), BF)] * 2
    shapes.append(jax.ShapeDtypeStruct(x.shape, BF))
    return kernel_call(
        hidden_kernel, shapes, [], x, mine, theirs, vec, bias, up0, up1, down
    )


def back_second(upstream, total, vec, act):
    shapes = [
        jax.ShapeDtypeStruct(total.shape, F32),
        jax.ShapeDtypeStruct(total.shape, BF),
        jax.ShapeDtypeStruct((act.shape[1], total.shape[1]), BF),
        jax.ShapeDtypeStruct((8, total.shape[1]), F32),
    ]
    body = functools.partial(back_second_kernel, len(upstream) > 1)
    return kernel_call(body, shapes, [], *upstream, total, vec, act)


def back_hidden(d_ffn, slope, normed_b, down, up0, up1):
    count, hidden = slope.shape
    width = normed_b.shape[1]
    shapes = [
        jax.ShapeDtypeStruct(up0.shape, BF),
        jax.ShapeDtypeStruct(up1.shape, BF),
        jax.ShapeDtypeStruct((count, width), BF),
        jax.ShapeDtypeStruct((1, hidden), F32),
    ]
    scratch = [pltpu.VMEM((count, hidden), BF)]
    return kernel_call(
        back_hidden_kernel, shapes, scratch, d_ffn, slope, normed_b, down, up0, up1
    )


def hidden_order(width, hidden_rows):
    group = width // (2 * hidden_rows)
    target = jnp.arange(width)
    source = (
        (target % (width // 2)) // hidden_rows * (2 * hidden_rows)
        + target // (width // 2) * hidden_rows
        + target % hidden_rows
    )
    del group
    return jnp.arange(width)[:, None] == source[None, :]


def shards(tokens, row_kind, w_qkv, w_out, w_up, w_down, bias_vectors, gains, bias_up, cotangent):
    chips = Chips()
    sequence = Sequence()
    core = chips.core
    count = chips.count
    device = 2 * chips.chip + core
    row_type = row_kind[0]
    rows, width = w_out.shape[1:]
    hidden = w_up.shape[2]
    hidden_rows = w_down.shape[1]
    half = width // 2
    panels = hidden // 2 // width
    own = tokens.shape[0]
    order = hidden_order(width, hidden_rows)

    pairs = HEADS // 4
    lane = half // pairs
    plan = Plan()
    state = State()

    def ordered(mine, theirs):
        return jnp.where(core == 0, mine, theirs), jnp.where(core == 0, theirs, mine)

    def both(value):
        return jnp.concatenate(ordered(value, swap(value, 1)), axis=0)

    def pack_qkv():
        cols = w_qkv.reshape(LAYERS, rows, 3, 2, pairs, lane)

        def side(which):
            return jnp.swapaxes(pick(cols, which, 3), 2, 3).reshape(LAYERS, rows, 3 * half)

        feature = jnp.arange(width)[None, :] - rows * device == jnp.arange(rows)[:, None]
        unit = jnp.arange(hidden // 2)[None, :] - hidden_rows * chips.chip
        unit = unit == jnp.arange(hidden_rows)[:, None]
        table = jnp.concatenate([bias_vectors, gains], axis=1).reshape(LAYERS * 8, rows)
        table = dot(table, feature.astype(BF)).astype(BF)
        units = dot(bias_up, unit.astype(BF)).astype(BF)
        got = swap(side(1 - core), 1)
        table = table + swap(table, 1)
        cols = merge(side(core), got, core, 1)
        for layer in range(LAYERS):
            last = cols[layer, :, :, width:]
            vectors = [table[8 * layer : 8 * layer + 8]]
            vectors += [units[layer : layer + 1, i * width :][:, :width] for i in range(panels)]
            vectors.append(jnp.zeros((8 - panels, width), BF))
            state.gathers[ATTN, layer] = Gather(
                chips, sequence, DIRECT[layer],
                jnp.concatenate(
                    [
                        cols[layer, :, :, :width].reshape(2 * rows, width),
                        jnp.concatenate([last[0], last[1]], axis=1),
                        w_out[layer],
                        *vectors,
                    ],
                    axis=0,
                ),
            )
        sequence.mark([state.gathers[ATTN, layer].piece for layer in range(LAYERS)])

    groups = hidden // width

    def pack_up():
        value = sequence.gate(w_up).reshape(LAYERS * rows, hidden)
        stacked = jnp.concatenate(
            [value[:, i * width : (i + 1) * width] for i in range(groups)], axis=0
        )
        stacked = dot(stacked, order.astype(BF)).astype(BF)
        mine, sent = ordered(stacked[:, :half], stacked[:, half:])
        first, second = ordered(mine, swap(sent, 1))
        for layer in range(LAYERS):
            parts = []
            for i in range(panels):
                for value in (first, second):
                    cut = [
                        value[((2 * i + j) * LAYERS + layer) * rows :][:rows] for j in range(2)
                    ]
                    parts.append(jnp.concatenate(cut, axis=1))
            state.gathers[FFN, layer] = Gather(
                chips, sequence, DIRECT[LAYERS + layer],
                jnp.concatenate(parts + [w_down[layer]], axis=0),
            )
        sequence.mark([state.gathers[FFN, layer].piece for layer in range(LAYERS)])

    def read_vectors(layer, table):
        table = jnp.sum(table.astype(F32), axis=0)
        vec = table[:8]
        bias_q, bias_v = (
            jnp.where(core == 0, vec[i : i + 1, :half], vec[i : i + 1, half:]) for i in range(2)
        )
        bias = []
        for p in range(pairs):
            cut = slice(p * lane, (p + 1) * lane)
            bias += [bias_q[:, cut], jnp.zeros((1, lane), F32), bias_v[:, cut]]
        state.vec[layer] = vec
        state.bias_qkv[layer] = jnp.concatenate(bias, axis=1)
        state.bias_up[layer] = jnp.concatenate(
            [table[8 + i : 9 + i] for i in range(panels)], axis=1
        )

    def tokens_start():
        value = sequence.gate(tokens)
        state.x_b[0] = both(value)
        state.x[0] = state.x_b[0].astype(F32)

    def cotangent_start():
        value = sequence.gate(cotangent)
        state.upstream = (both(value),)

    def out_exchange(layer):
        ends = [0, 2 * rows, 3 * rows, 4 * rows, 4 * rows + 16]
        first, last, out_all, table = state.gathers[ATTN, layer].finish(
            list(zip(ends[:-1], ends[1:]))
        )
        w_b = jnp.swapaxes(last.reshape(count, rows, 2, half), 1, 2)
        out_all = out_all.reshape(2, count // 2, rows, width)
        sent, w_b = pick(out_all, 1 - core, 0), w_b.reshape(width, half)
        read_vectors(layer, table)
        sequence.mark((sent, w_b, state.vec[layer]))
        full_out = merge(pick(out_all, core, 0), swap(sent, 1), core, 1).reshape(half, width)
        state.w_attn[layer] = (first.reshape(width, width), w_b, full_out)

    def hidden_weights(layer):
        ends = [2 * rows * i for i in range(panels + 1)]
        ends.append(ends[-1] + hidden_rows)
        *ups, down = state.gathers[FFN, layer].finish(list(zip(ends[:-1], ends[1:])))
        state.w_hidden[layer] = (
            down.reshape(hidden // 2, width), *(value.reshape(width, width) for value in ups)
        )

    def run_attention(layer):
        x_b, weights = sequence.gate((state.x_b[layer], state.w_attn[layer]))
        w_a, w_b, full_out = weights
        partial, *saved = attention(row_kind, x_b, w_a, w_b, state.bias_qkv[layer], full_out)
        sequence.mark(partial)
        state.w_attn[layer] = weights
        state.saved[layer] = (x_b, *saved)
        state.branch = (partial, swap(partial, 1))

    def run_hidden(layer):
        mine, theirs = sequence.gate(state.branch)
        down, up0, up1 = state.w_hidden[layer]
        first_sum, state.normed, *kept, partial = hidden_layer(
            state.x[layer], mine, theirs, state.vec[layer], state.bias_up[layer], up0, up1, down
        )
        sequence.mark(partial)
        state.first_sum[layer] = first_sum
        state.kept[layer] = kept
        state.branch = (partial, swap(partial, 1))

    def run_norm(layer):
        mine, theirs = sequence.gate(state.branch)
        second, x, x_b = norm_rows(state.normed, mine, theirs, state.vec[layer])
        state.second[layer], state.x[layer + 1], state.x_b[layer + 1] = second, x, x_b
        sequence.mark(second)

    def run_back_second(layer):
        upstream = sequence.gate(state.upstream)
        if layer < LAYERS - 1:
            upstream = (state.d_first, *upstream)
        act = state.kept[layer][1]
        d_second, d_ffn, g_down, sums = back_second(
            upstream, state.second[layer], state.vec[layer], act
        )
        state.d_second, state.d_ffn = d_second, d_ffn
        state.sums2[layer] = sums
        bundle = state.scatters[FFN, layer]
        bundle.start(0, [g_down.reshape(count, hidden_rows, width)])
        sequence.mark((d_ffn, bundle.sent))

    def run_back_hidden(layer):
        d_ffn = sequence.gate(state.d_ffn)
        normed_b, _, slope = state.kept[layer]
        *g_up, partial, units = back_hidden(d_ffn, slope, normed_b, *state.w_hidden[layer])
        bundle = state.scatters[FFN, layer]
        bundle.start(1, [value.reshape(count, 2 * rows, width) for value in g_up])
        sequence.mark((partial, bundle.sent))
        state.units[layer] = units
        state.branch = (partial, swap(partial, 1))

    def run_back_attention(layer):
        mine, theirs = sequence.gate(state.branch)
        x_b, qkv, context, lse = state.saved[layer]
        g_a, g_b, g_out, partial, sums, state.d_first, state.sums1[layer] = attention_backward(
            row_kind, state.d_second, mine, theirs, state.first_sum[layer], state.vec[layer],
            x_b, qkv, context, lse, *state.w_attn[layer],
        )
        sequence.mark(partial)
        state.pair[layer] = jnp.concatenate(
            [
                jnp.concatenate(
                    [sums[:, (3 * p + t) * lane :][:, :lane] for p in range(pairs)], axis=1
                )
                for t in (0, 2)
            ],
            axis=0,
        )
        if layer > 0:
            state.upstream = (partial, swap(partial, 1))
        else:
            mine, sent = ordered(partial[:own], partial[own:])
            state.upstream = (mine, swap(sent, 1))
        state.g_attn[layer] = (g_a, g_b, g_out)

    def sum_rows(layer):
        pair = state.pair[layer]
        nothing = jnp.zeros_like(pair)
        pair = jnp.concatenate(ordered(pair, nothing), axis=1)
        units = [state.units[layer][:, i * width :][:, :width] for i in range(panels)]
        small = jnp.concatenate([state.sums1[layer] + state.sums2[layer], pair, *units], axis=0)
        small = jnp.pad(small.astype(BF), ((0, 16 - small.shape[0]), (0, 0)))
        line = jnp.arange(16)[:, None]
        place = jnp.arange(width)[None, :]
        owner = jnp.where(
            line < 10, place // (2 * rows), ((line - 10) * width + place) // hidden_rows
        )
        mine = owner[None] == jnp.arange(count)[:, None, None]
        return jnp.where(mine, small[None], jnp.zeros((), BF))

    def back_terms(layer):
        g_a, g_b, g_out = sequence.gate(state.g_attn[layer])
        bundle = state.scatters[ATTN, layer]
        out_pair = g_out.reshape(count // 2, 2, rows, width)
        out_got = swap(pick(out_pair, 1 - core, 1), 1)
        out = merge(pick(out_pair, core, 1), out_got, core, 0).reshape(count, rows, width)
        g_b = g_b.reshape(count, 2, rows, half)
        last = jnp.concatenate([g_b[:, 0], g_b[:, 1]], axis=2)
        rest = jnp.concatenate([last, out, sum_rows(layer)], axis=1)
        rest = lax.optimization_barrier(rest)
        bundle.start(0, [g_a.reshape(count, 2 * rows, width), rest])
        sequence.mark(bundle.sent)

    def grad_end():
        mine, theirs = sequence.gate(state.upstream)
        d_first = lax.dynamic_slice_in_dim(state.d_first, core * own, own)
        state.grad_tokens = d_first + (mine.astype(F32) + theirs.astype(F32))
        sequence.mark(state.grad_tokens)

    def mixed_end():
        value = sequence.gate(state.x_b[LAYERS])
        state.mixed = lax.dynamic_slice_in_dim(value, core * own, own)
        sequence.mark(state.mixed)

    def finish_hidden(layer):
        down, *ups = state.scatters[FFN, layer].finish()
        sides = [
            jnp.concatenate([up[side * rows :][:rows] for up in ups], axis=1)
            for side in range(2)
        ]
        mine, sent = ordered(*sides)
        state.up_pair[layer] = (mine, swap(sent, 1))
        state.down[layer] = down

    def end_hidden(layer):
        first, second = ordered(*sequence.gate(state.up_pair[layer]))
        stacked = jnp.concatenate(
            [
                jnp.concatenate(
                    [value[:, i * half : (i + 1) * half] for value in (first, second)], axis=1
                )
                for i in range(groups)
            ],
            axis=0,
        )
        stacked = lax.dot_general(
            stacked, order.astype(F32), (((1,), (1,)), ((), ())),
            precision=lax.Precision.HIGHEST, preferred_element_type=F32,
        )
        state.up[layer] = jnp.concatenate(
            [stacked[i * rows : (i + 1) * rows] for i in range(groups)], axis=1
        )
        sequence.mark(state.up[layer])

    def finish_attention(layer):
        first, rest = state.scatters[ATTN, layer].finish()
        last, out, small = rest[:rows], rest[rows : 2 * rows], rest[2 * rows :]
        sides = [
            jnp.concatenate(
                [first[side * rows :][:rows], last[:, side * half :][:, :half]], axis=1
            )
            for side in range(2)
        ]
        mine, sent = ordered(*sides)
        pair = jnp.pad(small[8:], ((0, 0), (0, mine.shape[1] - width)))
        sent = jnp.concatenate([sent, pair], axis=0)
        state.qkv_pair[layer] = (mine, swap(sent, 1))
        state.out[layer] = out
        state.small_rows[layer] = small

    def end_attention(layer):
        mine, theirs = sequence.gate(state.qkv_pair[layer])
        small = state.small_rows[layer]
        small = jnp.concatenate([theirs[rows : rows + 2, :width] + small[8:10], small], axis=0)
        features = lax.dynamic_slice_in_dim(small, rows * device, rows, axis=1)
        per_row = width // hidden_rows
        units = lax.dynamic_slice(
            small,
            (12 + chips.chip // per_row, hidden_rows * (chips.chip % per_row)),
            (1, hidden_rows),
        )
        state.vectors[layer] = features[:6]
        state.gains[layer] = features[6:8]
        state.unit_sums[layer] = units[0]
        values = ordered(mine, theirs[:rows])
        state.qkv[layer] = jnp.concatenate(
            [
                value[:, (3 * p + t) * lane :][:, :lane]
                for t in range(3)
                for value in values
                for p in range(pairs)
            ],
            axis=1,
        )
        sequence.mark(state.qkv[layer])

    def call(function, *args):
        return lambda: function(*args)

    low = len(chips.low)
    size = (1.0, 2.0)
    add = plan.add

    def pair_send(label):
        return [(label, (("p", 0.0),), 1)]

    def plane(length):
        return (("x", length), ("y", length))

    add("pq", 0, 6.0, [], pack_qkv)
    add("pu", 2, 3.0, [("g", ATTN, 0)], pack_up)
    add("tok", 8, 0.5, ["pu"], tokens_start, pair_send("x0"))
    add("cot", 9, 0.5, [("m", 1, 0)], cotangent_start, pair_send("ct"))
    bundles = [(ATTN, 0), (FFN, 0), (ATTN, 1), (FFN, 1)]
    for rank, (kind, layer) in enumerate(bundles):
        needs = ["pq" if kind == ATTN else "pu"]

        def start(kind=kind, layer=layer):
            state.gathers[kind, layer].start()

        def advance(kind=kind, layer=layer):
            state.gathers[kind, layer].advance()

        units = 7.0 / 3 if kind == ATTN else 4.0
        z = UNIT * 2 * units
        if DIRECT[LAYERS * kind + layer]:
            need = ("z", kind, layer)
            links = (("z", 1.5 * z), ("w", 2 * z))
            add(("g", kind, layer), 1 + rank, 5.0, needs, start, [(need, links, 3)])
        else:
            need = ("y", kind, layer)
            links = (("z", 0.5 * z), ("w", z))
            add(("g", kind, layer), 1 + rank, 3.0, needs, start, [(need, links, 1)])
            sent = ("z", kind, layer)
            add(("h", kind, layer), 1 + rank, 2.2, [need], advance, [(sent, (("z", z),), 1)])
            need = sent
        length = UNIT * 2 * units
        for step in range(low):
            sent = ("xy", kind, layer, step)
            add(
                ("gs", kind, layer, step), 1 + rank, 3.0 + 0.5 * kind, [need], advance,
                [(sent, plane(length), 1)],
            )
            need = sent
            length *= 2
        if kind == ATTN:
            add(
                ("go", layer), 1 + rank, 5.0, [need], call(out_exchange, layer),
                pair_send(("w", kind, layer)),
            )
        else:
            add(("w", kind, layer), 1 + rank, 3.5, [need], call(hidden_weights, layer))
    need = "x0"
    for layer in range(LAYERS):
        add(
            ("m", 0, layer), 10, 12.7, [need, ("w", ATTN, layer)],
            call(run_attention, layer), pair_send(("p", 0, layer)),
        )
        add(
            ("m", 1, layer), 10, 6.0, [("p", 0, layer), ("w", FFN, layer)],
            call(run_hidden, layer), pair_send(("p", 1, layer)),
        )
        need = ("m", 2, layer)
        add(need, 10, 3.0, [("p", 1, layer)], call(run_norm, layer))
    add("mix", 20, 1.0, [need], mixed_end)

    needs = [need, "ct"]
    for layer in reversed(range(LAYERS)):
        state.scatters[FFN, layer] = Scatter(chips, sequence, 2)
        state.scatters[ATTN, layer] = Scatter(chips, sequence, 1)
        add(
            ("b", 0, layer), 10, 5.0, needs, call(run_back_second, layer),
            [(("r", FFN, layer, 0), plane(UNIT * 8), 1)],
        )
        add(
            ("b", 1, layer), 10, 6.5, [("b", 0, layer)], call(run_back_hidden, layer),
            [(("r", FFN, layer, 1), plane(UNIT * 8), 1)] + pair_send(("p", 2, layer)),
        )
        add(
            ("b", 2, layer), 10, 17.2, [("p", 2, layer)], call(run_back_attention, layer),
            pair_send(("p", 3, layer)),
        )
        add(
            ("b", 3, layer), 9.5, 6.0, [("b", 2, layer)], call(back_terms, layer),
            [(("r", ATTN, layer, 0), plane(UNIT * 28 / 3), 1)],
        )
        needs = [("p", 3, layer)]
        for kind in (FFN, ATTN):
            need = [("r", kind, layer, part) for part in range(1 + kind)]
            rank = 1 + 2 * (LAYERS - 1 - layer) + (kind == ATTN)

            def reduce(kind=kind, layer=layer):
                state.scatters[kind, layer].advance()

            units = 7.0 / 3 if kind == ATTN else 4.0
            length = UNIT * 2 * units
            for step in range(low - 1):
                sent = ("r", kind, layer, 2 + step)
                add(
                    ("rs", kind, layer, step), rank, 4.5 + kind, need, reduce,
                    [(sent, plane(length), 1)],
                )
                need = [sent]
                length /= 2
            z = UNIT * 2 * units
            sent = ("rz", kind, layer)
            add(("rs", kind, layer, low), rank, 4.0, need, reduce, [(sent, (("z", z),), 1)])
            need = sent
            links = (("z", 0.5 * z), ("w", z))
            sent = ("ry", kind, layer)
            add(("rs", kind, layer, low + 1), rank, 3.8, [need], reduce, [(sent, links, 1)])
            last = finish_hidden if kind == FFN else finish_attention
            add(
                ("rf", kind, layer), 19, 2.0, [sent], call(last, layer),
                pair_send(("re", kind, layer)),
            )
            last = end_hidden if kind == FFN else end_attention
            add(("ro", kind, layer), 20, 2.5, [("re", kind, layer)], call(last, layer))
    add("grad", 18, 1.2, needs, grad_end)
    plan.run()

    def stacked(values):
        return jnp.stack([values[layer] for layer in range(LAYERS)])

    return (
        state.mixed,
        state.grad_tokens,
        stacked(state.qkv),
        stacked(state.out),
        stacked(state.up),
        stacked(state.down),
        stacked(state.vectors),
        stacked(state.gains),
        stacked(state.unit_sums),
    )


def solution(mesh):
    placed = (
        P("fsdp", None),
        P("fsdp"),
        P(None, "fsdp", None),
        P(None, "fsdp", None),
        P(None, "fsdp", None),
        P(None, "fsdp", None),
        P(None, None, "fsdp"),
        P(None, None, "fsdp"),
        P(None, "fsdp"),
        P("fsdp", None),
    )
    return jax.shard_map(
        shards,
        mesh=mesh,
        in_specs=placed,
        out_specs=(
            P("fsdp", None),
            P("fsdp", None),
            P(None, "fsdp", None),
            P(None, "fsdp", None),
            P(None, "fsdp", None),
            P(None, "fsdp", None),
            P(None, None, "fsdp"),
            P(None, None, "fsdp"),
            P(None, "fsdp"),
        ),
        check_vma=False,
    )
```

```python
import functools

import jax
import jax.numpy as jnp
from jax import lax
from jax.experimental import pallas as pl
from jax.experimental.pallas import tpu as pltpu
from jax.sharding import PartitionSpec as P

HEADS = 12
HEAD_DIM = 64
LAYERS = 2
SHORT = 128
AXIS = "fsdp"

EPSILON = 1e-05
MASKED_SCORE = -1e30
BF = jnp.bfloat16
F32 = jnp.float32
LATENCY = 2.5
UNIT = 1.48
ATTN, FFN = 0, 1
OPEN_SENDS = 4
VMEM_LIMIT = 24 * 2**20
DIRECT = (False, False, False, False)
ORDER = (
    0, 16, 6, 1, 11, 17, 7, 18, 2, 21, 8, 12, 19, 9, 13, 3, 22, 20, 23, 10, 14, 24, 26,
    15, 27, 4, 28, 29, 25, 30, 5, 31, 33, 34, 35, 37, 36, 47, 32, 48, 38, 49, 39, 42, 51,
    43, 50, 52, 40, 44, 56, 53, 45, 57, 58, 54, 41, 55, 46, 59, 61, 60,
)


def dot(left, right):
    return jnp.dot(left, right, preferred_element_type=F32)


def dot_tn(left, right):
    return lax.dot_general(left, right, (((0,), (0,)), ((), ())), preferred_element_type=F32)


def dot_nt(left, right):
    return lax.dot_general(left, right, (((1,), (1,)), ((), ())), preferred_element_type=F32)


def swap(value, mask):
    pairs = [(source, source ^ mask) for source in range(lax.axis_size(AXIS))]
    return lax.ppermute(value, AXIS, pairs)


def merge(mine, theirs, bit, axis):
    first = jnp.where(bit == 0, mine, theirs)
    second = jnp.where(bit == 0, theirs, mine)
    return jnp.stack([first, second], axis=axis)


def pick(pair, index, axis):
    return lax.dynamic_index_in_dim(pair, index, axis, keepdims=False)


class Chips:
    def __init__(self):
        device = lax.axis_index(AXIS)
        self.count = lax.axis_size(AXIS) // 2
        self.core = device % 2
        self.chip = device // 2
        self.step = self.count // 4
        self.top = self.chip // self.step
        self.low = list(range(self.count.bit_length() - 3))

    def bit(self, place):
        return (self.chip // 2**place) % 2

    def plane_bit(self, step):
        return jnp.where(self.core == 0, self.bit(step), self.bit(len(self.low) - 1 - step))

    def plane_swap(self, value, step):
        masks = (2 * 2**step, 2 * 2 ** (len(self.low) - 1 - step))
        pairs = [(source, source ^ masks[source % 2]) for source in range(2 * self.count)]
        return lax.ppermute(value, AXIS, pairs)

    def half_places(self, step, own):
        bit = self.plane_bit(step)
        bit = bit if own else 1 - bit
        index = jnp.arange(2**step)
        return jnp.where(self.core == 0, 2**step * bit + index, 2 * index + bit)


class Sequence:
    def __init__(self):
        self.last = None

    def gate(self, values):
        if self.last is None:
            return values
        values, _ = lax.optimization_barrier((values, self.last))
        return values

    def mark(self, values):
        self.last = values


class State:
    def __getattr__(self, name):
        value = {}
        setattr(self, name, value)
        return value


class Plan:
    def __init__(self):
        self.pieces = []

    def add(self, name, rank, cost, needs, run, sends=()):
        self.pieces.append((name, rank, cost, needs, run, sends))

    def greedy(self):
        now = 0.0
        ready = {}
        free = {}
        open_sends = {}
        waiting = list(range(len(self.pieces)))
        order = []

        def fits(piece):
            held = sum(weight for label, weight in open_sends.items() if label not in piece[3])
            added = sum(weight for _, _, weight in piece[5])
            return added == 0 or held + added <= OPEN_SENDS

        while waiting:
            known = []
            for place in waiting:
                piece = self.pieces[place]
                if all(need in ready for need in piece[3]):
                    time = max([ready[need] for need in piece[3]], default=0.0)
                    known.append((time, piece[1], place))
            known = [entry for entry in known if fits(self.pieces[entry[2]])] or known
            able = [entry[1:] for entry in known if entry[0] <= now]
            place = min(able)[1] if able else min(known)[2]
            name, _, cost, needs, _, sends = self.pieces[place]
            now = max([now] + [ready[need] for need in needs]) + cost
            ready[name] = now
            for need in needs:
                open_sends.pop(need, None)
            for label, links, weight in sends:
                ready[label] = 0.0
                for link, length in links:
                    free[link] = max(now, free.get(link, 0.0)) + length
                    ready[label] = max(ready[label], free[link] + LATENCY)
                if weight > 0:
                    open_sends[label] = weight
            waiting.remove(place)
            order.append(place)
        return order

    def run(self):
        order = ORDER if len(ORDER) == len(self.pieces) else self.greedy()
        for place in order:
            self.pieces[place][4]()


class Gather:
    def __init__(self, chips, sequence, direct, piece):
        self.chips, self.sequence = chips, sequence
        self.direct = direct
        self.piece = piece
        self.steps_done = 0
        self.held = None

    def start(self):
        self.piece = self.sequence.gate(self.piece)
        self.sequence.mark(self.piece)
        if self.direct:
            self.coming = [swap(self.piece, 2 * self.chips.step * k) for k in (1, 2, 3)]
            self.steps_done = 1
        else:
            self.coming = swap(self.piece, 2 * 2 * self.chips.step)

    def advance(self):
        chips = self.chips
        coming = self.sequence.gate(self.coming)
        step = self.steps_done
        self.steps_done += 1
        if step == 0:
            self.held = merge_rows(self.piece[None, None], coming[None, None], chips.top // 2, 0)
            self.held = self.held.reshape((2,) + self.piece.shape)
            self.sequence.mark(self.held)
            self.coming = swap(self.held, 2 * chips.step)
            return
        if step == 1:
            if self.direct:
                parts = [self.piece] + coming
                parts = [merge(parts[i], parts[i + 1], chips.top % 2, 0) for i in (0, 2)]
                held = merge(parts[0], parts[1], chips.top // 2, 0)
            else:
                held = merge_rows(self.held[:, None], coming[:, None], chips.top % 2, 0)
            self.held = held.reshape((4, 1) + self.piece.shape)
        else:
            bit = chips.plane_bit(step - 2)
            self.held = merge_rows(self.held, coming, bit, chips.core)
        self.sequence.mark(self.held)
        self.coming = chips.plane_swap(self.held, step - 1)

    def finish(self, ranges):
        chips = self.chips
        while self.steps_done <= len(chips.low):
            self.advance()
        coming = self.sequence.gate(self.coming)
        bit = chips.plane_bit(self.steps_done - 2)
        results = merge_rows(self.held, coming, bit, chips.core, ranges)
        results = [whole.reshape((chips.count,) + whole.shape[2:]) for whole in results]
        self.sequence.mark(results)
        return results


def merge_kernel(ranges, place_ref, mine_ref, theirs_ref, *out_refs):
    half = mine_ref.shape[1]
    for lead in range(mine_ref.shape[0]):
        for index in range(half):
            for (start, stop), out_ref in zip(ranges, out_refs):
                out_ref[lead, place_ref[index]] = mine_ref[lead, index, start:stop]
                out_ref[lead, place_ref[half + index]] = theirs_ref[lead, index, start:stop]


def merge_rows(mine, theirs, bit, inner, ranges=None):
    half = mine.shape[1]
    cuts = ranges or [(0, mine.shape[2])]
    if all(edge % 16 == 0 for cut in cuts for edge in cut):
        index = jnp.arange(half)

        def place(own):
            return jnp.where(inner == 1, 2 * index + own, half * own + index)

        places = jnp.concatenate([place(bit), place(1 - bit)]).astype(jnp.int32)
        shapes = [
            jax.ShapeDtypeStruct((mine.shape[0], 2 * half, stop - start, mine.shape[3]), BF)
            for start, stop in cuts
        ]
        results = kernel_call(
            functools.partial(merge_kernel, cuts), shapes, [], places, mine, theirs
        )
    else:
        results = []
        for start, stop in cuts:
            cut = [value[:, :, start:stop] for value in (mine, theirs)]
            outer = merge(*cut, bit, 1)
            outer = outer.reshape((mine.shape[0], 2 * half) + outer.shape[3:])
            results.append(
                jnp.where(inner == 1, merge(*cut, bit, 2).reshape(outer.shape), outer)
            )
    return results if ranges else results[0]


class Scatter:
    def __init__(self, chips, sequence, count):
        self.chips, self.sequence = chips, sequence
        self.steps_done = 0
        self.arrays = [None] * count
        self.coming = [None] * count

    def start(self, part, arrays):
        chips = self.chips
        step = len(chips.low) - 1
        shape = (4, 2 ** len(chips.low))
        arrays = [value.reshape(shape + value.shape[1:]) for value in arrays]
        self.arrays[part] = arrays
        sent = send_rows(arrays, chips.half_places(step, False))
        self.coming[part] = chips.plane_swap(sent, step)
        self.sent = sent

    def advance(self):
        chips = self.chips
        coming = self.sequence.gate(self.coming)
        self.steps_done += 1
        step = len(chips.low) - 1 - self.steps_done
        if self.steps_done == 1:
            self.heights = [value.shape[2] for part in self.arrays for value in part]
            kept = chips.half_places(step + 1, True)
        else:
            self.arrays, coming = [[self.kept]], [coming]
            kept = jnp.arange(self.kept.shape[1])
        if step >= 0:
            sides = [chips.half_places(step, own) for own in (False, True)]
        else:
            bit = chips.top % 2 if step == -1 else chips.top // 2
            sides = [jnp.reshape(1 - bit, (1,)), jnp.reshape(bit, (1,))]
            lead = 2 if step == -1 else 1
            self.arrays = [
                [value.reshape((lead, 2) + value.shape[-2:]) for value in part]
                for part in self.arrays
            ]
            coming = [got.reshape((lead, 2) + got.shape[-2:]) for got in coming]
            kept = jnp.arange(2)
        sent, self.kept = fold_rows(self.arrays, coming, kept, sides)
        self.sequence.mark(sent)
        if step >= 0:
            self.coming = chips.plane_swap(sent, step)
        else:
            self.coming = swap(sent, 2 * chips.step if step == -1 else 4 * chips.step)

    def finish(self):
        coming = self.sequence.gate(self.coming)
        total = self.kept[0, 0] + coming[0, 0].astype(F32)
        self.sequence.mark(total)
        ends = [sum(self.heights[:i]) for i in range(len(self.heights) + 1)]
        return [total[start:stop] for start, stop in zip(ends[:-1], ends[1:])]


def send_kernel(heights, place_ref, *refs):
    *array_refs, sent_ref = refs
    for lead in range(sent_ref.shape[0]):
        for index in range(sent_ref.shape[1]):
            row = 0
            for height, ref in zip(heights, array_refs):
                sent_ref[lead, index, row : row + height] = ref[lead, place_ref[index]]
                row += height


def send_rows(arrays, places):
    heights = [value.shape[2] for value in arrays]
    shape = (arrays[0].shape[0], places.shape[0], sum(heights), arrays[0].shape[3])
    if any(height % 16 for height in heights):
        return jnp.concatenate([jnp.take(value, places, axis=1) for value in arrays], axis=2)
    (sent,) = kernel_call(
        functools.partial(send_kernel, heights), [jax.ShapeDtypeStruct(shape, BF)], [],
        places.astype(jnp.int32), *arrays,
    )
    return sent


def fold_kernel(layout, place_ref, *refs):
    *refs, sent_ref, kept_ref = refs
    count = sent_ref.shape[1]
    for lead in range(sent_ref.shape[0]):
        for index in range(count):
            for array, got, start, height, row in layout:
                for side, out_ref in enumerate((sent_ref, kept_ref)):
                    place = 2 * (count * side + index)
                    mine = refs[array][lead, place_ref[place]]
                    theirs = refs[got][lead, place_ref[place + 1], start : start + height]
                    total = mine.astype(F32) + theirs.astype(F32)
                    out_ref[lead, index, row : row + height] = total.astype(out_ref.dtype)


def fold_rows(parts, coming, kept, sides):
    arrays = [value for part in parts for value in part]
    layout = []
    row = 0
    for part, got in zip(range(len(parts)), range(len(arrays), len(arrays) + len(coming))):
        start = 0
        for value in parts[part]:
            height = value.shape[2]
            layout.append((len(layout), got, start, height, row))
            start += height
            row += height
    shape = (arrays[0].shape[0], sides[0].shape[0], row, arrays[0].shape[3])
    if any(value.shape[2] % 16 for value in arrays):
        totals = []
        for array, got, start, height, _ in layout:
            theirs = coming[got - len(arrays)][:, :, start : start + height]
            totals.append(jnp.take(arrays[array], kept, axis=1).astype(F32) + theirs.astype(F32))
        total = jnp.concatenate(totals, axis=2)
        return [jnp.take(total, side, axis=1).astype(kind) for side, kind in zip(sides, (BF, F32))]
    places = [jnp.stack([jnp.take(kept, side), side], axis=1).reshape(-1) for side in sides]
    return kernel_call(
        functools.partial(fold_kernel, layout),
        [jax.ShapeDtypeStruct(shape, kind) for kind in (BF, F32)], [],
        jnp.concatenate(places).astype(jnp.int32), *arrays, *coming,
    )


ROOT_HALF = 0.7071067811865476
DENSITY = 0.3989422804014327


def unit_rows(values):
    centre = values - jnp.mean(values, axis=1, keepdims=True)
    scale = lax.rsqrt(jnp.mean(centre * centre, axis=1, keepdims=True) + EPSILON)
    return centre * scale, scale


def norm_kernel(base_ref, mine_ref, theirs_ref, vec_ref, sum_ref, out_ref, out_b_ref):
    def chunk_step(chunk, carry):
        rows = pl.ds(pl.multiple_of(chunk * SHORT, SHORT), SHORT)
        total = base_ref[rows, :] + (
            mine_ref[rows, :].astype(F32) + theirs_ref[rows, :].astype(F32)
        ) + vec_ref[3:4, :]
        sum_ref[rows, :] = total
        unit, _ = unit_rows(total)
        output = unit * vec_ref[7:8, :] + vec_ref[5:6, :]
        out_ref[rows, :] = output
        out_b_ref[rows, :] = output.astype(BF)
        return carry

    lax.fori_loop(0, base_ref.shape[0] // SHORT, chunk_step, 0)


def hidden_kernel(
    x_ref, mine_ref, theirs_ref, vec_ref, bias_ref, up0_ref, up1_ref, down_ref,
    sum_ref, normed_ref, normed_b_ref, act_ref, slope_ref, partial_ref,
):
    def chunk_step(chunk, carry):
        rows = pl.ds(pl.multiple_of(chunk * SHORT, SHORT), SHORT)
        total = x_ref[rows, :] + (
            mine_ref[rows, :].astype(F32) + theirs_ref[rows, :].astype(F32) + vec_ref[2:3, :]
        )
        sum_ref[rows, :] = total
        unit, _ = unit_rows(total)
        normed = unit * vec_ref[6:7, :] + vec_ref[4:5, :]
        normed_ref[rows, :] = normed
        normed_b_ref[rows, :] = normed.astype(BF)
        return carry

    lax.fori_loop(0, x_ref.shape[0] // SHORT, chunk_step, 0)
    width = up0_ref.shape[1]
    step = 256
    for panel, up_ref in enumerate((up0_ref, up1_ref)):
        for start in range(0, width, step):
            place = panel * width + start
            pre = dot(normed_b_ref[...], up_ref[:, start : start + step])
            pre = pre + bias_ref[:, place : place + step]
            share = 0.5 + 0.5 * lax.erf(pre * ROOT_HALF)
            slope = share + pre * (DENSITY * jnp.exp(pre * pre * -0.5))
            act_ref[:, place : place + step] = (pre * share).astype(BF)
            slope_ref[:, place : place + step] = slope.astype(BF)
    partial_ref[...] = dot(act_ref[...], down_ref[...]).astype(BF)


def norm_back(upstream, total, gain):
    unit, scale = unit_rows(total)
    scaled = upstream * gain
    first = jnp.mean(scaled, axis=1, keepdims=True)
    second = jnp.mean(scaled * unit, axis=1, keepdims=True)
    return (
        scale * (scaled - first - unit * second),
        jnp.sum(upstream * unit, axis=0, keepdims=True),
        jnp.sum(upstream, axis=0, keepdims=True),
    )


def back_second_kernel(has_base, *refs):
    base_refs, refs = refs[: 3 if has_base else 1], refs[3 if has_base else 1 :]
    sum_ref, vec_ref, act_ref, d_second_ref, d_ffn_ref, g_down_ref, sums_ref = refs
    sums_ref[...] = jnp.zeros_like(sums_ref)

    def chunk_step(chunk, carry):
        rows = pl.ds(pl.multiple_of(chunk * SHORT, SHORT), SHORT)
        upstream = base_refs[0][rows, :].astype(F32)
        if has_base:
            upstream = upstream + (
                base_refs[1][rows, :].astype(F32) + base_refs[2][rows, :].astype(F32)
            )
        d_second, d_gain, d_shift = norm_back(upstream, sum_ref[rows, :], vec_ref[7:8, :])
        d_second_ref[rows, :] = d_second
        d_ffn = d_second.astype(BF)
        d_ffn_ref[rows, :] = d_ffn
        sums_ref[1:2, :] += jnp.sum(d_ffn.astype(F32), axis=0, keepdims=True)
        sums_ref[3:4, :] += d_shift
        sums_ref[5:6, :] += d_gain
        return carry

    lax.fori_loop(0, sum_ref.shape[0] // SHORT, chunk_step, 0)
    g_down_ref[...] = dot_tn(act_ref[...], d_ffn_ref[...]).astype(BF)


def back_hidden_kernel(
    d_ffn_ref, slope_ref, normed_b_ref, down_ref, up0_ref, up1_ref,
    g_up0_ref, g_up1_ref, partial_ref, sums_ref, d_pre_ref,
):
    hidden = slope_ref.shape[1]
    step = 256
    for place in range(0, hidden, step):
        d_act = dot_nt(d_ffn_ref[...], down_ref[place : place + step, :])
        d_pre = (d_act * slope_ref[:, place : place + step].astype(F32)).astype(BF)
        d_pre_ref[:, place : place + step] = d_pre
        sums_ref[:, place : place + step] = jnp.sum(d_pre.astype(F32), axis=0, keepdims=True)
    width = up0_ref.shape[1]
    g_up0_ref[...] = dot_tn(normed_b_ref[...], d_pre_ref[:, :width]).astype(BF)
    g_up1_ref[...] = dot_tn(normed_b_ref[...], d_pre_ref[:, width:]).astype(BF)
    partial_ref[...] = (
        dot_nt(d_pre_ref[:, :width], up0_ref[...]) + dot_nt(d_pre_ref[:, width:], up1_ref[...])
    ).astype(BF)


def back_first(
    d_second_ref, mine_ref, theirs_ref, sum_ref, vec_ref, d_first_ref, dbranch_ref, sums_ref
):
    sums_ref[...] = jnp.zeros_like(sums_ref)

    def chunk_step(chunk, carry):
        rows = pl.ds(pl.multiple_of(chunk * SHORT, SHORT), SHORT)
        upstream = d_second_ref[rows, :] + (
            mine_ref[rows, :].astype(F32) + theirs_ref[rows, :].astype(F32)
        )
        d_first, d_gain, d_shift = norm_back(upstream, sum_ref[rows, :], vec_ref[6:7, :])
        d_first_ref[rows, :] = d_first
        d_branch = d_first.astype(BF)
        dbranch_ref[rows, :] = d_branch
        sums_ref[0:1, :] += jnp.sum(d_branch.astype(F32), axis=0, keepdims=True)
        sums_ref[2:3, :] += d_shift
        sums_ref[4:5, :] += d_gain
        return carry

    lax.fori_loop(0, sum_ref.shape[0] // SHORT, chunk_step, 0)


def head_lanes(value, head):
    lane = lax.broadcasted_iota(jnp.int32, value.shape, 1)
    return (lane // (value.shape[1] // 2)) == head


def mask_row(kind, chunk, count):
    place = lax.broadcasted_iota(jnp.int32, (1, count), 1)
    allowed = (place // SHORT == chunk) | (kind == 1)
    return jnp.where(allowed, 0.0, MASKED_SCORE)


def attention_kernel(
    kind_ref, x_ref, wa_ref, wb_ref, bias_ref, wo_ref, partial_ref, qkv_ref, context_ref, lse_ref
):
    count = x_ref.shape[0]
    wide = wa_ref.shape[1]
    pair = 2 * HEAD_DIM
    kind = kind_ref[0]
    x = x_ref[...]
    bias = bias_ref[...]
    qkv_ref[:, :wide] = (dot(x, wa_ref[...]) + bias[:, :wide]).astype(BF)
    qkv_ref[:, wide:] = (dot(x, wb_ref[...]) + bias[:, wide:]).astype(BF)
    for p in range(HEADS // 4):
        keys = qkv_ref[:, (3 * p + 1) * pair : (3 * p + 2) * pair]
        values = qkv_ref[:, (3 * p + 2) * pair : (3 * p + 3) * pair]

        def chunk_step(chunk, carry):
            rows = pl.ds(pl.multiple_of(chunk * SHORT, SHORT), SHORT)
            queries = qkv_ref[rows, 3 * p * pair : (3 * p + 1) * pair] * jnp.asarray(0.125, BF)
            mask = mask_row(kind, chunk, count)
            found = []
            stats = lse_ref[rows, :] if p > 0 else jnp.zeros((SHORT, 128), F32)
            lane = lax.broadcasted_iota(jnp.int32, stats.shape, 1)
            for head in range(2):
                mine = jnp.where(head_lanes(queries, head), queries, jnp.zeros_like(queries))
                scores = dot_nt(mine, keys) + mask
                top = jnp.max(scores, axis=1, keepdims=True)
                powers = jnp.exp(scores - top)
                total = jnp.sum(powers, axis=1, keepdims=True)
                probs = powers * (1.0 / total)
                found.append(dot(probs.astype(BF), values))
                stats = jnp.where(lane == 2 * p + head, top + jnp.log(total), stats)
            lse_ref[rows, :] = stats
            both = jnp.where(head_lanes(found[0], 0), found[0], found[1])
            context_ref[rows, p * pair : (p + 1) * pair] = both.astype(BF)
            return carry

        lax.fori_loop(0, count // SHORT, chunk_step, 0)
    partial_ref[...] = dot(context_ref[...], wo_ref[...]).astype(BF)


def attention_backward_kernel(
    kind_ref, d_second_ref, mine_ref, theirs_ref, sum_ref, vec_ref,
    x_ref, qkv_ref, context_ref, lse_ref, wa_ref, wb_ref, wo_ref,
    ga_ref, gb_ref, gout_ref, partial_ref, sums_ref, d_first_ref, norm_sums_ref,
    dbranch_ref, dcontext_ref, dqkv_ref, dk_ref, dv_ref,
):
    back_first(
        d_second_ref, mine_ref, theirs_ref, sum_ref, vec_ref,
        d_first_ref, dbranch_ref, norm_sums_ref,
    )
    count = x_ref.shape[0]
    wide = wa_ref.shape[1]
    pair = 2 * HEAD_DIM
    kind = kind_ref[0]
    d_branch = dbranch_ref[...]
    dcontext_ref[...] = dot_nt(d_branch, wo_ref[...]).astype(BF)
    gout_ref[...] = dot_tn(context_ref[...], d_branch).astype(BF)
    for p in range(HEADS // 4):
        keys = qkv_ref[:, (3 * p + 1) * pair : (3 * p + 2) * pair]
        values = qkv_ref[:, (3 * p + 2) * pair : (3 * p + 3) * pair]
        dk_ref[...] = jnp.zeros_like(dk_ref)
        dv_ref[...] = jnp.zeros_like(dv_ref)

        def chunk_step(chunk, carry):
            rows = pl.ds(pl.multiple_of(chunk * SHORT, SHORT), SHORT)
            queries = qkv_ref[rows, 3 * p * pair : (3 * p + 1) * pair] * jnp.asarray(0.125, BF)
            d_context = dcontext_ref[rows, p * pair : (p + 1) * pair]
            mask = mask_row(kind, chunk, count)
            stats = lse_ref[rows, :]
            found = []
            for head in range(2):
                mine = jnp.where(head_lanes(queries, head), queries, jnp.zeros_like(queries))
                theirs = jnp.where(
                    head_lanes(d_context, head), d_context, jnp.zeros_like(d_context)
                )
                lse = stats[:, 2 * p + head : 2 * p + head + 1]
                probs = jnp.exp(dot_nt(mine, keys) + mask - lse)
                d_probs = dot_nt(theirs, values)
                row_dot = jnp.sum(d_probs * probs, axis=1, keepdims=True)
                d_scores = (probs * (d_probs - row_dot)).astype(BF)
                found.append(
                    (
                        dot(d_scores, keys) * 0.125,
                        dot_tn(d_scores, queries),
                        dot_tn(probs.astype(BF), d_context),
                    )
                )
            merged = [
                jnp.where(head_lanes(one, 0), one, other) for one, other in zip(*found)
            ]
            dqkv_ref[rows, 3 * p * pair : (3 * p + 1) * pair] = merged[0].astype(BF)
            dk_ref[...] += merged[1]
            dv_ref[...] += merged[2]
            return carry

        lax.fori_loop(0, count // SHORT, chunk_step, 0)
        dqkv_ref[:, (3 * p + 1) * pair : (3 * p + 2) * pair] = dk_ref[...].astype(BF)
        dqkv_ref[:, (3 * p + 2) * pair : (3 * p + 3) * pair] = dv_ref[...].astype(BF)
    d_a = dqkv_ref[:, :wide]
    d_b = dqkv_ref[:, wide:]
    x = x_ref[...]
    ga_ref[...] = dot_tn(x, d_a).astype(BF)
    gb_ref[...] = dot_tn(x, d_b).astype(BF)
    partial_ref[...] = (dot_nt(d_a, wa_ref[...]) + dot_nt(d_b, wb_ref[...])).astype(BF)
    sums_ref[:, :wide] = jnp.sum(d_a.astype(F32), axis=0, keepdims=True)
    sums_ref[:, wide:] = jnp.sum(d_b.astype(F32), axis=0, keepdims=True)


def kernel_call(body, shapes, scratch, *operands):
    in_vmem = pl.BlockSpec(memory_space=pltpu.VMEM)
    in_smem = pl.BlockSpec(memory_space=pltpu.SMEM)
    return pl.pallas_call(
        body,
        out_shape=shapes,
        in_specs=[in_smem if value.dtype == jnp.int32 else in_vmem for value in operands],
        out_specs=[in_vmem] * len(shapes),
        scratch_shapes=scratch,
        compiler_params=pltpu.CompilerParams(vmem_limit_bytes=VMEM_LIMIT),
        cost_estimate=pl.CostEstimate(flops=0, bytes_accessed=0, transcendentals=0),
    )(*operands)


def attention(row_kind, inputs_b, w_a, w_b, bias, w_out):
    count, width = inputs_b.shape
    half = w_out.shape[0]
    shapes = [
        jax.ShapeDtypeStruct((count, width), BF),
        jax.ShapeDtypeStruct((count, 3 * half), BF),
        jax.ShapeDtypeStruct((count, half), BF),
        jax.ShapeDtypeStruct((count, 128), F32),
    ]
    return kernel_call(
        attention_kernel, shapes, [], row_kind, inputs_b, w_a, w_b, bias, w_out
    )


def attention_backward(
    row_kind, d_second, mine, theirs, first_sum, vec, inputs_b, qkv, context, lse, w_a, w_b, w_out
):
    count, width = inputs_b.shape
    half = w_out.shape[0]
    shapes = [
        jax.ShapeDtypeStruct(w_a.shape, BF),
        jax.ShapeDtypeStruct(w_b.shape, BF),
        jax.ShapeDtypeStruct(w_out.shape, BF),
        jax.ShapeDtypeStruct((count, width), BF),
        jax.ShapeDtypeStruct((1, 3 * half), F32),
        jax.ShapeDtypeStruct((count, width), F32),
        jax.ShapeDtypeStruct((8, width), F32),
    ]
    scratch = [
        pltpu.VMEM((count, width), BF),
        pltpu.VMEM((count, half), BF),
        pltpu.VMEM((count, 3 * half), BF),
        pltpu.VMEM((count, 2 * HEAD_DIM), F32),
        pltpu.VMEM((count, 2 * HEAD_DIM), F32),
    ]
    return kernel_call(
        attention_backward_kernel, shapes, scratch, row_kind, d_second, mine, theirs, first_sum,
        vec, inputs_b, qkv, context, lse, w_a, w_b, w_out,
    )


def norm_rows(base, mine, theirs, vec):
    shapes = [jax.ShapeDtypeStruct(base.shape, kind) for kind in (F32, F32, BF)]
    return kernel_call(norm_kernel, shapes, [], base, mine, theirs, vec)


def hidden_layer(x, mine, theirs, vec, bias, up0, up1, down):
    count, hidden = x.shape[0], down.shape[0]
    shapes = [jax.ShapeDtypeStruct(x.shape, kind) for kind in (F32, F32, BF)]
    shapes += [jax.ShapeDtypeStruct((count, hidden), BF)] * 2
    shapes.append(jax.ShapeDtypeStruct(x.shape, BF))
    return kernel_call(
        hidden_kernel, shapes, [], x, mine, theirs, vec, bias, up0, up1, down
    )


def back_second(upstream, total, vec, act):
    shapes = [
        jax.ShapeDtypeStruct(total.shape, F32),
        jax.ShapeDtypeStruct(total.shape, BF),
        jax.ShapeDtypeStruct((act.shape[1], total.shape[1]), BF),
        jax.ShapeDtypeStruct((8, total.shape[1]), F32),
    ]
    body = functools.partial(back_second_kernel, len(upstream) > 1)
    return kernel_call(body, shapes, [], *upstream, total, vec, act)


def back_hidden(d_ffn, slope, normed_b, down, up0, up1):
    count, hidden = slope.shape
    width = normed_b.shape[1]
    shapes = [
        jax.ShapeDtypeStruct(up0.shape, BF),
        jax.ShapeDtypeStruct(up1.shape, BF),
        jax.ShapeDtypeStruct((count, width), BF),
        jax.ShapeDtypeStruct((1, hidden), F32),
    ]
    scratch = [pltpu.VMEM((count, hidden), BF)]
    return kernel_call(
        back_hidden_kernel, shapes, scratch, d_ffn, slope, normed_b, down, up0, up1
    )


def hidden_order(width, hidden_rows):
    group = width // (2 * hidden_rows)
    target = jnp.arange(width)
    source = (
        (target % (width // 2)) // hidden_rows * (2 * hidden_rows)
        + target // (width // 2) * hidden_rows
        + target % hidden_rows
    )
    del group
    return jnp.arange(width)[:, None] == source[None, :]


def shards(tokens, row_kind, w_qkv, w_out, w_up, w_down, bias_vectors, gains, bias_up, cotangent):
    chips = Chips()
    sequence = Sequence()
    core = chips.core
    count = chips.count
    device = 2 * chips.chip + core
    row_type = row_kind[0]
    rows, width = w_out.shape[1:]
    hidden = w_up.shape[2]
    hidden_rows = w_down.shape[1]
    half = width // 2
    panels = hidden // 2 // width
    own = tokens.shape[0]
    order = hidden_order(width, hidden_rows)

    pairs = HEADS // 4
    lane = half // pairs
    plan = Plan()
    state = State()

    def ordered(mine, theirs):
        return jnp.where(core == 0, mine, theirs), jnp.where(core == 0, theirs, mine)

    def pack_qkv():
        cols = w_qkv.reshape(LAYERS, rows, 3, 2, pairs, lane)

        def side(which):
            return jnp.swapaxes(pick(cols, which, 3), 2, 3).reshape(LAYERS, rows, 3 * half)

        feature = jnp.arange(width)[None, :] - rows * device == jnp.arange(rows)[:, None]
        unit = jnp.arange(hidden // 2)[None, :] - hidden_rows * chips.chip
        unit = unit == jnp.arange(hidden_rows)[:, None]
        table = jnp.concatenate([bias_vectors, gains], axis=1).reshape(LAYERS * 8, rows)
        table = dot(table, feature.astype(BF)).astype(BF)
        units = dot(bias_up, unit.astype(BF)).astype(BF)
        got = swap(side(1 - core), 1)
        table = table + swap(table, 1)
        cols = merge(side(core), got, core, 1)
        for layer in range(LAYERS):
            last = cols[layer, :, :, width:]
            vectors = [table[8 * layer : 8 * layer + 8]]
            vectors += [units[layer : layer + 1, i * width :][:, :width] for i in range(panels)]
            vectors.append(jnp.zeros((8 - panels, width), BF))
            state.gathers[ATTN, layer] = Gather(
                chips, sequence, DIRECT[layer],
                jnp.concatenate(
                    [
                        cols[layer, :, :, :width].reshape(2 * rows, width),
                        jnp.concatenate([last[0], last[1]], axis=1),
                        w_out[layer],
                        *vectors,
                    ],
                    axis=0,
                ),
            )
        sequence.mark([state.gathers[ATTN, layer].piece for layer in range(LAYERS)])

    groups = hidden // width

    def pack_up():
        value = sequence.gate(w_up).reshape(LAYERS * rows, hidden)
        stacked = jnp.concatenate(
            [value[:, i * width : (i + 1) * width] for i in range(groups)], axis=0
        )
        stacked = dot(stacked, order.astype(BF)).astype(BF)
        mine, sent = ordered(stacked[:, :half], stacked[:, half:])
        first, second = ordered(mine, swap(sent, 1))
        for layer in range(LAYERS):
            parts = []
            for i in range(panels):
                for value in (first, second):
                    cut = [
                        value[((2 * i + j) * LAYERS + layer) * rows :][:rows] for j in range(2)
                    ]
                    parts.append(jnp.concatenate(cut, axis=1))
            state.gathers[FFN, layer] = Gather(
                chips, sequence, DIRECT[LAYERS + layer],
                jnp.concatenate(parts + [w_down[layer]], axis=0),
            )
        sequence.mark([state.gathers[FFN, layer].piece for layer in range(LAYERS)])

    def read_vectors(layer, table):
        table = jnp.sum(table.astype(F32), axis=0)
        vec = table[:8]
        bias_q, bias_v = (
            jnp.where(core == 0, vec[i : i + 1, :half], vec[i : i + 1, half:]) for i in range(2)
        )
        bias = []
        for p in range(pairs):
            cut = slice(p * lane, (p + 1) * lane)
            bias += [bias_q[:, cut], jnp.zeros((1, lane), F32), bias_v[:, cut]]
        state.vec[layer] = vec
        state.bias_qkv[layer] = jnp.concatenate(bias, axis=1)
        state.bias_up[layer] = jnp.concatenate(
            [table[8 + i : 9 + i] for i in range(panels)], axis=1
        )

    def tokens_start():
        value = sequence.gate(tokens)
        sequence.mark(value)
        state.pair_tokens = (value, swap(value, 1))

    def tokens_end():
        values = sequence.gate(state.pair_tokens)
        state.x_b[0] = jnp.concatenate(ordered(*values), axis=0)
        state.x[0] = state.x_b[0].astype(F32)
        sequence.mark(state.x_b[0])

    def cotangent_start():
        value = sequence.gate(cotangent)
        sequence.mark(value)
        state.pair_cotangent = (value, swap(value, 1))

    def cotangent_end():
        values = sequence.gate(state.pair_cotangent)
        state.upstream = (jnp.concatenate(ordered(*values), axis=0),)
        sequence.mark(state.upstream)

    def out_exchange(layer):
        ends = [0, 2 * rows, 4 * rows, 4 * rows + 16]
        first, second, table = state.gathers[ATTN, layer].finish(list(zip(ends[:-1], ends[1:])))
        last, out_all = second[:, :rows], second[:, rows:]
        w_b = jnp.swapaxes(last.reshape(count, rows, 2, half), 1, 2)
        out_all = out_all.reshape(2, count // 2, rows, width)
        sent, w_b = pick(out_all, 1 - core, 0), w_b.reshape(width, half)
        read_vectors(layer, table)
        sequence.mark((sent, w_b, state.vec[layer]))
        full_out = merge(pick(out_all, core, 0), swap(sent, 1), core, 1).reshape(half, width)
        state.w_attn[layer] = (first.reshape(width, width), w_b, full_out)

    def hidden_weights(layer):
        ends = [2 * rows * i for i in range(panels + 1)]
        ends.append(ends[-1] + hidden_rows)
        *ups, down = state.gathers[FFN, layer].finish(list(zip(ends[:-1], ends[1:])))
        state.w_hidden[layer] = (
            down.reshape(hidden // 2, width), *(value.reshape(width, width) for value in ups)
        )

    def run_attention(layer):
        x_b, weights = sequence.gate((state.x_b[layer], state.w_attn[layer]))
        w_a, w_b, full_out = weights
        partial, *saved = attention(row_kind, x_b, w_a, w_b, state.bias_qkv[layer], full_out)
        sequence.mark(partial)
        state.w_attn[layer] = weights
        state.saved[layer] = (x_b, *saved)
        state.branch = (partial, swap(partial, 1))

    def run_hidden(layer):
        mine, theirs = sequence.gate(state.branch)
        down, up0, up1 = state.w_hidden[layer]
        first_sum, state.normed, *kept, partial = hidden_layer(
            state.x[layer], mine, theirs, state.vec[layer], state.bias_up[layer], up0, up1, down
        )
        sequence.mark(partial)
        state.first_sum[layer] = first_sum
        state.kept[layer] = kept
        state.branch = (partial, swap(partial, 1))

    def run_norm(layer):
        mine, theirs = sequence.gate(state.branch)
        second, x, x_b = norm_rows(state.normed, mine, theirs, state.vec[layer])
        state.second[layer], state.x[layer + 1], state.x_b[layer + 1] = second, x, x_b
        sequence.mark(second)

    def run_back_second(layer):
        upstream = sequence.gate(state.upstream)
        if layer < LAYERS - 1:
            upstream = (state.d_first, *upstream)
        act = state.kept[layer][1]
        d_second, d_ffn, g_down, sums = back_second(
            upstream, state.second[layer], state.vec[layer], act
        )
        state.d_second, state.d_ffn = d_second, d_ffn
        state.sums2[layer] = sums
        bundle = state.scatters[FFN, layer]
        bundle.start(0, [g_down.reshape(count, hidden_rows, width)])
        sequence.mark((d_ffn, bundle.sent))

    def run_back_hidden(layer):
        d_ffn = sequence.gate(state.d_ffn)
        normed_b, _, slope = state.kept[layer]
        *g_up, partial, units = back_hidden(d_ffn, slope, normed_b, *state.w_hidden[layer])
        bundle = state.scatters[FFN, layer]
        bundle.start(1, [value.reshape(count, 2 * rows, width) for value in g_up])
        sequence.mark((partial, bundle.sent))
        state.units[layer] = units
        state.branch = (partial, swap(partial, 1))

    def run_back_attention(layer):
        mine, theirs = sequence.gate(state.branch)
        x_b, qkv, context, lse = state.saved[layer]
        g_a, g_b, g_out, partial, sums, state.d_first, state.sums1[layer] = attention_backward(
            row_kind, state.d_second, mine, theirs, state.first_sum[layer], state.vec[layer],
            x_b, qkv, context, lse, *state.w_attn[layer],
        )
        sequence.mark(partial)
        state.pair[layer] = jnp.concatenate(
            [
                jnp.concatenate(
                    [sums[:, (3 * p + t) * lane :][:, :lane] for p in range(pairs)], axis=1
                )
                for t in (0, 2)
            ],
            axis=0,
        )
        if layer > 0:
            state.upstream = (partial, swap(partial, 1))
        else:
            mine, sent = ordered(partial[:own], partial[own:])
            state.upstream = (mine, swap(sent, 1))
        state.g_attn[layer] = (g_a, g_b, g_out)

    def sum_rows(layer):
        pair = state.pair[layer]
        nothing = jnp.zeros_like(pair)
        pair = jnp.concatenate(ordered(pair, nothing), axis=1)
        units = [state.units[layer][:, i * width :][:, :width] for i in range(panels)]
        small = jnp.concatenate([state.sums1[layer] + state.sums2[layer], pair, *units], axis=0)
        small = jnp.pad(small.astype(BF), ((0, 16 - small.shape[0]), (0, 0)))
        line = jnp.arange(16)[:, None]
        place = jnp.arange(width)[None, :]
        owner = jnp.where(
            line < 10, place // (2 * rows), ((line - 10) * width + place) // hidden_rows
        )
        mine = owner[None] == jnp.arange(count)[:, None, None]
        return jnp.where(mine, small[None], jnp.zeros((), BF))

    def back_terms(layer):
        g_a, g_b, g_out = sequence.gate(state.g_attn[layer])
        bundle = state.scatters[ATTN, layer]
        out_pair = g_out.reshape(count // 2, 2, rows, width)
        out_got = swap(pick(out_pair, 1 - core, 1), 1)
        out = merge(pick(out_pair, core, 1), out_got, core, 0).reshape(count, rows, width)
        g_b = g_b.reshape(count, 2, rows, half)
        last = jnp.concatenate([g_b[:, 0], g_b[:, 1]], axis=2)
        rest = jnp.concatenate([last, out, sum_rows(layer)], axis=1)
        rest = lax.optimization_barrier(rest)
        bundle.start(0, [g_a.reshape(count, 2 * rows, width), rest])
        sequence.mark(bundle.sent)

    def grad_end():
        mine, theirs = sequence.gate(state.upstream)
        d_first = lax.dynamic_slice_in_dim(state.d_first, core * own, own)
        state.grad_tokens = d_first + (mine.astype(F32) + theirs.astype(F32))
        sequence.mark(state.grad_tokens)

    def mixed_end():
        value = sequence.gate(state.x_b[LAYERS])
        state.mixed = lax.dynamic_slice_in_dim(value, core * own, own)
        sequence.mark(state.mixed)

    def finish_hidden(layer):
        down, *ups = state.scatters[FFN, layer].finish()
        sides = [
            jnp.concatenate([up[side * rows :][:rows] for up in ups], axis=1)
            for side in range(2)
        ]
        mine, sent = ordered(*sides)
        state.up_pair[layer] = (mine, swap(sent, 1))
        state.down[layer] = down

    def end_hidden(layer):
        first, second = ordered(*sequence.gate(state.up_pair[layer]))
        stacked = jnp.concatenate(
            [
                jnp.concatenate(
                    [value[:, i * half : (i + 1) * half] for value in (first, second)], axis=1
                )
                for i in range(groups)
            ],
            axis=0,
        )
        stacked = lax.dot_general(
            stacked, order.astype(F32), (((1,), (1,)), ((), ())),
            precision=lax.Precision.HIGHEST, preferred_element_type=F32,
        )
        state.up[layer] = jnp.concatenate(
            [stacked[i * rows : (i + 1) * rows] for i in range(groups)], axis=1
        )
        sequence.mark(state.up[layer])

    def finish_attention(layer):
        first, rest = state.scatters[ATTN, layer].finish()
        last, out, small = rest[:rows], rest[rows : 2 * rows], rest[2 * rows :]
        sides = [
            jnp.concatenate(
                [first[side * rows :][:rows], last[:, side * half :][:, :half]], axis=1
            )
            for side in range(2)
        ]
        mine, sent = ordered(*sides)
        pair = jnp.pad(small[8:], ((0, 0), (0, mine.shape[1] - width)))
        sent = jnp.concatenate([sent, pair], axis=0)
        state.qkv_pair[layer] = (mine, swap(sent, 1))
        state.out[layer] = out
        state.small_rows[layer] = small

    def end_attention(layer):
        mine, theirs = sequence.gate(state.qkv_pair[layer])
        small = state.small_rows[layer]
        small = jnp.concatenate([theirs[rows : rows + 2, :width] + small[8:10], small], axis=0)
        features = lax.dynamic_slice_in_dim(small, rows * device, rows, axis=1)
        per_row = width // hidden_rows
        units = lax.dynamic_slice(
            small,
            (12 + chips.chip // per_row, hidden_rows * (chips.chip % per_row)),
            (1, hidden_rows),
        )
        state.vectors[layer] = features[:6]
        state.gains[layer] = features[6:8]
        state.unit_sums[layer] = units[0]
        values = ordered(mine, theirs[:rows])
        state.qkv[layer] = jnp.concatenate(
            [
                value[:, (3 * p + t) * lane :][:, :lane]
                for t in range(3)
                for value in values
                for p in range(pairs)
            ],
            axis=1,
        )
        sequence.mark(state.qkv[layer])

    def call(function, *args):
        return lambda: function(*args)

    low = len(chips.low)
    size = (1.0, 2.0)
    add = plan.add

    def pair_send(label):
        return [(label, (("p", 0.0),), 1)]

    def plane(length):
        return (("x", length), ("y", length))

    add("pq", 0, 6.0, [], pack_qkv)
    add("pu", 2, 3.0, [("g", ATTN, 0)], pack_up)
    add("tok", 8, 0.5, ["pu"], tokens_start, pair_send("x0"))
    add("te", 7, 1.5, ["x0"], tokens_end)
    add("cot", 9, 0.5, [("m", 1, 0)], cotangent_start, pair_send("ct"))
    add("ce", 9, 1.2, ["ct"], cotangent_end)
    bundles = [(ATTN, 0), (FFN, 0), (ATTN, 1), (FFN, 1)]
    for rank, (kind, layer) in enumerate(bundles):
        needs = ["pq" if kind == ATTN else "pu"]

        def start(kind=kind, layer=layer):
            state.gathers[kind, layer].start()

        def advance(kind=kind, layer=layer):
            state.gathers[kind, layer].advance()

        units = 7.0 / 3 if kind == ATTN else 4.0
        z = UNIT * 2 * units
        if DIRECT[LAYERS * kind + layer]:
            need = ("z", kind, layer)
            links = (("z", 1.5 * z), ("w", 2 * z))
            add(("g", kind, layer), 1 + rank, 5.0, needs, start, [(need, links, 3)])
        else:
            need = ("y", kind, layer)
            links = (("z", 0.5 * z), ("w", z + 1.5))
            add(("g", kind, layer), 1 + rank, 3.5, needs, start, [(need, links, 1)])
            sent = ("z", kind, layer)
            add(("h", kind, layer), 1 + rank, 2.2, [need], advance, [(sent, (("z", z),), 1)])
            need = sent
        length = UNIT * 2 * units
        for step in range(low):
            sent = ("xy", kind, layer, step)
            add(
                ("gs", kind, layer, step), 1 + rank, 2.5 + 0.3 * kind, [need], advance,
                [(sent, plane(length), 1)],
            )
            need = sent
            length *= 2
        if kind == ATTN:
            add(
                ("go", layer), 1 + rank, 4.5, [need], call(out_exchange, layer),
                pair_send(("w", kind, layer)),
            )
        else:
            add(("w", kind, layer), 1 + rank, 1.6, [need], call(hidden_weights, layer))
    need = "te"
    for layer in range(LAYERS):
        add(
            ("m", 0, layer), 10, 12.7, [need, ("w", ATTN, layer)],
            call(run_attention, layer), pair_send(("p", 0, layer)),
        )
        add(
            ("m", 1, layer), 10, 6.0, [("p", 0, layer), ("w", FFN, layer)],
            call(run_hidden, layer), pair_send(("p", 1, layer)),
        )
        need = ("m", 2, layer)
        add(need, 10, 3.0, [("p", 1, layer)], call(run_norm, layer))
    add("mix", 20, 1.0, [need], mixed_end)

    needs = [need, "ce"]
    for layer in reversed(range(LAYERS)):
        state.scatters[FFN, layer] = Scatter(chips, sequence, 2)
        state.scatters[ATTN, layer] = Scatter(chips, sequence, 1)
        add(
            ("b", 0, layer), 10, 5.0, needs, call(run_back_second, layer),
            [(("r", FFN, layer, 0), plane(UNIT * 8), 1)],
        )
        add(
            ("b", 1, layer), 10, 6.5, [("b", 0, layer)], call(run_back_hidden, layer),
            [(("r", FFN, layer, 1), plane(UNIT * 8), 1)] + pair_send(("p", 2, layer)),
        )
        add(
            ("b", 2, layer), 10, 17.2, [("p", 2, layer)], call(run_back_attention, layer),
            pair_send(("p", 3, layer)),
        )
        add(
            ("b", 3, layer), 9.5, 6.0, [("b", 2, layer)], call(back_terms, layer),
            [(("r", ATTN, layer, 0), plane(UNIT * 28 / 3), 1)],
        )
        needs = [("p", 3, layer)]
        for kind in (FFN, ATTN):
            need = [("r", kind, layer, part) for part in range(1 + kind)]
            rank = 1 + 2 * (LAYERS - 1 - layer) + (kind == ATTN)

            def reduce(kind=kind, layer=layer):
                state.scatters[kind, layer].advance()

            units = 7.0 / 3 if kind == ATTN else 4.0
            length = UNIT * 2 * units
            for step in range(low - 1):
                sent = ("r", kind, layer, 2 + step)
                add(
                    ("rs", kind, layer, step), rank, 2.8 + 0.4 * kind, need, reduce,
                    [(sent, plane(length), 1)],
                )
                need = [sent]
                length /= 2
            z = UNIT * 2 * units
            sent = ("rz", kind, layer)
            add(("rs", kind, layer, low), rank, 2.2, need, reduce, [(sent, (("z", z),), 1)])
            need = sent
            links = (("z", 0.5 * z), ("w", z + 1.5))
            sent = ("ry", kind, layer)
            add(("rs", kind, layer, low + 1), rank, 3.5, [need], reduce, [(sent, links, 1)])
            last = finish_hidden if kind == FFN else finish_attention
            add(
                ("rf", kind, layer), 19, 2.0, [sent], call(last, layer),
                pair_send(("re", kind, layer)),
            )
            last = end_hidden if kind == FFN else end_attention
            add(("ro", kind, layer), 20, 2.5, [("re", kind, layer)], call(last, layer))
    add("grad", 18, 1.2, needs, grad_end)
    plan.run()

    def stacked(values):
        return jnp.stack([values[layer] for layer in range(LAYERS)])

    return (
        state.mixed,
        state.grad_tokens,
        stacked(state.qkv),
        stacked(state.out),
        stacked(state.up),
        stacked(state.down),
        stacked(state.vectors),
        stacked(state.gains),
        stacked(state.unit_sums),
    )


def solution(mesh):
    placed = (
        P("fsdp", None),
        P("fsdp"),
        P(None, "fsdp", None),
        P(None, "fsdp", None),
        P(None, "fsdp", None),
        P(None, "fsdp", None),
        P(None, None, "fsdp"),
        P(None, None, "fsdp"),
        P(None, "fsdp"),
        P("fsdp", None),
    )
    return jax.shard_map(
        shards,
        mesh=mesh,
        in_specs=placed,
        out_specs=(
            P("fsdp", None),
            P("fsdp", None),
            P(None, "fsdp", None),
            P(None, "fsdp", None),
            P(None, "fsdp", None),
            P(None, "fsdp", None),
            P(None, None, "fsdp"),
            P(None, None, "fsdp"),
            P(None, "fsdp"),
        ),
        check_vma=False,
    )
```

```python
import functools

import jax
import jax.numpy as jnp
from jax import lax
from jax.experimental import pallas as pl
from jax.experimental.pallas import tpu as pltpu
from jax.sharding import PartitionSpec as P

HEADS = 12
HEAD_DIM = 64
LAYERS = 2
SHORT = 128
AXIS = "fsdp"

EPSILON = 1e-05
MASKED_SCORE = -1e30
BF = jnp.bfloat16
F32 = jnp.float32
LATENCY = 2.5
UNIT = 1.48
ATTN, FFN = 0, 1
OPEN_SENDS = 5
VMEM_LIMIT = 8 * 2**20
EARLY = (False, False, True, True)
LATE = (False, True, False, True)
ORDER = (
    0, 6, 16, 7, 1, 11, 2, 12, 21, 8, 17, 22, 9, 18, 13, 19, 23, 14, 3, 10, 15, 20, 26,
    24, 25, 27, 28, 29, 4, 5, 30, 31, 33, 34, 35, 36, 37, 32, 47, 48, 42, 49, 38, 51, 50,
    52, 43, 56, 53, 39, 57, 44, 40, 58, 45, 54, 41, 61, 46, 59, 55, 60,
)


def dot(left, right):
    return jnp.dot(left, right, preferred_element_type=F32)


def dot_tn(left, right):
    return lax.dot_general(left, right, (((0,), (0,)), ((), ())), preferred_element_type=F32)


def dot_nt(left, right):
    return lax.dot_general(left, right, (((1,), (1,)), ((), ())), preferred_element_type=F32)


def swap(value, mask):
    pairs = [(source, source ^ mask) for source in range(lax.axis_size(AXIS))]
    return lax.ppermute(value, AXIS, pairs)


def merge(mine, theirs, bit, axis):
    first = jnp.where(bit == 0, mine, theirs)
    second = jnp.where(bit == 0, theirs, mine)
    return jnp.stack([first, second], axis=axis)


def pick(pair, index, axis):
    return lax.dynamic_index_in_dim(pair, index, axis, keepdims=False)


class Chips:
    def __init__(self):
        device = lax.axis_index(AXIS)
        self.count = lax.axis_size(AXIS) // 2
        self.core = device % 2
        self.chip = device // 2
        self.step = self.count // 4
        self.top = self.chip // self.step
        self.low = list(range(self.count.bit_length() - 3))

    def bit(self, place):
        return (self.chip // 2**place) % 2

    def plane_bit(self, step):
        return jnp.where(self.core == 0, self.bit(step), self.bit(len(self.low) - 1 - step))

    def plane_swap(self, value, step):
        masks = (2 * 2**step, 2 * 2 ** (len(self.low) - 1 - step))
        pairs = [(source, source ^ masks[source % 2]) for source in range(2 * self.count)]
        return lax.ppermute(value, AXIS, pairs)

    def half_places(self, step, own):
        bit = self.plane_bit(step)
        bit = bit if own else 1 - bit
        index = jnp.arange(2**step)
        return jnp.where(self.core == 0, 2**step * bit + index, 2 * index + bit)


class Sequence:
    def __init__(self):
        self.last = None

    def gate(self, values):
        if self.last is None:
            return values
        values, _ = lax.optimization_barrier((values, self.last))
        return values

    def mark(self, values):
        self.last = values


class State:
    def __getattr__(self, name):
        value = {}
        setattr(self, name, value)
        return value


class Plan:
    def __init__(self):
        self.pieces = []

    def add(self, name, rank, cost, needs, run, sends=()):
        self.pieces.append((name, rank, cost, needs, run, sends))

    def greedy(self):
        now = 0.0
        ready = {}
        free = {}
        open_sends = {}
        waiting = list(range(len(self.pieces)))
        order = []

        def fits(piece):
            held = sum(weight for label, weight in open_sends.items() if label not in piece[3])
            added = sum(weight for _, _, weight in piece[5])
            return added == 0 or held + added <= OPEN_SENDS

        while waiting:
            known = []
            for place in waiting:
                piece = self.pieces[place]
                if all(need in ready for need in piece[3]):
                    time = max([ready[need] for need in piece[3]], default=0.0)
                    known.append((time, piece[1], place))
            known = [entry for entry in known if fits(self.pieces[entry[2]])] or known
            able = [entry[1:] for entry in known if entry[0] <= now]
            place = min(able)[1] if able else min(known)[2]
            name, _, cost, needs, _, sends = self.pieces[place]
            now = max([now] + [ready[need] for need in needs]) + cost
            ready[name] = now
            for need in needs:
                open_sends.pop(need, None)
            for label, links, weight in sends:
                ready[label] = 0.0
                for link, length in links:
                    free[link] = max(now, free.get(link, 0.0)) + length
                    ready[label] = max(ready[label], free[link] + LATENCY)
                if weight > 0:
                    open_sends[label] = weight
            waiting.remove(place)
            order.append(place)
        return order

    def run(self):
        order = ORDER if len(ORDER) == len(self.pieces) else self.greedy()
        for place in order:
            self.pieces[place][4]()


class Gather:
    def __init__(self, chips, sequence, early, piece):
        self.chips, self.sequence = chips, sequence
        low = [("low", step) for step in range(len(chips.low))]
        top = [("top", 2), ("top", 1)]
        self.steps = low[:1] + top + low[1:] if early else top + low
        self.held = piece[None, None]

    def start(self):
        self.held = self.sequence.gate(self.held)
        self.sequence.mark(self.held)
        self.send()

    def send(self):
        kind, step = self.steps[0]
        if kind == "low":
            self.coming = self.chips.plane_swap(self.held, step)
        else:
            self.coming = swap(self.held, 2 * step * self.chips.step)

    def merged(self, ranges=None):
        chips = self.chips
        coming = self.sequence.gate(self.coming)
        kind, step = self.steps.pop(0)
        if kind == "low":
            return merge_rows(self.held, coming, chips.plane_bit(step), chips.core, ranges)
        lead, half, height, width = self.held.shape
        flat = [value.reshape(lead, 1, half * height, width) for value in (self.held, coming)]
        bit = chips.top // 2 if step == 2 else chips.top % 2
        return merge_rows(*flat, bit, 0).reshape(2 * lead, half, height, width)

    def advance(self):
        self.held = self.merged()
        self.sequence.mark(self.held)
        self.send()

    def finish(self, ranges):
        while len(self.steps) > 1:
            self.advance()
        results = self.merged(ranges)
        results = [whole.reshape((self.chips.count,) + whole.shape[2:]) for whole in results]
        self.sequence.mark(results)
        return results


def merge_kernel(ranges, place_ref, mine_ref, theirs_ref, *out_refs):
    half = mine_ref.shape[1]
    for lead in range(mine_ref.shape[0]):
        for index in range(half):
            for (start, stop), out_ref in zip(ranges, out_refs):
                out_ref[lead, place_ref[index]] = mine_ref[lead, index, start:stop]
                out_ref[lead, place_ref[half + index]] = theirs_ref[lead, index, start:stop]


def merge_rows(mine, theirs, bit, inner, ranges=None):
    half = mine.shape[1]
    cuts = ranges or [(0, mine.shape[2])]
    if all(edge % 16 == 0 for cut in cuts for edge in cut):
        index = jnp.arange(half)

        def place(own):
            return jnp.where(inner == 1, 2 * index + own, half * own + index)

        places = jnp.concatenate([place(bit), place(1 - bit)]).astype(jnp.int32)
        shapes = [
            jax.ShapeDtypeStruct((mine.shape[0], 2 * half, stop - start, mine.shape[3]), BF)
            for start, stop in cuts
        ]
        results = kernel_call(
            functools.partial(merge_kernel, cuts), shapes, [], places, mine, theirs
        )
    else:
        results = []
        for start, stop in cuts:
            cut = [value[:, :, start:stop] for value in (mine, theirs)]
            outer = merge(*cut, bit, 1)
            outer = outer.reshape((mine.shape[0], 2 * half) + outer.shape[3:])
            results.append(
                jnp.where(inner == 1, merge(*cut, bit, 2).reshape(outer.shape), outer)
            )
    return results if ranges else results[0]


class Scatter:
    def __init__(self, chips, sequence, count, late):
        self.chips, self.sequence = chips, sequence
        low = [("low", step) for step in range(len(chips.low) - 1)][::-1]
        top = [("top", 1), ("top", 2)]
        self.steps = low[:-1] + top + low[-1:] if late else low + top
        self.arrays = [None] * count
        self.coming = [None] * count
        self.heights = None

    def start(self, part, arrays):
        chips = self.chips
        step = len(chips.low) - 1
        shape = (4, 2 ** len(chips.low))
        arrays = [value.reshape(shape + value.shape[1:]) for value in arrays]
        self.arrays[part] = arrays
        sent = send_rows(arrays, chips.half_places(step, False))
        self.coming[part] = chips.plane_swap(sent, step)
        self.sent = sent

    def advance(self):
        chips = self.chips
        coming = self.sequence.gate(self.coming)
        if self.heights is None:
            self.heights = [value.shape[2] for part in self.arrays for value in part]
            kept = chips.half_places(len(chips.low) - 1, True)
        else:
            self.arrays, coming = [[self.kept]], [coming]
            kept = jnp.arange(self.kept.shape[1])
        kind, step = self.steps.pop(0)
        if kind == "low":
            sides = [chips.half_places(step, own) for own in (False, True)]
        else:
            bit = chips.top // 2 if step == 2 else chips.top % 2
            lead, places = self.arrays[0][0].shape[:2]
            half = coming[0].shape[1]
            self.arrays = [
                [value.reshape((lead // 2, 2 * places) + value.shape[2:]) for value in part]
                for part in self.arrays
            ]
            coming = [got.reshape((lead // 2, 2 * half) + got.shape[2:]) for got in coming]
            kept = jnp.concatenate([kept, places + kept])
            sides = [half * which + jnp.arange(half) for which in (1 - bit, bit)]
        sent, self.kept = fold_rows(self.arrays, coming, kept, sides)
        self.sequence.mark(sent)
        if kind == "low":
            self.coming = chips.plane_swap(sent, step)
        else:
            self.coming = swap(sent, 2 * step * chips.step)

    def finish(self):
        coming = self.sequence.gate(self.coming)
        total = self.kept[0, 0] + coming[0, 0].astype(F32)
        self.sequence.mark(total)
        ends = [sum(self.heights[:i]) for i in range(len(self.heights) + 1)]
        return [total[start:stop] for start, stop in zip(ends[:-1], ends[1:])]


def send_kernel(heights, place_ref, *refs):
    *array_refs, sent_ref = refs
    for lead in range(sent_ref.shape[0]):
        for index in range(sent_ref.shape[1]):
            row = 0
            for height, ref in zip(heights, array_refs):
                sent_ref[lead, index, row : row + height] = ref[lead, place_ref[index]]
                row += height


def send_rows(arrays, places):
    heights = [value.shape[2] for value in arrays]
    shape = (arrays[0].shape[0], places.shape[0], sum(heights), arrays[0].shape[3])
    if any(height % 16 for height in heights):
        return jnp.concatenate([jnp.take(value, places, axis=1) for value in arrays], axis=2)
    (sent,) = kernel_call(
        functools.partial(send_kernel, heights), [jax.ShapeDtypeStruct(shape, BF)], [],
        places.astype(jnp.int32), *arrays,
    )
    return sent


def fold_kernel(layout, place_ref, *refs):
    *refs, sent_ref, kept_ref = refs
    count = sent_ref.shape[1]
    for lead in range(sent_ref.shape[0]):
        for index in range(count):
            for array, got, start, height, row in layout:
                for side, out_ref in enumerate((sent_ref, kept_ref)):
                    place = 2 * (count * side + index)
                    mine = refs[array][lead, place_ref[place]]
                    theirs = refs[got][lead, place_ref[place + 1], start : start + height]
                    total = mine.astype(F32) + theirs.astype(F32)
                    out_ref[lead, index, row : row + height] = total.astype(out_ref.dtype)


def fold_rows(parts, coming, kept, sides):
    arrays = [value for part in parts for value in part]
    layout = []
    row = 0
    for part, got in zip(range(len(parts)), range(len(arrays), len(arrays) + len(coming))):
        start = 0
        for value in parts[part]:
            height = value.shape[2]
            layout.append((len(layout), got, start, height, row))
            start += height
            row += height
    shape = (arrays[0].shape[0], sides[0].shape[0], row, arrays[0].shape[3])
    if any(value.shape[2] % 16 for value in arrays):
        totals = []
        for array, got, start, height, _ in layout:
            theirs = coming[got - len(arrays)][:, :, start : start + height]
            totals.append(jnp.take(arrays[array], kept, axis=1).astype(F32) + theirs.astype(F32))
        total = jnp.concatenate(totals, axis=2)
        return [jnp.take(total, side, axis=1).astype(kind) for side, kind in zip(sides, (BF, F32))]
    places = [jnp.stack([jnp.take(kept, side), side], axis=1).reshape(-1) for side in sides]
    return kernel_call(
        functools.partial(fold_kernel, layout),
        [jax.ShapeDtypeStruct(shape, kind) for kind in (BF, F32)], [],
        jnp.concatenate(places).astype(jnp.int32), *arrays, *coming,
    )


ROOT_HALF = 0.7071067811865476
DENSITY = 0.3989422804014327


def unit_rows(values):
    centre = values - jnp.mean(values, axis=1, keepdims=True)
    scale = lax.rsqrt(jnp.mean(centre * centre, axis=1, keepdims=True) + EPSILON)
    return centre * scale, scale


def norm_kernel(base_ref, mine_ref, theirs_ref, vec_ref, sum_ref, out_ref, out_b_ref):
    def chunk_step(chunk, carry):
        rows = pl.ds(pl.multiple_of(chunk * SHORT, SHORT), SHORT)
        total = base_ref[rows, :] + (
            mine_ref[rows, :].astype(F32) + theirs_ref[rows, :].astype(F32)
        ) + vec_ref[3:4, :]
        sum_ref[rows, :] = total
        unit, _ = unit_rows(total)
        output = unit * vec_ref[7:8, :] + vec_ref[5:6, :]
        out_ref[rows, :] = output
        out_b_ref[rows, :] = output.astype(BF)
        return carry

    lax.fori_loop(0, base_ref.shape[0] // SHORT, chunk_step, 0)


def hidden_kernel(
    x_ref, mine_ref, theirs_ref, vec_ref, bias_ref, up0_ref, up1_ref, down_ref,
    sum_ref, normed_ref, normed_b_ref, act_ref, slope_ref, partial_ref,
):
    def chunk_step(chunk, carry):
        rows = pl.ds(pl.multiple_of(chunk * SHORT, SHORT), SHORT)
        total = x_ref[rows, :] + (
            mine_ref[rows, :].astype(F32) + theirs_ref[rows, :].astype(F32) + vec_ref[2:3, :]
        )
        sum_ref[rows, :] = total
        unit, _ = unit_rows(total)
        normed = unit * vec_ref[6:7, :] + vec_ref[4:5, :]
        normed_ref[rows, :] = normed
        normed_b_ref[rows, :] = normed.astype(BF)
        return carry

    lax.fori_loop(0, x_ref.shape[0] // SHORT, chunk_step, 0)
    width = up0_ref.shape[1]
    step = 256
    for panel, up_ref in enumerate((up0_ref, up1_ref)):
        for start in range(0, width, step):
            place = panel * width + start
            pre = dot(normed_b_ref[...], up_ref[:, start : start + step])
            pre = pre + bias_ref[:, place : place + step]
            share = 0.5 + 0.5 * lax.erf(pre * ROOT_HALF)
            slope = share + pre * (DENSITY * jnp.exp(pre * pre * -0.5))
            act_ref[:, place : place + step] = (pre * share).astype(BF)
            slope_ref[:, place : place + step] = slope.astype(BF)
    partial_ref[...] = dot(act_ref[...], down_ref[...]).astype(BF)


def norm_back(upstream, total, gain):
    unit, scale = unit_rows(total)
    scaled = upstream * gain
    first = jnp.mean(scaled, axis=1, keepdims=True)
    second = jnp.mean(scaled * unit, axis=1, keepdims=True)
    return (
        scale * (scaled - first - unit * second),
        jnp.sum(upstream * unit, axis=0, keepdims=True),
        jnp.sum(upstream, axis=0, keepdims=True),
    )


def back_second_kernel(has_base, *refs):
    base_refs, refs = refs[: 3 if has_base else 1], refs[3 if has_base else 1 :]
    sum_ref, vec_ref, act_ref, d_second_ref, d_ffn_ref, g_down_ref, sums_ref = refs
    sums_ref[...] = jnp.zeros_like(sums_ref)

    def chunk_step(chunk, carry):
        rows = pl.ds(pl.multiple_of(chunk * SHORT, SHORT), SHORT)
        upstream = base_refs[0][rows, :].astype(F32)
        if has_base:
            upstream = upstream + (
                base_refs[1][rows, :].astype(F32) + base_refs[2][rows, :].astype(F32)
            )
        d_second, d_gain, d_shift = norm_back(upstream, sum_ref[rows, :], vec_ref[7:8, :])
        d_second_ref[rows, :] = d_second
        d_ffn = d_second.astype(BF)
        d_ffn_ref[rows, :] = d_ffn
        sums_ref[1:2, :] += jnp.sum(d_ffn.astype(F32), axis=0, keepdims=True)
        sums_ref[3:4, :] += d_shift
        sums_ref[5:6, :] += d_gain
        return carry

    lax.fori_loop(0, sum_ref.shape[0] // SHORT, chunk_step, 0)
    g_down_ref[...] = dot_tn(act_ref[...], d_ffn_ref[...]).astype(BF)


def back_hidden_kernel(
    d_ffn_ref, slope_ref, normed_b_ref, down_ref, up0_ref, up1_ref,
    g_up0_ref, g_up1_ref, partial_ref, sums_ref, d_pre_ref,
):
    hidden = slope_ref.shape[1]
    step = 256
    for place in range(0, hidden, step):
        d_act = dot_nt(d_ffn_ref[...], down_ref[place : place + step, :])
        d_pre = (d_act * slope_ref[:, place : place + step].astype(F32)).astype(BF)
        d_pre_ref[:, place : place + step] = d_pre
        sums_ref[:, place : place + step] = jnp.sum(d_pre.astype(F32), axis=0, keepdims=True)
    width = up0_ref.shape[1]
    g_up0_ref[...] = dot_tn(normed_b_ref[...], d_pre_ref[:, :width]).astype(BF)
    g_up1_ref[...] = dot_tn(normed_b_ref[...], d_pre_ref[:, width:]).astype(BF)
    partial_ref[...] = (
        dot_nt(d_pre_ref[:, :width], up0_ref[...]) + dot_nt(d_pre_ref[:, width:], up1_ref[...])
    ).astype(BF)


def back_first(
    d_second_ref, mine_ref, theirs_ref, sum_ref, vec_ref, d_first_ref, dbranch_ref, sums_ref
):
    sums_ref[...] = jnp.zeros_like(sums_ref)

    def chunk_step(chunk, carry):
        rows = pl.ds(pl.multiple_of(chunk * SHORT, SHORT), SHORT)
        upstream = d_second_ref[rows, :] + (
            mine_ref[rows, :].astype(F32) + theirs_ref[rows, :].astype(F32)
        )
        d_first, d_gain, d_shift = norm_back(upstream, sum_ref[rows, :], vec_ref[6:7, :])
        d_first_ref[rows, :] = d_first
        d_branch = d_first.astype(BF)
        dbranch_ref[rows, :] = d_branch
        sums_ref[0:1, :] += jnp.sum(d_branch.astype(F32), axis=0, keepdims=True)
        sums_ref[2:3, :] += d_shift
        sums_ref[4:5, :] += d_gain
        return carry

    lax.fori_loop(0, sum_ref.shape[0] // SHORT, chunk_step, 0)


def head_lanes(value, head):
    lane = lax.broadcasted_iota(jnp.int32, value.shape, 1)
    return (lane // (value.shape[1] // 2)) == head


def mask_row(kind, chunk, count):
    place = lax.broadcasted_iota(jnp.int32, (1, count), 1)
    allowed = (place // SHORT == chunk) | (kind == 1)
    return jnp.where(allowed, 0.0, MASKED_SCORE)


def attention_kernel(
    kind_ref, x_ref, wa_ref, wb_ref, bias_ref, wo_ref, partial_ref, qkv_ref, context_ref, lse_ref
):
    count = x_ref.shape[0]
    wide = wa_ref.shape[1]
    pair = 2 * HEAD_DIM
    kind = kind_ref[0]
    x = x_ref[...]
    bias = bias_ref[...]
    qkv_ref[:, :wide] = (dot(x, wa_ref[...]) + bias[:, :wide]).astype(BF)
    qkv_ref[:, wide:] = (dot(x, wb_ref[...]) + bias[:, wide:]).astype(BF)
    for p in range(HEADS // 4):
        keys = qkv_ref[:, (3 * p + 1) * pair : (3 * p + 2) * pair]
        values = qkv_ref[:, (3 * p + 2) * pair : (3 * p + 3) * pair]

        def chunk_step(chunk, carry):
            rows = pl.ds(pl.multiple_of(chunk * SHORT, SHORT), SHORT)
            queries = qkv_ref[rows, 3 * p * pair : (3 * p + 1) * pair] * jnp.asarray(0.125, BF)
            mask = mask_row(kind, chunk, count)
            found = []
            stats = lse_ref[rows, :] if p > 0 else jnp.zeros((SHORT, 128), F32)
            lane = lax.broadcasted_iota(jnp.int32, stats.shape, 1)
            for head in range(2):
                mine = jnp.where(head_lanes(queries, head), queries, jnp.zeros_like(queries))
                scores = dot_nt(mine, keys) + mask
                top = jnp.max(scores, axis=1, keepdims=True)
                powers = jnp.exp(scores - top)
                total = jnp.sum(powers, axis=1, keepdims=True)
                probs = powers * (1.0 / total)
                found.append(dot(probs.astype(BF), values))
                stats = jnp.where(lane == 2 * p + head, top + jnp.log(total), stats)
            lse_ref[rows, :] = stats
            both = jnp.where(head_lanes(found[0], 0), found[0], found[1])
            context_ref[rows, p * pair : (p + 1) * pair] = both.astype(BF)
            return carry

        lax.fori_loop(0, count // SHORT, chunk_step, 0)
    partial_ref[...] = dot(context_ref[...], wo_ref[...]).astype(BF)


def attention_backward_kernel(
    kind_ref, d_second_ref, mine_ref, theirs_ref, sum_ref, vec_ref,
    x_ref, qkv_ref, context_ref, lse_ref, wa_ref, wb_ref, wo_ref,
    ga_ref, gb_ref, gout_ref, partial_ref, sums_ref, d_first_ref, norm_sums_ref,
    dbranch_ref, dcontext_ref, dqkv_ref, dk_ref, dv_ref,
):
    back_first(
        d_second_ref, mine_ref, theirs_ref, sum_ref, vec_ref,
        d_first_ref, dbranch_ref, norm_sums_ref,
    )
    count = x_ref.shape[0]
    wide = wa_ref.shape[1]
    pair = 2 * HEAD_DIM
    kind = kind_ref[0]
    d_branch = dbranch_ref[...]
    dcontext_ref[...] = dot_nt(d_branch, wo_ref[...]).astype(BF)
    gout_ref[...] = dot_tn(context_ref[...], d_branch).astype(BF)
    for p in range(HEADS // 4):
        keys = qkv_ref[:, (3 * p + 1) * pair : (3 * p + 2) * pair]
        values = qkv_ref[:, (3 * p + 2) * pair : (3 * p + 3) * pair]
        dk_ref[...] = jnp.zeros_like(dk_ref)
        dv_ref[...] = jnp.zeros_like(dv_ref)

        def chunk_step(chunk, carry):
            rows = pl.ds(pl.multiple_of(chunk * SHORT, SHORT), SHORT)
            queries = qkv_ref[rows, 3 * p * pair : (3 * p + 1) * pair] * jnp.asarray(0.125, BF)
            d_context = dcontext_ref[rows, p * pair : (p + 1) * pair]
            mask = mask_row(kind, chunk, count)
            stats = lse_ref[rows, :]
            found = []
            for head in range(2):
                mine = jnp.where(head_lanes(queries, head), queries, jnp.zeros_like(queries))
                theirs = jnp.where(
                    head_lanes(d_context, head), d_context, jnp.zeros_like(d_context)
                )
                lse = stats[:, 2 * p + head : 2 * p + head + 1]
                probs = jnp.exp(dot_nt(mine, keys) + mask - lse)
                d_probs = dot_nt(theirs, values)
                row_dot = jnp.sum(d_probs * probs, axis=1, keepdims=True)
                d_scores = (probs * (d_probs - row_dot)).astype(BF)
                found.append(
                    (
                        dot(d_scores, keys) * 0.125,
                        dot_tn(d_scores, queries),
                        dot_tn(probs.astype(BF), d_context),
                    )
                )
            merged = [
                jnp.where(head_lanes(one, 0), one, other) for one, other in zip(*found)
            ]
            dqkv_ref[rows, 3 * p * pair : (3 * p + 1) * pair] = merged[0].astype(BF)
            dk_ref[...] += merged[1]
            dv_ref[...] += merged[2]
            return carry

        lax.fori_loop(0, count // SHORT, chunk_step, 0)
        dqkv_ref[:, (3 * p + 1) * pair : (3 * p + 2) * pair] = dk_ref[...].astype(BF)
        dqkv_ref[:, (3 * p + 2) * pair : (3 * p + 3) * pair] = dv_ref[...].astype(BF)
    d_a = dqkv_ref[:, :wide]
    d_b = dqkv_ref[:, wide:]
    x = x_ref[...]
    ga_ref[...] = dot_tn(x, d_a).astype(BF)
    gb_ref[...] = dot_tn(x, d_b).astype(BF)
    partial_ref[...] = (dot_nt(d_a, wa_ref[...]) + dot_nt(d_b, wb_ref[...])).astype(BF)
    sums_ref[:, :wide] = jnp.sum(d_a.astype(F32), axis=0, keepdims=True)
    sums_ref[:, wide:] = jnp.sum(d_b.astype(F32), axis=0, keepdims=True)


def kernel_call(body, shapes, scratch, *operands):
    in_vmem = pl.BlockSpec(memory_space=pltpu.VMEM)
    in_smem = pl.BlockSpec(memory_space=pltpu.SMEM)
    return pl.pallas_call(
        body,
        out_shape=shapes,
        in_specs=[in_smem if value.dtype == jnp.int32 else in_vmem for value in operands],
        out_specs=[in_vmem] * len(shapes),
        scratch_shapes=scratch,
        compiler_params=pltpu.CompilerParams(vmem_limit_bytes=VMEM_LIMIT),
        cost_estimate=pl.CostEstimate(flops=0, bytes_accessed=0, transcendentals=0),
    )(*operands)


def attention(row_kind, inputs_b, w_a, w_b, bias, w_out):
    count, width = inputs_b.shape
    half = w_out.shape[0]
    shapes = [
        jax.ShapeDtypeStruct((count, width), BF),
        jax.ShapeDtypeStruct((count, 3 * half), BF),
        jax.ShapeDtypeStruct((count, half), BF),
        jax.ShapeDtypeStruct((count, 128), F32),
    ]
    return kernel_call(
        attention_kernel, shapes, [], row_kind, inputs_b, w_a, w_b, bias, w_out
    )


def attention_backward(
    row_kind, d_second, mine, theirs, first_sum, vec, inputs_b, qkv, context, lse, w_a, w_b, w_out
):
    count, width = inputs_b.shape
    half = w_out.shape[0]
    shapes = [
        jax.ShapeDtypeStruct(w_a.shape, BF),
        jax.ShapeDtypeStruct(w_b.shape, BF),
        jax.ShapeDtypeStruct(w_out.shape, BF),
        jax.ShapeDtypeStruct((count, width), BF),
        jax.ShapeDtypeStruct((1, 3 * half), F32),
        jax.ShapeDtypeStruct((count, width), F32),
        jax.ShapeDtypeStruct((8, width), F32),
    ]
    scratch = [
        pltpu.VMEM((count, width), BF),
        pltpu.VMEM((count, half), BF),
        pltpu.VMEM((count, 3 * half), BF),
        pltpu.VMEM((count, 2 * HEAD_DIM), F32),
        pltpu.VMEM((count, 2 * HEAD_DIM), F32),
    ]
    return kernel_call(
        attention_backward_kernel, shapes, scratch, row_kind, d_second, mine, theirs, first_sum,
        vec, inputs_b, qkv, context, lse, w_a, w_b, w_out,
    )


def norm_rows(base, mine, theirs, vec):
    shapes = [jax.ShapeDtypeStruct(base.shape, kind) for kind in (F32, F32, BF)]
    return kernel_call(norm_kernel, shapes, [], base, mine, theirs, vec)


def hidden_layer(x, mine, theirs, vec, bias, up0, up1, down):
    count, hidden = x.shape[0], down.shape[0]
    shapes = [jax.ShapeDtypeStruct(x.shape, kind) for kind in (F32, F32, BF)]
    shapes += [jax.ShapeDtypeStruct((count, hidden), BF)] * 2
    shapes.append(jax.ShapeDtypeStruct(x.shape, BF))
    return kernel_call(
        hidden_kernel, shapes, [], x, mine, theirs, vec, bias, up0, up1, down
    )


def back_second(upstream, total, vec, act):
    shapes = [
        jax.ShapeDtypeStruct(total.shape, F32),
        jax.ShapeDtypeStruct(total.shape, BF),
        jax.ShapeDtypeStruct((act.shape[1], total.shape[1]), BF),
        jax.ShapeDtypeStruct((8, total.shape[1]), F32),
    ]
    body = functools.partial(back_second_kernel, len(upstream) > 1)
    return kernel_call(body, shapes, [], *upstream, total, vec, act)


def back_hidden(d_ffn, slope, normed_b, down, up0, up1):
    count, hidden = slope.shape
    width = normed_b.shape[1]
    shapes = [
        jax.ShapeDtypeStruct(up0.shape, BF),
        jax.ShapeDtypeStruct(up1.shape, BF),
        jax.ShapeDtypeStruct((count, width), BF),
        jax.ShapeDtypeStruct((1, hidden), F32),
    ]
    scratch = [pltpu.VMEM((count, hidden), BF)]
    return kernel_call(
        back_hidden_kernel, shapes, scratch, d_ffn, slope, normed_b, down, up0, up1
    )


def hidden_order(width, hidden_rows):
    group = width // (2 * hidden_rows)
    target = jnp.arange(width)
    source = (
        (target % (width // 2)) // hidden_rows * (2 * hidden_rows)
        + target // (width // 2) * hidden_rows
        + target % hidden_rows
    )
    del group
    return jnp.arange(width)[:, None] == source[None, :]


def shards(tokens, row_kind, w_qkv, w_out, w_up, w_down, bias_vectors, gains, bias_up, cotangent):
    chips = Chips()
    sequence = Sequence()
    core = chips.core
    count = chips.count
    device = 2 * chips.chip + core
    row_type = row_kind[0]
    rows, width = w_out.shape[1:]
    hidden = w_up.shape[2]
    hidden_rows = w_down.shape[1]
    half = width // 2
    panels = hidden // 2 // width
    own = tokens.shape[0]
    order = hidden_order(width, hidden_rows)

    pairs = HEADS // 4
    lane = half // pairs
    plan = Plan()
    state = State()

    def ordered(mine, theirs):
        return jnp.where(core == 0, mine, theirs), jnp.where(core == 0, theirs, mine)

    def pack_qkv():
        cols = w_qkv.reshape(LAYERS, rows, 3, 2, pairs, lane)

        def side(which):
            return jnp.swapaxes(pick(cols, which, 3), 2, 3).reshape(LAYERS, rows, 3 * half)

        feature = jnp.arange(width)[None, :] - rows * device == jnp.arange(rows)[:, None]
        unit = jnp.arange(hidden // 2)[None, :] - hidden_rows * chips.chip
        unit = unit == jnp.arange(hidden_rows)[:, None]
        table = jnp.concatenate([bias_vectors, gains], axis=1).reshape(LAYERS * 8, rows)
        table = dot(table, feature.astype(BF)).astype(BF)
        units = dot(bias_up, unit.astype(BF)).astype(BF)
        got = swap(side(1 - core), 1)
        table = table + swap(table, 1)
        cols = merge(side(core), got, core, 1)
        for layer in range(LAYERS):
            last = cols[layer, :, :, width:]
            vectors = [table[8 * layer : 8 * layer + 8]]
            vectors += [units[layer : layer + 1, i * width :][:, :width] for i in range(panels)]
            vectors.append(jnp.zeros((8 - panels, width), BF))
            state.gathers[ATTN, layer] = Gather(
                chips, sequence, EARLY[layer],
                jnp.concatenate(
                    [
                        cols[layer, :, :, :width].reshape(2 * rows, width),
                        jnp.concatenate([last[0], last[1]], axis=1),
                        w_out[layer],
                        *vectors,
                    ],
                    axis=0,
                ),
            )
        sequence.mark([state.gathers[ATTN, layer].held for layer in range(LAYERS)])

    groups = hidden // width

    def pack_up():
        value = sequence.gate(w_up).reshape(LAYERS * rows, hidden)
        stacked = jnp.concatenate(
            [value[:, i * width : (i + 1) * width] for i in range(groups)], axis=0
        )
        stacked = dot(stacked, order.astype(BF)).astype(BF)
        mine, sent = ordered(stacked[:, :half], stacked[:, half:])
        first, second = ordered(mine, swap(sent, 1))
        for layer in range(LAYERS):
            parts = []
            for i in range(panels):
                for value in (first, second):
                    cut = [
                        value[((2 * i + j) * LAYERS + layer) * rows :][:rows] for j in range(2)
                    ]
                    parts.append(jnp.concatenate(cut, axis=1))
            state.gathers[FFN, layer] = Gather(
                chips, sequence, EARLY[LAYERS + layer],
                jnp.concatenate(parts + [w_down[layer]], axis=0),
            )
        sequence.mark([state.gathers[FFN, layer].held for layer in range(LAYERS)])

    def read_vectors(layer, table):
        table = jnp.sum(table.astype(F32), axis=0)
        vec = table[:8]
        bias_q, bias_v = (
            jnp.where(core == 0, vec[i : i + 1, :half], vec[i : i + 1, half:]) for i in range(2)
        )
        bias = []
        for p in range(pairs):
            cut = slice(p * lane, (p + 1) * lane)
            bias += [bias_q[:, cut], jnp.zeros((1, lane), F32), bias_v[:, cut]]
        state.vec[layer] = vec
        state.bias_qkv[layer] = jnp.concatenate(bias, axis=1)
        state.bias_up[layer] = jnp.concatenate(
            [table[8 + i : 9 + i] for i in range(panels)], axis=1
        )

    def tokens_start():
        value = sequence.gate(tokens)
        sequence.mark(value)
        state.pair_tokens = (value, swap(value, 1))

    def tokens_end():
        values = sequence.gate(state.pair_tokens)
        state.x_b[0] = jnp.concatenate(ordered(*values), axis=0)
        state.x[0] = state.x_b[0].astype(F32)
        sequence.mark(state.x_b[0])

    def cotangent_start():
        value = sequence.gate(cotangent)
        sequence.mark(value)
        state.pair_cotangent = (value, swap(value, 1))

    def cotangent_end():
        values = sequence.gate(state.pair_cotangent)
        state.upstream = (jnp.concatenate(ordered(*values), axis=0),)
        sequence.mark(state.upstream)

    def out_exchange(layer):
        ends = [0, 2 * rows, 4 * rows, 4 * rows + 16]
        first, second, table = state.gathers[ATTN, layer].finish(list(zip(ends[:-1], ends[1:])))
        last, out_all = second[:, :rows], second[:, rows:]
        w_b = jnp.swapaxes(last.reshape(count, rows, 2, half), 1, 2)
        out_all = out_all.reshape(2, count // 2, rows, width)
        sent, w_b = pick(out_all, 1 - core, 0), w_b.reshape(width, half)
        read_vectors(layer, table)
        sequence.mark((sent, w_b, state.vec[layer]))
        full_out = merge(pick(out_all, core, 0), swap(sent, 1), core, 1).reshape(half, width)
        state.w_attn[layer] = (first.reshape(width, width), w_b, full_out)

    def hidden_weights(layer):
        ends = [2 * rows * i for i in range(panels + 1)]
        ends.append(ends[-1] + hidden_rows)
        *ups, down = state.gathers[FFN, layer].finish(list(zip(ends[:-1], ends[1:])))
        state.w_hidden[layer] = (
            down.reshape(hidden // 2, width), *(value.reshape(width, width) for value in ups)
        )

    def run_attention(layer):
        x_b, weights = sequence.gate((state.x_b[layer], state.w_attn[layer]))
        w_a, w_b, full_out = weights
        partial, *saved = attention(row_kind, x_b, w_a, w_b, state.bias_qkv[layer], full_out)
        sequence.mark(partial)
        state.w_attn[layer] = weights
        state.saved[layer] = (x_b, *saved)
        state.branch = (partial, swap(partial, 1))

    def run_hidden(layer):
        mine, theirs = sequence.gate(state.branch)
        down, up0, up1 = state.w_hidden[layer]
        first_sum, state.normed, *kept, partial = hidden_layer(
            state.x[layer], mine, theirs, state.vec[layer], state.bias_up[layer], up0, up1, down
        )
        sequence.mark(partial)
        state.first_sum[layer] = first_sum
        state.kept[layer] = kept
        state.branch = (partial, swap(partial, 1))

    def run_norm(layer):
        mine, theirs = sequence.gate(state.branch)
        second, x, x_b = norm_rows(state.normed, mine, theirs, state.vec[layer])
        state.second[layer], state.x[layer + 1], state.x_b[layer + 1] = second, x, x_b
        sequence.mark(second)

    def run_back_second(layer):
        upstream = sequence.gate(state.upstream)
        if layer < LAYERS - 1:
            upstream = (state.d_first, *upstream)
        act = state.kept[layer][1]
        d_second, d_ffn, g_down, sums = back_second(
            upstream, state.second[layer], state.vec[layer], act
        )
        state.d_second, state.d_ffn = d_second, d_ffn
        state.sums2[layer] = sums
        bundle = state.scatters[FFN, layer]
        bundle.start(0, [g_down.reshape(count, hidden_rows, width)])
        sequence.mark((d_ffn, bundle.sent))

    def run_back_hidden(layer):
        d_ffn = sequence.gate(state.d_ffn)
        normed_b, _, slope = state.kept[layer]
        *g_up, partial, units = back_hidden(d_ffn, slope, normed_b, *state.w_hidden[layer])
        bundle = state.scatters[FFN, layer]
        bundle.start(1, [value.reshape(count, 2 * rows, width) for value in g_up])
        sequence.mark((partial, bundle.sent))
        state.units[layer] = units
        state.branch = (partial, swap(partial, 1))

    def run_back_attention(layer):
        mine, theirs = sequence.gate(state.branch)
        x_b, qkv, context, lse = state.saved[layer]
        g_a, g_b, g_out, partial, sums, state.d_first, state.sums1[layer] = attention_backward(
            row_kind, state.d_second, mine, theirs, state.first_sum[layer], state.vec[layer],
            x_b, qkv, context, lse, *state.w_attn[layer],
        )
        sequence.mark(partial)
        state.pair[layer] = jnp.concatenate(
            [
                jnp.concatenate(
                    [sums[:, (3 * p + t) * lane :][:, :lane] for p in range(pairs)], axis=1
                )
                for t in (0, 2)
            ],
            axis=0,
        )
        if layer > 0:
            state.upstream = (partial, swap(partial, 1))
        else:
            mine, sent = ordered(partial[:own], partial[own:])
            state.upstream = (mine, swap(sent, 1))
        state.g_attn[layer] = (g_a, g_b, g_out)

    def sum_rows(layer):
        pair = state.pair[layer]
        nothing = jnp.zeros_like(pair)
        pair = jnp.concatenate(ordered(pair, nothing), axis=1)
        units = [state.units[layer][:, i * width :][:, :width] for i in range(panels)]
        small = jnp.concatenate([state.sums1[layer] + state.sums2[layer], pair, *units], axis=0)
        small = jnp.pad(small.astype(BF), ((0, 16 - small.shape[0]), (0, 0)))
        line = jnp.arange(16)[:, None]
        place = jnp.arange(width)[None, :]
        owner = jnp.where(
            line < 10, place // (2 * rows), ((line - 10) * width + place) // hidden_rows
        )
        mine = owner[None] == jnp.arange(count)[:, None, None]
        return jnp.where(mine, small[None], jnp.zeros((), BF))

    def back_terms(layer):
        g_a, g_b, g_out = sequence.gate(state.g_attn[layer])
        bundle = state.scatters[ATTN, layer]
        out_pair = g_out.reshape(count // 2, 2, rows, width)
        out_got = swap(pick(out_pair, 1 - core, 1), 1)
        out = merge(pick(out_pair, core, 1), out_got, core, 0).reshape(count, rows, width)
        g_b = g_b.reshape(count, 2, rows, half)
        last = jnp.concatenate([g_b[:, 0], g_b[:, 1]], axis=2)
        rest = jnp.concatenate([last, out, sum_rows(layer)], axis=1)
        rest = lax.optimization_barrier(rest)
        bundle.start(0, [g_a.reshape(count, 2 * rows, width), rest])
        sequence.mark(bundle.sent)

    def grad_end():
        mine, theirs = sequence.gate(state.upstream)
        d_first = lax.dynamic_slice_in_dim(state.d_first, core * own, own)
        state.grad_tokens = d_first + (mine.astype(F32) + theirs.astype(F32))
        sequence.mark(state.grad_tokens)

    def mixed_end():
        value = sequence.gate(state.x_b[LAYERS])
        state.mixed = lax.dynamic_slice_in_dim(value, core * own, own)
        sequence.mark(state.mixed)

    def finish_hidden(layer):
        down, *ups = state.scatters[FFN, layer].finish()
        sides = [
            jnp.concatenate([up[side * rows :][:rows] for up in ups], axis=1)
            for side in range(2)
        ]
        mine, sent = ordered(*sides)
        state.up_pair[layer] = (mine, swap(sent, 1))
        state.down[layer] = down

    def end_hidden(layer):
        first, second = ordered(*sequence.gate(state.up_pair[layer]))
        stacked = jnp.concatenate(
            [
                jnp.concatenate(
                    [value[:, i * half : (i + 1) * half] for value in (first, second)], axis=1
                )
                for i in range(groups)
            ],
            axis=0,
        )
        stacked = lax.dot_general(
            stacked, order.astype(F32), (((1,), (1,)), ((), ())),
            precision=lax.Precision.HIGHEST, preferred_element_type=F32,
        )
        state.up[layer] = jnp.concatenate(
            [stacked[i * rows : (i + 1) * rows] for i in range(groups)], axis=1
        )
        sequence.mark(state.up[layer])

    def finish_attention(layer):
        first, rest = state.scatters[ATTN, layer].finish()
        last, out, small = rest[:rows], rest[rows : 2 * rows], rest[2 * rows :]
        sides = [
            jnp.concatenate(
                [first[side * rows :][:rows], last[:, side * half :][:, :half]], axis=1
            )
            for side in range(2)
        ]
        mine, sent = ordered(*sides)
        pair = jnp.pad(small[8:], ((0, 0), (0, mine.shape[1] - width)))
        sent = jnp.concatenate([sent, pair], axis=0)
        state.qkv_pair[layer] = (mine, swap(sent, 1))
        state.out[layer] = out
        state.small_rows[layer] = small

    def end_attention(layer):
        mine, theirs = sequence.gate(state.qkv_pair[layer])
        small = state.small_rows[layer]
        small = jnp.concatenate([theirs[rows : rows + 2, :width] + small[8:10], small], axis=0)
        features = lax.dynamic_slice_in_dim(small, rows * device, rows, axis=1)
        per_row = width // hidden_rows
        units = lax.dynamic_slice(
            small,
            (12 + chips.chip // per_row, hidden_rows * (chips.chip % per_row)),
            (1, hidden_rows),
        )
        state.vectors[layer] = features[:6]
        state.gains[layer] = features[6:8]
        state.unit_sums[layer] = units[0]
        values = ordered(mine, theirs[:rows])
        state.qkv[layer] = jnp.concatenate(
            [
                value[:, (3 * p + t) * lane :][:, :lane]
                for t in range(3)
                for value in values
                for p in range(pairs)
            ],
            axis=1,
        )
        sequence.mark(state.qkv[layer])

    def call(function, *args):
        return lambda: function(*args)

    low = len(chips.low)
    size = (1.0, 2.0)
    add = plan.add

    def pair_send(label):
        return [(label, (("p", 0.0),), 1)]

    def plane(length):
        return (("x", length), ("y", length))

    add("pq", 0, 6.0, [], pack_qkv)
    add("pu", 2, 3.0, [("g", ATTN, 0)], pack_up)
    add("tok", 8, 0.5, ["pu"], tokens_start, pair_send("x0"))
    add("te", 7, 1.5, ["x0"], tokens_end)
    add("cot", 9, 0.5, [("m", 1, 0)], cotangent_start, pair_send("ct"))
    add("ce", 9, 1.2, ["ct"], cotangent_end)
    bundles = [(ATTN, 0), (FFN, 0), (ATTN, 1), (FFN, 1)]
    for rank, (kind, layer) in enumerate(bundles):
        needs = ["pq" if kind == ATTN else "pu"]

        def start(kind=kind, layer=layer):
            state.gathers[kind, layer].start()

        def advance(kind=kind, layer=layer):
            state.gathers[kind, layer].advance()

        units = 7.0 / 3 if kind == ATTN else 4.0
        tops = [("top", 2), ("top", 1)]
        lows = [("low", step) for step in range(low)]
        early = EARLY[LAYERS * kind + layer]
        steps = lows[:1] + tops + lows[1:] if early else tops + lows
        need = None
        held = 1
        for number, (bits, step) in enumerate(steps):
            length = UNIT / 2 * units * held
            held *= 2
            if bits == "low":
                links = plane(length)
            elif step == 2:
                links = (("z", 2 * length), ("w", 4 * length + 1.5))
            else:
                links = (("z", 2 * length),)
            sent = ("gx", kind, layer, number)
            if number == 0:
                add(("g", kind, layer), 1 + rank, 3.5, needs, start, [(sent, links, 1)])
            else:
                add(
                    ("gs", kind, layer, number), 1 + rank, 1.0 + 0.1 * held + (2.8 if len(links) > 1 and links[1][0] == "w" else 1.4),
                    [need], advance, [(sent, links, 1)],
                )
            need = sent
        if kind == ATTN:
            add(
                ("go", layer), 1 + rank, 4.5, [need], call(out_exchange, layer),
                pair_send(("w", kind, layer)),
            )
        else:
            add(("w", kind, layer), 1 + rank, 1.6, [need], call(hidden_weights, layer))
    need = "te"
    for layer in range(LAYERS):
        add(
            ("m", 0, layer), 10, 12.7, [need, ("w", ATTN, layer)],
            call(run_attention, layer), pair_send(("p", 0, layer)),
        )
        add(
            ("m", 1, layer), 10, 6.0, [("p", 0, layer), ("w", FFN, layer)],
            call(run_hidden, layer), pair_send(("p", 1, layer)),
        )
        need = ("m", 2, layer)
        add(need, 10, 3.0, [("p", 1, layer)], call(run_norm, layer))
    add("mix", 20, 1.0, [need], mixed_end)

    needs = [need, "ce"]
    for layer in reversed(range(LAYERS)):
        state.scatters[FFN, layer] = Scatter(chips, sequence, 2, LATE[LAYERS + layer])
        state.scatters[ATTN, layer] = Scatter(chips, sequence, 1, LATE[layer])
        add(
            ("b", 0, layer), 10, 5.0, needs, call(run_back_second, layer),
            [(("r", FFN, layer, 0), plane(UNIT * 8), 1)],
        )
        add(
            ("b", 1, layer), 10, 6.5, [("b", 0, layer)], call(run_back_hidden, layer),
            [(("r", FFN, layer, 1), plane(UNIT * 8), 1)] + pair_send(("p", 2, layer)),
        )
        add(
            ("b", 2, layer), 10, 17.2, [("p", 2, layer)], call(run_back_attention, layer),
            pair_send(("p", 3, layer)),
        )
        add(
            ("b", 3, layer), 9.5, 6.0, [("b", 2, layer)], call(back_terms, layer),
            [(("r", ATTN, layer, 0), plane(UNIT * 28 / 3), 1)],
        )
        needs = [("p", 3, layer)]
        for kind in (FFN, ATTN):
            need = [("r", kind, layer, part) for part in range(1 + kind)]
            rank = 1 + 2 * (LAYERS - 1 - layer) + (kind == ATTN)

            def reduce(kind=kind, layer=layer):
                state.scatters[kind, layer].advance()

            units = 7.0 / 3 if kind == ATTN else 4.0
            tops = [("top", 1), ("top", 2)]
            lows = [("low", step) for step in range(low - 1)][::-1]
            late = LATE[LAYERS * kind + layer]
            steps = lows[:-1] + tops + lows[-1:] if late else lows + tops
            held = 2 * count // 4
            for number, (bits, step) in enumerate(steps):
                held //= 2
                length = UNIT / 2 * units * held
                cost = 1.0 + 0.1 * held
                if bits == "low":
                    cost, links = cost + 1.4, plane(length)
                elif step == 2:
                    cost, links = cost + 2.8, (("z", 2 * length), ("w", 4 * length + 1.5))
                else:
                    cost, links = cost + 1.4, (("z", 2 * length),)
                sent = ("rx", kind, layer, number)
                add(("rs", kind, layer, number), rank, cost, need, reduce, [(sent, links, 1)])
                need = [sent]
            last = finish_hidden if kind == FFN else finish_attention
            add(
                ("rf", kind, layer), 19, 2.0, need, call(last, layer),
                pair_send(("re", kind, layer)),
            )
            last = end_hidden if kind == FFN else end_attention
            add(("ro", kind, layer), 20, 2.5, [("re", kind, layer)], call(last, layer))
    add("grad", 18, 1.2, needs, grad_end)
    plan.run()

    def stacked(values):
        return jnp.stack([values[layer] for layer in range(LAYERS)])

    return (
        state.mixed,
        state.grad_tokens,
        stacked(state.qkv),
        stacked(state.out),
        stacked(state.up),
        stacked(state.down),
        stacked(state.vectors),
        stacked(state.gains),
        stacked(state.unit_sums),
    )


def solution(mesh):
    placed = (
        P("fsdp", None),
        P("fsdp"),
        P(None, "fsdp", None),
        P(None, "fsdp", None),
        P(None, "fsdp", None),
        P(None, "fsdp", None),
        P(None, None, "fsdp"),
        P(None, None, "fsdp"),
        P(None, "fsdp"),
        P("fsdp", None),
    )
    return jax.shard_map(
        shards,
        mesh=mesh,
        in_specs=placed,
        out_specs=(
            P("fsdp", None),
            P("fsdp", None),
            P(None, "fsdp", None),
            P(None, "fsdp", None),
            P(None, "fsdp", None),
            P(None, "fsdp", None),
            P(None, None, "fsdp"),
            P(None, None, "fsdp"),
            P(None, "fsdp"),
        ),
        check_vma=False,
    )
```

```python
import functools

import jax
import jax.numpy as jnp
from jax import lax
from jax.experimental import pallas as pl
from jax.experimental.pallas import tpu as pltpu
from jax.sharding import PartitionSpec as P

HEADS = 12
HEAD_DIM = 64
LAYERS = 2
SHORT = 128
AXIS = "fsdp"

EPSILON = 1e-05
MASKED_SCORE = -1e30
BF = jnp.bfloat16
F32 = jnp.float32
LATENCY = 2.5
UNIT = 1.48
ATTN, FFN = 0, 1
OPEN_SENDS = 5
VMEM_LIMIT = 16 * 2**20
EARLY = (False, False, False, False)
LATE = (False, False, False, False)
ORDER = (
    0, 6, 1, 2, 11, 7, 16, 8, 3, 12, 21, 9, 13, 17, 14, 10, 22, 23, 18, 26, 15, 19, 27,
    28, 24, 20, 4, 29, 25, 30, 5, 31, 33, 34, 35, 36, 37, 47, 48, 49, 38, 42, 51, 39, 43,
    50, 52, 44, 61, 40, 56, 53, 45, 57, 58, 54, 59, 32, 55, 60, 41, 46,
)


def dot(left, right):
    return jnp.dot(left, right, preferred_element_type=F32)


def dot_tn(left, right):
    return lax.dot_general(left, right, (((0,), (0,)), ((), ())), preferred_element_type=F32)


def dot_nt(left, right):
    return lax.dot_general(left, right, (((1,), (1,)), ((), ())), preferred_element_type=F32)


def swap(value, mask):
    pairs = [(source, source ^ mask) for source in range(lax.axis_size(AXIS))]
    return lax.ppermute(value, AXIS, pairs)


def merge(mine, theirs, bit, axis):
    first = jnp.where(bit == 0, mine, theirs)
    second = jnp.where(bit == 0, theirs, mine)
    return jnp.stack([first, second], axis=axis)


def pick(pair, index, axis):
    return lax.dynamic_index_in_dim(pair, index, axis, keepdims=False)


class Chips:
    def __init__(self):
        device = lax.axis_index(AXIS)
        self.count = lax.axis_size(AXIS) // 2
        self.core = device % 2
        self.chip = device // 2
        self.step = self.count // 4
        self.top = self.chip // self.step
        self.low = list(range(self.count.bit_length() - 3))
        self.info = self.table()

    def bit(self, place):
        return (self.chip // 2**place) % 2

    def plane_bit(self, step):
        return jnp.where(self.core == 0, self.bit(step), self.bit(len(self.low) - 1 - step))

    def plane_swap(self, value, step):
        masks = (2 * 2**step, 2 * 2 ** (len(self.low) - 1 - step))
        pairs = [(source, source ^ masks[source % 2]) for source in range(2 * self.count)]
        return lax.ppermute(value, AXIS, pairs)

    def table(self):
        bits = [self.plane_bit(step) for step in range(len(self.low))]
        entries = [self.core] + bits + [self.top % 2, self.top // 2]
        return jnp.stack(entries).astype(jnp.int32)


def half_place(table, step, index, own):
    bit = table[1 + step]
    bit = bit if own else 1 - bit
    return jnp.where(table[0] == 0, 2**step * bit + index, 2 * index + bit)


def merge_place(table, kind, step, low, half, index, own):
    if kind == "low":
        return half_place(table, step, index, own)
    bit = table[low + step]
    return half * (bit if own else 1 - bit) + index


class Sequence:
    def __init__(self):
        self.last = None

    def gate(self, values):
        if self.last is None:
            return values
        values, _ = lax.optimization_barrier((values, self.last))
        return values

    def mark(self, values):
        self.last = values


class State:
    def __getattr__(self, name):
        value = {}
        setattr(self, name, value)
        return value


class Plan:
    def __init__(self):
        self.pieces = []

    def add(self, name, rank, cost, needs, run, sends=()):
        self.pieces.append((name, rank, cost, needs, run, sends))

    def greedy(self):
        now = 0.0
        ready = {}
        free = {}
        open_sends = {}
        waiting = list(range(len(self.pieces)))
        order = []

        def fits(piece):
            held = sum(weight for label, weight in open_sends.items() if label not in piece[3])
            added = sum(weight for _, _, weight in piece[5])
            return added == 0 or held + added <= OPEN_SENDS

        while waiting:
            known = []
            for place in waiting:
                piece = self.pieces[place]
                if all(need in ready for need in piece[3]):
                    time = max([ready[need] for need in piece[3]], default=0.0)
                    known.append((time, piece[1], place))
            known = [entry for entry in known if fits(self.pieces[entry[2]])] or known
            able = [entry[1:] for entry in known if entry[0] <= now]
            place = min(able)[1] if able else min(known)[2]
            name, _, cost, needs, _, sends = self.pieces[place]
            now = max([now] + [ready[need] for need in needs]) + cost
            ready[name] = now
            for need in needs:
                open_sends.pop(need, None)
            for label, links, weight in sends:
                ready[label] = 0.0
                for link, length in links:
                    free[link] = max(now, free.get(link, 0.0)) + length
                    ready[label] = max(ready[label], free[link] + LATENCY)
                if weight > 0:
                    open_sends[label] = weight
            waiting.remove(place)
            order.append(place)
        return order

    def run(self):
        order = ORDER if len(ORDER) == len(self.pieces) else self.greedy()
        for place in order:
            self.pieces[place][4]()


class Gather:
    def __init__(self, chips, sequence, early, piece):
        self.chips, self.sequence = chips, sequence
        low = [("low", step) for step in range(len(chips.low))]
        top = [("top", 2), ("top", 1)]
        self.steps = low[:1] + top + low[1:] if early else top + low
        self.held = piece[None, None]

    def start(self):
        self.held = self.sequence.gate(self.held)
        self.sequence.mark(self.held)
        self.send()

    def send(self):
        kind, step = self.steps[0]
        if kind == "low":
            self.coming = self.chips.plane_swap(self.held, step)
        else:
            self.coming = swap(self.held, 2 * step * self.chips.step)

    def merged(self, ranges=None):
        chips = self.chips
        coming = self.sequence.gate(self.coming)
        kind, step = self.steps.pop(0)
        if kind == "low":
            return merge_rows(chips, kind, step, self.held, coming, ranges)
        lead, half, height, width = self.held.shape
        flat = [value.reshape(lead, 1, half * height, width) for value in (self.held, coming)]
        return merge_rows(chips, kind, step, *flat).reshape(2 * lead, half, height, width)

    def advance(self):
        self.held = self.merged()
        self.sequence.mark(self.held)
        self.send()

    def finish(self, ranges):
        while len(self.steps) > 1:
            self.advance()
        results = self.merged(ranges)
        results = [whole.reshape((self.chips.count,) + whole.shape[2:]) for whole in results]
        self.sequence.mark(results)
        return results


def merge_kernel(ranges, place, table_ref, mine_ref, theirs_ref, *out_refs):
    for index in range(mine_ref.shape[1]):
        own, other = place(table_ref, index, True), place(table_ref, index, False)
        for lead in range(mine_ref.shape[0]):
            for (start, stop), out_ref in zip(ranges, out_refs):
                out_ref[lead, own] = mine_ref[lead, index, start:stop]
                out_ref[lead, other] = theirs_ref[lead, index, start:stop]


def merge_rows(chips, kind, step, mine, theirs, ranges=None):
    half = mine.shape[1]
    cuts = ranges or [(0, mine.shape[2])]

    def place(table, index, own):
        return merge_place(table, kind, step, len(chips.low), half, index, own)

    shapes = [
        jax.ShapeDtypeStruct((mine.shape[0], 2 * half, stop - start, mine.shape[3]), BF)
        for start, stop in cuts
    ]
    if all(edge % 16 == 0 for cut in cuts for edge in cut):
        results = kernel_call(
            functools.partial(merge_kernel, cuts, place), shapes, [], chips.info, mine, theirs
        )
    else:
        sides = [place(chips.info, jnp.arange(half), own) for own in (True, False)]
        results = []
        for (start, stop), shape in zip(cuts, shapes):
            whole = jnp.zeros(shape.shape, BF)
            for side, value in zip(sides, (mine, theirs)):
                whole = whole.at[:, side].set(value[:, :, start:stop])
            results.append(whole)
    return results if ranges else results[0]


class Scatter:
    def __init__(self, chips, sequence, count, late):
        self.chips, self.sequence = chips, sequence
        low = [("low", step) for step in range(len(chips.low) - 1)][::-1]
        top = [("top", 1), ("top", 2)]
        self.steps = low[:-1] + top + low[-1:] if late else low + top
        self.arrays = [None] * count
        self.coming = [None] * count
        self.heights = None

    def start(self, part, arrays):
        chips = self.chips
        step = len(chips.low) - 1
        shape = (4, 2 ** len(chips.low))
        arrays = [value.reshape(shape + value.shape[1:]) for value in arrays]
        self.arrays[part] = arrays
        sent = send_rows(chips, step, arrays)
        self.coming[part] = chips.plane_swap(sent, step)
        self.sent = sent

    def advance(self):
        chips = self.chips
        coming = self.sequence.gate(self.coming)
        first = self.heights is None
        if first:
            self.heights = [value.shape[2] for part in self.arrays for value in part]
        else:
            self.arrays, coming = [[self.kept]], [coming]
        kind, step = self.steps.pop(0)
        if kind == "top":
            self.arrays = [
                [value.reshape((-1, 2 * value.shape[1]) + value.shape[2:]) for value in part]
                for part in self.arrays
            ]
            coming = [got.reshape((-1, 2 * got.shape[1]) + got.shape[2:]) for got in coming]
        sent, self.kept = fold_rows(chips, kind, step, first, self.arrays, coming)
        self.sequence.mark(sent)
        if kind == "low":
            self.coming = chips.plane_swap(sent, step)
        else:
            self.coming = swap(sent, 2 * step * chips.step)

    def finish(self):
        coming = self.sequence.gate(self.coming)
        total = self.kept[0, 0] + coming[0, 0].astype(F32)
        self.sequence.mark(total)
        ends = [sum(self.heights[:i]) for i in range(len(self.heights) + 1)]
        return [total[start:stop] for start, stop in zip(ends[:-1], ends[1:])]


def send_kernel(step, heights, table_ref, *refs):
    *array_refs, sent_ref = refs
    for index in range(sent_ref.shape[1]):
        place = half_place(table_ref, step, index, False)
        for lead in range(sent_ref.shape[0]):
            row = 0
            for height, ref in zip(heights, array_refs):
                sent_ref[lead, index, row : row + height] = ref[lead, place]
                row += height


def send_rows(chips, step, arrays):
    heights = [value.shape[2] for value in arrays]
    shape = (arrays[0].shape[0], 2**step, sum(heights), arrays[0].shape[3])
    if any(height % 16 for height in heights):
        places = half_place(chips.info, step, jnp.arange(2**step), False)
        return jnp.concatenate([jnp.take(value, places, axis=1) for value in arrays], axis=2)
    (sent,) = kernel_call(
        functools.partial(send_kernel, step, heights), [jax.ShapeDtypeStruct(shape, BF)], [],
        chips.info, *arrays,
    )
    return sent


def fold_kernel(layout, place, table_ref, *refs):
    *refs, sent_ref, kept_ref = refs
    for index in range(sent_ref.shape[1]):
        for own, out_ref in enumerate((sent_ref, kept_ref)):
            source, came = place(table_ref, index, own == 1)
            for lead in range(sent_ref.shape[0]):
                for array, got, start, height, row in layout:
                    mine = refs[array][lead, source]
                    theirs = refs[got][lead, came, start : start + height]
                    total = mine.astype(F32) + theirs.astype(F32)
                    out_ref[lead, index, row : row + height] = total.astype(out_ref.dtype)


def fold_rows(chips, kind, step, first, parts, coming):
    arrays = [value for part in parts for value in part]
    layout = []
    row = 0
    for part, got in zip(range(len(parts)), range(len(arrays), len(arrays) + len(coming))):
        start = 0
        for value in parts[part]:
            height = value.shape[2]
            layout.append((len(layout), got, start, height, row))
            start += height
            row += height
    half = coming[0].shape[1] // 2
    low = len(chips.low)

    def place(table, index, own):
        if kind == "low":
            came = half_place(table, step, index, own)
            return (half_place(table, low - 1, came, True) if first else came), came
        bit = table[low + step]
        bit = bit if own else 1 - bit
        came = half * bit + index
        if not first:
            return came, came
        return 2**low * bit + half_place(table, low - 1, index, True), came

    shape = (arrays[0].shape[0], half, row, arrays[0].shape[3])
    if any(value.shape[2] % 16 for value in arrays):
        results = []
        for own, dtype in ((False, BF), (True, F32)):
            source, came = place(chips.info, jnp.arange(half), own)
            totals = []
            for array, got, start, height, _ in layout:
                theirs = jnp.take(coming[got - len(arrays)], came, axis=1)
                theirs = theirs[:, :, start : start + height].astype(F32)
                totals.append(jnp.take(arrays[array], source, axis=1).astype(F32) + theirs)
            results.append(jnp.concatenate(totals, axis=2).astype(dtype))
        return results
    return kernel_call(
        functools.partial(fold_kernel, layout, place),
        [jax.ShapeDtypeStruct(shape, kind) for kind in (BF, F32)], [],
        chips.info, *arrays, *coming,
    )


ROOT_HALF = 0.7071067811865476
DENSITY = 0.3989422804014327


def unit_rows(values):
    centre = values - jnp.mean(values, axis=1, keepdims=True)
    scale = lax.rsqrt(jnp.mean(centre * centre, axis=1, keepdims=True) + EPSILON)
    return centre * scale, scale


def norm_kernel(base_ref, mine_ref, theirs_ref, vec_ref, sum_ref, out_ref, out_b_ref):
    def chunk_step(chunk, carry):
        rows = pl.ds(pl.multiple_of(chunk * SHORT, SHORT), SHORT)
        total = base_ref[rows, :] + (
            mine_ref[rows, :].astype(F32) + theirs_ref[rows, :].astype(F32)
        ) + vec_ref[3:4, :]
        sum_ref[rows, :] = total
        unit, _ = unit_rows(total)
        output = unit * vec_ref[7:8, :] + vec_ref[5:6, :]
        out_ref[rows, :] = output
        out_b_ref[rows, :] = output.astype(BF)
        return carry

    lax.fori_loop(0, base_ref.shape[0] // SHORT, chunk_step, 0)


def hidden_kernel(
    x_ref, mine_ref, theirs_ref, vec_ref, bias_ref, up0_ref, up1_ref, down_ref,
    sum_ref, normed_ref, normed_b_ref, act_ref, slope_ref, partial_ref,
):
    def chunk_step(chunk, carry):
        rows = pl.ds(pl.multiple_of(chunk * SHORT, SHORT), SHORT)
        total = x_ref[rows, :] + (
            mine_ref[rows, :].astype(F32) + theirs_ref[rows, :].astype(F32) + vec_ref[2:3, :]
        )
        sum_ref[rows, :] = total
        unit, _ = unit_rows(total)
        normed = unit * vec_ref[6:7, :] + vec_ref[4:5, :]
        normed_ref[rows, :] = normed
        normed_b_ref[rows, :] = normed.astype(BF)
        return carry

    lax.fori_loop(0, x_ref.shape[0] // SHORT, chunk_step, 0)
    width = up0_ref.shape[1]
    step = 256
    for panel, up_ref in enumerate((up0_ref, up1_ref)):
        for start in range(0, width, step):
            place = panel * width + start
            pre = dot(normed_b_ref[...], up_ref[:, start : start + step])
            pre = pre + bias_ref[:, place : place + step]
            share = 0.5 + 0.5 * lax.erf(pre * ROOT_HALF)
            slope = share + pre * (DENSITY * jnp.exp(pre * pre * -0.5))
            act_ref[:, place : place + step] = (pre * share).astype(BF)
            slope_ref[:, place : place + step] = slope.astype(BF)
    partial_ref[...] = dot(act_ref[...], down_ref[...]).astype(BF)


def norm_back(upstream, total, gain):
    unit, scale = unit_rows(total)
    scaled = upstream * gain
    first = jnp.mean(scaled, axis=1, keepdims=True)
    second = jnp.mean(scaled * unit, axis=1, keepdims=True)
    return (
        scale * (scaled - first - unit * second),
        jnp.sum(upstream * unit, axis=0, keepdims=True),
        jnp.sum(upstream, axis=0, keepdims=True),
    )


def back_second_kernel(has_base, *refs):
    base_refs, refs = refs[: 3 if has_base else 1], refs[3 if has_base else 1 :]
    sum_ref, vec_ref, act_ref, d_second_ref, d_ffn_ref, g_down_ref, sums_ref = refs
    sums_ref[...] = jnp.zeros_like(sums_ref)

    def chunk_step(chunk, carry):
        rows = pl.ds(pl.multiple_of(chunk * SHORT, SHORT), SHORT)
        upstream = base_refs[0][rows, :].astype(F32)
        if has_base:
            upstream = upstream + (
                base_refs[1][rows, :].astype(F32) + base_refs[2][rows, :].astype(F32)
            )
        d_second, d_gain, d_shift = norm_back(upstream, sum_ref[rows, :], vec_ref[7:8, :])
        d_second_ref[rows, :] = d_second
        d_ffn = d_second.astype(BF)
        d_ffn_ref[rows, :] = d_ffn
        sums_ref[1:2, :] += jnp.sum(d_ffn.astype(F32), axis=0, keepdims=True)
        sums_ref[3:4, :] += d_shift
        sums_ref[5:6, :] += d_gain
        return carry

    lax.fori_loop(0, sum_ref.shape[0] // SHORT, chunk_step, 0)
    g_down_ref[...] = dot_tn(act_ref[...], d_ffn_ref[...]).astype(BF)


def back_hidden_kernel(
    d_ffn_ref, slope_ref, normed_b_ref, down_ref, up0_ref, up1_ref,
    g_up0_ref, g_up1_ref, partial_ref, sums_ref, d_pre_ref,
):
    hidden = slope_ref.shape[1]
    step = 256
    for place in range(0, hidden, step):
        d_act = dot_nt(d_ffn_ref[...], down_ref[place : place + step, :])
        d_pre = (d_act * slope_ref[:, place : place + step].astype(F32)).astype(BF)
        d_pre_ref[:, place : place + step] = d_pre
        sums_ref[:, place : place + step] = jnp.sum(d_pre.astype(F32), axis=0, keepdims=True)
    width = up0_ref.shape[1]
    g_up0_ref[...] = dot_tn(normed_b_ref[...], d_pre_ref[:, :width]).astype(BF)
    g_up1_ref[...] = dot_tn(normed_b_ref[...], d_pre_ref[:, width:]).astype(BF)
    partial_ref[...] = (
        dot_nt(d_pre_ref[:, :width], up0_ref[...]) + dot_nt(d_pre_ref[:, width:], up1_ref[...])
    ).astype(BF)


def back_first(
    d_second_ref, mine_ref, theirs_ref, sum_ref, vec_ref, d_first_ref, dbranch_ref, sums_ref
):
    sums_ref[...] = jnp.zeros_like(sums_ref)

    def chunk_step(chunk, carry):
        rows = pl.ds(pl.multiple_of(chunk * SHORT, SHORT), SHORT)
        upstream = d_second_ref[rows, :] + (
            mine_ref[rows, :].astype(F32) + theirs_ref[rows, :].astype(F32)
        )
        d_first, d_gain, d_shift = norm_back(upstream, sum_ref[rows, :], vec_ref[6:7, :])
        d_first_ref[rows, :] = d_first
        d_branch = d_first.astype(BF)
        dbranch_ref[rows, :] = d_branch
        sums_ref[0:1, :] += jnp.sum(d_branch.astype(F32), axis=0, keepdims=True)
        sums_ref[2:3, :] += d_shift
        sums_ref[4:5, :] += d_gain
        return carry

    lax.fori_loop(0, sum_ref.shape[0] // SHORT, chunk_step, 0)


def head_lanes(value, head):
    lane = lax.broadcasted_iota(jnp.int32, value.shape, 1)
    return (lane // (value.shape[1] // 2)) == head


def mask_row(kind, chunk, count):
    place = lax.broadcasted_iota(jnp.int32, (1, count), 1)
    allowed = (place // SHORT == chunk) | (kind == 1)
    return jnp.where(allowed, 0.0, MASKED_SCORE)


def attention_kernel(
    kind_ref, x_ref, wa_ref, wb_ref, bias_ref, wo_ref, partial_ref, qkv_ref, context_ref, lse_ref
):
    count = x_ref.shape[0]
    wide = wa_ref.shape[1]
    pair = 2 * HEAD_DIM
    kind = kind_ref[0]
    x = x_ref[...]
    bias = bias_ref[...]
    qkv_ref[:, :wide] = (dot(x, wa_ref[...]) + bias[:, :wide]).astype(BF)
    qkv_ref[:, wide:] = (dot(x, wb_ref[...]) + bias[:, wide:]).astype(BF)
    for p in range(HEADS // 4):
        keys = qkv_ref[:, (3 * p + 1) * pair : (3 * p + 2) * pair]
        values = qkv_ref[:, (3 * p + 2) * pair : (3 * p + 3) * pair]

        def chunk_step(chunk, carry):
            rows = pl.ds(pl.multiple_of(chunk * SHORT, SHORT), SHORT)
            queries = qkv_ref[rows, 3 * p * pair : (3 * p + 1) * pair] * jnp.asarray(0.125, BF)
            mask = mask_row(kind, chunk, count)
            found = []
            stats = lse_ref[rows, :] if p > 0 else jnp.zeros((SHORT, 128), F32)
            lane = lax.broadcasted_iota(jnp.int32, stats.shape, 1)
            for head in range(2):
                mine = jnp.where(head_lanes(queries, head), queries, jnp.zeros_like(queries))
                scores = dot_nt(mine, keys) + mask
                top = jnp.max(scores, axis=1, keepdims=True)
                powers = jnp.exp(scores - top)
                total = jnp.sum(powers, axis=1, keepdims=True)
                probs = powers * (1.0 / total)
                found.append(dot(probs.astype(BF), values))
                stats = jnp.where(lane == 2 * p + head, top + jnp.log(total), stats)
            lse_ref[rows, :] = stats
            both = jnp.where(head_lanes(found[0], 0), found[0], found[1])
            context_ref[rows, p * pair : (p + 1) * pair] = both.astype(BF)
            return carry

        lax.fori_loop(0, count // SHORT, chunk_step, 0)
    partial_ref[...] = dot(context_ref[...], wo_ref[...]).astype(BF)


def attention_backward_kernel(
    kind_ref, d_second_ref, mine_ref, theirs_ref, sum_ref, vec_ref,
    x_ref, qkv_ref, context_ref, lse_ref, wa_ref, wb_ref, wo_ref,
    ga_ref, gb_ref, gout_ref, partial_ref, sums_ref, d_first_ref, norm_sums_ref,
    dbranch_ref, dcontext_ref, dqkv_ref, dk_ref, dv_ref,
):
    back_first(
        d_second_ref, mine_ref, theirs_ref, sum_ref, vec_ref,
        d_first_ref, dbranch_ref, norm_sums_ref,
    )
    count = x_ref.shape[0]
    wide = wa_ref.shape[1]
    pair = 2 * HEAD_DIM
    kind = kind_ref[0]
    d_branch = dbranch_ref[...]
    dcontext_ref[...] = dot_nt(d_branch, wo_ref[...]).astype(BF)
    gout_ref[...] = dot_tn(context_ref[...], d_branch).astype(BF)
    for p in range(HEADS // 4):
        keys = qkv_ref[:, (3 * p + 1) * pair : (3 * p + 2) * pair]
        values = qkv_ref[:, (3 * p + 2) * pair : (3 * p + 3) * pair]
        dk_ref[...] = jnp.zeros_like(dk_ref)
        dv_ref[...] = jnp.zeros_like(dv_ref)

        def chunk_step(chunk, carry):
            rows = pl.ds(pl.multiple_of(chunk * SHORT, SHORT), SHORT)
            queries = qkv_ref[rows, 3 * p * pair : (3 * p + 1) * pair] * jnp.asarray(0.125, BF)
            d_context = dcontext_ref[rows, p * pair : (p + 1) * pair]
            mask = mask_row(kind, chunk, count)
            stats = lse_ref[rows, :]
            found = []
            for head in range(2):
                mine = jnp.where(head_lanes(queries, head), queries, jnp.zeros_like(queries))
                theirs = jnp.where(
                    head_lanes(d_context, head), d_context, jnp.zeros_like(d_context)
                )
                lse = stats[:, 2 * p + head : 2 * p + head + 1]
                probs = jnp.exp(dot_nt(mine, keys) + mask - lse)
                d_probs = dot_nt(theirs, values)
                row_dot = jnp.sum(d_probs * probs, axis=1, keepdims=True)
                d_scores = (probs * (d_probs - row_dot)).astype(BF)
                found.append(
                    (
                        dot(d_scores, keys) * 0.125,
                        dot_tn(d_scores, queries),
                        dot_tn(probs.astype(BF), d_context),
                    )
                )
            merged = [
                jnp.where(head_lanes(one, 0), one, other) for one, other in zip(*found)
            ]
            dqkv_ref[rows, 3 * p * pair : (3 * p + 1) * pair] = merged[0].astype(BF)
            dk_ref[...] += merged[1]
            dv_ref[...] += merged[2]
            return carry

        lax.fori_loop(0, count // SHORT, chunk_step, 0)
        dqkv_ref[:, (3 * p + 1) * pair : (3 * p + 2) * pair] = dk_ref[...].astype(BF)
        dqkv_ref[:, (3 * p + 2) * pair : (3 * p + 3) * pair] = dv_ref[...].astype(BF)
    d_a = dqkv_ref[:, :wide]
    d_b = dqkv_ref[:, wide:]
    x = x_ref[...]
    ga_ref[...] = dot_tn(x, d_a).astype(BF)
    gb_ref[...] = dot_tn(x, d_b).astype(BF)
    partial_ref[...] = (dot_nt(d_a, wa_ref[...]) + dot_nt(d_b, wb_ref[...])).astype(BF)
    sums_ref[:, :wide] = jnp.sum(d_a.astype(F32), axis=0, keepdims=True)
    sums_ref[:, wide:] = jnp.sum(d_b.astype(F32), axis=0, keepdims=True)


def kernel_call(body, shapes, scratch, *operands):
    in_vmem = pl.BlockSpec(memory_space=pltpu.VMEM)
    in_smem = pl.BlockSpec(memory_space=pltpu.SMEM)
    return pl.pallas_call(
        body,
        out_shape=shapes,
        in_specs=[in_smem if value.dtype == jnp.int32 else in_vmem for value in operands],
        out_specs=[in_vmem] * len(shapes),
        scratch_shapes=scratch,
        compiler_params=pltpu.CompilerParams(vmem_limit_bytes=VMEM_LIMIT),
        cost_estimate=pl.CostEstimate(flops=0, bytes_accessed=0, transcendentals=0),
    )(*operands)


def attention(row_kind, inputs_b, w_a, w_b, bias, w_out):
    count, width = inputs_b.shape
    half = w_out.shape[0]
    shapes = [
        jax.ShapeDtypeStruct((count, width), BF),
        jax.ShapeDtypeStruct((count, 3 * half), BF),
        jax.ShapeDtypeStruct((count, half), BF),
        jax.ShapeDtypeStruct((count, 128), F32),
    ]
    return kernel_call(
        attention_kernel, shapes, [], row_kind, inputs_b, w_a, w_b, bias, w_out
    )


def attention_backward(
    row_kind, d_second, mine, theirs, first_sum, vec, inputs_b, qkv, context, lse, w_a, w_b, w_out
):
    count, width = inputs_b.shape
    half = w_out.shape[0]
    shapes = [
        jax.ShapeDtypeStruct(w_a.shape, BF),
        jax.ShapeDtypeStruct(w_b.shape, BF),
        jax.ShapeDtypeStruct(w_out.shape, BF),
        jax.ShapeDtypeStruct((count, width), BF),
        jax.ShapeDtypeStruct((1, 3 * half), F32),
        jax.ShapeDtypeStruct((count, width), F32),
        jax.ShapeDtypeStruct((8, width), F32),
    ]
    scratch = [
        pltpu.VMEM((count, width), BF),
        pltpu.VMEM((count, half), BF),
        pltpu.VMEM((count, 3 * half), BF),
        pltpu.VMEM((count, 2 * HEAD_DIM), F32),
        pltpu.VMEM((count, 2 * HEAD_DIM), F32),
    ]
    return kernel_call(
        attention_backward_kernel, shapes, scratch, row_kind, d_second, mine, theirs, first_sum,
        vec, inputs_b, qkv, context, lse, w_a, w_b, w_out,
    )


def norm_rows(base, mine, theirs, vec):
    shapes = [jax.ShapeDtypeStruct(base.shape, kind) for kind in (F32, F32, BF)]
    return kernel_call(norm_kernel, shapes, [], base, mine, theirs, vec)


def hidden_layer(x, mine, theirs, vec, bias, up0, up1, down):
    count, hidden = x.shape[0], down.shape[0]
    shapes = [jax.ShapeDtypeStruct(x.shape, kind) for kind in (F32, F32, BF)]
    shapes += [jax.ShapeDtypeStruct((count, hidden), BF)] * 2
    shapes.append(jax.ShapeDtypeStruct(x.shape, BF))
    return kernel_call(
        hidden_kernel, shapes, [], x, mine, theirs, vec, bias, up0, up1, down
    )


def back_second(upstream, total, vec, act):
    shapes = [
        jax.ShapeDtypeStruct(total.shape, F32),
        jax.ShapeDtypeStruct(total.shape, BF),
        jax.ShapeDtypeStruct((act.shape[1], total.shape[1]), BF),
        jax.ShapeDtypeStruct((8, total.shape[1]), F32),
    ]
    body = functools.partial(back_second_kernel, len(upstream) > 1)
    return kernel_call(body, shapes, [], *upstream, total, vec, act)


def back_hidden(d_ffn, slope, normed_b, down, up0, up1):
    count, hidden = slope.shape
    width = normed_b.shape[1]
    shapes = [
        jax.ShapeDtypeStruct(up0.shape, BF),
        jax.ShapeDtypeStruct(up1.shape, BF),
        jax.ShapeDtypeStruct((count, width), BF),
        jax.ShapeDtypeStruct((1, hidden), F32),
    ]
    scratch = [pltpu.VMEM((count, hidden), BF)]
    return kernel_call(
        back_hidden_kernel, shapes, scratch, d_ffn, slope, normed_b, down, up0, up1
    )


def hidden_order(width, hidden_rows):
    group = width // (2 * hidden_rows)
    target = jnp.arange(width)
    source = (
        (target % (width // 2)) // hidden_rows * (2 * hidden_rows)
        + target // (width // 2) * hidden_rows
        + target % hidden_rows
    )
    del group
    return jnp.arange(width)[:, None] == source[None, :]


def shards(tokens, row_kind, w_qkv, w_out, w_up, w_down, bias_vectors, gains, bias_up, cotangent):
    chips = Chips()
    sequence = Sequence()
    core = chips.core
    count = chips.count
    device = 2 * chips.chip + core
    row_type = row_kind[0]
    rows, width = w_out.shape[1:]
    hidden = w_up.shape[2]
    hidden_rows = w_down.shape[1]
    half = width // 2
    panels = hidden // 2 // width
    own = tokens.shape[0]
    order = hidden_order(width, hidden_rows)

    pairs = HEADS // 4
    lane = half // pairs
    plan = Plan()
    state = State()

    def ordered(mine, theirs):
        return jnp.where(core == 0, mine, theirs), jnp.where(core == 0, theirs, mine)

    def pack_qkv():
        cols = w_qkv.reshape(LAYERS, rows, 3, 2, pairs, lane)

        def side(which):
            return jnp.swapaxes(pick(cols, which, 3), 2, 3).reshape(LAYERS, rows, 3 * half)

        feature = jnp.arange(width)[None, :] - rows * device == jnp.arange(rows)[:, None]
        unit = jnp.arange(hidden // 2)[None, :] - hidden_rows * chips.chip
        unit = unit == jnp.arange(hidden_rows)[:, None]
        table = jnp.concatenate([bias_vectors, gains], axis=1).reshape(LAYERS * 8, rows)
        table = dot(table, feature.astype(BF)).astype(BF)
        units = dot(bias_up, unit.astype(BF)).astype(BF)
        got = swap(side(1 - core), 1)
        table = table + swap(table, 1)
        cols = merge(side(core), got, core, 1)
        for layer in range(LAYERS):
            last = cols[layer, :, :, width:].reshape(2 * rows, half)
            outs = jnp.concatenate([w_out[layer, :, :half], w_out[layer, :, half:]], axis=0)
            vectors = [table[8 * layer : 8 * layer + 8]]
            vectors += [units[layer : layer + 1, i * width :][:, :width] for i in range(panels)]
            vectors.append(jnp.zeros((8 - panels, width), BF))
            state.gathers[ATTN, layer] = Gather(
                chips, sequence, EARLY[layer],
                jnp.concatenate(
                    [
                        cols[layer, :, :, :width].reshape(2 * rows, width),
                        jnp.concatenate([last, outs], axis=1),
                        *vectors,
                    ],
                    axis=0,
                ),
            )
        sequence.mark([state.gathers[ATTN, layer].held for layer in range(LAYERS)])

    groups = hidden // width

    def pack_up():
        value = sequence.gate(w_up).reshape(LAYERS * rows, hidden)
        stacked = jnp.concatenate(
            [value[:, i * width : (i + 1) * width] for i in range(groups)], axis=0
        )
        stacked = dot(stacked, order.astype(BF)).astype(BF)
        mine, sent = ordered(stacked[:, :half], stacked[:, half:])
        first, second = ordered(mine, swap(sent, 1))
        for layer in range(LAYERS):
            parts = []
            for i in range(panels):
                for value in (first, second):
                    cut = [
                        value[((2 * i + j) * LAYERS + layer) * rows :][:rows] for j in range(2)
                    ]
                    parts.append(jnp.concatenate(cut, axis=1))
            state.gathers[FFN, layer] = Gather(
                chips, sequence, EARLY[LAYERS + layer],
                jnp.concatenate(parts + [w_down[layer]], axis=0),
            )
        sequence.mark([state.gathers[FFN, layer].held for layer in range(LAYERS)])

    def read_vectors(layer, table):
        table = jnp.sum(table.astype(F32), axis=0)
        vec = table[:8]
        bias_q, bias_v = (
            jnp.where(core == 0, vec[i : i + 1, :half], vec[i : i + 1, half:]) for i in range(2)
        )
        bias = []
        for p in range(pairs):
            cut = slice(p * lane, (p + 1) * lane)
            bias += [bias_q[:, cut], jnp.zeros((1, lane), F32), bias_v[:, cut]]
        state.vec[layer] = vec
        state.bias_qkv[layer] = jnp.concatenate(bias, axis=1)
        state.bias_up[layer] = jnp.concatenate(
            [table[8 + i : 9 + i] for i in range(panels)], axis=1
        )

    def tokens_start():
        value = sequence.gate(tokens)
        sequence.mark(value)
        state.pair_tokens = (value, swap(value, 1))

    def tokens_end():
        values = sequence.gate(state.pair_tokens)
        state.x_b[0] = jnp.concatenate(ordered(*values), axis=0)
        state.x[0] = state.x_b[0].astype(F32)
        sequence.mark(state.x_b[0])

    def cotangent_start():
        value = sequence.gate(cotangent)
        sequence.mark(value)
        state.pair_cotangent = (value, swap(value, 1))

    def cotangent_end():
        values = sequence.gate(state.pair_cotangent)
        state.upstream = (jnp.concatenate(ordered(*values), axis=0),)
        sequence.mark(state.upstream)

    def out_exchange(layer):
        ends = [0, 2 * rows, 4 * rows, 4 * rows + 16]
        first, second, table = state.gathers[ATTN, layer].finish(list(zip(ends[:-1], ends[1:])))
        w_b = second[:, :, :half].reshape(width, half)
        out_all = second[:, :, half:].reshape(2, count // 2, 2 * rows, half)
        sent = pick(out_all, 1 - core, 0)
        read_vectors(layer, table)
        sequence.mark((sent, w_b, state.vec[layer]))
        parts = ordered(pick(out_all, core, 0), swap(sent, 1))
        parts = [jnp.concatenate([part[:, :rows], part[:, rows:]], axis=2) for part in parts]
        full_out = jnp.stack(parts, axis=1).reshape(half, width)
        state.w_attn[layer] = (first.reshape(width, width), w_b, full_out)

    def hidden_weights(layer):
        ends = [2 * rows * i for i in range(panels + 1)]
        ends.append(ends[-1] + hidden_rows)
        *ups, down = state.gathers[FFN, layer].finish(list(zip(ends[:-1], ends[1:])))
        state.w_hidden[layer] = (
            down.reshape(hidden // 2, width), *(value.reshape(width, width) for value in ups)
        )

    def run_attention(layer):
        x_b, weights = sequence.gate((state.x_b[layer], state.w_attn[layer]))
        w_a, w_b, full_out = weights
        partial, *saved = attention(row_kind, x_b, w_a, w_b, state.bias_qkv[layer], full_out)
        sequence.mark(partial)
        state.w_attn[layer] = weights
        state.saved[layer] = (x_b, *saved)
        state.branch = (partial, swap(partial, 1))

    def run_hidden(layer):
        mine, theirs = sequence.gate(state.branch)
        down, up0, up1 = state.w_hidden[layer]
        first_sum, state.normed, *kept, partial = hidden_layer(
            state.x[layer], mine, theirs, state.vec[layer], state.bias_up[layer], up0, up1, down
        )
        sequence.mark(partial)
        state.first_sum[layer] = first_sum
        state.kept[layer] = kept
        state.branch = (partial, swap(partial, 1))

    def run_norm(layer):
        mine, theirs = sequence.gate(state.branch)
        second, x, x_b = norm_rows(state.normed, mine, theirs, state.vec[layer])
        state.second[layer], state.x[layer + 1], state.x_b[layer + 1] = second, x, x_b
        sequence.mark(second)

    def run_back_second(layer):
        upstream = sequence.gate(state.upstream)
        if layer < LAYERS - 1:
            upstream = (state.d_first, *upstream)
        act = state.kept[layer][1]
        d_second, d_ffn, g_down, sums = back_second(
            upstream, state.second[layer], state.vec[layer], act
        )
        state.d_second, state.d_ffn = d_second, d_ffn
        state.sums2[layer] = sums
        bundle = state.scatters[FFN, layer]
        bundle.start(0, [g_down.reshape(count, hidden_rows, width)])
        sequence.mark((d_ffn, bundle.sent))

    def run_back_hidden(layer):
        d_ffn = sequence.gate(state.d_ffn)
        normed_b, _, slope = state.kept[layer]
        *g_up, partial, units = back_hidden(d_ffn, slope, normed_b, *state.w_hidden[layer])
        bundle = state.scatters[FFN, layer]
        bundle.start(1, [value.reshape(count, 2 * rows, width) for value in g_up])
        sequence.mark((partial, bundle.sent))
        state.units[layer] = units
        state.branch = (partial, swap(partial, 1))

    def run_back_attention(layer):
        mine, theirs = sequence.gate(state.branch)
        x_b, qkv, context, lse = state.saved[layer]
        g_a, g_b, g_out, partial, sums, state.d_first, state.sums1[layer] = attention_backward(
            row_kind, state.d_second, mine, theirs, state.first_sum[layer], state.vec[layer],
            x_b, qkv, context, lse, *state.w_attn[layer],
        )
        sequence.mark(partial)
        state.pair[layer] = jnp.concatenate(
            [
                jnp.concatenate(
                    [sums[:, (3 * p + t) * lane :][:, :lane] for p in range(pairs)], axis=1
                )
                for t in (0, 2)
            ],
            axis=0,
        )
        if layer > 0:
            state.upstream = (partial, swap(partial, 1))
        else:
            mine, sent = ordered(partial[:own], partial[own:])
            state.upstream = (mine, swap(sent, 1))
        state.g_attn[layer] = (g_a, g_b, g_out)

    def sum_rows(layer):
        pair = state.pair[layer]
        nothing = jnp.zeros_like(pair)
        pair = jnp.concatenate(ordered(pair, nothing), axis=1)
        units = [state.units[layer][:, i * width :][:, :width] for i in range(panels)]
        small = jnp.concatenate([state.sums1[layer] + state.sums2[layer], pair, *units], axis=0)
        small = jnp.pad(small.astype(BF), ((0, 16 - small.shape[0]), (0, 0)))
        line = jnp.arange(16)[:, None]
        place = jnp.arange(width)[None, :]
        owner = jnp.where(
            line < 10, place // (2 * rows), ((line - 10) * width + place) // hidden_rows
        )
        mine = owner[None] == jnp.arange(count)[:, None, None]
        return jnp.where(mine, small[None], jnp.zeros((), BF))

    def back_terms(layer):
        g_a, g_b, g_out = sequence.gate(state.g_attn[layer])
        bundle = state.scatters[ATTN, layer]
        out_pair = g_out.reshape(count // 2, 2, rows, width)
        out_got = swap(pick(out_pair, 1 - core, 1), 1)
        out = merge(pick(out_pair, core, 1), out_got, core, 0).reshape(count, rows, width)
        g_b = g_b.reshape(count, 2 * rows, half)
        out = jnp.concatenate([out[:, :, :half], out[:, :, half:]], axis=1)
        rest = jnp.concatenate([g_b, out], axis=2)
        rest = jnp.concatenate([rest, sum_rows(layer)], axis=1)
        rest = lax.optimization_barrier(rest)
        bundle.start(0, [g_a.reshape(count, 2 * rows, width), rest])
        sequence.mark(bundle.sent)

    def grad_end():
        mine, theirs = sequence.gate(state.upstream)
        d_first = lax.dynamic_slice_in_dim(state.d_first, core * own, own)
        state.grad_tokens = d_first + (mine.astype(F32) + theirs.astype(F32))
        sequence.mark(state.grad_tokens)

    def mixed_end():
        value = sequence.gate(state.x_b[LAYERS])
        state.mixed = lax.dynamic_slice_in_dim(value, core * own, own)
        sequence.mark(state.mixed)

    def finish_hidden(layer):
        down, *ups = state.scatters[FFN, layer].finish()
        sides = [
            jnp.concatenate([up[side * rows :][:rows] for up in ups], axis=1)
            for side in range(2)
        ]
        mine, sent = ordered(*sides)
        state.up_pair[layer] = (mine, swap(sent, 1))
        state.down[layer] = down

    def end_hidden(layer):
        first, second = ordered(*sequence.gate(state.up_pair[layer]))
        stacked = jnp.concatenate(
            [
                jnp.concatenate(
                    [value[:, i * half : (i + 1) * half] for value in (first, second)], axis=1
                )
                for i in range(groups)
            ],
            axis=0,
        )
        stacked = lax.dot_general(
            stacked, order.astype(F32), (((1,), (1,)), ((), ())),
            precision=lax.Precision.HIGHEST, preferred_element_type=F32,
        )
        state.up[layer] = jnp.concatenate(
            [stacked[i * rows : (i + 1) * rows] for i in range(groups)], axis=1
        )
        sequence.mark(state.up[layer])

    def finish_attention(layer):
        first, rest = state.scatters[ATTN, layer].finish()
        last, out, small = rest[: 2 * rows, :half], rest[: 2 * rows, half:], rest[2 * rows :]
        out = jnp.concatenate([out[:rows], out[rows:]], axis=1)
        sides = [
            jnp.concatenate([value[side * rows :][:rows] for value in (first, last)], axis=1)
            for side in range(2)
        ]
        mine, sent = ordered(*sides)
        pair = jnp.pad(small[8:], ((0, 0), (0, mine.shape[1] - width)))
        sent = jnp.concatenate([sent, pair], axis=0)
        state.qkv_pair[layer] = (mine, swap(sent, 1))
        state.out[layer] = out
        state.small_rows[layer] = small

    def end_attention(layer):
        mine, theirs = sequence.gate(state.qkv_pair[layer])
        small = state.small_rows[layer]
        small = jnp.concatenate([theirs[rows : rows + 2, :width] + small[8:10], small], axis=0)
        features = lax.dynamic_slice_in_dim(small, rows * device, rows, axis=1)
        per_row = width // hidden_rows
        units = lax.dynamic_slice(
            small,
            (12 + chips.chip // per_row, hidden_rows * (chips.chip % per_row)),
            (1, hidden_rows),
        )
        state.vectors[layer] = features[:6]
        state.gains[layer] = features[6:8]
        state.unit_sums[layer] = units[0]
        values = ordered(mine, theirs[:rows])
        state.qkv[layer] = jnp.concatenate(
            [
                value[:, (3 * p + t) * lane :][:, :lane]
                for t in range(3)
                for value in values
                for p in range(pairs)
            ],
            axis=1,
        )
        sequence.mark(state.qkv[layer])

    def call(function, *args):
        return lambda: function(*args)

    low = len(chips.low)
    size = (1.0, 2.0)
    add = plan.add

    def pair_send(label):
        return [(label, (("p", 0.0),), 1)]

    def plane(length):
        return (("x", length), ("y", length))

    add("pq", 0, 6.0, [], pack_qkv)
    add("pu", 2, 3.0, [("g", ATTN, 0)], pack_up)
    add("tok", 8, 0.5, ["pu"], tokens_start, pair_send("x0"))
    add("te", 7, 1.5, ["x0"], tokens_end)
    add("cot", 9, 0.5, [("m", 1, 0)], cotangent_start, pair_send("ct"))
    add("ce", 9, 1.2, ["ct"], cotangent_end)
    bundles = [(ATTN, 0), (FFN, 0), (ATTN, 1), (FFN, 1)]
    for rank, (kind, layer) in enumerate(bundles):
        needs = ["pq" if kind == ATTN else "pu"]

        def start(kind=kind, layer=layer):
            state.gathers[kind, layer].start()

        def advance(kind=kind, layer=layer):
            state.gathers[kind, layer].advance()

        units = 7.0 / 3 if kind == ATTN else 4.0
        tops = [("top", 2), ("top", 1)]
        lows = [("low", step) for step in range(low)]
        early = EARLY[LAYERS * kind + layer]
        steps = lows[:1] + tops + lows[1:] if early else tops + lows
        need = None
        held = 1
        for number, (bits, step) in enumerate(steps):
            length = UNIT / 2 * units * held
            held *= 2
            if bits == "low":
                links = plane(length)
            elif step == 2:
                links = (("z", 2 * length), ("w", 5 * length + 1.5))
            else:
                links = (("z", 2 * length),)
            sent = ("gx", kind, layer, number)
            if number == 0:
                add(("g", kind, layer), 1 + rank, 3.5, needs, start, [(sent, links, 1)])
            else:
                add(
                    ("gs", kind, layer, number), 1 + rank, 1.0 + 0.1 * held + (2.8 if len(links) > 1 and links[1][0] == "w" else 1.4),
                    [need], advance, [(sent, links, 1)],
                )
            need = sent
        if kind == ATTN:
            add(
                ("go", layer), 1 + rank, 4.5, [need], call(out_exchange, layer),
                pair_send(("w", kind, layer)),
            )
        else:
            add(("w", kind, layer), 1 + rank, 1.6, [need], call(hidden_weights, layer))
    need = "te"
    for layer in range(LAYERS):
        add(
            ("m", 0, layer), 10, 12.7, [need, ("w", ATTN, layer)],
            call(run_attention, layer), pair_send(("p", 0, layer)),
        )
        add(
            ("m", 1, layer), 10, 6.0, [("p", 0, layer), ("w", FFN, layer)],
            call(run_hidden, layer), pair_send(("p", 1, layer)),
        )
        need = ("m", 2, layer)
        add(need, 10, 3.0, [("p", 1, layer)], call(run_norm, layer))
    add("mix", 20, 1.0, [need], mixed_end)

    needs = [need, "ce"]
    for layer in reversed(range(LAYERS)):
        state.scatters[FFN, layer] = Scatter(chips, sequence, 2, LATE[LAYERS + layer])
        state.scatters[ATTN, layer] = Scatter(chips, sequence, 1, LATE[layer])
        add(
            ("b", 0, layer), 10, 5.0, needs, call(run_back_second, layer),
            [(("r", FFN, layer, 0), plane(UNIT * 8), 1)],
        )
        add(
            ("b", 1, layer), 10, 6.5, [("b", 0, layer)], call(run_back_hidden, layer),
            [(("r", FFN, layer, 1), plane(UNIT * 8), 1)] + pair_send(("p", 2, layer)),
        )
        add(
            ("b", 2, layer), 10, 17.2, [("p", 2, layer)], call(run_back_attention, layer),
            pair_send(("p", 3, layer)),
        )
        add(
            ("b", 3, layer), 9.5, 6.0, [("b", 2, layer)], call(back_terms, layer),
            [(("r", ATTN, layer, 0), plane(UNIT * 28 / 3), 1)],
        )
        needs = [("p", 3, layer)]
        for kind in (FFN, ATTN):
            need = [("r", kind, layer, part) for part in range(1 + kind)]
            rank = 1 + 2 * (LAYERS - 1 - layer) + (kind == ATTN)

            def reduce(kind=kind, layer=layer):
                state.scatters[kind, layer].advance()

            units = 7.0 / 3 if kind == ATTN else 4.0
            tops = [("top", 1), ("top", 2)]
            lows = [("low", step) for step in range(low - 1)][::-1]
            late = LATE[LAYERS * kind + layer]
            steps = lows[:-1] + tops + lows[-1:] if late else lows + tops
            held = 2 * count // 4
            for number, (bits, step) in enumerate(steps):
                held //= 2
                length = UNIT / 2 * units * held
                cost = 1.0 + 0.1 * held
                if bits == "low":
                    cost, links = cost + 1.4, plane(length)
                elif step == 2:
                    cost, links = cost + 2.8, (("z", 2 * length), ("w", 5 * length + 1.5))
                else:
                    cost, links = cost + 1.4, (("z", 2 * length),)
                sent = ("rx", kind, layer, number)
                add(("rs", kind, layer, number), rank, cost, need, reduce, [(sent, links, 1)])
                need = [sent]
            last = finish_hidden if kind == FFN else finish_attention
            add(
                ("rf", kind, layer), 19, 2.0, need, call(last, layer),
                pair_send(("re", kind, layer)),
            )
            last = end_hidden if kind == FFN else end_attention
            add(("ro", kind, layer), 20, 2.5, [("re", kind, layer)], call(last, layer))
    add("grad", 18, 1.2, needs, grad_end)
    plan.run()

    def stacked(values):
        return jnp.stack([values[layer] for layer in range(LAYERS)])

    return (
        state.mixed,
        state.grad_tokens,
        stacked(state.qkv),
        stacked(state.out),
        stacked(state.up),
        stacked(state.down),
        stacked(state.vectors),
        stacked(state.gains),
        stacked(state.unit_sums),
    )


def solution(mesh):
    placed = (
        P("fsdp", None),
        P("fsdp"),
        P(None, "fsdp", None),
        P(None, "fsdp", None),
        P(None, "fsdp", None),
        P(None, "fsdp", None),
        P(None, None, "fsdp"),
        P(None, None, "fsdp"),
        P(None, "fsdp"),
        P("fsdp", None),
    )
    return jax.shard_map(
        shards,
        mesh=mesh,
        in_specs=placed,
        out_specs=(
            P("fsdp", None),
            P("fsdp", None),
            P(None, "fsdp", None),
            P(None, "fsdp", None),
            P(None, "fsdp", None),
            P(None, "fsdp", None),
            P(None, None, "fsdp"),
            P(None, None, "fsdp"),
            P(None, "fsdp"),
        ),
        check_vma=False,
    )
```

```python
import functools

import jax
import jax.numpy as jnp
from jax import lax
from jax.experimental import pallas as pl
from jax.experimental.pallas import tpu as pltpu
from jax.sharding import PartitionSpec as P

HEADS = 12
HEAD_DIM = 64
LAYERS = 2
SHORT = 128
AXIS = "fsdp"

EPSILON = 1e-05
MASKED_SCORE = -1e30
BF = jnp.bfloat16
F32 = jnp.float32
LATENCY = 2.5
UNIT = 1.48
ATTN, FFN = 0, 1
OPEN_SENDS = 5
VMEM_LIMIT = 16 * 2**20
EARLY = (False, False, False, False)
LATE = (False, False, False, False)
ORDER = (
    0, 6, 1, 2, 7, 11, 16, 8, 3, 12, 21, 9, 13, 17, 14, 10, 22, 15, 23, 18, 26, 19, 24,
    27, 28, 20, 4, 29, 25, 5, 30, 31, 33, 34, 35, 36, 37, 47, 48, 49, 38, 42, 51, 43, 39,
    50, 52, 44, 61, 40, 56, 53, 45, 57, 58, 54, 59, 32, 55, 60, 41, 46,
)


def dot(left, right):
    return jnp.dot(left, right, preferred_element_type=F32)


def dot_tn(left, right):
    return lax.dot_general(left, right, (((0,), (0,)), ((), ())), preferred_element_type=F32)


def dot_nt(left, right):
    return lax.dot_general(left, right, (((1,), (1,)), ((), ())), preferred_element_type=F32)


def swap(value, mask):
    pairs = [(source, source ^ mask) for source in range(lax.axis_size(AXIS))]
    return lax.ppermute(value, AXIS, pairs)


def merge(mine, theirs, bit, axis):
    first = jnp.where(bit == 0, mine, theirs)
    second = jnp.where(bit == 0, theirs, mine)
    return jnp.stack([first, second], axis=axis)


def pick(pair, index, axis):
    return lax.dynamic_index_in_dim(pair, index, axis, keepdims=False)


class Chips:
    def __init__(self):
        device = lax.axis_index(AXIS)
        self.count = lax.axis_size(AXIS) // 2
        self.core = device % 2
        self.chip = device // 2
        self.step = self.count // 4
        self.top = self.chip // self.step
        self.low = list(range(self.count.bit_length() - 3))
        self.info = self.table()

    def bit(self, place):
        return (self.chip // 2**place) % 2

    def plane_bit(self, step):
        return jnp.where(self.core == 0, self.bit(step), self.bit(len(self.low) - 1 - step))

    def plane_swap(self, value, step):
        masks = (2 * 2**step, 2 * 2 ** (len(self.low) - 1 - step))
        pairs = [(source, source ^ masks[source % 2]) for source in range(2 * self.count)]
        return lax.ppermute(value, AXIS, pairs)

    def table(self):
        bits = [self.plane_bit(step) for step in range(len(self.low))]
        entries = [self.core] + bits + [self.top % 2, self.top // 2]
        return jnp.stack(entries).astype(jnp.int32)


def half_place(table, step, index, own):
    bit = table[1 + step]
    bit = bit if own else 1 - bit
    return jnp.where(table[0] == 0, 2**step * bit + index, 2 * index + bit)


def merge_place(table, kind, step, low, half, index, own):
    if kind == "low":
        return half_place(table, step, index, own)
    bit = table[low + step]
    return half * (bit if own else 1 - bit) + index


class Sequence:
    def __init__(self):
        self.last = None

    def gate(self, values):
        if self.last is None:
            return values
        values, _ = lax.optimization_barrier((values, self.last))
        return values

    def mark(self, values):
        self.last = values


class State:
    def __getattr__(self, name):
        value = {}
        setattr(self, name, value)
        return value


class Plan:
    def __init__(self):
        self.pieces = []

    def add(self, name, rank, cost, needs, run, sends=()):
        self.pieces.append((name, rank, cost, needs, run, sends))

    def greedy(self):
        now = 0.0
        ready = {}
        free = {}
        open_sends = {}
        waiting = list(range(len(self.pieces)))
        order = []

        def fits(piece):
            held = sum(weight for label, weight in open_sends.items() if label not in piece[3])
            added = sum(weight for _, _, weight in piece[5])
            return added == 0 or held + added <= OPEN_SENDS

        while waiting:
            known = []
            for place in waiting:
                piece = self.pieces[place]
                if all(need in ready for need in piece[3]):
                    time = max([ready[need] for need in piece[3]], default=0.0)
                    known.append((time, piece[1], place))
            known = [entry for entry in known if fits(self.pieces[entry[2]])] or known
            able = [entry[1:] for entry in known if entry[0] <= now]
            place = min(able)[1] if able else min(known)[2]
            name, _, cost, needs, _, sends = self.pieces[place]
            now = max([now] + [ready[need] for need in needs]) + cost
            ready[name] = now
            for need in needs:
                open_sends.pop(need, None)
            for label, links, weight in sends:
                ready[label] = 0.0
                for link, length in links:
                    free[link] = max(now, free.get(link, 0.0)) + length
                    ready[label] = max(ready[label], free[link] + LATENCY)
                if weight > 0:
                    open_sends[label] = weight
            waiting.remove(place)
            order.append(place)
        return order

    def run(self):
        order = ORDER if len(ORDER) == len(self.pieces) else self.greedy()
        for place in order:
            self.pieces[place][4]()


class Gather:
    def __init__(self, chips, sequence, early, piece):
        self.chips, self.sequence = chips, sequence
        low = [("low", step) for step in range(len(chips.low))]
        top = [("top", 2), ("top", 1)]
        self.steps = low[:1] + top + low[1:] if early else top + low
        self.held = piece[None, None]

    def start(self):
        self.held = self.sequence.gate(self.held)
        self.sequence.mark(self.held)
        self.send()

    def send(self):
        kind, step = self.steps[0]
        if kind == "low":
            self.coming = self.chips.plane_swap(self.held, step)
        else:
            self.coming = swap(self.held, 2 * step * self.chips.step)

    def merged(self, ranges=None):
        chips = self.chips
        coming = self.sequence.gate(self.coming)
        kind, step = self.steps.pop(0)
        if kind == "low":
            return merge_rows(chips, kind, step, self.held, coming, ranges)
        lead, half, height, width = self.held.shape
        flat = [value.reshape(lead, 1, half * height, width) for value in (self.held, coming)]
        return merge_rows(chips, kind, step, *flat).reshape(2 * lead, half, height, width)

    def advance(self):
        self.held = self.merged()
        self.sequence.mark(self.held)
        self.send()

    def finish(self, ranges):
        while len(self.steps) > 1:
            self.advance()
        results = self.merged(ranges)
        results = [whole.reshape((self.chips.count,) + whole.shape[2:]) for whole in results]
        self.sequence.mark(results)
        return results


def merge_kernel(ranges, place, table_ref, mine_ref, theirs_ref, *out_refs):
    for index in range(mine_ref.shape[1]):
        own, other = place(table_ref, index, True), place(table_ref, index, False)
        for lead in range(mine_ref.shape[0]):
            for (start, stop), out_ref in zip(ranges, out_refs):
                out_ref[lead, own] = mine_ref[lead, index, start:stop]
                out_ref[lead, other] = theirs_ref[lead, index, start:stop]


def merge_rows(chips, kind, step, mine, theirs, ranges=None):
    half = mine.shape[1]
    cuts = ranges or [(0, mine.shape[2])]

    def place(table, index, own):
        return merge_place(table, kind, step, len(chips.low), half, index, own)

    shapes = [
        jax.ShapeDtypeStruct((mine.shape[0], 2 * half, stop - start, mine.shape[3]), BF)
        for start, stop in cuts
    ]
    if all(edge % 16 == 0 for cut in cuts for edge in cut):
        results = kernel_call(
            functools.partial(merge_kernel, cuts, place), shapes, [], chips.info, mine, theirs
        )
    else:
        sides = [place(chips.info, jnp.arange(half), own) for own in (True, False)]
        results = []
        for (start, stop), shape in zip(cuts, shapes):
            whole = jnp.zeros(shape.shape, BF)
            for side, value in zip(sides, (mine, theirs)):
                whole = whole.at[:, side].set(value[:, :, start:stop])
            results.append(whole)
    return results if ranges else results[0]


class Scatter:
    def __init__(self, chips, sequence, count, late):
        self.chips, self.sequence = chips, sequence
        low = [("low", step) for step in range(len(chips.low) - 1)][::-1]
        top = [("top", 1), ("top", 2)]
        self.steps = low[:-1] + top + low[-1:] if late else low + top
        self.arrays = [None] * count
        self.coming = [None] * count
        self.heights = None

    def start(self, part, arrays):
        chips = self.chips
        step = len(chips.low) - 1
        shape = (4, 2 ** len(chips.low))
        arrays = [value.reshape(shape + value.shape[1:]) for value in arrays]
        self.arrays[part] = arrays
        sent = send_rows(chips, step, arrays)
        self.coming[part] = chips.plane_swap(sent, step)
        self.sent = sent

    def advance(self):
        chips = self.chips
        coming = self.sequence.gate(self.coming)
        first = self.heights is None
        if first:
            self.heights = [value.shape[2] for part in self.arrays for value in part]
        else:
            self.arrays, coming = [[self.kept]], [coming]
        kind, step = self.steps.pop(0)
        if kind == "top":
            self.arrays = [
                [value.reshape((-1, 2 * value.shape[1]) + value.shape[2:]) for value in part]
                for part in self.arrays
            ]
            coming = [got.reshape((-1, 2 * got.shape[1]) + got.shape[2:]) for got in coming]
        sent, self.kept = fold_rows(chips, kind, step, first, self.arrays, coming)
        self.sequence.mark(sent)
        if kind == "low":
            self.coming = chips.plane_swap(sent, step)
        else:
            self.coming = swap(sent, 2 * step * chips.step)

    def finish(self):
        coming = self.sequence.gate(self.coming)
        total = self.kept[0, 0] + coming[0, 0].astype(F32)
        self.sequence.mark(total)
        ends = [sum(self.heights[:i]) for i in range(len(self.heights) + 1)]
        return [total[start:stop] for start, stop in zip(ends[:-1], ends[1:])]


def send_kernel(step, heights, table_ref, *refs):
    *array_refs, sent_ref = refs
    for index in range(sent_ref.shape[1]):
        place = half_place(table_ref, step, index, False)
        for lead in range(sent_ref.shape[0]):
            row = 0
            for height, ref in zip(heights, array_refs):
                sent_ref[lead, index, row : row + height] = ref[lead, place]
                row += height


def send_rows(chips, step, arrays):
    heights = [value.shape[2] for value in arrays]
    shape = (arrays[0].shape[0], 2**step, sum(heights), arrays[0].shape[3])
    if any(height % 16 for height in heights):
        places = half_place(chips.info, step, jnp.arange(2**step), False)
        return jnp.concatenate([jnp.take(value, places, axis=1) for value in arrays], axis=2)
    (sent,) = kernel_call(
        functools.partial(send_kernel, step, heights), [jax.ShapeDtypeStruct(shape, BF)], [],
        chips.info, *arrays,
    )
    return sent


def fold_kernel(layout, place, table_ref, *refs):
    *refs, sent_ref, kept_ref = refs
    for index in range(sent_ref.shape[1]):
        for own, out_ref in enumerate((sent_ref, kept_ref)):
            source, came = place(table_ref, index, own == 1)
            for lead in range(sent_ref.shape[0]):
                for array, got, start, height, row in layout:
                    mine = refs[array][lead, source]
                    theirs = refs[got][lead, came, start : start + height]
                    total = mine.astype(F32) + theirs.astype(F32)
                    out_ref[lead, index, row : row + height] = total.astype(out_ref.dtype)


def fold_rows(chips, kind, step, first, parts, coming):
    arrays = [value for part in parts for value in part]
    layout = []
    row = 0
    for part, got in zip(range(len(parts)), range(len(arrays), len(arrays) + len(coming))):
        start = 0
        for value in parts[part]:
            height = value.shape[2]
            layout.append((len(layout), got, start, height, row))
            start += height
            row += height
    half = coming[0].shape[1] // 2
    low = len(chips.low)

    def place(table, index, own):
        if kind == "low":
            came = half_place(table, step, index, own)
            return (half_place(table, low - 1, came, True) if first else came), came
        bit = table[low + step]
        bit = bit if own else 1 - bit
        came = half * bit + index
        if not first:
            return came, came
        return 2**low * bit + half_place(table, low - 1, index, True), came

    shape = (arrays[0].shape[0], half, row, arrays[0].shape[3])
    if any(value.shape[2] % 16 for value in arrays):
        results = []
        for own, dtype in ((False, BF), (True, F32)):
            source, came = place(chips.info, jnp.arange(half), own)
            totals = []
            for array, got, start, height, _ in layout:
                theirs = jnp.take(coming[got - len(arrays)], came, axis=1)
                theirs = theirs[:, :, start : start + height].astype(F32)
                totals.append(jnp.take(arrays[array], source, axis=1).astype(F32) + theirs)
            results.append(jnp.concatenate(totals, axis=2).astype(dtype))
        return results
    return kernel_call(
        functools.partial(fold_kernel, layout, place),
        [jax.ShapeDtypeStruct(shape, kind) for kind in (BF, F32)], [],
        chips.info, *arrays, *coming,
    )


ROOT_HALF = 0.7071067811865476
DENSITY = 0.3989422804014327


def unit_rows(values):
    centre = values - jnp.mean(values, axis=1, keepdims=True)
    scale = lax.rsqrt(jnp.mean(centre * centre, axis=1, keepdims=True) + EPSILON)
    return centre * scale, scale


def norm_kernel(base_ref, mine_ref, theirs_ref, vec_ref, sum_ref, out_ref, out_b_ref):
    def chunk_step(chunk, carry):
        rows = pl.ds(pl.multiple_of(chunk * SHORT, SHORT), SHORT)
        total = base_ref[rows, :] + (
            mine_ref[rows, :].astype(F32) + theirs_ref[rows, :].astype(F32)
        ) + vec_ref[3:4, :]
        sum_ref[rows, :] = total
        unit, _ = unit_rows(total)
        output = unit * vec_ref[7:8, :] + vec_ref[5:6, :]
        out_ref[rows, :] = output
        out_b_ref[rows, :] = output.astype(BF)
        return carry

    lax.fori_loop(0, base_ref.shape[0] // SHORT, chunk_step, 0)


def hidden_kernel(
    x_ref, mine_ref, theirs_ref, vec_ref, bias_ref, up0_ref, up1_ref, down_ref,
    sum_ref, normed_ref, normed_b_ref, act_ref, slope_ref, partial_ref,
):
    def chunk_step(chunk, carry):
        rows = pl.ds(pl.multiple_of(chunk * SHORT, SHORT), SHORT)
        total = x_ref[rows, :] + (
            mine_ref[rows, :].astype(F32) + theirs_ref[rows, :].astype(F32) + vec_ref[2:3, :]
        )
        sum_ref[rows, :] = total
        unit, _ = unit_rows(total)
        normed = unit * vec_ref[6:7, :] + vec_ref[4:5, :]
        normed_ref[rows, :] = normed
        normed_b_ref[rows, :] = normed.astype(BF)
        return carry

    lax.fori_loop(0, x_ref.shape[0] // SHORT, chunk_step, 0)
    width = up0_ref.shape[1]
    step = 256
    for panel, up_ref in enumerate((up0_ref, up1_ref)):
        for start in range(0, width, step):
            place = panel * width + start
            pre = dot(normed_b_ref[...], up_ref[:, start : start + step])
            pre = pre + bias_ref[:, place : place + step]
            share = 0.5 + 0.5 * lax.erf(pre * ROOT_HALF)
            slope = share + pre * (DENSITY * jnp.exp(pre * pre * -0.5))
            act_ref[:, place : place + step] = (pre * share).astype(BF)
            slope_ref[:, place : place + step] = slope.astype(BF)
    partial_ref[...] = dot(act_ref[...], down_ref[...]).astype(BF)


def norm_back(upstream, total, gain):
    unit, scale = unit_rows(total)
    scaled = upstream * gain
    first = jnp.mean(scaled, axis=1, keepdims=True)
    second = jnp.mean(scaled * unit, axis=1, keepdims=True)
    return (
        scale * (scaled - first - unit * second),
        jnp.sum(upstream * unit, axis=0, keepdims=True),
        jnp.sum(upstream, axis=0, keepdims=True),
    )


def back_second_kernel(has_base, *refs):
    base_refs, refs = refs[: 3 if has_base else 1], refs[3 if has_base else 1 :]
    sum_ref, vec_ref, act_ref, d_second_ref, d_ffn_ref, g_down_ref, sums_ref = refs
    sums_ref[...] = jnp.zeros_like(sums_ref)

    def chunk_step(chunk, carry):
        rows = pl.ds(pl.multiple_of(chunk * SHORT, SHORT), SHORT)
        upstream = base_refs[0][rows, :].astype(F32)
        if has_base:
            upstream = upstream + (
                base_refs[1][rows, :].astype(F32) + base_refs[2][rows, :].astype(F32)
            )
        d_second, d_gain, d_shift = norm_back(upstream, sum_ref[rows, :], vec_ref[7:8, :])
        d_second_ref[rows, :] = d_second
        d_ffn = d_second.astype(BF)
        d_ffn_ref[rows, :] = d_ffn
        sums_ref[1:2, :] += jnp.sum(d_ffn.astype(F32), axis=0, keepdims=True)
        sums_ref[3:4, :] += d_shift
        sums_ref[5:6, :] += d_gain
        return carry

    lax.fori_loop(0, sum_ref.shape[0] // SHORT, chunk_step, 0)
    g_down_ref[...] = dot_tn(act_ref[...], d_ffn_ref[...]).astype(BF)


def back_hidden_kernel(
    d_ffn_ref, slope_ref, normed_b_ref, down_ref, up0_ref, up1_ref,
    g_up0_ref, g_up1_ref, partial_ref, sums_ref, d_pre_ref,
):
    hidden = slope_ref.shape[1]
    step = 256
    for place in range(0, hidden, step):
        d_act = dot_nt(d_ffn_ref[...], down_ref[place : place + step, :])
        d_pre = (d_act * slope_ref[:, place : place + step].astype(F32)).astype(BF)
        d_pre_ref[:, place : place + step] = d_pre
        sums_ref[:, place : place + step] = jnp.sum(d_pre.astype(F32), axis=0, keepdims=True)
    width = up0_ref.shape[1]
    g_up0_ref[...] = dot_tn(normed_b_ref[...], d_pre_ref[:, :width]).astype(BF)
    g_up1_ref[...] = dot_tn(normed_b_ref[...], d_pre_ref[:, width:]).astype(BF)
    partial_ref[...] = (
        dot_nt(d_pre_ref[:, :width], up0_ref[...]) + dot_nt(d_pre_ref[:, width:], up1_ref[...])
    ).astype(BF)


def back_first(
    d_second_ref, mine_ref, theirs_ref, sum_ref, vec_ref, d_first_ref, dbranch_ref, sums_ref
):
    sums_ref[...] = jnp.zeros_like(sums_ref)

    def chunk_step(chunk, carry):
        rows = pl.ds(pl.multiple_of(chunk * SHORT, SHORT), SHORT)
        upstream = d_second_ref[rows, :] + (
            mine_ref[rows, :].astype(F32) + theirs_ref[rows, :].astype(F32)
        )
        d_first, d_gain, d_shift = norm_back(upstream, sum_ref[rows, :], vec_ref[6:7, :])
        d_first_ref[rows, :] = d_first
        d_branch = d_first.astype(BF)
        dbranch_ref[rows, :] = d_branch
        sums_ref[0:1, :] += jnp.sum(d_branch.astype(F32), axis=0, keepdims=True)
        sums_ref[2:3, :] += d_shift
        sums_ref[4:5, :] += d_gain
        return carry

    lax.fori_loop(0, sum_ref.shape[0] // SHORT, chunk_step, 0)


def head_lanes(value, head):
    lane = lax.broadcasted_iota(jnp.int32, value.shape, 1)
    return (lane // (value.shape[1] // 2)) == head


def mask_row(kind, chunk, count):
    place = lax.broadcasted_iota(jnp.int32, (1, count), 1)
    allowed = (place // SHORT == chunk) | (kind == 1)
    return jnp.where(allowed, 0.0, MASKED_SCORE)


def attention_kernel(
    kind_ref, x_ref, wa_ref, wb_ref, bias_ref, wo_ref, partial_ref, qkv_ref, context_ref, lse_ref
):
    count = x_ref.shape[0]
    wide = wa_ref.shape[1]
    pair = 2 * HEAD_DIM
    kind = kind_ref[0]
    x = x_ref[...]
    bias = bias_ref[...]
    qkv_ref[:, :wide] = (dot(x, wa_ref[...]) + bias[:, :wide]).astype(BF)
    qkv_ref[:, wide:] = (dot(x, wb_ref[...]) + bias[:, wide:]).astype(BF)
    for p in range(HEADS // 4):
        keys = qkv_ref[:, (3 * p + 1) * pair : (3 * p + 2) * pair]
        values = qkv_ref[:, (3 * p + 2) * pair : (3 * p + 3) * pair]

        def chunk_step(chunk, carry):
            rows = pl.ds(pl.multiple_of(chunk * SHORT, SHORT), SHORT)
            queries = qkv_ref[rows, 3 * p * pair : (3 * p + 1) * pair] * jnp.asarray(0.125, BF)
            mask = mask_row(kind, chunk, count)
            found = []
            stats = lse_ref[rows, :] if p > 0 else jnp.zeros((SHORT, 128), F32)
            lane = lax.broadcasted_iota(jnp.int32, stats.shape, 1)
            for head in range(2):
                mine = jnp.where(head_lanes(queries, head), queries, jnp.zeros_like(queries))
                scores = dot_nt(mine, keys) + mask
                top = jnp.max(scores, axis=1, keepdims=True)
                powers = jnp.exp(scores - top)
                total = jnp.sum(powers, axis=1, keepdims=True)
                probs = powers * (1.0 / total)
                found.append(dot(probs.astype(BF), values))
                stats = jnp.where(lane == 2 * p + head, top + jnp.log(total), stats)
            lse_ref[rows, :] = stats
            both = jnp.where(head_lanes(found[0], 0), found[0], found[1])
            context_ref[rows, p * pair : (p + 1) * pair] = both.astype(BF)
            return carry

        lax.fori_loop(0, count // SHORT, chunk_step, 0)
    partial_ref[...] = dot(context_ref[...], wo_ref[...]).astype(BF)


def attention_backward_kernel(
    kind_ref, d_second_ref, mine_ref, theirs_ref, sum_ref, vec_ref,
    x_ref, qkv_ref, context_ref, lse_ref, wa_ref, wb_ref, wo_ref,
    ga_ref, gb_ref, gout_ref, partial_ref, sums_ref, d_first_ref, norm_sums_ref,
    dbranch_ref, dcontext_ref, dqkv_ref, dk_ref, dv_ref,
):
    back_first(
        d_second_ref, mine_ref, theirs_ref, sum_ref, vec_ref,
        d_first_ref, dbranch_ref, norm_sums_ref,
    )
    count = x_ref.shape[0]
    wide = wa_ref.shape[1]
    pair = 2 * HEAD_DIM
    kind = kind_ref[0]
    d_branch = dbranch_ref[...]
    dcontext_ref[...] = dot_nt(d_branch, wo_ref[...]).astype(BF)
    gout_ref[...] = dot_tn(context_ref[...], d_branch).astype(BF)
    for p in range(HEADS // 4):
        keys = qkv_ref[:, (3 * p + 1) * pair : (3 * p + 2) * pair]
        values = qkv_ref[:, (3 * p + 2) * pair : (3 * p + 3) * pair]
        dk_ref[...] = jnp.zeros_like(dk_ref)
        dv_ref[...] = jnp.zeros_like(dv_ref)

        def chunk_step(chunk, carry):
            rows = pl.ds(pl.multiple_of(chunk * SHORT, SHORT), SHORT)
            queries = qkv_ref[rows, 3 * p * pair : (3 * p + 1) * pair] * jnp.asarray(0.125, BF)
            d_context = dcontext_ref[rows, p * pair : (p + 1) * pair]
            mask = mask_row(kind, chunk, count)
            stats = lse_ref[rows, :]
            found = []
            for head in range(2):
                mine = jnp.where(head_lanes(queries, head), queries, jnp.zeros_like(queries))
                theirs = jnp.where(
                    head_lanes(d_context, head), d_context, jnp.zeros_like(d_context)
                )
                lse = stats[:, 2 * p + head : 2 * p + head + 1]
                probs = jnp.exp(dot_nt(mine, keys) + mask - lse)
                d_probs = dot_nt(theirs, values)
                row_dot = jnp.sum(d_probs * probs, axis=1, keepdims=True)
                d_scores = (probs * (d_probs - row_dot)).astype(BF)
                found.append(
                    (
                        dot(d_scores, keys) * 0.125,
                        dot_tn(d_scores, queries),
                        dot_tn(probs.astype(BF), d_context),
                    )
                )
            merged = [
                jnp.where(head_lanes(one, 0), one, other) for one, other in zip(*found)
            ]
            dqkv_ref[rows, 3 * p * pair : (3 * p + 1) * pair] = merged[0].astype(BF)
            dk_ref[...] += merged[1]
            dv_ref[...] += merged[2]
            return carry

        lax.fori_loop(0, count // SHORT, chunk_step, 0)
        dqkv_ref[:, (3 * p + 1) * pair : (3 * p + 2) * pair] = dk_ref[...].astype(BF)
        dqkv_ref[:, (3 * p + 2) * pair : (3 * p + 3) * pair] = dv_ref[...].astype(BF)
    d_a = dqkv_ref[:, :wide]
    d_b = dqkv_ref[:, wide:]
    x = x_ref[...]
    ga_ref[...] = dot_tn(x, d_a).astype(BF)
    gb_ref[...] = dot_tn(x, d_b).astype(BF)
    partial_ref[...] = (dot_nt(d_a, wa_ref[...]) + dot_nt(d_b, wb_ref[...])).astype(BF)
    sums_ref[:, :wide] = jnp.sum(d_a.astype(F32), axis=0, keepdims=True)
    sums_ref[:, wide:] = jnp.sum(d_b.astype(F32), axis=0, keepdims=True)


def kernel_call(body, shapes, scratch, *operands):
    in_vmem = pl.BlockSpec(memory_space=pltpu.VMEM)
    in_smem = pl.BlockSpec(memory_space=pltpu.SMEM)
    return pl.pallas_call(
        body,
        out_shape=shapes,
        in_specs=[in_smem if value.dtype == jnp.int32 else in_vmem for value in operands],
        out_specs=[in_vmem] * len(shapes),
        scratch_shapes=scratch,
        compiler_params=pltpu.CompilerParams(vmem_limit_bytes=VMEM_LIMIT),
        cost_estimate=pl.CostEstimate(flops=0, bytes_accessed=0, transcendentals=0),
    )(*operands)


def attention(row_kind, inputs_b, w_a, w_b, bias, w_out):
    count, width = inputs_b.shape
    half = w_out.shape[0]
    shapes = [
        jax.ShapeDtypeStruct((count, width), BF),
        jax.ShapeDtypeStruct((count, 3 * half), BF),
        jax.ShapeDtypeStruct((count, half), BF),
        jax.ShapeDtypeStruct((count, 128), F32),
    ]
    return kernel_call(
        attention_kernel, shapes, [], row_kind, inputs_b, w_a, w_b, bias, w_out
    )


def attention_backward(
    row_kind, d_second, mine, theirs, first_sum, vec, inputs_b, qkv, context, lse, w_a, w_b, w_out
):
    count, width = inputs_b.shape
    half = w_out.shape[0]
    shapes = [
        jax.ShapeDtypeStruct(w_a.shape, BF),
        jax.ShapeDtypeStruct(w_b.shape, BF),
        jax.ShapeDtypeStruct(w_out.shape, BF),
        jax.ShapeDtypeStruct((count, width), BF),
        jax.ShapeDtypeStruct((1, 3 * half), F32),
        jax.ShapeDtypeStruct((count, width), F32),
        jax.ShapeDtypeStruct((8, width), F32),
    ]
    scratch = [
        pltpu.VMEM((count, width), BF),
        pltpu.VMEM((count, half), BF),
        pltpu.VMEM((count, 3 * half), BF),
        pltpu.VMEM((count, 2 * HEAD_DIM), F32),
        pltpu.VMEM((count, 2 * HEAD_DIM), F32),
    ]
    return kernel_call(
        attention_backward_kernel, shapes, scratch, row_kind, d_second, mine, theirs, first_sum,
        vec, inputs_b, qkv, context, lse, w_a, w_b, w_out,
    )


def norm_rows(base, mine, theirs, vec):
    shapes = [jax.ShapeDtypeStruct(base.shape, kind) for kind in (F32, F32, BF)]
    return kernel_call(norm_kernel, shapes, [], base, mine, theirs, vec)


def hidden_layer(x, mine, theirs, vec, bias, up0, up1, down):
    count, hidden = x.shape[0], down.shape[0]
    shapes = [jax.ShapeDtypeStruct(x.shape, kind) for kind in (F32, F32, BF)]
    shapes += [jax.ShapeDtypeStruct((count, hidden), BF)] * 2
    shapes.append(jax.ShapeDtypeStruct(x.shape, BF))
    return kernel_call(
        hidden_kernel, shapes, [], x, mine, theirs, vec, bias, up0, up1, down
    )


def back_second(upstream, total, vec, act):
    shapes = [
        jax.ShapeDtypeStruct(total.shape, F32),
        jax.ShapeDtypeStruct(total.shape, BF),
        jax.ShapeDtypeStruct((act.shape[1], total.shape[1]), BF),
        jax.ShapeDtypeStruct((8, total.shape[1]), F32),
    ]
    body = functools.partial(back_second_kernel, len(upstream) > 1)
    return kernel_call(body, shapes, [], *upstream, total, vec, act)


def back_hidden(d_ffn, slope, normed_b, down, up0, up1):
    count, hidden = slope.shape
    width = normed_b.shape[1]
    shapes = [
        jax.ShapeDtypeStruct(up0.shape, BF),
        jax.ShapeDtypeStruct(up1.shape, BF),
        jax.ShapeDtypeStruct((count, width), BF),
        jax.ShapeDtypeStruct((1, hidden), F32),
    ]
    scratch = [pltpu.VMEM((count, hidden), BF)]
    return kernel_call(
        back_hidden_kernel, shapes, scratch, d_ffn, slope, normed_b, down, up0, up1
    )


def hidden_order(width, hidden_rows):
    group = width // (2 * hidden_rows)
    target = jnp.arange(width)
    source = (
        (target % (width // 2)) // hidden_rows * (2 * hidden_rows)
        + target // (width // 2) * hidden_rows
        + target % hidden_rows
    )
    del group
    return jnp.arange(width)[:, None] == source[None, :]


def shards(tokens, row_kind, w_qkv, w_out, w_up, w_down, bias_vectors, gains, bias_up, cotangent):
    chips = Chips()
    sequence = Sequence()
    core = chips.core
    count = chips.count
    device = 2 * chips.chip + core
    row_type = row_kind[0]
    rows, width = w_out.shape[1:]
    hidden = w_up.shape[2]
    hidden_rows = w_down.shape[1]
    half = width // 2
    panels = hidden // 2 // width
    own = tokens.shape[0]
    order = hidden_order(width, hidden_rows)

    pairs = HEADS // 4
    lane = half // pairs
    plan = Plan()
    state = State()

    def ordered(mine, theirs):
        return jnp.where(core == 0, mine, theirs), jnp.where(core == 0, theirs, mine)

    def pack_qkv():
        cols = w_qkv.reshape(LAYERS, rows, 3, 2, pairs, lane)

        def side(which):
            return jnp.swapaxes(pick(cols, which, 3), 2, 3).reshape(LAYERS, rows, 3 * half)

        feature = jnp.arange(width)[None, :] - rows * device == jnp.arange(rows)[:, None]
        unit = jnp.arange(hidden // 2)[None, :] - hidden_rows * chips.chip
        unit = unit == jnp.arange(hidden_rows)[:, None]
        table = jnp.concatenate([bias_vectors, gains], axis=1).reshape(LAYERS * 8, rows)
        table = dot(table, feature.astype(BF)).astype(BF)
        units = dot(bias_up, unit.astype(BF)).astype(BF)
        got = swap(side(1 - core), 1)
        table = table + swap(table, 1)
        cols = merge(side(core), got, core, 1)
        for layer in range(LAYERS):
            last = cols[layer, :, :, width:].reshape(2 * rows, half)
            outs = jnp.concatenate([w_out[layer, :, :half], w_out[layer, :, half:]], axis=0)
            vectors = [table[8 * layer : 8 * layer + 8]]
            vectors += [units[layer : layer + 1, i * width :][:, :width] for i in range(panels)]
            vectors.append(jnp.zeros((8 - panels, width), BF))
            state.gathers[ATTN, layer] = Gather(
                chips, sequence, EARLY[layer],
                jnp.concatenate(
                    [
                        cols[layer, :, :, :width].reshape(2 * rows, width),
                        jnp.concatenate([last, outs], axis=1),
                        *vectors,
                    ],
                    axis=0,
                ),
            )
        sequence.mark([state.gathers[ATTN, layer].held for layer in range(LAYERS)])

    groups = hidden // width

    def pack_up():
        value = sequence.gate(w_up).reshape(LAYERS * rows, hidden)
        stacked = jnp.concatenate(
            [value[:, i * width : (i + 1) * width] for i in range(groups)], axis=0
        )
        stacked = dot(stacked, order.astype(BF)).astype(BF)
        mine, sent = ordered(stacked[:, :half], stacked[:, half:])
        first, second = ordered(mine, swap(sent, 1))
        for layer in range(LAYERS):
            parts = []
            for i in range(panels):
                for value in (first, second):
                    cut = [
                        value[((2 * i + j) * LAYERS + layer) * rows :][:rows] for j in range(2)
                    ]
                    parts.append(jnp.concatenate(cut, axis=1))
            state.gathers[FFN, layer] = Gather(
                chips, sequence, EARLY[LAYERS + layer],
                jnp.concatenate(parts + [w_down[layer]], axis=0),
            )
        sequence.mark([state.gathers[FFN, layer].held for layer in range(LAYERS)])

    def read_vectors(layer, table):
        table = jnp.sum(table.astype(F32), axis=0)
        vec = table[:8]
        bias_q, bias_v = (
            jnp.where(core == 0, vec[i : i + 1, :half], vec[i : i + 1, half:]) for i in range(2)
        )
        bias = []
        for p in range(pairs):
            cut = slice(p * lane, (p + 1) * lane)
            bias += [bias_q[:, cut], jnp.zeros((1, lane), F32), bias_v[:, cut]]
        state.vec[layer] = vec
        state.bias_qkv[layer] = jnp.concatenate(bias, axis=1)
        state.bias_up[layer] = jnp.concatenate(
            [table[8 + i : 9 + i] for i in range(panels)], axis=1
        )

    def tokens_start():
        value = sequence.gate(tokens)
        sequence.mark(value)
        state.pair_tokens = (value, swap(value, 1))

    def tokens_end():
        values = sequence.gate(state.pair_tokens)
        state.x_b[0] = jnp.concatenate(ordered(*values), axis=0)
        state.x[0] = state.x_b[0].astype(F32)
        sequence.mark(state.x_b[0])

    def cotangent_start():
        value = sequence.gate(cotangent)
        sequence.mark(value)
        state.pair_cotangent = (value, swap(value, 1))

    def cotangent_end():
        values = sequence.gate(state.pair_cotangent)
        state.upstream = (jnp.concatenate(ordered(*values), axis=0),)
        sequence.mark(state.upstream)

    def out_exchange(layer):
        ends = [0, 2 * rows, 4 * rows, 4 * rows + 16]
        first, second, table = state.gathers[ATTN, layer].finish(list(zip(ends[:-1], ends[1:])))
        w_b = second[:, :, :half].reshape(width, half)
        out_all = second[:, :, half:].reshape(2, count // 2, 2 * rows, half)
        sent = pick(out_all, 1 - core, 0)
        read_vectors(layer, table)
        sequence.mark((sent, w_b, state.vec[layer]))
        parts = ordered(pick(out_all, core, 0), swap(sent, 1))
        parts = [jnp.concatenate([part[:, :rows], part[:, rows:]], axis=2) for part in parts]
        full_out = jnp.stack(parts, axis=1).reshape(half, width)
        state.w_attn[layer] = (first.reshape(width, width), w_b, full_out)

    def hidden_weights(layer):
        ends = [2 * rows * i for i in range(panels + 1)]
        ends.append(ends[-1] + hidden_rows)
        *ups, down = state.gathers[FFN, layer].finish(list(zip(ends[:-1], ends[1:])))
        state.w_hidden[layer] = (
            down.reshape(hidden // 2, width), *(value.reshape(width, width) for value in ups)
        )

    def run_attention(layer):
        x_b, weights = sequence.gate((state.x_b[layer], state.w_attn[layer]))
        w_a, w_b, full_out = weights
        partial, *saved = attention(row_kind, x_b, w_a, w_b, state.bias_qkv[layer], full_out)
        sequence.mark(partial)
        state.w_attn[layer] = weights
        state.saved[layer] = (x_b, *saved)
        state.branch = (partial, swap(partial, 1))

    def run_hidden(layer):
        mine, theirs = sequence.gate(state.branch)
        down, up0, up1 = state.w_hidden[layer]
        first_sum, state.normed, *kept, partial = hidden_layer(
            state.x[layer], mine, theirs, state.vec[layer], state.bias_up[layer], up0, up1, down
        )
        sequence.mark(partial)
        state.first_sum[layer] = first_sum
        state.kept[layer] = kept
        state.branch = (partial, swap(partial, 1))

    def run_norm(layer):
        mine, theirs = sequence.gate(state.branch)
        second, x, x_b = norm_rows(state.normed, mine, theirs, state.vec[layer])
        state.second[layer], state.x[layer + 1], state.x_b[layer + 1] = second, x, x_b
        sequence.mark(second)

    def run_back_second(layer):
        upstream = sequence.gate(state.upstream)
        if layer < LAYERS - 1:
            upstream = (state.d_first, *upstream)
        act = state.kept[layer][1]
        d_second, d_ffn, g_down, sums = back_second(
            upstream, state.second[layer], state.vec[layer], act
        )
        state.d_second, state.d_ffn = d_second, d_ffn
        state.sums2[layer] = sums
        bundle = state.scatters[FFN, layer]
        bundle.start(0, [g_down.reshape(count, hidden_rows, width)])
        sequence.mark((d_ffn, bundle.sent))

    def run_back_hidden(layer):
        d_ffn = sequence.gate(state.d_ffn)
        normed_b, _, slope = state.kept[layer]
        *g_up, partial, units = back_hidden(d_ffn, slope, normed_b, *state.w_hidden[layer])
        bundle = state.scatters[FFN, layer]
        bundle.start(1, [value.reshape(count, 2 * rows, width) for value in g_up])
        sequence.mark((partial, bundle.sent))
        state.units[layer] = units
        state.branch = (partial, swap(partial, 1))

    def run_back_attention(layer):
        mine, theirs = sequence.gate(state.branch)
        x_b, qkv, context, lse = state.saved[layer]
        g_a, g_b, g_out, partial, sums, state.d_first, state.sums1[layer] = attention_backward(
            row_kind, state.d_second, mine, theirs, state.first_sum[layer], state.vec[layer],
            x_b, qkv, context, lse, *state.w_attn[layer],
        )
        sequence.mark(partial)
        state.pair[layer] = jnp.concatenate(
            [
                jnp.concatenate(
                    [sums[:, (3 * p + t) * lane :][:, :lane] for p in range(pairs)], axis=1
                )
                for t in (0, 2)
            ],
            axis=0,
        )
        if layer > 0:
            state.upstream = (partial, swap(partial, 1))
        else:
            mine, sent = ordered(partial[:own], partial[own:])
            state.upstream = (mine, swap(sent, 1))
        state.g_attn[layer] = (g_a, g_b, g_out)

    def sum_rows(layer):
        pair = state.pair[layer]
        nothing = jnp.zeros_like(pair)
        pair = jnp.concatenate(ordered(pair, nothing), axis=1)
        units = [state.units[layer][:, i * width :][:, :width] for i in range(panels)]
        small = jnp.concatenate([state.sums1[layer] + state.sums2[layer], pair, *units], axis=0)
        small = jnp.pad(small.astype(BF), ((0, 16 - small.shape[0]), (0, 0)))
        line = jnp.arange(16)[:, None]
        place = jnp.arange(width)[None, :]
        owner = jnp.where(
            line < 10, place // (2 * rows), ((line - 10) * width + place) // hidden_rows
        )
        mine = owner[None] == jnp.arange(count)[:, None, None]
        return jnp.where(mine, small[None], jnp.zeros((), BF))

    def back_terms(layer):
        g_a, g_b, g_out = sequence.gate(state.g_attn[layer])
        bundle = state.scatters[ATTN, layer]
        out_pair = g_out.reshape(count // 2, 2, rows, width)
        out_got = swap(pick(out_pair, 1 - core, 1), 1)
        out = merge(pick(out_pair, core, 1), out_got, core, 0).reshape(count, rows, width)
        g_b = g_b.reshape(count, 2 * rows, half)
        out = jnp.concatenate([out[:, :, :half], out[:, :, half:]], axis=1)
        rest = jnp.concatenate([g_b, out], axis=2)
        rest = jnp.concatenate([rest, sum_rows(layer)], axis=1)
        rest = lax.optimization_barrier(rest)
        bundle.start(0, [g_a.reshape(count, 2 * rows, width), rest])
        sequence.mark(bundle.sent)

    def grad_end():
        mine, theirs = sequence.gate(state.upstream)
        d_first = lax.dynamic_slice_in_dim(state.d_first, core * own, own)
        state.grad_tokens = d_first + (mine.astype(F32) + theirs.astype(F32))
        sequence.mark(state.grad_tokens)

    def mixed_end():
        value = sequence.gate(state.x_b[LAYERS])
        state.mixed = lax.dynamic_slice_in_dim(value, core * own, own)
        sequence.mark(state.mixed)

    def finish_hidden(layer):
        down, *ups = state.scatters[FFN, layer].finish()
        sides = [
            jnp.concatenate([up[side * rows :][:rows] for up in ups], axis=1)
            for side in range(2)
        ]
        mine, sent = ordered(*sides)
        state.up_pair[layer] = (mine, swap(sent, 1))
        state.down[layer] = down

    def end_hidden(layer):
        first, second = ordered(*sequence.gate(state.up_pair[layer]))
        stacked = jnp.concatenate(
            [
                jnp.concatenate(
                    [value[:, i * half : (i + 1) * half] for value in (first, second)], axis=1
                )
                for i in range(groups)
            ],
            axis=0,
        )
        stacked = lax.dot_general(
            stacked, order.astype(F32), (((1,), (1,)), ((), ())),
            precision=lax.Precision.HIGHEST, preferred_element_type=F32,
        )
        state.up[layer] = jnp.concatenate(
            [stacked[i * rows : (i + 1) * rows] for i in range(groups)], axis=1
        )
        sequence.mark(state.up[layer])

    def finish_attention(layer):
        first, rest = state.scatters[ATTN, layer].finish()
        last, out, small = rest[: 2 * rows, :half], rest[: 2 * rows, half:], rest[2 * rows :]
        out = jnp.concatenate([out[:rows], out[rows:]], axis=1)
        sides = [
            jnp.concatenate([value[side * rows :][:rows] for value in (first, last)], axis=1)
            for side in range(2)
        ]
        mine, sent = ordered(*sides)
        pair = jnp.pad(small[8:], ((0, 0), (0, mine.shape[1] - width)))
        sent = jnp.concatenate([sent, pair], axis=0)
        state.qkv_pair[layer] = (mine, swap(sent, 1))
        state.out[layer] = out
        state.small_rows[layer] = small

    def end_attention(layer):
        mine, theirs = sequence.gate(state.qkv_pair[layer])
        small = state.small_rows[layer]
        small = jnp.concatenate([theirs[rows : rows + 2, :width] + small[8:10], small], axis=0)
        features = lax.dynamic_slice_in_dim(small, rows * device, rows, axis=1)
        per_row = width // hidden_rows
        units = lax.dynamic_slice(
            small,
            (12 + chips.chip // per_row, hidden_rows * (chips.chip % per_row)),
            (1, hidden_rows),
        )
        state.vectors[layer] = features[:6]
        state.gains[layer] = features[6:8]
        state.unit_sums[layer] = units[0]
        values = ordered(mine, theirs[:rows])
        state.qkv[layer] = jnp.concatenate(
            [
                value[:, (3 * p + t) * lane :][:, :lane]
                for t in range(3)
                for value in values
                for p in range(pairs)
            ],
            axis=1,
        )
        sequence.mark(state.qkv[layer])

    def call(function, *args):
        return lambda: function(*args)

    low = len(chips.low)
    size = (1.0, 2.0)
    add = plan.add

    def pair_send(label):
        return [(label, (("p", 0.0),), 1)]

    def plane(length):
        return (("x", length), ("y", length))

    add("pq", 0, 6.0, [], pack_qkv)
    add("pu", 2, 3.0, [("g", ATTN, 0)], pack_up)
    add("tok", 8, 0.5, ["pu"], tokens_start, pair_send("x0"))
    add("te", 7, 1.5, ["x0"], tokens_end)
    add("cot", 9, 0.5, [("m", 1, 0)], cotangent_start, pair_send("ct"))
    add("ce", 9, 1.2, ["ct"], cotangent_end)
    bundles = [(ATTN, 0), (FFN, 0), (ATTN, 1), (FFN, 1)]
    for rank, (kind, layer) in enumerate(bundles):
        needs = ["pq" if kind == ATTN else "pu"]

        def start(kind=kind, layer=layer):
            state.gathers[kind, layer].start()

        def advance(kind=kind, layer=layer):
            state.gathers[kind, layer].advance()

        units = 7.0 / 3 if kind == ATTN else 4.0
        tops = [("top", 2), ("top", 1)]
        lows = [("low", step) for step in range(low)]
        early = EARLY[LAYERS * kind + layer]
        steps = lows[:1] + tops + lows[1:] if early else tops + lows
        need = None
        held = 1
        for number, (bits, step) in enumerate(steps):
            length = UNIT / 2 * units * held
            held *= 2
            if bits == "low":
                links = plane(length)
            elif step == 2:
                links = (("z", 2 * length), ("w", 5 * length + 1.5))
            else:
                links = (("z", 2 * length),)
            sent = ("gx", kind, layer, number)
            if number == 0:
                add(("g", kind, layer), 1 + rank, 3.5, needs, start, [(sent, links, 1)])
            else:
                add(
                    ("gs", kind, layer, number), 1 + rank, 1.0 + 0.1 * held + (2.8 if len(links) > 1 and links[1][0] == "w" else 1.4),
                    [need], advance, [(sent, links, 1)],
                )
            need = sent
        if kind == ATTN:
            add(
                ("go", layer), 1 + rank, 4.5, [need], call(out_exchange, layer),
                pair_send(("w", kind, layer)),
            )
        else:
            add(("w", kind, layer), 1 + rank, 1.6, [need], call(hidden_weights, layer))
    need = "te"
    for layer in range(LAYERS):
        add(
            ("m", 0, layer), 10, 12.7, [need, ("w", ATTN, layer)],
            call(run_attention, layer), pair_send(("p", 0, layer)),
        )
        add(
            ("m", 1, layer), 10, 6.0, [("p", 0, layer), ("w", FFN, layer)],
            call(run_hidden, layer), pair_send(("p", 1, layer)),
        )
        need = ("m", 2, layer)
        add(need, 10, 3.0, [("p", 1, layer)], call(run_norm, layer))
    add("mix", 20, 1.0, [need], mixed_end)

    needs = [need, "ce"]
    for layer in reversed(range(LAYERS)):
        state.scatters[FFN, layer] = Scatter(chips, sequence, 2, LATE[LAYERS + layer])
        state.scatters[ATTN, layer] = Scatter(chips, sequence, 1, LATE[layer])
        add(
            ("b", 0, layer), 10, 5.0, needs, call(run_back_second, layer),
            [(("r", FFN, layer, 0), plane(UNIT * 8), 1)],
        )
        add(
            ("b", 1, layer), 10, 6.5, [("b", 0, layer)], call(run_back_hidden, layer),
            [(("r", FFN, layer, 1), plane(UNIT * 8), 1)] + pair_send(("p", 2, layer)),
        )
        add(
            ("b", 2, layer), 10, 17.2, [("p", 2, layer)], call(run_back_attention, layer),
            pair_send(("p", 3, layer)),
        )
        add(
            ("b", 3, layer), 9.5, 6.0, [("b", 2, layer)], call(back_terms, layer),
            [(("r", ATTN, layer, 0), plane(UNIT * 28 / 3), 1)],
        )
        needs = [("p", 3, layer)]
        for kind in (FFN, ATTN):
            need = [("r", kind, layer, part) for part in range(1 + kind)]
            rank = 1 + 2 * (LAYERS - 1 - layer) + (kind == ATTN)

            def reduce(kind=kind, layer=layer):
                state.scatters[kind, layer].advance()

            units = 7.0 / 3 if kind == ATTN else 4.0
            tops = [("top", 1), ("top", 2)]
            lows = [("low", step) for step in range(low - 1)][::-1]
            late = LATE[LAYERS * kind + layer]
            steps = lows[:-1] + tops + lows[-1:] if late else lows + tops
            held = 2 * count // 4
            for number, (bits, step) in enumerate(steps):
                held //= 2
                length = UNIT / 2 * units * held
                cost = 1.0 + 0.1 * held
                if bits == "low":
                    cost, links = cost + 1.4, plane(length)
                elif step == 2:
                    cost, links = cost + 2.8, (("z", 2 * length), ("w", 5 * length + 1.5))
                else:
                    cost, links = cost + 1.4, (("z", 2 * length),)
                sent = ("rx", kind, layer, number)
                add(("rs", kind, layer, number), rank, cost, need, reduce, [(sent, links, 1)])
                need = [sent]
            last = finish_hidden if kind == FFN else finish_attention
            add(
                ("rf", kind, layer), 19, 2.0, need, call(last, layer),
                pair_send(("re", kind, layer)),
            )
            last = end_hidden if kind == FFN else end_attention
            add(("ro", kind, layer), 20, 2.5, [("re", kind, layer)], call(last, layer))
    add("grad", 18, 1.2, needs, grad_end)
    plan.run()

    def stacked(values):
        return jnp.stack([values[layer] for layer in range(LAYERS)])

    return (
        state.mixed,
        state.grad_tokens,
        stacked(state.qkv),
        stacked(state.out),
        stacked(state.up),
        stacked(state.down),
        stacked(state.vectors),
        stacked(state.gains),
        stacked(state.unit_sums),
    )


def solution(mesh):
    placed = (
        P("fsdp", None),
        P("fsdp"),
        P(None, "fsdp", None),
        P(None, "fsdp", None),
        P(None, "fsdp", None),
        P(None, "fsdp", None),
        P(None, None, "fsdp"),
        P(None, None, "fsdp"),
        P(None, "fsdp"),
        P("fsdp", None),
    )
    return jax.shard_map(
        shards,
        mesh=mesh,
        in_specs=placed,
        out_specs=(
            P("fsdp", None),
            P("fsdp", None),
            P(None, "fsdp", None),
            P(None, "fsdp", None),
            P(None, "fsdp", None),
            P(None, "fsdp", None),
            P(None, None, "fsdp"),
            P(None, None, "fsdp"),
            P(None, "fsdp"),
        ),
        check_vma=False,
    )
```

```python
import functools

import jax
import jax.numpy as jnp
from jax import lax
from jax.experimental import pallas as pl
from jax.experimental.pallas import tpu as pltpu
from jax.sharding import PartitionSpec as P

HEADS = 12
HEAD_DIM = 64
LAYERS = 2
SHORT = 128
AXIS = "fsdp"

EPSILON = 1e-05
MASKED_SCORE = -1e30
BF = jnp.bfloat16
F32 = jnp.float32
LATENCY = 2.5
UNIT = 1.48
ATTN, FFN = 0, 1
OPEN_SENDS = 5
VMEM_LIMIT = 16 * 2**20
EARLY = (False, False, False, False)
LATE = (False, False, False, False)
ORDER = (
    0, 6, 1, 2, 7, 11, 16, 8, 3, 12, 21, 9, 13, 17, 14, 10, 22, 15, 23, 18, 26, 19, 24,
    27, 28, 20, 4, 29, 5, 25, 30, 31, 33, 34, 35, 36, 37, 47, 48, 49, 38, 42, 51, 43, 39,
    50, 52, 61, 40, 44, 56, 53, 45, 57, 58, 54, 59, 55, 60, 46, 41, 32,
)


def dot(left, right):
    return jnp.dot(left, right, preferred_element_type=F32)


def dot_tn(left, right):
    return lax.dot_general(left, right, (((0,), (0,)), ((), ())), preferred_element_type=F32)


def dot_nt(left, right):
    return lax.dot_general(left, right, (((1,), (1,)), ((), ())), preferred_element_type=F32)


def swap(value, mask):
    pairs = [(source, source ^ mask) for source in range(lax.axis_size(AXIS))]
    return lax.ppermute(value, AXIS, pairs)


def merge(mine, theirs, bit, axis):
    first = jnp.where(bit == 0, mine, theirs)
    second = jnp.where(bit == 0, theirs, mine)
    return jnp.stack([first, second], axis=axis)


def pick(pair, index, axis):
    return lax.dynamic_index_in_dim(pair, index, axis, keepdims=False)


class Chips:
    def __init__(self):
        device = lax.axis_index(AXIS)
        self.count = lax.axis_size(AXIS) // 2
        self.core = device % 2
        self.chip = device // 2
        self.step = self.count // 4
        self.top = self.chip // self.step
        self.low = list(range(self.count.bit_length() - 3))
        self.info = self.table()

    def bit(self, place):
        return (self.chip // 2**place) % 2

    def plane_bit(self, step):
        return jnp.where(self.core == 0, self.bit(step), self.bit(len(self.low) - 1 - step))

    def plane_swap(self, value, step):
        masks = (2 * 2**step, 2 * 2 ** (len(self.low) - 1 - step))
        pairs = [(source, source ^ masks[source % 2]) for source in range(2 * self.count)]
        return lax.ppermute(value, AXIS, pairs)

    def table(self):
        bits = [self.plane_bit(step) for step in range(len(self.low))]
        entries = [self.core] + bits + [self.top % 2, self.top // 2]
        return jnp.stack(entries).astype(jnp.int32)


def half_place(table, step, index, own):
    bit = table[1 + step]
    bit = bit if own else 1 - bit
    return jnp.where(table[0] == 0, 2**step * bit + index, 2 * index + bit)


def merge_place(table, kind, step, low, half, index, own):
    if kind == "low":
        return half_place(table, step, index, own)
    bit = table[low + step]
    return half * (bit if own else 1 - bit) + index


class Sequence:
    def __init__(self):
        self.last = None

    def gate(self, values):
        if self.last is None:
            return values
        values, _ = lax.optimization_barrier((values, self.last))
        return values

    def mark(self, values):
        self.last = values


class State:
    def __getattr__(self, name):
        value = {}
        setattr(self, name, value)
        return value


class Plan:
    def __init__(self):
        self.pieces = []

    def add(self, name, rank, cost, needs, run, sends=()):
        self.pieces.append((name, rank, cost, needs, run, sends))

    def greedy(self):
        now = 0.0
        ready = {}
        free = {}
        open_sends = {}
        waiting = list(range(len(self.pieces)))
        order = []

        def fits(piece):
            held = sum(weight for label, weight in open_sends.items() if label not in piece[3])
            added = sum(weight for _, _, weight in piece[5])
            return added == 0 or held + added <= OPEN_SENDS

        while waiting:
            known = []
            for place in waiting:
                piece = self.pieces[place]
                if all(need in ready for need in piece[3]):
                    time = max([ready[need] for need in piece[3]], default=0.0)
                    known.append((time, piece[1], place))
            known = [entry for entry in known if fits(self.pieces[entry[2]])] or known
            able = [entry[1:] for entry in known if entry[0] <= now]
            place = min(able)[1] if able else min(known)[2]
            name, _, cost, needs, _, sends = self.pieces[place]
            now = max([now] + [ready[need] for need in needs]) + cost
            ready[name] = now
            for need in needs:
                open_sends.pop(need, None)
            for label, links, weight in sends:
                ready[label] = 0.0
                for link, length in links:
                    free[link] = max(now, free.get(link, 0.0)) + length
                    ready[label] = max(ready[label], free[link] + LATENCY)
                if weight > 0:
                    open_sends[label] = weight
            waiting.remove(place)
            order.append(place)
        return order

    def run(self):
        order = ORDER if len(ORDER) == len(self.pieces) else self.greedy()
        for place in order:
            self.pieces[place][4]()


class Gather:
    def __init__(self, chips, sequence, early, piece):
        self.chips, self.sequence = chips, sequence
        low = [("low", step) for step in range(len(chips.low))]
        top = [("top", 2), ("top", 1)]
        self.steps = low[:1] + top + low[1:] if early else top + low
        self.held = piece[None, None]

    def start(self):
        self.held = self.sequence.gate(self.held)
        self.sequence.mark(self.held)
        self.send()

    def send(self):
        kind, step = self.steps[0]
        if kind == "low":
            self.coming = self.chips.plane_swap(self.held, step)
        else:
            self.coming = swap(self.held, 2 * step * self.chips.step)

    def merged(self, ranges=None):
        chips = self.chips
        coming = self.sequence.gate(self.coming)
        kind, step = self.steps.pop(0)
        if kind == "low":
            return merge_rows(chips, kind, step, self.held, coming, ranges)
        lead, half, height, width = self.held.shape
        flat = [value.reshape(lead, 1, half * height, width) for value in (self.held, coming)]
        return merge_rows(chips, kind, step, *flat).reshape(2 * lead, half, height, width)

    def advance(self):
        self.held = self.merged()
        self.sequence.mark(self.held)
        self.send()

    def finish(self, ranges):
        while len(self.steps) > 1:
            self.advance()
        results = self.merged(ranges)
        results = [whole.reshape((self.chips.count,) + whole.shape[2:]) for whole in results]
        self.sequence.mark(results)
        return results


def merge_kernel(ranges, place, table_ref, mine_ref, theirs_ref, *out_refs):
    for index in range(mine_ref.shape[1]):
        own, other = place(table_ref, index, True), place(table_ref, index, False)
        for lead in range(mine_ref.shape[0]):
            for (start, stop), out_ref in zip(ranges, out_refs):
                out_ref[lead, own] = mine_ref[lead, index, start:stop]
                out_ref[lead, other] = theirs_ref[lead, index, start:stop]


def merge_rows(chips, kind, step, mine, theirs, ranges=None):
    half = mine.shape[1]
    cuts = ranges or [(0, mine.shape[2])]

    def place(table, index, own):
        return merge_place(table, kind, step, len(chips.low), half, index, own)

    shapes = [
        jax.ShapeDtypeStruct((mine.shape[0], 2 * half, stop - start, mine.shape[3]), BF)
        for start, stop in cuts
    ]
    if all(edge % 16 == 0 for cut in cuts for edge in cut):
        results = kernel_call(
            functools.partial(merge_kernel, cuts, place), shapes, [], chips.info, mine, theirs
        )
    else:
        sides = [place(chips.info, jnp.arange(half), own) for own in (True, False)]
        results = []
        for (start, stop), shape in zip(cuts, shapes):
            whole = jnp.zeros(shape.shape, BF)
            for side, value in zip(sides, (mine, theirs)):
                whole = whole.at[:, side].set(value[:, :, start:stop])
            results.append(whole)
    return results if ranges else results[0]


class Scatter:
    def __init__(self, chips, sequence, count, late):
        self.chips, self.sequence = chips, sequence
        low = [("low", step) for step in range(len(chips.low) - 1)][::-1]
        top = [("top", 1), ("top", 2)]
        self.steps = low[:-1] + top + low[-1:] if late else low + top
        self.arrays = [None] * count
        self.coming = [None] * count
        self.heights = None

    def start(self, part, arrays):
        chips = self.chips
        step = len(chips.low) - 1
        shape = (4, 2 ** len(chips.low))
        arrays = [value.reshape(shape + value.shape[1:]) for value in arrays]
        self.arrays[part] = arrays
        sent = send_rows(chips, step, arrays)
        self.coming[part] = chips.plane_swap(sent, step)
        self.sent = sent

    def advance(self):
        chips = self.chips
        coming = self.sequence.gate(self.coming)
        first = self.heights is None
        if first:
            self.heights = [value.shape[2] for part in self.arrays for value in part]
        else:
            self.arrays, coming = [[self.kept]], [coming]
        kind, step = self.steps.pop(0)
        if kind == "top":
            self.arrays = [
                [value.reshape((-1, 2 * value.shape[1]) + value.shape[2:]) for value in part]
                for part in self.arrays
            ]
            coming = [got.reshape((-1, 2 * got.shape[1]) + got.shape[2:]) for got in coming]
        sent, self.kept = fold_rows(chips, kind, step, first, self.arrays, coming)
        self.sequence.mark(sent)
        if kind == "low":
            self.coming = chips.plane_swap(sent, step)
        else:
            self.coming = swap(sent, 2 * step * chips.step)

    def finish(self):
        coming = self.sequence.gate(self.coming)
        total = self.kept[0, 0] + coming[0, 0].astype(F32)
        self.sequence.mark(total)
        ends = [sum(self.heights[:i]) for i in range(len(self.heights) + 1)]
        return [total[start:stop] for start, stop in zip(ends[:-1], ends[1:])]


def send_kernel(step, heights, table_ref, *refs):
    *array_refs, sent_ref = refs
    for index in range(sent_ref.shape[1]):
        place = half_place(table_ref, step, index, False)
        for lead in range(sent_ref.shape[0]):
            row = 0
            for height, ref in zip(heights, array_refs):
                sent_ref[lead, index, row : row + height] = ref[lead, place]
                row += height


def send_rows(chips, step, arrays):
    heights = [value.shape[2] for value in arrays]
    shape = (arrays[0].shape[0], 2**step, sum(heights), arrays[0].shape[3])
    if any(height % 16 for height in heights):
        places = half_place(chips.info, step, jnp.arange(2**step), False)
        return jnp.concatenate([jnp.take(value, places, axis=1) for value in arrays], axis=2)
    (sent,) = kernel_call(
        functools.partial(send_kernel, step, heights), [jax.ShapeDtypeStruct(shape, BF)], [],
        chips.info, *arrays,
    )
    return sent


def fold_kernel(layout, place, table_ref, *refs):
    *refs, sent_ref, kept_ref = refs
    for index in range(sent_ref.shape[1]):
        for own, out_ref in enumerate((sent_ref, kept_ref)):
            source, came = place(table_ref, index, own == 1)
            for lead in range(sent_ref.shape[0]):
                for array, got, start, height, row in layout:
                    mine = refs[array][lead, source]
                    theirs = refs[got][lead, came, start : start + height]
                    total = mine.astype(F32) + theirs.astype(F32)
                    out_ref[lead, index, row : row + height] = total.astype(out_ref.dtype)


def fold_rows(chips, kind, step, first, parts, coming):
    arrays = [value for part in parts for value in part]
    layout = []
    row = 0
    for part, got in zip(range(len(parts)), range(len(arrays), len(arrays) + len(coming))):
        start = 0
        for value in parts[part]:
            height = value.shape[2]
            layout.append((len(layout), got, start, height, row))
            start += height
            row += height
    half = coming[0].shape[1] // 2
    low = len(chips.low)

    def place(table, index, own):
        if kind == "low":
            came = half_place(table, step, index, own)
            return (half_place(table, low - 1, came, True) if first else came), came
        bit = table[low + step]
        bit = bit if own else 1 - bit
        came = half * bit + index
        if not first:
            return came, came
        return 2**low * bit + half_place(table, low - 1, index, True), came

    shape = (arrays[0].shape[0], half, row, arrays[0].shape[3])
    if any(value.shape[2] % 16 for value in arrays):
        results = []
        for own, dtype in ((False, BF), (True, F32)):
            source, came = place(chips.info, jnp.arange(half), own)
            totals = []
            for array, got, start, height, _ in layout:
                theirs = jnp.take(coming[got - len(arrays)], came, axis=1)
                theirs = theirs[:, :, start : start + height].astype(F32)
                totals.append(jnp.take(arrays[array], source, axis=1).astype(F32) + theirs)
            results.append(jnp.concatenate(totals, axis=2).astype(dtype))
        return results
    return kernel_call(
        functools.partial(fold_kernel, layout, place),
        [jax.ShapeDtypeStruct(shape, kind) for kind in (BF, F32)], [],
        chips.info, *arrays, *coming,
    )


ROOT_HALF = 0.7071067811865476
DENSITY = 0.3989422804014327


def unit_rows(values):
    centre = values - jnp.mean(values, axis=1, keepdims=True)
    scale = lax.rsqrt(jnp.mean(centre * centre, axis=1, keepdims=True) + EPSILON)
    return centre * scale, scale


def norm_kernel(base_ref, mine_ref, theirs_ref, vec_ref, sum_ref, out_ref, out_b_ref):
    def chunk_step(chunk, carry):
        rows = pl.ds(pl.multiple_of(chunk * SHORT, SHORT), SHORT)
        total = base_ref[rows, :] + (
            mine_ref[rows, :].astype(F32) + theirs_ref[rows, :].astype(F32)
        ) + vec_ref[3:4, :]
        sum_ref[rows, :] = total
        unit, _ = unit_rows(total)
        output = unit * vec_ref[7:8, :] + vec_ref[5:6, :]
        out_ref[rows, :] = output
        out_b_ref[rows, :] = output.astype(BF)
        return carry

    lax.fori_loop(0, base_ref.shape[0] // SHORT, chunk_step, 0)


def hidden_kernel(
    x_ref, mine_ref, theirs_ref, vec_ref, bias_ref, up0_ref, up1_ref, down_ref,
    sum_ref, normed_ref, normed_b_ref, act_ref, slope_ref, partial_ref,
):
    def chunk_step(chunk, carry):
        rows = pl.ds(pl.multiple_of(chunk * SHORT, SHORT), SHORT)
        total = x_ref[rows, :] + (
            mine_ref[rows, :].astype(F32) + theirs_ref[rows, :].astype(F32) + vec_ref[2:3, :]
        )
        sum_ref[rows, :] = total
        unit, _ = unit_rows(total)
        normed = unit * vec_ref[6:7, :] + vec_ref[4:5, :]
        normed_ref[rows, :] = normed
        normed_b_ref[rows, :] = normed.astype(BF)
        return carry

    lax.fori_loop(0, x_ref.shape[0] // SHORT, chunk_step, 0)
    width = up0_ref.shape[1]
    step = 256
    for panel, up_ref in enumerate((up0_ref, up1_ref)):
        for start in range(0, width, step):
            place = panel * width + start
            pre = dot(normed_b_ref[...], up_ref[:, start : start + step])
            pre = pre + bias_ref[:, place : place + step]
            share = 0.5 + 0.5 * lax.erf(pre * ROOT_HALF)
            slope = share + pre * (DENSITY * jnp.exp(pre * pre * -0.5))
            act_ref[:, place : place + step] = (pre * share).astype(BF)
            slope_ref[:, place : place + step] = slope.astype(BF)
    partial_ref[...] = dot(act_ref[...], down_ref[...]).astype(BF)


def norm_back(upstream, total, gain):
    unit, scale = unit_rows(total)
    scaled = upstream * gain
    first = jnp.mean(scaled, axis=1, keepdims=True)
    second = jnp.mean(scaled * unit, axis=1, keepdims=True)
    return (
        scale * (scaled - first - unit * second),
        jnp.sum(upstream * unit, axis=0, keepdims=True),
        jnp.sum(upstream, axis=0, keepdims=True),
    )


def back_second_kernel(has_base, *refs):
    base_refs, refs = refs[: 3 if has_base else 1], refs[3 if has_base else 1 :]
    sum_ref, vec_ref, act_ref, d_second_ref, d_ffn_ref, g_down_ref, sums_ref = refs
    sums_ref[...] = jnp.zeros_like(sums_ref)

    def chunk_step(chunk, carry):
        rows = pl.ds(pl.multiple_of(chunk * SHORT, SHORT), SHORT)
        upstream = base_refs[0][rows, :].astype(F32)
        if has_base:
            upstream = upstream + (
                base_refs[1][rows, :].astype(F32) + base_refs[2][rows, :].astype(F32)
            )
        d_second, d_gain, d_shift = norm_back(upstream, sum_ref[rows, :], vec_ref[7:8, :])
        d_second_ref[rows, :] = d_second
        d_ffn = d_second.astype(BF)
        d_ffn_ref[rows, :] = d_ffn
        sums_ref[1:2, :] += jnp.sum(d_ffn.astype(F32), axis=0, keepdims=True)
        sums_ref[3:4, :] += d_shift
        sums_ref[5:6, :] += d_gain
        return carry

    lax.fori_loop(0, sum_ref.shape[0] // SHORT, chunk_step, 0)
    g_down_ref[...] = dot_tn(act_ref[...], d_ffn_ref[...]).astype(BF)


def back_hidden_kernel(
    d_ffn_ref, slope_ref, normed_b_ref, down_ref, up0_ref, up1_ref,
    g_up0_ref, g_up1_ref, partial_ref, sums_ref, d_pre_ref,
):
    hidden = slope_ref.shape[1]
    step = 256
    for place in range(0, hidden, step):
        d_act = dot_nt(d_ffn_ref[...], down_ref[place : place + step, :])
        d_pre = (d_act * slope_ref[:, place : place + step].astype(F32)).astype(BF)
        d_pre_ref[:, place : place + step] = d_pre
        sums_ref[:, place : place + step] = jnp.sum(d_pre.astype(F32), axis=0, keepdims=True)
    width = up0_ref.shape[1]
    g_up0_ref[...] = dot_tn(normed_b_ref[...], d_pre_ref[:, :width]).astype(BF)
    g_up1_ref[...] = dot_tn(normed_b_ref[...], d_pre_ref[:, width:]).astype(BF)
    partial_ref[...] = (
        dot_nt(d_pre_ref[:, :width], up0_ref[...]) + dot_nt(d_pre_ref[:, width:], up1_ref[...])
    ).astype(BF)


def back_first(
    d_second_ref, mine_ref, theirs_ref, sum_ref, vec_ref, d_first_ref, dbranch_ref, sums_ref
):
    sums_ref[...] = jnp.zeros_like(sums_ref)

    def chunk_step(chunk, carry):
        rows = pl.ds(pl.multiple_of(chunk * SHORT, SHORT), SHORT)
        upstream = d_second_ref[rows, :] + (
            mine_ref[rows, :].astype(F32) + theirs_ref[rows, :].astype(F32)
        )
        d_first, d_gain, d_shift = norm_back(upstream, sum_ref[rows, :], vec_ref[6:7, :])
        d_first_ref[rows, :] = d_first
        d_branch = d_first.astype(BF)
        dbranch_ref[rows, :] = d_branch
        sums_ref[0:1, :] += jnp.sum(d_branch.astype(F32), axis=0, keepdims=True)
        sums_ref[2:3, :] += d_shift
        sums_ref[4:5, :] += d_gain
        return carry

    lax.fori_loop(0, sum_ref.shape[0] // SHORT, chunk_step, 0)


def head_lanes(value, head):
    lane = lax.broadcasted_iota(jnp.int32, value.shape, 1)
    return (lane // (value.shape[1] // 2)) == head


def mask_row(kind, chunk, count):
    place = lax.broadcasted_iota(jnp.int32, (1, count), 1)
    allowed = (place // SHORT == chunk) | (kind == 1)
    return jnp.where(allowed, 0.0, MASKED_SCORE)


def attention_kernel(
    kind_ref, x_ref, wa_ref, wb_ref, bias_ref, wo_ref, partial_ref, qkv_ref, context_ref, lse_ref
):
    count = x_ref.shape[0]
    wide = wa_ref.shape[1]
    pair = 2 * HEAD_DIM
    kind = kind_ref[0]
    x = x_ref[...]
    bias = bias_ref[...]
    qkv_ref[:, :wide] = (dot(x, wa_ref[...]) + bias[:, :wide]).astype(BF)
    qkv_ref[:, wide:] = (dot(x, wb_ref[...]) + bias[:, wide:]).astype(BF)
    for p in range(HEADS // 4):
        keys = qkv_ref[:, (3 * p + 1) * pair : (3 * p + 2) * pair]
        values = qkv_ref[:, (3 * p + 2) * pair : (3 * p + 3) * pair]

        def chunk_step(chunk, carry):
            rows = pl.ds(pl.multiple_of(chunk * SHORT, SHORT), SHORT)
            queries = qkv_ref[rows, 3 * p * pair : (3 * p + 1) * pair] * jnp.asarray(0.125, BF)
            mask = mask_row(kind, chunk, count)
            found = []
            stats = lse_ref[rows, :] if p > 0 else jnp.zeros((SHORT, 128), F32)
            lane = lax.broadcasted_iota(jnp.int32, stats.shape, 1)
            for head in range(2):
                mine = jnp.where(head_lanes(queries, head), queries, jnp.zeros_like(queries))
                scores = dot_nt(mine, keys) + mask
                top = jnp.max(scores, axis=1, keepdims=True)
                powers = jnp.exp(scores - top)
                total = jnp.sum(powers, axis=1, keepdims=True)
                probs = powers * (1.0 / total)
                found.append(dot(probs.astype(BF), values))
                stats = jnp.where(lane == 2 * p + head, top + jnp.log(total), stats)
            lse_ref[rows, :] = stats
            both = jnp.where(head_lanes(found[0], 0), found[0], found[1])
            context_ref[rows, p * pair : (p + 1) * pair] = both.astype(BF)
            return carry

        lax.fori_loop(0, count // SHORT, chunk_step, 0)
    partial_ref[...] = dot(context_ref[...], wo_ref[...]).astype(BF)


def attention_backward_kernel(
    kind_ref, d_second_ref, mine_ref, theirs_ref, sum_ref, vec_ref,
    x_ref, qkv_ref, context_ref, lse_ref, wa_ref, wb_ref, wo_ref,
    ga_ref, gb_ref, gout_ref, partial_ref, sums_ref, d_first_ref, norm_sums_ref,
    dbranch_ref, dcontext_ref, dqkv_ref, dk_ref, dv_ref,
):
    back_first(
        d_second_ref, mine_ref, theirs_ref, sum_ref, vec_ref,
        d_first_ref, dbranch_ref, norm_sums_ref,
    )
    count = x_ref.shape[0]
    wide = wa_ref.shape[1]
    pair = 2 * HEAD_DIM
    kind = kind_ref[0]
    d_branch = dbranch_ref[...]
    dcontext_ref[...] = dot_nt(d_branch, wo_ref[...]).astype(BF)
    gout_ref[...] = dot_tn(context_ref[...], d_branch).astype(BF)
    for p in range(HEADS // 4):
        keys = qkv_ref[:, (3 * p + 1) * pair : (3 * p + 2) * pair]
        values = qkv_ref[:, (3 * p + 2) * pair : (3 * p + 3) * pair]
        dk_ref[...] = jnp.zeros_like(dk_ref)
        dv_ref[...] = jnp.zeros_like(dv_ref)

        def chunk_step(chunk, carry):
            rows = pl.ds(pl.multiple_of(chunk * SHORT, SHORT), SHORT)
            queries = qkv_ref[rows, 3 * p * pair : (3 * p + 1) * pair] * jnp.asarray(0.125, BF)
            d_context = dcontext_ref[rows, p * pair : (p + 1) * pair]
            mask = mask_row(kind, chunk, count)
            stats = lse_ref[rows, :]
            found = []
            for head in range(2):
                mine = jnp.where(head_lanes(queries, head), queries, jnp.zeros_like(queries))
                theirs = jnp.where(
                    head_lanes(d_context, head), d_context, jnp.zeros_like(d_context)
                )
                lse = stats[:, 2 * p + head : 2 * p + head + 1]
                probs = jnp.exp(dot_nt(mine, keys) + mask - lse)
                d_probs = dot_nt(theirs, values)
                row_dot = jnp.sum(d_probs * probs, axis=1, keepdims=True)
                d_scores = (probs * (d_probs - row_dot)).astype(BF)
                found.append(
                    (
                        dot(d_scores, keys) * 0.125,
                        dot_tn(d_scores, queries),
                        dot_tn(probs.astype(BF), d_context),
                    )
                )
            merged = [
                jnp.where(head_lanes(one, 0), one, other) for one, other in zip(*found)
            ]
            dqkv_ref[rows, 3 * p * pair : (3 * p + 1) * pair] = merged[0].astype(BF)
            dk_ref[...] += merged[1]
            dv_ref[...] += merged[2]
            return carry

        lax.fori_loop(0, count // SHORT, chunk_step, 0)
        dqkv_ref[:, (3 * p + 1) * pair : (3 * p + 2) * pair] = dk_ref[...].astype(BF)
        dqkv_ref[:, (3 * p + 2) * pair : (3 * p + 3) * pair] = dv_ref[...].astype(BF)
    d_a = dqkv_ref[:, :wide]
    d_b = dqkv_ref[:, wide:]
    x = x_ref[...]
    ga_ref[...] = dot_tn(x, d_a).astype(BF)
    gb_ref[...] = dot_tn(x, d_b).astype(BF)
    partial_ref[...] = (dot_nt(d_a, wa_ref[...]) + dot_nt(d_b, wb_ref[...])).astype(BF)
    sums_ref[:, :wide] = jnp.sum(d_a.astype(F32), axis=0, keepdims=True)
    sums_ref[:, wide:] = jnp.sum(d_b.astype(F32), axis=0, keepdims=True)


def kernel_call(body, shapes, scratch, *operands):
    in_vmem = pl.BlockSpec(memory_space=pltpu.VMEM)
    in_smem = pl.BlockSpec(memory_space=pltpu.SMEM)
    return pl.pallas_call(
        body,
        out_shape=shapes,
        in_specs=[in_smem if value.dtype == jnp.int32 else in_vmem for value in operands],
        out_specs=[in_vmem] * len(shapes),
        scratch_shapes=scratch,
        compiler_params=pltpu.CompilerParams(vmem_limit_bytes=VMEM_LIMIT),
        cost_estimate=pl.CostEstimate(flops=0, bytes_accessed=0, transcendentals=0),
    )(*operands)


def attention(row_kind, inputs_b, w_a, w_b, bias, w_out):
    count, width = inputs_b.shape
    half = w_out.shape[0]
    shapes = [
        jax.ShapeDtypeStruct((count, width), BF),
        jax.ShapeDtypeStruct((count, 3 * half), BF),
        jax.ShapeDtypeStruct((count, half), BF),
        jax.ShapeDtypeStruct((count, 128), F32),
    ]
    return kernel_call(
        attention_kernel, shapes, [], row_kind, inputs_b, w_a, w_b, bias, w_out
    )


def attention_backward(
    row_kind, d_second, mine, theirs, first_sum, vec, inputs_b, qkv, context, lse, w_a, w_b, w_out
):
    count, width = inputs_b.shape
    half = w_out.shape[0]
    shapes = [
        jax.ShapeDtypeStruct(w_a.shape, BF),
        jax.ShapeDtypeStruct(w_b.shape, BF),
        jax.ShapeDtypeStruct(w_out.shape, BF),
        jax.ShapeDtypeStruct((count, width), BF),
        jax.ShapeDtypeStruct((1, 3 * half), F32),
        jax.ShapeDtypeStruct((count, width), F32),
        jax.ShapeDtypeStruct((8, width), F32),
    ]
    scratch = [
        pltpu.VMEM((count, width), BF),
        pltpu.VMEM((count, half), BF),
        pltpu.VMEM((count, 3 * half), BF),
        pltpu.VMEM((count, 2 * HEAD_DIM), F32),
        pltpu.VMEM((count, 2 * HEAD_DIM), F32),
    ]
    return kernel_call(
        attention_backward_kernel, shapes, scratch, row_kind, d_second, mine, theirs, first_sum,
        vec, inputs_b, qkv, context, lse, w_a, w_b, w_out,
    )


def norm_rows(base, mine, theirs, vec):
    shapes = [jax.ShapeDtypeStruct(base.shape, kind) for kind in (F32, F32, BF)]
    return kernel_call(norm_kernel, shapes, [], base, mine, theirs, vec)


def hidden_layer(x, mine, theirs, vec, bias, up0, up1, down):
    count, hidden = x.shape[0], down.shape[0]
    shapes = [jax.ShapeDtypeStruct(x.shape, kind) for kind in (F32, F32, BF)]
    shapes += [jax.ShapeDtypeStruct((count, hidden), BF)] * 2
    shapes.append(jax.ShapeDtypeStruct(x.shape, BF))
    return kernel_call(
        hidden_kernel, shapes, [], x, mine, theirs, vec, bias, up0, up1, down
    )


def back_second(upstream, total, vec, act):
    shapes = [
        jax.ShapeDtypeStruct(total.shape, F32),
        jax.ShapeDtypeStruct(total.shape, BF),
        jax.ShapeDtypeStruct((act.shape[1], total.shape[1]), BF),
        jax.ShapeDtypeStruct((8, total.shape[1]), F32),
    ]
    body = functools.partial(back_second_kernel, len(upstream) > 1)
    return kernel_call(body, shapes, [], *upstream, total, vec, act)


def back_hidden(d_ffn, slope, normed_b, down, up0, up1):
    count, hidden = slope.shape
    width = normed_b.shape[1]
    shapes = [
        jax.ShapeDtypeStruct(up0.shape, BF),
        jax.ShapeDtypeStruct(up1.shape, BF),
        jax.ShapeDtypeStruct((count, width), BF),
        jax.ShapeDtypeStruct((1, hidden), F32),
    ]
    scratch = [pltpu.VMEM((count, hidden), BF)]
    return kernel_call(
        back_hidden_kernel, shapes, scratch, d_ffn, slope, normed_b, down, up0, up1
    )


def hidden_order(width, hidden_rows):
    group = width // (2 * hidden_rows)
    target = jnp.arange(width)
    source = (
        (target % (width // 2)) // hidden_rows * (2 * hidden_rows)
        + target // (width // 2) * hidden_rows
        + target % hidden_rows
    )
    del group
    return jnp.arange(width)[:, None] == source[None, :]


def shards(tokens, row_kind, w_qkv, w_out, w_up, w_down, bias_vectors, gains, bias_up, cotangent):
    chips = Chips()
    sequence = Sequence()
    core = chips.core
    count = chips.count
    device = 2 * chips.chip + core
    row_type = row_kind[0]
    rows, width = w_out.shape[1:]
    hidden = w_up.shape[2]
    hidden_rows = w_down.shape[1]
    half = width // 2
    panels = hidden // 2 // width
    own = tokens.shape[0]
    order = hidden_order(width, hidden_rows)

    pairs = HEADS // 4
    lane = half // pairs
    plan = Plan()
    state = State()

    def ordered(mine, theirs):
        return jnp.where(core == 0, mine, theirs), jnp.where(core == 0, theirs, mine)

    def pack_qkv():
        cols = w_qkv.reshape(LAYERS, rows, 3, 2, pairs, lane)

        def side(which):
            return jnp.swapaxes(pick(cols, which, 3), 2, 3).reshape(LAYERS, rows, 3 * half)

        feature = jnp.arange(width)[None, :] - rows * device == jnp.arange(rows)[:, None]
        unit = jnp.arange(hidden // 2)[None, :] - hidden_rows * chips.chip
        unit = unit == jnp.arange(hidden_rows)[:, None]
        table = jnp.concatenate([bias_vectors, gains], axis=1).reshape(LAYERS * 8, rows)
        table = dot(table, feature.astype(BF)).astype(BF)
        units = dot(bias_up, unit.astype(BF)).astype(BF)
        got = swap(side(1 - core), 1)
        table = table + swap(table, 1)
        cols = merge(side(core), got, core, 1)
        for layer in range(LAYERS):
            last = cols[layer, :, :, width:].reshape(2 * rows, half)
            outs = jnp.concatenate([w_out[layer, :, :half], w_out[layer, :, half:]], axis=0)
            vectors = [table[8 * layer : 8 * layer + 8]]
            vectors += [units[layer : layer + 1, i * width :][:, :width] for i in range(panels)]
            vectors.append(jnp.zeros((8 - panels, width), BF))
            state.gathers[ATTN, layer] = Gather(
                chips, sequence, EARLY[layer],
                jnp.concatenate(
                    [
                        cols[layer, :, :, :width].reshape(2 * rows, width),
                        jnp.concatenate([last, outs], axis=1),
                        *vectors,
                    ],
                    axis=0,
                ),
            )
        sequence.mark([state.gathers[ATTN, layer].held for layer in range(LAYERS)])

    groups = hidden // width

    def pack_up():
        value = sequence.gate(w_up).reshape(LAYERS * rows, hidden)
        stacked = jnp.concatenate(
            [value[:, i * width : (i + 1) * width] for i in range(groups)], axis=0
        )
        stacked = dot(stacked, order.astype(BF)).astype(BF)
        mine, sent = ordered(stacked[:, :half], stacked[:, half:])
        first, second = ordered(mine, swap(sent, 1))
        for layer in range(LAYERS):
            parts = []
            for i in range(panels):
                for value in (first, second):
                    cut = [
                        value[((2 * i + j) * LAYERS + layer) * rows :][:rows] for j in range(2)
                    ]
                    parts.append(jnp.concatenate(cut, axis=1))
            state.gathers[FFN, layer] = Gather(
                chips, sequence, EARLY[LAYERS + layer],
                jnp.concatenate(parts + [w_down[layer]], axis=0),
            )
        sequence.mark([state.gathers[FFN, layer].held for layer in range(LAYERS)])

    def read_vectors(layer, table):
        table = jnp.sum(table.astype(F32), axis=0)
        vec = table[:8]
        bias_q, bias_v = (
            jnp.where(core == 0, vec[i : i + 1, :half], vec[i : i + 1, half:]) for i in range(2)
        )
        bias = []
        for p in range(pairs):
            cut = slice(p * lane, (p + 1) * lane)
            bias += [bias_q[:, cut], jnp.zeros((1, lane), F32), bias_v[:, cut]]
        state.vec[layer] = vec
        state.bias_qkv[layer] = jnp.concatenate(bias, axis=1)
        state.bias_up[layer] = jnp.concatenate(
            [table[8 + i : 9 + i] for i in range(panels)], axis=1
        )

    def tokens_start():
        value = sequence.gate(tokens)
        sequence.mark(value)
        state.pair_tokens = (value, swap(value, 1))

    def tokens_end():
        values = sequence.gate(state.pair_tokens)
        state.x_b[0] = jnp.concatenate(ordered(*values), axis=0)
        state.x[0] = state.x_b[0].astype(F32)
        sequence.mark(state.x_b[0])

    def cotangent_start():
        value = sequence.gate(cotangent)
        sequence.mark(value)
        state.pair_cotangent = (value, swap(value, 1))

    def cotangent_end():
        values = sequence.gate(state.pair_cotangent)
        state.upstream = (jnp.concatenate(ordered(*values), axis=0),)
        sequence.mark(state.upstream)

    def out_exchange(layer):
        ends = [0, 2 * rows, 4 * rows, 4 * rows + 16]
        first, second, table = state.gathers[ATTN, layer].finish(list(zip(ends[:-1], ends[1:])))
        w_b = second[:, :, :half].reshape(width, half)
        out_all = second[:, :, half:].reshape(2, count // 2, 2 * rows, half)
        sent = pick(out_all, 1 - core, 0)
        read_vectors(layer, table)
        sequence.mark((sent, w_b, state.vec[layer]))
        parts = ordered(pick(out_all, core, 0), swap(sent, 1))
        parts = [jnp.concatenate([part[:, :rows], part[:, rows:]], axis=2) for part in parts]
        full_out = jnp.stack(parts, axis=1).reshape(half, width)
        state.w_attn[layer] = (first.reshape(width, width), w_b, full_out)

    def hidden_weights(layer):
        ends = [2 * rows * i for i in range(panels + 1)]
        ends.append(ends[-1] + hidden_rows)
        *ups, down = state.gathers[FFN, layer].finish(list(zip(ends[:-1], ends[1:])))
        state.w_hidden[layer] = (
            down.reshape(hidden // 2, width), *(value.reshape(width, width) for value in ups)
        )

    def run_attention(layer):
        x_b, weights = sequence.gate((state.x_b[layer], state.w_attn[layer]))
        w_a, w_b, full_out = weights
        partial, *saved = attention(row_kind, x_b, w_a, w_b, state.bias_qkv[layer], full_out)
        sequence.mark(partial)
        state.w_attn[layer] = weights
        state.saved[layer] = (x_b, *saved)
        state.branch = (partial, swap(partial, 1))

    def run_hidden(layer):
        mine, theirs = sequence.gate(state.branch)
        down, up0, up1 = state.w_hidden[layer]
        first_sum, state.normed, *kept, partial = hidden_layer(
            state.x[layer], mine, theirs, state.vec[layer], state.bias_up[layer], up0, up1, down
        )
        sequence.mark(partial)
        state.first_sum[layer] = first_sum
        state.kept[layer] = kept
        state.branch = (partial, swap(partial, 1))

    def run_norm(layer):
        mine, theirs = sequence.gate(state.branch)
        second, x, x_b = norm_rows(state.normed, mine, theirs, state.vec[layer])
        state.second[layer], state.x[layer + 1], state.x_b[layer + 1] = second, x, x_b
        sequence.mark(second)

    def run_back_second(layer):
        upstream = sequence.gate(state.upstream)
        if layer < LAYERS - 1:
            upstream = (state.d_first, *upstream)
        act = state.kept[layer][1]
        d_second, d_ffn, g_down, sums = back_second(
            upstream, state.second[layer], state.vec[layer], act
        )
        state.d_second, state.d_ffn = d_second, d_ffn
        state.sums2[layer] = sums
        bundle = state.scatters[FFN, layer]
        bundle.start(0, [g_down.reshape(count, hidden_rows, width)])
        sequence.mark((d_ffn, bundle.sent))

    def run_back_hidden(layer):
        d_ffn = sequence.gate(state.d_ffn)
        normed_b, _, slope = state.kept[layer]
        *g_up, partial, units = back_hidden(d_ffn, slope, normed_b, *state.w_hidden[layer])
        bundle = state.scatters[FFN, layer]
        bundle.start(1, [value.reshape(count, 2 * rows, width) for value in g_up])
        sequence.mark((partial, bundle.sent))
        state.units[layer] = units
        state.branch = (partial, swap(partial, 1))

    def run_back_attention(layer):
        mine, theirs = sequence.gate(state.branch)
        x_b, qkv, context, lse = state.saved[layer]
        g_a, g_b, g_out, partial, sums, state.d_first, state.sums1[layer] = attention_backward(
            row_kind, state.d_second, mine, theirs, state.first_sum[layer], state.vec[layer],
            x_b, qkv, context, lse, *state.w_attn[layer],
        )
        sequence.mark(partial)
        state.pair[layer] = jnp.concatenate(
            [
                jnp.concatenate(
                    [sums[:, (3 * p + t) * lane :][:, :lane] for p in range(pairs)], axis=1
                )
                for t in (0, 2)
            ],
            axis=0,
        )
        if layer > 0:
            state.upstream = (partial, swap(partial, 1))
        else:
            mine, sent = ordered(partial[:own], partial[own:])
            state.upstream = (mine, swap(sent, 1))
        state.g_attn[layer] = (g_a, g_b, g_out)

    def sum_rows(layer):
        pair = state.pair[layer]
        nothing = jnp.zeros_like(pair)
        pair = jnp.concatenate(ordered(pair, nothing), axis=1)
        units = [state.units[layer][:, i * width :][:, :width] for i in range(panels)]
        small = jnp.concatenate([state.sums1[layer] + state.sums2[layer], pair, *units], axis=0)
        small = jnp.pad(small.astype(BF), ((0, 16 - small.shape[0]), (0, 0)))
        line = jnp.arange(16)[:, None]
        place = jnp.arange(width)[None, :]
        owner = jnp.where(
            line < 10, place // (2 * rows), ((line - 10) * width + place) // hidden_rows
        )
        mine = owner[None] == jnp.arange(count)[:, None, None]
        return jnp.where(mine, small[None], jnp.zeros((), BF))

    def back_terms(layer):
        g_a, g_b, g_out = sequence.gate(state.g_attn[layer])
        bundle = state.scatters[ATTN, layer]
        out_pair = g_out.reshape(count // 2, 2, rows, width)
        out_got = swap(pick(out_pair, 1 - core, 1), 1)
        out = merge(pick(out_pair, core, 1), out_got, core, 0).reshape(count, rows, width)
        g_b = g_b.reshape(count, 2 * rows, half)
        out = jnp.concatenate([out[:, :, :half], out[:, :, half:]], axis=1)
        rest = jnp.concatenate([g_b, out], axis=2)
        rest = jnp.concatenate([rest, sum_rows(layer)], axis=1)
        rest = lax.optimization_barrier(rest)
        bundle.start(0, [g_a.reshape(count, 2 * rows, width), rest])
        sequence.mark(bundle.sent)

    def grad_end():
        mine, theirs = sequence.gate(state.upstream)
        d_first = lax.dynamic_slice_in_dim(state.d_first, core * own, own)
        state.grad_tokens = d_first + (mine.astype(F32) + theirs.astype(F32))
        sequence.mark(state.grad_tokens)

    def mixed_end():
        value = sequence.gate(state.x_b[LAYERS])
        state.mixed = lax.dynamic_slice_in_dim(value, core * own, own)
        sequence.mark(state.mixed)

    def finish_hidden(layer):
        down, *ups = state.scatters[FFN, layer].finish()
        sides = [
            jnp.concatenate([up[side * rows :][:rows] for up in ups], axis=1)
            for side in range(2)
        ]
        mine, sent = ordered(*sides)
        state.up_pair[layer] = (mine, swap(sent, 1))
        state.down[layer] = down

    def end_hidden(layer):
        first, second = ordered(*sequence.gate(state.up_pair[layer]))
        stacked = jnp.concatenate(
            [
                jnp.concatenate(
                    [value[:, i * half : (i + 1) * half] for value in (first, second)], axis=1
                )
                for i in range(groups)
            ],
            axis=0,
        )
        stacked = lax.dot_general(
            stacked, order.astype(F32), (((1,), (1,)), ((), ())),
            precision=lax.Precision.HIGHEST, preferred_element_type=F32,
        )
        state.up[layer] = jnp.concatenate(
            [stacked[i * rows : (i + 1) * rows] for i in range(groups)], axis=1
        )
        sequence.mark(state.up[layer])

    def finish_attention(layer):
        first, rest = state.scatters[ATTN, layer].finish()
        last, out, small = rest[: 2 * rows, :half], rest[: 2 * rows, half:], rest[2 * rows :]
        out = jnp.concatenate([out[:rows], out[rows:]], axis=1)
        sides = [
            jnp.concatenate([value[side * rows :][:rows] for value in (first, last)], axis=1)
            for side in range(2)
        ]
        mine, sent = ordered(*sides)
        pair = jnp.pad(small[8:], ((0, 0), (0, mine.shape[1] - width)))
        sent = jnp.concatenate([sent, pair], axis=0)
        state.qkv_pair[layer] = (mine, swap(sent, 1))
        state.out[layer] = out
        state.small_rows[layer] = small

    def end_attention(layer):
        mine, theirs = sequence.gate(state.qkv_pair[layer])
        small = state.small_rows[layer]
        small = jnp.concatenate([theirs[rows : rows + 2, :width] + small[8:10], small], axis=0)
        features = lax.dynamic_slice_in_dim(small, rows * device, rows, axis=1)
        per_row = width // hidden_rows
        units = lax.dynamic_slice(
            small,
            (12 + chips.chip // per_row, hidden_rows * (chips.chip % per_row)),
            (1, hidden_rows),
        )
        state.vectors[layer] = features[:6]
        state.gains[layer] = features[6:8]
        state.unit_sums[layer] = units[0]
        values = ordered(mine, theirs[:rows])
        state.qkv[layer] = jnp.concatenate(
            [
                value[:, (3 * p + t) * lane :][:, :lane]
                for t in range(3)
                for value in values
                for p in range(pairs)
            ],
            axis=1,
        )
        sequence.mark(state.qkv[layer])

    def call(function, *args):
        return lambda: function(*args)

    low = len(chips.low)
    size = (1.0, 2.0)
    add = plan.add

    def pair_send(label):
        return [(label, (("p", 0.0),), 1)]

    def plane(length):
        return (("x", length), ("y", length))

    add("pq", 0, 6.0, [], pack_qkv)
    add("pu", 2, 3.0, [("g", ATTN, 0)], pack_up)
    add("tok", 8, 0.5, ["pu"], tokens_start, pair_send("x0"))
    add("te", 7, 1.5, ["x0"], tokens_end)
    add("cot", 9, 0.5, [("m", 1, 0)], cotangent_start, pair_send("ct"))
    add("ce", 9, 1.2, ["ct"], cotangent_end)
    bundles = [(ATTN, 0), (FFN, 0), (ATTN, 1), (FFN, 1)]
    for rank, (kind, layer) in enumerate(bundles):
        needs = ["pq" if kind == ATTN else "pu"]

        def start(kind=kind, layer=layer):
            state.gathers[kind, layer].start()

        def advance(kind=kind, layer=layer):
            state.gathers[kind, layer].advance()

        units = 7.0 / 3 if kind == ATTN else 4.0
        tops = [("top", 2), ("top", 1)]
        lows = [("low", step) for step in range(low)]
        early = EARLY[LAYERS * kind + layer]
        steps = lows[:1] + tops + lows[1:] if early else tops + lows
        need = None
        held = 1
        for number, (bits, step) in enumerate(steps):
            length = UNIT / 2 * units * held
            held *= 2
            if bits == "low":
                links = plane(length)
            elif step == 2:
                links = (("z", 2 * length), ("w", 5 * length + 1.5))
            else:
                links = (("z", 2 * length),)
            sent = ("gx", kind, layer, number)
            if number == 0:
                add(("g", kind, layer), 1 + rank, 3.5, needs, start, [(sent, links, 1)])
            else:
                add(
                    ("gs", kind, layer, number), 1 + rank, 1.0 + 0.1 * held + (2.8 if len(links) > 1 and links[1][0] == "w" else 1.4),
                    [need], advance, [(sent, links, 1)],
                )
            need = sent
        if kind == ATTN:
            add(
                ("go", layer), 1 + rank, 4.5, [need], call(out_exchange, layer),
                pair_send(("w", kind, layer)),
            )
        else:
            add(("w", kind, layer), 1 + rank, 1.6, [need], call(hidden_weights, layer))
    need = "te"
    for layer in range(LAYERS):
        add(
            ("m", 0, layer), 10, 12.7, [need, ("w", ATTN, layer)],
            call(run_attention, layer), pair_send(("p", 0, layer)),
        )
        add(
            ("m", 1, layer), 10, 6.0, [("p", 0, layer), ("w", FFN, layer)],
            call(run_hidden, layer), pair_send(("p", 1, layer)),
        )
        need = ("m", 2, layer)
        add(need, 10, 3.0, [("p", 1, layer)], call(run_norm, layer))
    add("mix", 20, 1.0, [need], mixed_end)

    needs = [need, "ce"]
    for layer in reversed(range(LAYERS)):
        state.scatters[FFN, layer] = Scatter(chips, sequence, 2, LATE[LAYERS + layer])
        state.scatters[ATTN, layer] = Scatter(chips, sequence, 1, LATE[layer])
        add(
            ("b", 0, layer), 10, 5.0, needs, call(run_back_second, layer),
            [(("r", FFN, layer, 0), plane(UNIT * 8), 1)],
        )
        add(
            ("b", 1, layer), 10, 6.5, [("b", 0, layer)], call(run_back_hidden, layer),
            [(("r", FFN, layer, 1), plane(UNIT * 8), 1)] + pair_send(("p", 2, layer)),
        )
        add(
            ("b", 2, layer), 10, 17.2, [("p", 2, layer)], call(run_back_attention, layer),
            pair_send(("p", 3, layer)),
        )
        add(
            ("b", 3, layer), 9.5, 6.0, [("b", 2, layer)], call(back_terms, layer),
            [(("r", ATTN, layer, 0), plane(UNIT * 28 / 3), 1)],
        )
        needs = [("p", 3, layer)]
        for kind in (FFN, ATTN):
            need = [("r", kind, layer, part) for part in range(1 + kind)]
            rank = 1 + 2 * (LAYERS - 1 - layer) + (kind == ATTN)

            def reduce(kind=kind, layer=layer):
                state.scatters[kind, layer].advance()

            units = 7.0 / 3 if kind == ATTN else 4.0
            tops = [("top", 1), ("top", 2)]
            lows = [("low", step) for step in range(low - 1)][::-1]
            late = LATE[LAYERS * kind + layer]
            steps = lows[:-1] + tops + lows[-1:] if late else lows + tops
            held = 2 * count // 4
            for number, (bits, step) in enumerate(steps):
                held //= 2
                length = UNIT / 2 * units * held
                cost = 1.0 + 0.1 * held
                if bits == "low":
                    cost, links = cost + 1.4, plane(length)
                elif step == 2:
                    cost, links = cost + 2.8, (("z", 2 * length), ("w", 5 * length + 1.5))
                else:
                    cost, links = cost + 1.4, (("z", 2 * length),)
                sent = ("rx", kind, layer, number)
                add(("rs", kind, layer, number), rank, cost, need, reduce, [(sent, links, 1)])
                need = [sent]
            last = finish_hidden if kind == FFN else finish_attention
            add(
                ("rf", kind, layer), 19, 2.0, need, call(last, layer),
                pair_send(("re", kind, layer)),
            )
            last = end_hidden if kind == FFN else end_attention
            add(("ro", kind, layer), 20, 2.5, [("re", kind, layer)], call(last, layer))
    add("grad", 18, 1.2, needs, grad_end)
    plan.run()

    def stacked(values):
        return jnp.stack([values[layer] for layer in range(LAYERS)])

    return (
        state.mixed,
        state.grad_tokens,
        stacked(state.qkv),
        stacked(state.out),
        stacked(state.up),
        stacked(state.down),
        stacked(state.vectors),
        stacked(state.gains),
        stacked(state.unit_sums),
    )


def solution(mesh):
    placed = (
        P("fsdp", None),
        P("fsdp"),
        P(None, "fsdp", None),
        P(None, "fsdp", None),
        P(None, "fsdp", None),
        P(None, "fsdp", None),
        P(None, None, "fsdp"),
        P(None, None, "fsdp"),
        P(None, "fsdp"),
        P("fsdp", None),
    )
    return jax.shard_map(
        shards,
        mesh=mesh,
        in_specs=placed,
        out_specs=(
            P("fsdp", None),
            P("fsdp", None),
            P(None, "fsdp", None),
            P(None, "fsdp", None),
            P(None, "fsdp", None),
            P(None, "fsdp", None),
            P(None, None, "fsdp"),
            P(None, None, "fsdp"),
            P(None, "fsdp"),
        ),
        check_vma=False,
    )
```

```python
import functools

import jax
import jax.numpy as jnp
from jax import lax
from jax.experimental import pallas as pl
from jax.experimental.pallas import tpu as pltpu
from jax.sharding import PartitionSpec as P

HEADS = 12
HEAD_DIM = 64
LAYERS = 2
SHORT = 128
AXIS = "fsdp"

EPSILON = 1e-05
MASKED_SCORE = -1e30
BF = jnp.bfloat16
F32 = jnp.float32
LATENCY = 2.5
UNIT = 1.48
ATTN, FFN = 0, 1
OPEN_SENDS = 5
VMEM_LIMIT = 16 * 2**20
EARLY = (False, False, False, False)
LATE = (False, False, False, False)
ORDER = (
    0, 6, 1, 2, 7, 11, 16, 8, 3, 12, 21, 9, 13, 17, 14, 10, 22, 15, 23, 18, 26, 19, 24,
    27, 28, 20, 4, 29, 5, 25, 30, 31, 33, 34, 35, 36, 37, 47, 48, 49, 38, 42, 51, 39, 43,
    50, 52, 61, 40, 44, 56, 53, 45, 57, 58, 54, 59, 55, 60, 46, 41, 32,
)


def dot(left, right):
    return jnp.dot(left, right, preferred_element_type=F32)


def dot_tn(left, right):
    return lax.dot_general(left, right, (((0,), (0,)), ((), ())), preferred_element_type=F32)


def dot_nt(left, right):
    return lax.dot_general(left, right, (((1,), (1,)), ((), ())), preferred_element_type=F32)


def swap(value, mask):
    pairs = [(source, source ^ mask) for source in range(lax.axis_size(AXIS))]
    return lax.ppermute(value, AXIS, pairs)


def merge(mine, theirs, bit, axis):
    first = jnp.where(bit == 0, mine, theirs)
    second = jnp.where(bit == 0, theirs, mine)
    return jnp.stack([first, second], axis=axis)


def pick(pair, index, axis):
    return lax.dynamic_index_in_dim(pair, index, axis, keepdims=False)


class Chips:
    def __init__(self):
        device = lax.axis_index(AXIS)
        self.count = lax.axis_size(AXIS) // 2
        self.core = device % 2
        self.chip = device // 2
        self.step = self.count // 4
        self.top = self.chip // self.step
        self.low = list(range(self.count.bit_length() - 3))
        self.info = self.table()

    def bit(self, place):
        return (self.chip // 2**place) % 2

    def plane_bit(self, step):
        return jnp.where(self.core == 0, self.bit(step), self.bit(len(self.low) - 1 - step))

    def plane_swap(self, value, step):
        masks = (2 * 2**step, 2 * 2 ** (len(self.low) - 1 - step))
        pairs = [(source, source ^ masks[source % 2]) for source in range(2 * self.count)]
        return lax.ppermute(value, AXIS, pairs)

    def table(self):
        bits = [self.plane_bit(step) for step in range(len(self.low))]
        entries = [self.core] + bits + [self.top % 2, self.top // 2]
        return jnp.stack(entries).astype(jnp.int32)


def half_place(table, step, index, own):
    bit = table[1 + step]
    bit = bit if own else 1 - bit
    return jnp.where(table[0] == 0, 2**step * bit + index, 2 * index + bit)


def merge_place(table, kind, step, low, half, index, own):
    if kind == "low":
        return half_place(table, step, index, own)
    bit = table[low + step]
    return half * (bit if own else 1 - bit) + index


class Sequence:
    def __init__(self):
        self.last = None

    def gate(self, values):
        if self.last is None:
            return values
        values, _ = lax.optimization_barrier((values, self.last))
        return values

    def mark(self, values):
        self.last = values


class State:
    def __getattr__(self, name):
        value = {}
        setattr(self, name, value)
        return value


class Plan:
    def __init__(self):
        self.pieces = []

    def add(self, name, rank, cost, needs, run, sends=()):
        self.pieces.append((name, rank, cost, needs, run, sends))

    def greedy(self):
        now = 0.0
        ready = {}
        free = {}
        open_sends = {}
        waiting = list(range(len(self.pieces)))
        order = []

        def fits(piece):
            held = sum(weight for label, weight in open_sends.items() if label not in piece[3])
            added = sum(weight for _, _, weight in piece[5])
            return added == 0 or held + added <= OPEN_SENDS

        while waiting:
            known = []
            for place in waiting:
                piece = self.pieces[place]
                if all(need in ready for need in piece[3]):
                    time = max([ready[need] for need in piece[3]], default=0.0)
                    known.append((time, piece[1], place))
            known = [entry for entry in known if fits(self.pieces[entry[2]])] or known
            able = [entry[1:] for entry in known if entry[0] <= now]
            place = min(able)[1] if able else min(known)[2]
            name, _, cost, needs, _, sends = self.pieces[place]
            now = max([now] + [ready[need] for need in needs]) + cost
            ready[name] = now
            for need in needs:
                open_sends.pop(need, None)
            for label, links, weight in sends:
                ready[label] = 0.0
                for link, length in links:
                    free[link] = max(now, free.get(link, 0.0)) + length
                    ready[label] = max(ready[label], free[link] + LATENCY)
                if weight > 0:
                    open_sends[label] = weight
            waiting.remove(place)
            order.append(place)
        return order

    def run(self):
        order = ORDER if len(ORDER) == len(self.pieces) else self.greedy()
        for place in order:
            self.pieces[place][4]()


class Gather:
    def __init__(self, chips, sequence, early, piece):
        self.chips, self.sequence = chips, sequence
        low = [("low", step) for step in range(len(chips.low))]
        top = [("top", 2), ("top", 1)]
        self.steps = low[:1] + top + low[1:] if early else top + low
        self.held = piece[None, None]

    def start(self):
        self.held = self.sequence.gate(self.held)
        self.sequence.mark(self.held)
        self.send()

    def send(self):
        kind, step = self.steps[0]
        if kind == "low":
            self.coming = self.chips.plane_swap(self.held, step)
        else:
            self.coming = swap(self.held, 2 * step * self.chips.step)

    def merged(self, ranges=None):
        chips = self.chips
        coming = self.sequence.gate(self.coming)
        kind, step = self.steps.pop(0)
        if kind == "low":
            return merge_rows(chips, kind, step, self.held, coming, ranges)
        lead, half, height, width = self.held.shape
        flat = [value.reshape(lead, 1, half * height, width) for value in (self.held, coming)]
        return merge_rows(chips, kind, step, *flat).reshape(2 * lead, half, height, width)

    def advance(self):
        self.held = self.merged()
        self.sequence.mark(self.held)
        self.send()

    def finish(self, ranges):
        while len(self.steps) > 1:
            self.advance()
        results = self.merged(ranges)
        results = [whole.reshape((self.chips.count,) + whole.shape[2:]) for whole in results]
        self.sequence.mark(results)
        return results


def merge_kernel(ranges, place, table_ref, mine_ref, theirs_ref, *out_refs):
    for index in range(mine_ref.shape[1]):
        own, other = place(table_ref, index, True), place(table_ref, index, False)
        for lead in range(mine_ref.shape[0]):
            for (start, stop), out_ref in zip(ranges, out_refs):
                out_ref[lead, own] = mine_ref[lead, index, start:stop]
                out_ref[lead, other] = theirs_ref[lead, index, start:stop]


def merge_rows(chips, kind, step, mine, theirs, ranges=None):
    half = mine.shape[1]
    cuts = ranges or [(0, mine.shape[2])]

    def place(table, index, own):
        return merge_place(table, kind, step, len(chips.low), half, index, own)

    shapes = [
        jax.ShapeDtypeStruct((mine.shape[0], 2 * half, stop - start, mine.shape[3]), BF)
        for start, stop in cuts
    ]
    if all(edge % 16 == 0 for cut in cuts for edge in cut):
        results = kernel_call(
            functools.partial(merge_kernel, cuts, place), shapes, [], chips.info, mine, theirs
        )
    else:
        sides = [place(chips.info, jnp.arange(half), own) for own in (True, False)]
        results = []
        for (start, stop), shape in zip(cuts, shapes):
            whole = jnp.zeros(shape.shape, BF)
            for side, value in zip(sides, (mine, theirs)):
                whole = whole.at[:, side].set(value[:, :, start:stop])
            results.append(whole)
    return results if ranges else results[0]


class Scatter:
    def __init__(self, chips, sequence, count, late):
        self.chips, self.sequence = chips, sequence
        low = [("low", step) for step in range(len(chips.low) - 1)][::-1]
        top = [("top", 1), ("top", 2)]
        self.steps = low[:-1] + top + low[-1:] if late else low + top
        self.arrays = [None] * count
        self.coming = [None] * count
        self.heights = None

    def start(self, part, arrays):
        chips = self.chips
        step = len(chips.low) - 1
        shape = (4, 2 ** len(chips.low))
        arrays = [value.reshape(shape + value.shape[1:]) for value in arrays]
        self.arrays[part] = arrays
        sent = send_rows(chips, step, arrays)
        self.coming[part] = chips.plane_swap(sent, step)
        self.sent = sent

    def advance(self):
        chips = self.chips
        coming = self.sequence.gate(self.coming)
        first = self.heights is None
        if first:
            self.heights = [value.shape[2] for part in self.arrays for value in part]
        else:
            self.arrays, coming = [[self.kept]], [coming]
        kind, step = self.steps.pop(0)
        if kind == "top":
            self.arrays = [
                [value.reshape((-1, 2 * value.shape[1]) + value.shape[2:]) for value in part]
                for part in self.arrays
            ]
            coming = [got.reshape((-1, 2 * got.shape[1]) + got.shape[2:]) for got in coming]
        sent, self.kept = fold_rows(chips, kind, step, first, self.arrays, coming)
        self.sequence.mark(sent)
        if kind == "low":
            self.coming = chips.plane_swap(sent, step)
        else:
            self.coming = swap(sent, 2 * step * chips.step)

    def finish(self):
        coming = self.sequence.gate(self.coming)
        total = self.kept[0, 0] + coming[0, 0].astype(F32)
        self.sequence.mark(total)
        ends = [sum(self.heights[:i]) for i in range(len(self.heights) + 1)]
        return [total[start:stop] for start, stop in zip(ends[:-1], ends[1:])]


def send_kernel(step, heights, table_ref, *refs):
    *array_refs, sent_ref = refs
    for index in range(sent_ref.shape[1]):
        place = half_place(table_ref, step, index, False)
        for lead in range(sent_ref.shape[0]):
            row = 0
            for height, ref in zip(heights, array_refs):
                sent_ref[lead, index, row : row + height] = ref[lead, place]
                row += height


def send_rows(chips, step, arrays):
    heights = [value.shape[2] for value in arrays]
    shape = (arrays[0].shape[0], 2**step, sum(heights), arrays[0].shape[3])
    if any(height % 16 for height in heights):
        places = half_place(chips.info, step, jnp.arange(2**step), False)
        return jnp.concatenate([jnp.take(value, places, axis=1) for value in arrays], axis=2)
    (sent,) = kernel_call(
        functools.partial(send_kernel, step, heights), [jax.ShapeDtypeStruct(shape, BF)], [],
        chips.info, *arrays,
    )
    return sent


def fold_kernel(layout, place, table_ref, *refs):
    *refs, sent_ref, kept_ref = refs
    for index in range(sent_ref.shape[1]):
        for own, out_ref in enumerate((sent_ref, kept_ref)):
            source, came = place(table_ref, index, own == 1)
            for lead in range(sent_ref.shape[0]):
                for array, got, start, height, row in layout:
                    mine = refs[array][lead, source]
                    theirs = refs[got][lead, came, start : start + height]
                    total = mine.astype(F32) + theirs.astype(F32)
                    out_ref[lead, index, row : row + height] = total.astype(out_ref.dtype)


def fold_rows(chips, kind, step, first, parts, coming):
    arrays = [value for part in parts for value in part]
    layout = []
    row = 0
    for part, got in zip(range(len(parts)), range(len(arrays), len(arrays) + len(coming))):
        start = 0
        for value in parts[part]:
            height = value.shape[2]
            layout.append((len(layout), got, start, height, row))
            start += height
            row += height
    half = coming[0].shape[1] // 2
    low = len(chips.low)

    def place(table, index, own):
        if kind == "low":
            came = half_place(table, step, index, own)
            return (half_place(table, low - 1, came, True) if first else came), came
        bit = table[low + step]
        bit = bit if own else 1 - bit
        came = half * bit + index
        if not first:
            return came, came
        return 2**low * bit + half_place(table, low - 1, index, True), came

    shape = (arrays[0].shape[0], half, row, arrays[0].shape[3])
    if any(value.shape[2] % 16 for value in arrays):
        results = []
        for own, dtype in ((False, BF), (True, F32)):
            source, came = place(chips.info, jnp.arange(half), own)
            totals = []
            for array, got, start, height, _ in layout:
                theirs = jnp.take(coming[got - len(arrays)], came, axis=1)
                theirs = theirs[:, :, start : start + height].astype(F32)
                totals.append(jnp.take(arrays[array], source, axis=1).astype(F32) + theirs)
            results.append(jnp.concatenate(totals, axis=2).astype(dtype))
        return results
    return kernel_call(
        functools.partial(fold_kernel, layout, place),
        [jax.ShapeDtypeStruct(shape, kind) for kind in (BF, F32)], [],
        chips.info, *arrays, *coming,
    )


ROOT_HALF = 0.7071067811865476
DENSITY = 0.3989422804014327


def unit_rows(values):
    centre = values - jnp.mean(values, axis=1, keepdims=True)
    scale = lax.rsqrt(jnp.mean(centre * centre, axis=1, keepdims=True) + EPSILON)
    return centre * scale, scale


def norm_kernel(base_ref, mine_ref, theirs_ref, vec_ref, sum_ref, out_ref, out_b_ref):
    def chunk_step(chunk, carry):
        rows = pl.ds(pl.multiple_of(chunk * SHORT, SHORT), SHORT)
        total = base_ref[rows, :] + (
            mine_ref[rows, :].astype(F32) + theirs_ref[rows, :].astype(F32)
        ) + vec_ref[3:4, :]
        sum_ref[rows, :] = total
        unit, _ = unit_rows(total)
        output = unit * vec_ref[7:8, :] + vec_ref[5:6, :]
        out_ref[rows, :] = output
        out_b_ref[rows, :] = output.astype(BF)
        return carry

    lax.fori_loop(0, base_ref.shape[0] // SHORT, chunk_step, 0)


def hidden_kernel(
    x_ref, mine_ref, theirs_ref, vec_ref, bias_ref, up0_ref, up1_ref, down_ref,
    sum_ref, normed_ref, normed_b_ref, act_ref, slope_ref, partial_ref,
):
    def chunk_step(chunk, carry):
        rows = pl.ds(pl.multiple_of(chunk * SHORT, SHORT), SHORT)
        total = x_ref[rows, :] + (
            mine_ref[rows, :].astype(F32) + theirs_ref[rows, :].astype(F32) + vec_ref[2:3, :]
        )
        sum_ref[rows, :] = total
        unit, _ = unit_rows(total)
        normed = unit * vec_ref[6:7, :] + vec_ref[4:5, :]
        normed_ref[rows, :] = normed
        normed_b_ref[rows, :] = normed.astype(BF)
        return carry

    lax.fori_loop(0, x_ref.shape[0] // SHORT, chunk_step, 0)
    width = up0_ref.shape[1]
    step = 256
    for panel, up_ref in enumerate((up0_ref, up1_ref)):
        for start in range(0, width, step):
            place = panel * width + start
            pre = dot(normed_b_ref[...], up_ref[:, start : start + step])
            pre = pre + bias_ref[:, place : place + step]
            share = 0.5 + 0.5 * lax.erf(pre * ROOT_HALF)
            slope = share + pre * (DENSITY * jnp.exp(pre * pre * -0.5))
            act_ref[:, place : place + step] = (pre * share).astype(BF)
            slope_ref[:, place : place + step] = slope.astype(BF)
    partial_ref[...] = dot(act_ref[...], down_ref[...]).astype(BF)


def norm_back(upstream, total, gain):
    unit, scale = unit_rows(total)
    scaled = upstream * gain
    first = jnp.mean(scaled, axis=1, keepdims=True)
    second = jnp.mean(scaled * unit, axis=1, keepdims=True)
    return (
        scale * (scaled - first - unit * second),
        jnp.sum(upstream * unit, axis=0, keepdims=True),
        jnp.sum(upstream, axis=0, keepdims=True),
    )


def back_second_kernel(has_base, *refs):
    base_refs, refs = refs[: 3 if has_base else 1], refs[3 if has_base else 1 :]
    sum_ref, vec_ref, act_ref, d_second_ref, d_ffn_ref, g_down_ref, sums_ref = refs
    sums_ref[...] = jnp.zeros_like(sums_ref)

    def chunk_step(chunk, carry):
        rows = pl.ds(pl.multiple_of(chunk * SHORT, SHORT), SHORT)
        upstream = base_refs[0][rows, :].astype(F32)
        if has_base:
            upstream = upstream + (
                base_refs[1][rows, :].astype(F32) + base_refs[2][rows, :].astype(F32)
            )
        d_second, d_gain, d_shift = norm_back(upstream, sum_ref[rows, :], vec_ref[7:8, :])
        d_second_ref[rows, :] = d_second
        d_ffn = d_second.astype(BF)
        d_ffn_ref[rows, :] = d_ffn
        sums_ref[1:2, :] += jnp.sum(d_ffn.astype(F32), axis=0, keepdims=True)
        sums_ref[3:4, :] += d_shift
        sums_ref[5:6, :] += d_gain
        return carry

    lax.fori_loop(0, sum_ref.shape[0] // SHORT, chunk_step, 0)
    g_down_ref[...] = dot_tn(act_ref[...], d_ffn_ref[...]).astype(BF)


def back_hidden_kernel(
    d_ffn_ref, slope_ref, normed_b_ref, down_ref, up0_ref, up1_ref,
    g_up0_ref, g_up1_ref, partial_ref, sums_ref, d_pre_ref,
):
    hidden = slope_ref.shape[1]
    step = 256
    for place in range(0, hidden, step):
        d_act = dot_nt(d_ffn_ref[...], down_ref[place : place + step, :])
        d_pre = (d_act * slope_ref[:, place : place + step].astype(F32)).astype(BF)
        d_pre_ref[:, place : place + step] = d_pre
        sums_ref[:, place : place + step] = jnp.sum(d_pre.astype(F32), axis=0, keepdims=True)
    width = up0_ref.shape[1]
    g_up0_ref[...] = dot_tn(normed_b_ref[...], d_pre_ref[:, :width]).astype(BF)
    g_up1_ref[...] = dot_tn(normed_b_ref[...], d_pre_ref[:, width:]).astype(BF)
    partial_ref[...] = (
        dot_nt(d_pre_ref[:, :width], up0_ref[...]) + dot_nt(d_pre_ref[:, width:], up1_ref[...])
    ).astype(BF)


def back_first(
    d_second_ref, mine_ref, theirs_ref, sum_ref, vec_ref, d_first_ref, dbranch_ref, sums_ref
):
    sums_ref[...] = jnp.zeros_like(sums_ref)

    def chunk_step(chunk, carry):
        rows = pl.ds(pl.multiple_of(chunk * SHORT, SHORT), SHORT)
        upstream = d_second_ref[rows, :] + (
            mine_ref[rows, :].astype(F32) + theirs_ref[rows, :].astype(F32)
        )
        d_first, d_gain, d_shift = norm_back(upstream, sum_ref[rows, :], vec_ref[6:7, :])
        d_first_ref[rows, :] = d_first
        d_branch = d_first.astype(BF)
        dbranch_ref[rows, :] = d_branch
        sums_ref[0:1, :] += jnp.sum(d_branch.astype(F32), axis=0, keepdims=True)
        sums_ref[2:3, :] += d_shift
        sums_ref[4:5, :] += d_gain
        return carry

    lax.fori_loop(0, sum_ref.shape[0] // SHORT, chunk_step, 0)


def head_lanes(value, head):
    lane = lax.broadcasted_iota(jnp.int32, value.shape, 1)
    return (lane // (value.shape[1] // 2)) == head


def mask_row(kind, chunk, count):
    place = lax.broadcasted_iota(jnp.int32, (1, count), 1)
    allowed = (place // SHORT == chunk) | (kind == 1)
    return jnp.where(allowed, 0.0, MASKED_SCORE)


def attention_kernel(
    kind_ref, x_ref, wa_ref, wb_ref, bias_ref, wo_ref, partial_ref, qkv_ref, context_ref, lse_ref
):
    count = x_ref.shape[0]
    wide = wa_ref.shape[1]
    pair = 2 * HEAD_DIM
    kind = kind_ref[0]
    x = x_ref[...]
    bias = bias_ref[...]
    qkv_ref[:, :wide] = (dot(x, wa_ref[...]) + bias[:, :wide]).astype(BF)
    qkv_ref[:, wide:] = (dot(x, wb_ref[...]) + bias[:, wide:]).astype(BF)
    for p in range(HEADS // 4):
        keys = qkv_ref[:, (3 * p + 1) * pair : (3 * p + 2) * pair]
        values = qkv_ref[:, (3 * p + 2) * pair : (3 * p + 3) * pair]

        def chunk_step(chunk, carry):
            rows = pl.ds(pl.multiple_of(chunk * SHORT, SHORT), SHORT)
            queries = qkv_ref[rows, 3 * p * pair : (3 * p + 1) * pair] * jnp.asarray(0.125, BF)
            mask = mask_row(kind, chunk, count)
            found = []
            stats = lse_ref[rows, :] if p > 0 else jnp.zeros((SHORT, 128), F32)
            lane = lax.broadcasted_iota(jnp.int32, stats.shape, 1)
            for head in range(2):
                mine = jnp.where(head_lanes(queries, head), queries, jnp.zeros_like(queries))
                scores = dot_nt(mine, keys) + mask
                top = jnp.max(scores, axis=1, keepdims=True)
                powers = jnp.exp(scores - top)
                total = jnp.sum(powers, axis=1, keepdims=True)
                probs = powers * (1.0 / total)
                found.append(dot(probs.astype(BF), values))
                stats = jnp.where(lane == 2 * p + head, top + jnp.log(total), stats)
            lse_ref[rows, :] = stats
            both = jnp.where(head_lanes(found[0], 0), found[0], found[1])
            context_ref[rows, p * pair : (p + 1) * pair] = both.astype(BF)
            return carry

        lax.fori_loop(0, count // SHORT, chunk_step, 0)
    partial_ref[...] = dot(context_ref[...], wo_ref[...]).astype(BF)


def attention_backward_kernel(
    kind_ref, d_second_ref, mine_ref, theirs_ref, sum_ref, vec_ref,
    x_ref, qkv_ref, context_ref, lse_ref, wa_ref, wb_ref, wo_ref,
    ga_ref, gb_ref, gout_ref, partial_ref, sums_ref, d_first_ref, norm_sums_ref,
    dbranch_ref, dcontext_ref, dqkv_ref, dk_ref, dv_ref,
):
    back_first(
        d_second_ref, mine_ref, theirs_ref, sum_ref, vec_ref,
        d_first_ref, dbranch_ref, norm_sums_ref,
    )
    count = x_ref.shape[0]
    wide = wa_ref.shape[1]
    pair = 2 * HEAD_DIM
    kind = kind_ref[0]
    d_branch = dbranch_ref[...]
    dcontext_ref[...] = dot_nt(d_branch, wo_ref[...]).astype(BF)
    gout_ref[...] = dot_tn(context_ref[...], d_branch).astype(BF)
    for p in range(HEADS // 4):
        keys = qkv_ref[:, (3 * p + 1) * pair : (3 * p + 2) * pair]
        values = qkv_ref[:, (3 * p + 2) * pair : (3 * p + 3) * pair]
        dk_ref[...] = jnp.zeros_like(dk_ref)
        dv_ref[...] = jnp.zeros_like(dv_ref)

        def chunk_step(chunk, carry):
            rows = pl.ds(pl.multiple_of(chunk * SHORT, SHORT), SHORT)
            queries = qkv_ref[rows, 3 * p * pair : (3 * p + 1) * pair] * jnp.asarray(0.125, BF)
            d_context = dcontext_ref[rows, p * pair : (p + 1) * pair]
            mask = mask_row(kind, chunk, count)
            stats = lse_ref[rows, :]
            found = []
            for head in range(2):
                mine = jnp.where(head_lanes(queries, head), queries, jnp.zeros_like(queries))
                theirs = jnp.where(
                    head_lanes(d_context, head), d_context, jnp.zeros_like(d_context)
                )
                lse = stats[:, 2 * p + head : 2 * p + head + 1]
                probs = jnp.exp(dot_nt(mine, keys) + mask - lse)
                d_probs = dot_nt(theirs, values)
                row_dot = jnp.sum(d_probs * probs, axis=1, keepdims=True)
                d_scores = (probs * (d_probs - row_dot)).astype(BF)
                found.append(
                    (
                        dot(d_scores, keys) * 0.125,
                        dot_tn(d_scores, queries),
                        dot_tn(probs.astype(BF), d_context),
                    )
                )
            merged = [
                jnp.where(head_lanes(one, 0), one, other) for one, other in zip(*found)
            ]
            dqkv_ref[rows, 3 * p * pair : (3 * p + 1) * pair] = merged[0].astype(BF)
            dk_ref[...] += merged[1]
            dv_ref[...] += merged[2]
            return carry

        lax.fori_loop(0, count // SHORT, chunk_step, 0)
        dqkv_ref[:, (3 * p + 1) * pair : (3 * p + 2) * pair] = dk_ref[...].astype(BF)
        dqkv_ref[:, (3 * p + 2) * pair : (3 * p + 3) * pair] = dv_ref[...].astype(BF)
    d_a = dqkv_ref[:, :wide]
    d_b = dqkv_ref[:, wide:]
    x = x_ref[...]
    ga_ref[...] = dot_tn(x, d_a).astype(BF)
    gb_ref[...] = dot_tn(x, d_b).astype(BF)
    partial_ref[...] = (dot_nt(d_a, wa_ref[...]) + dot_nt(d_b, wb_ref[...])).astype(BF)
    sums_ref[:, :wide] = jnp.sum(d_a.astype(F32), axis=0, keepdims=True)
    sums_ref[:, wide:] = jnp.sum(d_b.astype(F32), axis=0, keepdims=True)


def kernel_call(body, shapes, scratch, *operands):
    in_vmem = pl.BlockSpec(memory_space=pltpu.VMEM)
    in_smem = pl.BlockSpec(memory_space=pltpu.SMEM)
    return pl.pallas_call(
        body,
        out_shape=shapes,
        in_specs=[in_smem if value.dtype == jnp.int32 else in_vmem for value in operands],
        out_specs=[in_vmem] * len(shapes),
        scratch_shapes=scratch,
        compiler_params=pltpu.CompilerParams(vmem_limit_bytes=VMEM_LIMIT),
        cost_estimate=pl.CostEstimate(flops=0, bytes_accessed=0, transcendentals=0),
    )(*operands)


def attention(row_kind, inputs_b, w_a, w_b, bias, w_out):
    count, width = inputs_b.shape
    half = w_out.shape[0]
    shapes = [
        jax.ShapeDtypeStruct((count, width), BF),
        jax.ShapeDtypeStruct((count, 3 * half), BF),
        jax.ShapeDtypeStruct((count, half), BF),
        jax.ShapeDtypeStruct((count, 128), F32),
    ]
    return kernel_call(
        attention_kernel, shapes, [], row_kind, inputs_b, w_a, w_b, bias, w_out
    )


def attention_backward(
    row_kind, d_second, mine, theirs, first_sum, vec, inputs_b, qkv, context, lse, w_a, w_b, w_out
):
    count, width = inputs_b.shape
    half = w_out.shape[0]
    shapes = [
        jax.ShapeDtypeStruct(w_a.shape, BF),
        jax.ShapeDtypeStruct(w_b.shape, BF),
        jax.ShapeDtypeStruct(w_out.shape, BF),
        jax.ShapeDtypeStruct((count, width), BF),
        jax.ShapeDtypeStruct((1, 3 * half), F32),
        jax.ShapeDtypeStruct((count, width), F32),
        jax.ShapeDtypeStruct((8, width), F32),
    ]
    scratch = [
        pltpu.VMEM((count, width), BF),
        pltpu.VMEM((count, half), BF),
        pltpu.VMEM((count, 3 * half), BF),
        pltpu.VMEM((count, 2 * HEAD_DIM), F32),
        pltpu.VMEM((count, 2 * HEAD_DIM), F32),
    ]
    return kernel_call(
        attention_backward_kernel, shapes, scratch, row_kind, d_second, mine, theirs, first_sum,
        vec, inputs_b, qkv, context, lse, w_a, w_b, w_out,
    )


def norm_rows(base, mine, theirs, vec):
    shapes = [jax.ShapeDtypeStruct(base.shape, kind) for kind in (F32, F32, BF)]
    return kernel_call(norm_kernel, shapes, [], base, mine, theirs, vec)


def hidden_layer(x, mine, theirs, vec, bias, up0, up1, down):
    count, hidden = x.shape[0], down.shape[0]
    shapes = [jax.ShapeDtypeStruct(x.shape, kind) for kind in (F32, F32, BF)]
    shapes += [jax.ShapeDtypeStruct((count, hidden), BF)] * 2
    shapes.append(jax.ShapeDtypeStruct(x.shape, BF))
    return kernel_call(
        hidden_kernel, shapes, [], x, mine, theirs, vec, bias, up0, up1, down
    )


def back_second(upstream, total, vec, act):
    shapes = [
        jax.ShapeDtypeStruct(total.shape, F32),
        jax.ShapeDtypeStruct(total.shape, BF),
        jax.ShapeDtypeStruct((act.shape[1], total.shape[1]), BF),
        jax.ShapeDtypeStruct((8, total.shape[1]), F32),
    ]
    body = functools.partial(back_second_kernel, len(upstream) > 1)
    return kernel_call(body, shapes, [], *upstream, total, vec, act)


def back_hidden(d_ffn, slope, normed_b, down, up0, up1):
    count, hidden = slope.shape
    width = normed_b.shape[1]
    shapes = [
        jax.ShapeDtypeStruct(up0.shape, BF),
        jax.ShapeDtypeStruct(up1.shape, BF),
        jax.ShapeDtypeStruct((count, width), BF),
        jax.ShapeDtypeStruct((1, hidden), F32),
    ]
    scratch = [pltpu.VMEM((count, hidden), BF)]
    return kernel_call(
        back_hidden_kernel, shapes, scratch, d_ffn, slope, normed_b, down, up0, up1
    )


def hidden_order(width, hidden_rows):
    group = width // (2 * hidden_rows)
    target = jnp.arange(width)
    source = (
        (target % (width // 2)) // hidden_rows * (2 * hidden_rows)
        + target // (width // 2) * hidden_rows
        + target % hidden_rows
    )
    del group
    return jnp.arange(width)[:, None] == source[None, :]


def shards(tokens, row_kind, w_qkv, w_out, w_up, w_down, bias_vectors, gains, bias_up, cotangent):
    chips = Chips()
    sequence = Sequence()
    core = chips.core
    count = chips.count
    device = 2 * chips.chip + core
    row_type = row_kind[0]
    rows, width = w_out.shape[1:]
    hidden = w_up.shape[2]
    hidden_rows = w_down.shape[1]
    half = width // 2
    panels = hidden // 2 // width
    own = tokens.shape[0]
    order = hidden_order(width, hidden_rows)

    pairs = HEADS // 4
    lane = half // pairs
    plan = Plan()
    state = State()

    def ordered(mine, theirs):
        return jnp.where(core == 0, mine, theirs), jnp.where(core == 0, theirs, mine)

    def pack_qkv():
        cols = w_qkv.reshape(LAYERS, rows, 3, 2, pairs, lane)

        def side(which):
            return jnp.swapaxes(pick(cols, which, 3), 2, 3).reshape(LAYERS, rows, 3 * half)

        feature = jnp.arange(width)[None, :] - rows * device == jnp.arange(rows)[:, None]
        unit = jnp.arange(hidden // 2)[None, :] - hidden_rows * chips.chip
        unit = unit == jnp.arange(hidden_rows)[:, None]
        table = jnp.concatenate([bias_vectors, gains], axis=1).reshape(LAYERS * 8, rows)
        table = dot(table, feature.astype(BF)).astype(BF)
        units = dot(bias_up, unit.astype(BF)).astype(BF)
        got = swap(side(1 - core), 1)
        table = table + swap(table, 1)
        cols = merge(side(core), got, core, 1)
        for layer in range(LAYERS):
            last = cols[layer, :, :, width:].reshape(2 * rows, half)
            outs = jnp.concatenate([w_out[layer, :, :half], w_out[layer, :, half:]], axis=0)
            vectors = [table[8 * layer : 8 * layer + 8]]
            vectors += [units[layer : layer + 1, i * width :][:, :width] for i in range(panels)]
            vectors.append(jnp.zeros((8 - panels, width), BF))
            state.gathers[ATTN, layer] = Gather(
                chips, sequence, EARLY[layer],
                jnp.concatenate(
                    [
                        cols[layer, :, :, :width].reshape(2 * rows, width),
                        jnp.concatenate([last, outs], axis=1),
                        *vectors,
                    ],
                    axis=0,
                ),
            )
        sequence.mark([state.gathers[ATTN, layer].held for layer in range(LAYERS)])

    groups = hidden // width

    def pack_up():
        value = sequence.gate(w_up).reshape(LAYERS * rows, hidden)
        stacked = jnp.concatenate(
            [value[:, i * width : (i + 1) * width] for i in range(groups)], axis=0
        )
        stacked = dot(stacked, order.astype(BF)).astype(BF)
        mine, sent = ordered(stacked[:, :half], stacked[:, half:])
        first, second = ordered(mine, swap(sent, 1))
        for layer in range(LAYERS):
            parts = []
            for i in range(panels):
                for value in (first, second):
                    cut = [
                        value[((2 * i + j) * LAYERS + layer) * rows :][:rows] for j in range(2)
                    ]
                    parts.append(jnp.concatenate(cut, axis=1))
            state.gathers[FFN, layer] = Gather(
                chips, sequence, EARLY[LAYERS + layer],
                jnp.concatenate(parts + [w_down[layer]], axis=0),
            )
        sequence.mark([state.gathers[FFN, layer].held for layer in range(LAYERS)])

    def read_vectors(layer, table):
        table = jnp.sum(table.astype(F32), axis=0)
        vec = table[:8]
        bias_q, bias_v = (
            jnp.where(core == 0, vec[i : i + 1, :half], vec[i : i + 1, half:]) for i in range(2)
        )
        bias = []
        for p in range(pairs):
            cut = slice(p * lane, (p + 1) * lane)
            bias += [bias_q[:, cut], jnp.zeros((1, lane), F32), bias_v[:, cut]]
        state.vec[layer] = vec
        state.bias_qkv[layer] = jnp.concatenate(bias, axis=1)
        state.bias_up[layer] = jnp.concatenate(
            [table[8 + i : 9 + i] for i in range(panels)], axis=1
        )

    def tokens_start():
        value = sequence.gate(tokens)
        sequence.mark(value)
        state.pair_tokens = (value, swap(value, 1))

    def tokens_end():
        values = sequence.gate(state.pair_tokens)
        state.x_b[0] = jnp.concatenate(ordered(*values), axis=0)
        state.x[0] = state.x_b[0].astype(F32)
        sequence.mark(state.x_b[0])

    def cotangent_start():
        value = sequence.gate(cotangent)
        sequence.mark(value)
        state.pair_cotangent = (value, swap(value, 1))

    def cotangent_end():
        values = sequence.gate(state.pair_cotangent)
        state.upstream = (jnp.concatenate(ordered(*values), axis=0),)
        sequence.mark(state.upstream)

    def out_exchange(layer):
        ends = [0, 2 * rows, 4 * rows, 4 * rows + 16]
        first, second, table = state.gathers[ATTN, layer].finish(list(zip(ends[:-1], ends[1:])))
        w_b = second[:, :, :half].reshape(width, half)
        out_all = second[:, :, half:].reshape(2, count // 2, 2 * rows, half)
        sent = pick(out_all, 1 - core, 0)
        read_vectors(layer, table)
        sequence.mark((sent, w_b, state.vec[layer]))
        parts = ordered(pick(out_all, core, 0), swap(sent, 1))
        parts = [jnp.concatenate([part[:, :rows], part[:, rows:]], axis=2) for part in parts]
        full_out = jnp.stack(parts, axis=1).reshape(half, width)
        state.w_attn[layer] = (first.reshape(width, width), w_b, full_out)

    def hidden_weights(layer):
        ends = [2 * rows * i for i in range(panels + 1)]
        ends.append(ends[-1] + hidden_rows)
        *ups, down = state.gathers[FFN, layer].finish(list(zip(ends[:-1], ends[1:])))
        state.w_hidden[layer] = (
            down.reshape(hidden // 2, width), *(value.reshape(width, width) for value in ups)
        )

    def run_attention(layer):
        x_b, weights = sequence.gate((state.x_b[layer], state.w_attn[layer]))
        w_a, w_b, full_out = weights
        partial, *saved = attention(row_kind, x_b, w_a, w_b, state.bias_qkv[layer], full_out)
        sequence.mark(partial)
        state.w_attn[layer] = weights
        state.saved[layer] = (x_b, *saved)
        state.branch = (partial, swap(partial, 1))

    def run_hidden(layer):
        mine, theirs = sequence.gate(state.branch)
        down, up0, up1 = state.w_hidden[layer]
        first_sum, state.normed, *kept, partial = hidden_layer(
            state.x[layer], mine, theirs, state.vec[layer], state.bias_up[layer], up0, up1, down
        )
        sequence.mark(partial)
        state.first_sum[layer] = first_sum
        state.kept[layer] = kept
        state.branch = (partial, swap(partial, 1))

    def run_norm(layer):
        mine, theirs = sequence.gate(state.branch)
        second, x, x_b = norm_rows(state.normed, mine, theirs, state.vec[layer])
        state.second[layer], state.x[layer + 1], state.x_b[layer + 1] = second, x, x_b
        sequence.mark(second)

    def run_back_second(layer):
        upstream = sequence.gate(state.upstream)
        if layer < LAYERS - 1:
            upstream = (state.d_first, *upstream)
        act = state.kept[layer][1]
        d_second, d_ffn, g_down, sums = back_second(
            upstream, state.second[layer], state.vec[layer], act
        )
        state.d_second, state.d_ffn = d_second, d_ffn
        state.sums2[layer] = sums
        bundle = state.scatters[FFN, layer]
        bundle.start(0, [g_down.reshape(count, hidden_rows, width)])
        sequence.mark((d_ffn, bundle.sent))

    def run_back_hidden(layer):
        d_ffn = sequence.gate(state.d_ffn)
        normed_b, _, slope = state.kept[layer]
        *g_up, partial, units = back_hidden(d_ffn, slope, normed_b, *state.w_hidden[layer])
        bundle = state.scatters[FFN, layer]
        bundle.start(1, [value.reshape(count, 2 * rows, width) for value in g_up])
        sequence.mark((partial, bundle.sent))
        state.units[layer] = units
        state.branch = (partial, swap(partial, 1))

    def run_back_attention(layer):
        mine, theirs = sequence.gate(state.branch)
        x_b, qkv, context, lse = state.saved[layer]
        g_a, g_b, g_out, partial, sums, state.d_first, state.sums1[layer] = attention_backward(
            row_kind, state.d_second, mine, theirs, state.first_sum[layer], state.vec[layer],
            x_b, qkv, context, lse, *state.w_attn[layer],
        )
        sequence.mark(partial)
        state.pair[layer] = jnp.concatenate(
            [
                jnp.concatenate(
                    [sums[:, (3 * p + t) * lane :][:, :lane] for p in range(pairs)], axis=1
                )
                for t in (0, 2)
            ],
            axis=0,
        )
        if layer > 0:
            state.upstream = (partial, swap(partial, 1))
        else:
            mine, sent = ordered(partial[:own], partial[own:])
            state.upstream = (mine, swap(sent, 1))
        state.g_attn[layer] = (g_a, g_b, g_out)

    def sum_rows(layer):
        pair = state.pair[layer]
        nothing = jnp.zeros_like(pair)
        pair = jnp.concatenate(ordered(pair, nothing), axis=1)
        units = [state.units[layer][:, i * width :][:, :width] for i in range(panels)]
        small = jnp.concatenate([state.sums1[layer] + state.sums2[layer], pair, *units], axis=0)
        small = jnp.pad(small.astype(BF), ((0, 16 - small.shape[0]), (0, 0)))
        line = jnp.arange(16)[:, None]
        place = jnp.arange(width)[None, :]
        owner = jnp.where(
            line < 10, place // (2 * rows), ((line - 10) * width + place) // hidden_rows
        )
        mine = owner[None] == jnp.arange(count)[:, None, None]
        return jnp.where(mine, small[None], jnp.zeros((), BF))

    def back_terms(layer):
        g_a, g_b, g_out = sequence.gate(state.g_attn[layer])
        bundle = state.scatters[ATTN, layer]
        out_pair = g_out.reshape(count // 2, 2, rows, width)
        out_got = swap(pick(out_pair, 1 - core, 1), 1)
        out = merge(pick(out_pair, core, 1), out_got, core, 0).reshape(count, rows, width)
        g_b = g_b.reshape(count, 2 * rows, half)
        out = jnp.concatenate([out[:, :, :half], out[:, :, half:]], axis=1)
        rest = jnp.concatenate([g_b, out], axis=2)
        rest = jnp.concatenate([rest, sum_rows(layer)], axis=1)
        rest = lax.optimization_barrier(rest)
        bundle.start(0, [g_a.reshape(count, 2 * rows, width), rest])
        sequence.mark(bundle.sent)

    def grad_end():
        mine, theirs = sequence.gate(state.upstream)
        d_first = lax.dynamic_slice_in_dim(state.d_first, core * own, own)
        state.grad_tokens = d_first + (mine.astype(F32) + theirs.astype(F32))
        sequence.mark(state.grad_tokens)

    def mixed_end():
        value = sequence.gate(state.x_b[LAYERS])
        state.mixed = lax.dynamic_slice_in_dim(value, core * own, own)
        sequence.mark(state.mixed)

    def finish_hidden(layer):
        down, *ups = state.scatters[FFN, layer].finish()
        sides = [
            jnp.concatenate([up[side * rows :][:rows] for up in ups], axis=1)
            for side in range(2)
        ]
        mine, sent = ordered(*sides)
        state.up_pair[layer] = (mine, swap(sent, 1))
        state.down[layer] = down

    def end_hidden(layer):
        first, second = ordered(*sequence.gate(state.up_pair[layer]))
        stacked = jnp.concatenate(
            [
                jnp.concatenate(
                    [value[:, i * half : (i + 1) * half] for value in (first, second)], axis=1
                )
                for i in range(groups)
            ],
            axis=0,
        )
        stacked = lax.dot_general(
            stacked, order.astype(F32), (((1,), (1,)), ((), ())),
            precision=lax.Precision.HIGHEST, preferred_element_type=F32,
        )
        state.up[layer] = jnp.concatenate(
            [stacked[i * rows : (i + 1) * rows] for i in range(groups)], axis=1
        )
        sequence.mark(state.up[layer])

    def finish_attention(layer):
        first, rest = state.scatters[ATTN, layer].finish()
        last, out, small = rest[: 2 * rows, :half], rest[: 2 * rows, half:], rest[2 * rows :]
        out = jnp.concatenate([out[:rows], out[rows:]], axis=1)
        sides = [
            jnp.concatenate([value[side * rows :][:rows] for value in (first, last)], axis=1)
            for side in range(2)
        ]
        mine, sent = ordered(*sides)
        pair = jnp.pad(small[8:], ((0, 0), (0, mine.shape[1] - width)))
        sent = jnp.concatenate([sent, pair], axis=0)
        state.qkv_pair[layer] = (mine, swap(sent, 1))
        state.out[layer] = out
        state.small_rows[layer] = small

    def end_attention(layer):
        mine, theirs = sequence.gate(state.qkv_pair[layer])
        small = state.small_rows[layer]
        small = jnp.concatenate([theirs[rows : rows + 2, :width] + small[8:10], small], axis=0)
        features = lax.dynamic_slice_in_dim(small, rows * device, rows, axis=1)
        per_row = width // hidden_rows
        units = lax.dynamic_slice(
            small,
            (12 + chips.chip // per_row, hidden_rows * (chips.chip % per_row)),
            (1, hidden_rows),
        )
        state.vectors[layer] = features[:6]
        state.gains[layer] = features[6:8]
        state.unit_sums[layer] = units[0]
        values = ordered(mine, theirs[:rows])
        state.qkv[layer] = jnp.concatenate(
            [
                value[:, (3 * p + t) * lane :][:, :lane]
                for t in range(3)
                for value in values
                for p in range(pairs)
            ],
            axis=1,
        )
        sequence.mark(state.qkv[layer])

    def call(function, *args):
        return lambda: function(*args)

    low = len(chips.low)
    size = (1.0, 2.0)
    add = plan.add

    def pair_send(label):
        return [(label, (("p", 0.0),), 1)]

    def plane(length):
        return (("x", length), ("y", length))

    add("pq", 0, 6.0, [], pack_qkv)
    add("pu", 2, 3.0, [("g", ATTN, 0)], pack_up)
    add("tok", 8, 0.5, ["pu"], tokens_start, pair_send("x0"))
    add("te", 7, 1.5, ["x0"], tokens_end)
    add("cot", 9, 0.5, [("m", 1, 0)], cotangent_start, pair_send("ct"))
    add("ce", 9, 1.2, ["ct"], cotangent_end)
    bundles = [(ATTN, 0), (FFN, 0), (ATTN, 1), (FFN, 1)]
    for rank, (kind, layer) in enumerate(bundles):
        needs = ["pq" if kind == ATTN else "pu"]

        def start(kind=kind, layer=layer):
            state.gathers[kind, layer].start()

        def advance(kind=kind, layer=layer):
            state.gathers[kind, layer].advance()

        units = 7.0 / 3 if kind == ATTN else 4.0
        tops = [("top", 2), ("top", 1)]
        lows = [("low", step) for step in range(low)]
        early = EARLY[LAYERS * kind + layer]
        steps = lows[:1] + tops + lows[1:] if early else tops + lows
        need = None
        held = 1
        for number, (bits, step) in enumerate(steps):
            length = UNIT / 2 * units * held
            held *= 2
            if bits == "low":
                links = plane(length)
            elif step == 2:
                links = (("z", 2 * length), ("w", 5 * length + 1.5))
            else:
                links = (("z", 2 * length),)
            sent = ("gx", kind, layer, number)
            if number == 0:
                add(("g", kind, layer), 1 + rank, 3.5, needs, start, [(sent, links, 1)])
            else:
                add(
                    ("gs", kind, layer, number), 1 + rank, 1.0 + 0.1 * held + (2.8 if len(links) > 1 and links[1][0] == "w" else 1.4),
                    [need], advance, [(sent, links, 1)],
                )
            need = sent
        if kind == ATTN:
            add(
                ("go", layer), 1 + rank, 4.5, [need], call(out_exchange, layer),
                pair_send(("w", kind, layer)),
            )
        else:
            add(("w", kind, layer), 1 + rank, 1.6, [need], call(hidden_weights, layer))
    need = "te"
    for layer in range(LAYERS):
        add(
            ("m", 0, layer), 10, 12.7, [need, ("w", ATTN, layer)],
            call(run_attention, layer), pair_send(("p", 0, layer)),
        )
        add(
            ("m", 1, layer), 10, 6.0, [("p", 0, layer), ("w", FFN, layer)],
            call(run_hidden, layer), pair_send(("p", 1, layer)),
        )
        need = ("m", 2, layer)
        add(need, 10, 3.0, [("p", 1, layer)], call(run_norm, layer))
    add("mix", 20, 1.0, [need], mixed_end)

    needs = [need, "ce"]
    for layer in reversed(range(LAYERS)):
        state.scatters[FFN, layer] = Scatter(chips, sequence, 2, LATE[LAYERS + layer])
        state.scatters[ATTN, layer] = Scatter(chips, sequence, 1, LATE[layer])
        add(
            ("b", 0, layer), 10, 5.0, needs, call(run_back_second, layer),
            [(("r", FFN, layer, 0), plane(UNIT * 8), 1)],
        )
        add(
            ("b", 1, layer), 10, 6.5, [("b", 0, layer)], call(run_back_hidden, layer),
            [(("r", FFN, layer, 1), plane(UNIT * 8), 1)] + pair_send(("p", 2, layer)),
        )
        add(
            ("b", 2, layer), 10, 17.2, [("p", 2, layer)], call(run_back_attention, layer),
            pair_send(("p", 3, layer)),
        )
        add(
            ("b", 3, layer), 9.5, 6.0, [("b", 2, layer)], call(back_terms, layer),
            [(("r", ATTN, layer, 0), plane(UNIT * 28 / 3), 1)],
        )
        needs = [("p", 3, layer)]
        for kind in (FFN, ATTN):
            need = [("r", kind, layer, part) for part in range(1 + kind)]
            rank = 1 + 2 * (LAYERS - 1 - layer) + (kind == ATTN)

            def reduce(kind=kind, layer=layer):
                state.scatters[kind, layer].advance()

            units = 7.0 / 3 if kind == ATTN else 4.0
            tops = [("top", 1), ("top", 2)]
            lows = [("low", step) for step in range(low - 1)][::-1]
            late = LATE[LAYERS * kind + layer]
            steps = lows[:-1] + tops + lows[-1:] if late else lows + tops
            held = 2 * count // 4
            for number, (bits, step) in enumerate(steps):
                held //= 2
                length = UNIT / 2 * units * held
                cost = 1.0 + 0.1 * held
                if bits == "low":
                    cost, links = cost + 1.4, plane(length)
                elif step == 2:
                    cost, links = cost + 2.8, (("z", 2 * length), ("w", 5 * length + 1.5))
                else:
                    cost, links = cost + 1.4, (("z", 2 * length),)
                sent = ("rx", kind, layer, number)
                add(("rs", kind, layer, number), rank, cost, need, reduce, [(sent, links, 1)])
                need = [sent]
            last = finish_hidden if kind == FFN else finish_attention
            add(
                ("rf", kind, layer), 19, 2.0, need, call(last, layer),
                pair_send(("re", kind, layer)),
            )
            last = end_hidden if kind == FFN else end_attention
            add(("ro", kind, layer), 20, 2.5, [("re", kind, layer)], call(last, layer))
    add("grad", 18, 1.2, needs, grad_end)
    plan.run()

    def stacked(values):
        return jnp.stack([values[layer] for layer in range(LAYERS)])

    return (
        state.mixed,
        state.grad_tokens,
        stacked(state.qkv),
        stacked(state.out),
        stacked(state.up),
        stacked(state.down),
        stacked(state.vectors),
        stacked(state.gains),
        stacked(state.unit_sums),
    )


def solution(mesh):
    placed = (
        P("fsdp", None),
        P("fsdp"),
        P(None, "fsdp", None),
        P(None, "fsdp", None),
        P(None, "fsdp", None),
        P(None, "fsdp", None),
        P(None, None, "fsdp"),
        P(None, None, "fsdp"),
        P(None, "fsdp"),
        P("fsdp", None),
    )
    return jax.shard_map(
        shards,
        mesh=mesh,
        in_specs=placed,
        out_specs=(
            P("fsdp", None),
            P("fsdp", None),
            P(None, "fsdp", None),
            P(None, "fsdp", None),
            P(None, "fsdp", None),
            P(None, "fsdp", None),
            P(None, None, "fsdp"),
            P(None, None, "fsdp"),
            P(None, "fsdp"),
        ),
        check_vma=False,
    )
```
